32 devices in a mesh: dp: 2 (over y), ctx: 4 (over x, core), tensor: 4 (over z).
Axes of the slice: x: 2, y: 2, z: 4, core: 2. Of those that a mesh axis runs over, the one named last changes fastest.
Arguments:
- tokens: bfloat16 [8, 320, 1024], P('dp', 'ctx'), may hold values from -6 to 6
- keep_mask: int32 [8, 256], P('dp'), may hold values from 0 to 1, as said below
- cotangent: bfloat16 [8, 320, 1024], P('dp', 'ctx'), may hold values from -6 to 6
- first_gain: bfloat16 [1024], P(('dp', 'ctx')), may hold values from 0.099609375 to 1.8984375
- first_shift: bfloat16 [1024], P(('dp', 'ctx')), may hold values from -4 to 4
- attend_in: bfloat16 [1024, 3, 1024], P(('dp', 'ctx'), None, 'tensor'), may hold values from -0.1875 to 0.1875
- attend_bias: bfloat16 [2, 16, 64], P(None, 'tensor', ('dp', 'ctx')), may hold values from -0.59765625 to 0.59765625
- attend_out: bfloat16 [1024, 1024], P('tensor', ('dp', 'ctx')), may hold values from -0.75 to 0.75
- out_bias: bfloat16 [1024], P(('dp', 'ctx')), may hold values from -4 to 4
- second_gain: bfloat16 [1024], P(('dp', 'ctx')), may hold values from 0.099609375 to 1.8984375
- second_shift: bfloat16 [1024], P(('dp', 'ctx')), may hold values from -4 to 4
- expand_in: bfloat16 [1024, 4096], P(('dp', 'ctx'), 'tensor'), may hold values from -0.1875 to 0.1875
- expand_bias: bfloat16 [64, 64], P('tensor', ('dp', 'ctx')), may hold values from -3 to 3
- contract_out: bfloat16 [4096, 1024], P('tensor', ('dp', 'ctx')), may hold values from -0.09375 to 0.09375
- contract_bias: bfloat16 [1024], P(('dp', 'ctx')), may hold values from -4 to 4
Outputs:
- block_out: bfloat16 [8, 320, 1024], P('dp', 'ctx')
- tokens_grad: bfloat16 [8, 320, 1024], P('dp', 'ctx')
- first_gain_grad: float32 [1024], P(('dp', 'ctx'))
- first_shift_grad: float32 [1024], P(('dp', 'ctx'))
- attend_in_grad: float32 [1024, 3, 1024], P(('dp', 'ctx'), None, 'tensor')
- attend_bias_grad: float32 [2, 16, 64], P(None, 'tensor', ('dp', 'ctx'))
- attend_out_grad: float32 [1024, 1024], P('tensor', ('dp', 'ctx'))
- out_bias_grad: float32 [1024], P(('dp', 'ctx'))
- second_gain_grad: float32 [1024], P(('dp', 'ctx'))
- second_shift_grad: float32 [1024], P(('dp', 'ctx'))
- expand_in_grad: float32 [1024, 4096], P(('dp', 'ctx'), 'tensor')
- expand_bias_grad: float32 [64, 64], P('tensor', ('dp', 'ctx'))
- contract_out_grad: float32 [4096, 1024], P('tensor', ('dp', 'ctx'))
- contract_bias_grad: float32 [1024], P(('dp', 'ctx'))
The draws below stay inside these ranges and needn't reach their ends.
Inputs may be any that keep to these rules, and one draw needn't show every extreme that they name: `keep_mask`: in every aligned block of 2 images one image, drawn from the seed, keeps all 256 patches. The kept patches' tokens fill the slots from 64 on; the slots after them are padding.
All inputs are finite; a program needn't handle non-finite values.
Results may differ from the reference program's by a relative error of at most 0.02.
Values may be sent and summed in bfloat16 or wider, within the bound.
A program may use at most 64 MiB of HBM per device.

```python
import jax
import jax.numpy as jnp
from jax import lax

D = 1024
HEADS = 16
HD = 64
FF = 4096
BUFFER = 64
PATCHES = 256
IMG_MB = 2
SLOTS = 320
IMAGES = 8


def draw_keep_mask(key, part):
    key = jax.random.fold_in(key, 11)
    rate_key, bit_key, pick_key = jax.random.split(key, 3)
    rates = jax.random.randint(rate_key, (IMAGES, 1), 77, 257)
    bits = jax.random.randint(bit_key, (IMAGES, PATCHES), 0, 256)
    chosen = jax.random.randint(pick_key, (IMAGES // IMG_MB, 1), 0, IMG_MB)
    position = jnp.arange(IMG_MB)[None, :]
    complete = (position == chosen).reshape(IMAGES, 1)
    kept = jnp.logical_or(bits < rates, complete)
    return kept.astype(jnp.int32)


def shard_levels(stream_key, dims, cuts, low, high):
    def one(axis_at, parts):
        heights = jax.random.uniform(jax.random.fold_in(jax.random.fold_in(stream_key, 6), axis_at), (parts,), jnp.float32, low / len(cuts), high / len(cuts))
        return jnp.repeat(jnp.exp(heights), dims[axis_at] // parts).reshape((-1,) + (1,) * (len(dims) - axis_at - 1))

    level = one(*cuts[0])
    for cut in cuts[1:]:
        level = level * one(*cut)
    return level


def centred(key, shape, scale, bound, cuts=(), held_as=jnp.bfloat16):
    values = jax.random.normal(key, shape, jnp.float32) * scale
    if len(cuts) > 0:
        values = shard_levels(key, shape, cuts, -0.22, 0.18) * values
    return jnp.clip(values, min=-bound, max=bound).astype(held_as)


def setup_inputs(seed: int = 0) -> dict:
    seeds = jax.random.split(jax.random.key(seed), 16)
    tokens = centred(seeds[0], (IMAGES, SLOTS, D), 1.0, 6.0, ((0, 2), (1, 4)))
    keep_mask = draw_keep_mask(jax.random.fold_in(seeds[15], 71), 0)
    cotangent = centred(seeds[2], (IMAGES, SLOTS, D), 1.0, 6.0, ((0, 2), (1, 4)))
    first_gain = jnp.clip(1.0 + 0.18 * jax.random.normal(seeds[3], (D,), jnp.float32), 0.099609375, 1.8984375).astype(jnp.bfloat16)
    first_shift = centred(seeds[4], (D,), 0.3, 4.0, ((0, 8),))
    attend_in = centred(seeds[5], (D, 3, D), D ** -0.5, 0.1875, ((0, 8), (2, 4)))
    attend_bias = centred(seeds[6], (2, HEADS, HD), 0.1, 0.59765625, ((1, 4), (2, 8)))
    attend_out = centred(seeds[7], (D, D), (D // 16) ** -0.5, 0.75, ((0, 4), (1, 8)))
    out_bias = centred(seeds[8], (D,), 0.3, 4.0, ((0, 8),))
    second_gain = jnp.clip(1.0 + 0.18 * jax.random.normal(seeds[9], (D,), jnp.float32), 0.099609375, 1.8984375).astype(jnp.bfloat16)
    second_shift = centred(seeds[10], (D,), 0.3, 4.0, ((0, 8),))
    expand_in = centred(seeds[11], (D, FF), D ** -0.5, 0.1875, ((0, 8), (1, 4)))
    expand_bias = centred(seeds[12], (FF // HD, HD), 0.5, 3.0, ((0, 4), (1, 8)))
    contract_out = centred(seeds[13], (FF, D), FF ** -0.5, 0.09375, ((0, 4), (1, 8)))
    contract_bias = centred(seeds[14], (D,), 0.3, 4.0, ((0, 8),))
    return dict(tokens=tokens, keep_mask=keep_mask, cotangent=cotangent, first_gain=first_gain, first_shift=first_shift, attend_in=attend_in, attend_bias=attend_bias, attend_out=attend_out, out_bias=out_bias, second_gain=second_gain, second_shift=second_shift, expand_in=expand_in, expand_bias=expand_bias, contract_out=contract_out, contract_bias=contract_bias)


@jax.custom_vjp
def low(v):
    return lax.optimization_barrier(v.astype(jnp.bfloat16)).astype(jnp.float32)

@jax.custom_vjp
def low_back(v):
    return v

def low_keep(v):
    return (low(v), None)

def low_pass(kept, grad):
    return (grad,)

def back_keep(v):
    return (v, None)

def back_low(kept, grad):
    return (low(grad),)
low.defvjp(low_keep, low_pass)
low_back.defvjp(back_keep, back_low)
highest = lax.Precision.HIGHEST
eps = 1e-06
neg_big = -1e+30
root_half = 0.7071067811865476

def layer_norm(values, gain, shift):
    mean = lax.optimization_barrier(jnp.mean(values, axis=-1, keepdims=True))
    centered = values - mean
    spread = lax.optimization_barrier(jnp.mean(centered * centered, axis=-1, keepdims=True))
    return centered * lax.rsqrt(spread + eps) * gain + shift

def group_forward(params, images, lengths):
    first_gain, first_shift, attend_in, attend_bias, attend_out, out_bias, second_gain, second_shift, expand_in, expand_bias, contract_out, contract_bias = params
    count = images.shape[0]
    hidden_one = low(layer_norm(images, first_gain, first_shift))
    projected = jnp.einsum('gsd,dcf->gscf', hidden_one, attend_in, precision=highest)
    queries = low(low_back(projected[:, :, 0] + attend_bias[0].reshape(-1)))
    keys = low(low_back(projected[:, :, 1]))
    values = low(low_back(projected[:, :, 2] + attend_bias[1].reshape(-1)))
    query_heads = queries.reshape(count, SLOTS, HEADS, HD)
    key_heads = keys.reshape(count, SLOTS, HEADS, HD)
    value_heads = values.reshape(count, SLOTS, HEADS, HD)
    scores = low_back(jnp.einsum('gqhc,gkhc->ghqk', query_heads, key_heads, precision=highest) * HD ** (-0.5))
    slot_ids = jnp.arange(SLOTS)
    live = slot_ids[None, :] < lengths[:, None]
    scores = jnp.where(live[:, None, None, :], scores, neg_big)
    top = lax.optimization_barrier(jnp.max(scores, axis=-1, keepdims=True))
    expo = jnp.exp(scores - top)
    probs = low(expo / lax.optimization_barrier(jnp.sum(expo, axis=-1, keepdims=True)))
    mixed = jnp.einsum('ghqk,gkhc->gqhc', probs, value_heads, precision=highest).reshape(count, SLOTS, D)
    mixed = low(low_back(mixed))
    first = images + low_back(jnp.einsum('gsf,fd->gsd', mixed, attend_out, precision=highest)) + out_bias
    hidden_two = low(layer_norm(first, second_gain, second_shift))
    inner = low_back(jnp.einsum('gsd,df->gsf', hidden_two, expand_in, precision=highest) + expand_bias.reshape(-1))
    activ = low(0.5 * inner * (1.0 + lax.erf(inner * root_half)))
    second = first + low_back(jnp.einsum('gsf,fd->gsd', activ, contract_out, precision=highest)) + contract_bias
    return jnp.where(live[:, :, None], second, 0.0)

def reference(tokens, keep_mask, cotangent, first_gain, first_shift, attend_in, attend_bias, attend_out, out_bias, second_gain, second_shift, expand_in, expand_bias, contract_out, contract_bias):
    lengths = (BUFFER + lax.optimization_barrier(jnp.sum(keep_mask, axis=1))).astype(jnp.int32)
    params = (first_gain.astype(jnp.float32), first_shift.astype(jnp.float32), attend_in.astype(jnp.float32), attend_bias.astype(jnp.float32), attend_out.astype(jnp.float32), out_bias.astype(jnp.float32), second_gain.astype(jnp.float32), second_shift.astype(jnp.float32), expand_in.astype(jnp.float32), expand_bias.astype(jnp.float32), contract_out.astype(jnp.float32), contract_bias.astype(jnp.float32))
    groups = IMAGES // IMG_MB
    images = tokens.astype(jnp.float32).reshape(groups, IMG_MB, SLOTS, D)
    group_lengths = lengths.reshape(groups, IMG_MB)
    checked = jax.checkpoint(group_forward)

    def forward(weights, pictures):

        def one_group(pair):
            return checked(weights, pair[0], pair[1])
        return lax.map(one_group, (pictures, group_lengths))
    second, pullback = jax.vjp(forward, params, images)
    grads, image_grads = pullback(cotangent.astype(jnp.float32).reshape(second.shape))
    return (second.reshape(IMAGES, SLOTS, D).astype(jnp.bfloat16), image_grads.reshape(IMAGES, SLOTS, D).astype(jnp.bfloat16), grads[0], grads[1], grads[2], grads[3], grads[4], grads[5], grads[6], grads[7], grads[8], grads[9], grads[10], grads[11])
```

```python
import functools

import jax
import jax.numpy as jnp
from jax import lax
from jax.experimental import pallas as pl
from jax.experimental.pallas import tpu as pltpu
from jax.sharding import PartitionSpec as P

HD = 64
BUFFER = 64
LANES = 128
ROWS = 16
TILE = 256
MESH = pl.DeviceIdType.MESH
F32 = jnp.float32
BF16 = jnp.bfloat16

eps = 1e-06
neg_big = -1e30
root_half = 0.7071067811865476
inv_root_two_pi = 0.3989422804014327


def flip(index, bits):
    out, bit = index, 1
    while bit <= bits:
        if bits & bit:
            out = out + bit - 2 * bit * lax.rem(lax.div(index, bit), 2)
        bit *= 2
    return out


def nn(left, right):
    return jnp.dot(left, right, preferred_element_type=F32)


def nt(left, right):
    return lax.dot_general(left, right, (((1,), (1,)), ((), ())), preferred_element_type=F32)


def tn(left, right):
    return lax.dot_general(left, right, (((0,), (0,)), ((), ())), preferred_element_type=F32)


def norm_parts(values):
    mean = jnp.mean(values, axis=-1, keepdims=True)
    centered = values - mean
    spread = jnp.mean(centered * centered, axis=-1, keepdims=True)
    inv = lax.rsqrt(spread + eps)
    return centered * inv, inv


def block_kernel(
    sizes,
    tok,
    cot,
    keep,
    win,
    wot,
    wup,
    wdt,
    vec,
    out_block,
    out_tokens,
    out_win,
    out_wot,
    out_wup,
    out_wdt,
    out_vec,
    g_win,
    g_wot,
    g_wup,
    g_wdt,
    g_vec,
    vx,
    n1,
    h1,
    qkv,
    wq,
    wk,
    stat,
    alng,
    mixed,
    first,
    h2,
    ga,
    act,
    gi,
    part2,
    parts,
    part1,
    recv2,
    recvs,
    recv1,
    gfirst,
    gdown,
    gball,
    gm,
    do,
    dqkv,
    gv,
    vr_sib,
    vr_plane,
    vr_z,
    b_win,
    b_wot,
    b_wup,
    b_wdt,
    s_win,
    s_wot,
    s_wup,
    s_wdt,
    t_win,
    t_wot,
    t_wup,
    t_wdt,
    r_win,
    r_wot,
    r_wup,
    r_wdt,
    send_sem,
    recv_sem,
    local_sem,
):
    n_dp, n_ctx, n_t, images, slots, width, wide, hidden, part_rows, cut = sizes
    rows = images * slots
    total = slots * n_ctx
    heads = wide // HD
    half = n_ctx // 2
    group = n_dp * half
    scale = HD ** (-0.5)
    dp = lax.axis_index("dp")
    ctx = lax.axis_index("ctx")
    z = lax.axis_index("tensor")
    high, core = lax.div(ctx, 2), lax.rem(ctx, 2)
    me = dp * half + high
    sib = (dp, flip(ctx, 1), z)

    def plane(k):
        other = flip(me, k)
        return (lax.div(other, half), lax.rem(other, half) * 2 + core, z)

    def ctx_at(k):
        return flip(high, k) * 2 + core

    def zpeer(k):
        return (dp, ctx, flip(z, k))

    own = pl.ds(pl.multiple_of(ctx * slots, ROWS), slots)
    mine = pl.ds(pl.multiple_of(z * slots, ROWS), slots)

    def slot_at(index):
        return pl.ds(pl.multiple_of(index * slots, ROWS), slots)

    def lane_at(index, size):
        return pl.ds(pl.multiple_of(index * size, size), size)

    count = [0, 0]
    pending = []

    def send(src, dst, device):
        index = count[0]
        count[0] += 1
        copy = pltpu.make_async_remote_copy(
            src_ref=src,
            dst_ref=dst,
            send_sem=send_sem.at[index],
            recv_sem=recv_sem.at[index],
            device_id=device,
            device_id_type=MESH,
        )
        copy.start()
        pending.append(copy)
        return copy

    def complete(copy):
        pending[:] = [other for other in pending if other is not copy]
        copy.wait()

    def local(src, dst):
        index = count[1]
        count[1] += 1
        copy = pltpu.make_async_copy(src, dst, local_sem.at[index])
        copy.start()
        return copy

    planes = range(1, group)
    zs = range(1, n_t)

    barrier = pltpu.get_barrier_semaphore()
    for device in [plane(k) for k in planes] + [sib] + [zpeer(k) for k in zs]:
        pl.semaphore_signal(barrier, inc=1, device_id=device, device_id_type=MESH)
    pl.semaphore_wait(barrier, group + n_t - 1)

    def gather_start(src, at):
        keep_own = local(src, at(me, core))
        far = [send(src, at(me, core), plane(k)) for k in planes]
        near = send(src, at(me, core), sib)
        return keep_own, far, near

    def gather_forward(started, at):
        started[0].wait()
        out = []
        for k in planes:
            started[1][k - 1].wait_recv()
            there = at(flip(me, k), core)
            out.append(send(there, there, sib))
        return out

    def gather_finish(started, passed):
        started[2].wait_recv()
        for copy in passed:
            copy.wait_recv()

    def ctx_start(at):
        far = [send(at(ctx), at(ctx), (dp, ctx_at(k), z)) for k in range(1, half)]
        return far, send(at(ctx), at(ctx), sib)

    def ctx_forward(started, at):
        out = []
        for k in range(1, half):
            started[0][k - 1].wait_recv()
            out.append(send(at(ctx_at(k)), at(ctx_at(k)), sib))
        return out

    def ctx_finish(started, passed):
        started[1].wait_recv()
        for copy in passed:
            copy.wait_recv()

    def at_win(m, c):
        return g_win.at[m, c]

    def at_wot(m, c):
        return g_wot.at[m, c, :, lane_at(z, wide)]

    def at_wup(m, c):
        return g_wup.at[m, c]

    def at_wdt(m, c):
        return g_wdt.at[m, c]

    def at_vec(m, c):
        return g_vec.at[m, c]

    gv[...] = jnp.zeros_like(gv)
    vec_started = gather_start(vec, at_vec)
    win_started = gather_start(win, at_win)
    wot_started = gather_start(wot, at_wot)

    def first_norm(step, carry):
        at = pl.ds(pl.multiple_of(step * ROWS, ROWS), ROWS)
        normed, _ = norm_parts(tok[at, :].astype(F32))
        n1[at, :] = normed
        return carry

    lax.fori_loop(0, rows // ROWS, first_norm, 0)
    wup_started = gather_start(wup, at_wup)

    vec_passed = gather_forward(vec_started, at_vec)
    gather_finish(vec_started, vec_passed)
    piece = width // (2 * group)
    source = lax.broadcasted_iota(jnp.int32, (LANES, width), 0)
    target = lax.broadcasted_iota(jnp.int32, (LANES, width), 1)
    unit = (target // HD == source // cut).astype(jnp.int32)
    inside = target % HD - source % cut

    def place(index, carry):
        by_width, by_unit = carry
        shares = g_vec[lax.div(index, 2), lax.rem(index, 2)]
        one = jnp.where(target - source == index * piece, 1.0, 0.0).astype(BF16)
        two = jnp.where((unit == 1) & (inside == index * cut), 1.0, 0.0).astype(BF16)
        return by_width + nn(shares, one), by_unit + nn(shares, two)

    zero = jnp.zeros((ROWS, width), F32)
    by_width, by_unit = lax.fori_loop(0, 2 * group, place, (zero, zero))
    row_id = lax.broadcasted_iota(jnp.int32, (ROWS, width), 0)
    vx[...] = jnp.where(row_id < 6, by_width, by_unit)

    def first_hidden(step, carry):
        at = pl.ds(pl.multiple_of(step * ROWS, ROWS), ROWS)
        h1[at, :] = (n1[at, :] * vx[0:1, :] + vx[1:2, :]).astype(BF16)
        return carry

    lax.fori_loop(0, rows // ROWS, first_hidden, 0)

    lengths = BUFFER + jnp.sum(keep[...], axis=1, keepdims=True)
    slot_id = lax.broadcasted_iota(jnp.int32, (slots, 1), 0) + ctx * slots
    key_id = lax.broadcasted_iota(jnp.int32, (1, total), 1)
    head_of = lax.broadcasted_iota(jnp.int32, (slots, wide), 1) // HD
    spot = lax.broadcasted_iota(jnp.int32, (slots, total), 1) == slot_id

    def stack_heads(block):
        wider = block.astype(F32)
        return jnp.concatenate(
            [jnp.where(head_of == h, wider, 0.0).astype(BF16) for h in range(heads)], axis=0
        )

    def pick_heads(block):
        out = jnp.where(head_of == 0, block[0:slots], 0.0)
        for h in range(1, heads):
            out = jnp.where(head_of == h, block[h * slots : (h + 1) * slots], out)
        return out

    def put_rows(ref, image, column):
        for h in range(heads):
            part = jnp.where(spot, column[h * slots : (h + 1) * slots], 0.0)
            line = image * heads + h
            ref[ctx, line : line + 1, :] = jnp.sum(part, axis=0, keepdims=True)

    win_passed = gather_forward(win_started, at_win)
    wot_passed = gather_forward(wot_started, at_wot)
    def wot_half(index, c):
        return g_wot.at[:, c, :, lane_at(index, wide)]

    wot_z = [send(wot_half(z, core), wot_half(z, core), zpeer(k)) for k in zs]
    gather_finish(win_started, win_passed)

    def project(j, bias):
        weight = g_win[:, :, :, j * wide : (j + 1) * wide].reshape(width, wide)
        out = nn(h1[...], weight)
        if bias is not None:
            out = out + vx[bias : bias + 1, 0:wide]
        qkv[:, own, j * wide : (j + 1) * wide] = out.astype(BF16).reshape(images, slots, wide)

    project(1, None)
    project(2, 8)

    def at_kv(index):
        return qkv.at[:, slot_at(index), wide : 3 * wide]

    def at_q(index):
        return qkv.at[:, slot_at(index), 0:wide]

    kv_started = ctx_start(at_kv)
    project(0, 7)
    q_started = ctx_start(at_q)
    wdt_started = gather_start(wdt, at_wdt)
    kv_passed = ctx_forward(kv_started, at_kv)
    ctx_finish(kv_started, kv_passed)

    def at_mixed(index, image):
        return mixed.at[image * slots : (image + 1) * slots, lane_at(index, wide)]

    mixed_sent = []
    for image in range(images):
        key_live = key_id < lengths[image : image + 1, :]
        stacked = stack_heads(qkv[image, own, 0:wide])
        scores = nt(stacked, qkv[image, :, wide : 2 * wide]) * scale
        scores = jnp.where(key_live, scores, neg_big)
        top = jnp.max(scores, axis=-1, keepdims=True)
        expo = jnp.exp(scores - top)
        whole = jnp.sum(expo, axis=-1, keepdims=True)
        probs = expo / whole
        wq[image] = probs
        put_rows(stat, image, top + jnp.log(whole))
        out = nn(probs.astype(BF16), qkv[image, :, 2 * wide : 3 * wide])
        mixed[image * slots : (image + 1) * slots, lane_at(z, wide)] = pick_heads(out).astype(BF16)
        mixed_sent.append(
            [send(at_mixed(z, image), at_mixed(z, image), zpeer(k)) for k in zs]
        )

    def at_stat(index):
        return stat.at[index]

    stat_started = ctx_start(at_stat)
    q_passed = ctx_forward(q_started, at_q)
    stat_passed = ctx_forward(stat_started, at_stat)
    gather_finish(wot_started, wot_passed)
    wup_passed = gather_forward(wup_started, at_wup)
    wot_more = []
    for k in zs:
        wot_z[k - 1].wait_recv()
        there = wot_half(flip(z, k), core)
        wot_more.append(send(there, there, sib))
    wdt_passed = gather_forward(wdt_started, at_wdt)

    row_live = []
    for image in range(images):
        row_live.append(slot_id < lengths[image : image + 1, :])
        at = slice(image * slots, (image + 1) * slots)
        gdown[at, :] = jnp.where(row_live[image], cot[at, :].astype(F32), 0.0).astype(BF16)
    gather_finish(wdt_started, wdt_passed)

    def down_back(step, carry):
        at = lane_at(step, TILE)
        ga[:, at] = nn(gdown[...], g_wdt[:, :, :, at].reshape(width, TILE))
        return carry

    lax.fori_loop(0, hidden // TILE, down_back, 0)

    ctx_finish(q_started, q_passed)
    ctx_finish(stat_started, stat_passed)
    for image in range(images):
        stacked = stack_heads(qkv[image, own, wide : 2 * wide])
        scores = nt(stacked, qkv[image, :, 0:wide]) * scale
        for h in range(heads):
            line = image * heads + h
            level = stat[0, line : line + 1, :]
            for other in range(1, n_ctx):
                level = level + stat[other, line : line + 1, :]
            block = scores[h * slots : (h + 1) * slots]
            block = jnp.where(row_live[image], block, neg_big)
            wk[image, h * slots : (h + 1) * slots, :] = jnp.exp(block - level)

    for copies in mixed_sent:
        for copy in copies:
            copy.wait_recv()
    for copy in wot_more:
        copy.wait_recv()

    def project_out(step, carry):
        some = group // (width // TILE)
        weight = g_wot[pl.ds(step * some, some)].reshape(TILE, n_t * wide)
        first[:, lane_at(step, TILE)] = nt(mixed[...], weight)
        return carry

    lax.fori_loop(0, width // TILE, project_out, 0)

    def second_norm(step, carry):
        at = pl.ds(pl.multiple_of(step * ROWS, ROWS), ROWS)
        value = tok[at, :].astype(F32) + first[at, :] + vx[2:3, :]
        first[at, :] = value
        normed, _ = norm_parts(value)
        h2[at, :] = (normed * vx[3:4, :] + vx[4:5, :]).astype(BF16)
        return carry

    lax.fori_loop(0, rows // ROWS, second_norm, 0)

    gather_finish(wup_started, wup_passed)

    def expand(step, carry):
        at = lane_at(step, TILE)
        inner = nn(h2[...], g_wup[:, :, :, at].reshape(width, TILE)) + vx[6:7, at]
        share = 0.5 * (1.0 + lax.erf(inner * root_half))
        act[:, at] = (inner * share).astype(BF16)
        slope = share + inner * jnp.exp(-0.5 * inner * inner) * inv_root_two_pi
        grad = (ga[:, at] * slope).astype(BF16)
        gi[:, at] = grad
        gv[8:9, at] = jnp.sum(grad.astype(F32), axis=0, keepdims=True)
        return carry

    lax.fori_loop(0, hidden // TILE, expand, 0)

    def up_back(step, carry):
        some = group // (width // TILE)
        weight = g_wup[pl.ds(step * some, some)].reshape(TILE, hidden)
        part2[:, lane_at(step, TILE)] = nt(gi[...], weight).astype(BF16)
        return carry

    lax.fori_loop(0, width // TILE, up_back, 0)

    def scatter(part, recv):
        return [
            send(part.at[slot_at(flip(z, k)), :], recv.at[k - 1], zpeer(k)) for k in reversed(zs)
        ]

    def arrived(part, recv, at):
        out = part[pl.ds(pl.multiple_of(z * slots + at, ROWS), ROWS), :].astype(F32)
        for k in zs:
            out = out + recv[k - 1, pl.ds(pl.multiple_of(at, ROWS), ROWS), :].astype(F32)
        return out

    sent2 = scatter(part2, recv2)

    def wide_grad(buf, left, right, lanes):
        def one(step, carry):
            at = lane_at(step, TILE)
            out = tn(left[...], right[:, at]).astype(BF16)
            buf[:, :, :, at] = out.reshape(group, 2, piece, TILE)
            return carry

        lax.fori_loop(0, lanes // TILE, one, 0)

    def grad_near(buf, near):
        return send(buf.at[:, 1 - core], near, sib)

    def grad_far(copy, buf, near, both, recv):
        copy.wait_recv()

        def one(m, carry):
            both[m] = (buf[m, core].astype(F32) + near[m].astype(F32)).astype(BF16)
            return carry

        lax.fori_loop(0, group, one, 0)
        return [send(both.at[flip(me, k)], recv.at[k - 1], plane(k)) for k in planes]

    def grad_last(copies, both, recv, out):
        for copy in copies:
            copy.wait_recv()
        value = both[me].astype(F32)
        for k in planes:
            value = value + recv[k - 1].astype(F32)
        out[...] = value

    def contract(step, carry):
        some = group // (width // TILE)
        weight = g_wdt[pl.ds(step * some, some)].reshape(TILE, hidden)
        parts[:, lane_at(step, TILE)] = nt(act[...], weight).astype(BF16)
        return carry

    lax.fori_loop(0, width // TILE, contract, 0)
    sents = scatter(parts, recvs)
    wide_grad(b_wdt, gdown, act, hidden)
    wdt_near = grad_near(b_wdt, s_wdt)
    wide_grad(b_wup, h2, gi, hidden)
    wup_near = grad_near(b_wup, s_wup)
    wdt_far = grad_far(wdt_near, b_wdt, s_wdt, t_wdt, r_wdt)
    wup_far = grad_far(wup_near, b_wup, s_wup, t_wup, r_wup)

    for copy in sent2:
        copy.wait_recv()
    own_live = slot_id < jnp.sum(
        jnp.where(lax.broadcasted_iota(jnp.int32, (images, 1), 0) == z, lengths, 0),
        axis=0,
        keepdims=True,
    )

    def add_line(line, value):
        gv[line : line + 1, :] += jnp.sum(value, axis=0, keepdims=True)

    def second_back(step, carry):
        at = step * ROWS
        here = pl.ds(pl.multiple_of(z * slots + at, ROWS), ROWS)
        grad = arrived(part2, recv2, at)
        normed, inv = norm_parts(first[here, :])
        add_line(3, grad * normed)
        add_line(4, grad)
        scaled = grad * vx[3:4, :]
        inner = (
            scaled
            - jnp.mean(scaled, axis=-1, keepdims=True)
            - normed * jnp.mean(scaled * normed, axis=-1, keepdims=True)
        )
        rows_grad = gdown[here, :].astype(F32)
        add_line(5, rows_grad)
        value = rows_grad + inner * inv
        add_line(2, value)
        gfirst[pl.ds(pl.multiple_of(at, ROWS), ROWS), :] = value
        return carry

    lax.fori_loop(0, slots // ROWS, second_back, 0)
    gball[mine, :] = gfirst[...].astype(BF16)

    def mixed_back(step, carry):
        at = lane_at(step, wide)
        weight = g_wot[:, :, :, at].reshape(width, wide)
        gm[:, at] = nn(gball[mine, :], weight).astype(BF16)
        return carry

    lax.fori_loop(0, n_t, mixed_back, 0)
    to_heads = [
        send(gm.at[:, lane_at(flip(z, k), wide)], do.at[z, own, :], zpeer(k)) for k in reversed(zs)
    ]
    do[z, own, :] = gm[:, lane_at(z, wide)]

    rows_sent = [send(gball.at[mine, :], gball.at[mine, :], zpeer(k)) for k in zs]
    for copy in to_heads:
        copy.wait_recv()

    def at_do(index):
        return do.at[:, slot_at(index), :]

    do_started = ctx_start(at_do)

    for image in range(images):
        stacked = stack_heads(do[image, own, :])
        grad_probs = nt(stacked, qkv[image, :, 2 * wide : 3 * wide])
        weights = wq[image]
        along = jnp.sum(grad_probs * weights, axis=-1, keepdims=True)
        put_rows(alng, image, along)
        grad_scores = (weights * (grad_probs - along)).astype(BF16)
        out = pick_heads(nn(grad_scores, qkv[image, :, wide : 2 * wide])) * scale
        dqkv[image * slots : (image + 1) * slots, 0:wide] = out.astype(BF16)

    def at_along(index):
        return alng.at[index]

    along_started = ctx_start(at_along)
    do_passed = ctx_forward(do_started, at_do)
    along_passed = ctx_forward(along_started, at_along)
    ctx_finish(do_started, do_passed)
    ctx_finish(along_started, along_passed)

    for image in range(images):
        stacked = stack_heads(qkv[image, own, 2 * wide : 3 * wide])
        grad_probs = nt(stacked, do[image])
        weights = wk[image]
        lines = []
        for h in range(heads):
            line = image * heads + h
            level = alng[0, line : line + 1, :]
            for other in range(1, n_ctx):
                level = level + alng[other, line : line + 1, :]
            lines.append(grad_probs[h * slots : (h + 1) * slots] - level)
        grad_scores = (weights * jnp.concatenate(lines, axis=0)).astype(BF16)
        at = slice(image * slots, (image + 1) * slots)
        out = pick_heads(nn(grad_scores, qkv[image, :, 0:wide])) * scale
        dqkv[at, wide : 2 * wide] = out.astype(BF16)
        out = pick_heads(nn(weights.astype(BF16), do[image]))
        dqkv[at, 2 * wide : 3 * wide] = out.astype(BF16)

    def in_back(step, carry):
        some = group // (width // TILE)
        weight = g_win[pl.ds(step * some, some)].reshape(TILE, 3 * wide)
        part1[:, lane_at(step, TILE)] = nt(dqkv[...], weight).astype(BF16)
        return carry

    lax.fori_loop(0, width // TILE, in_back, 0)
    sent1 = scatter(part1, recv1)

    wide_grad(b_win, h1, dqkv, 3 * wide)
    win_near = grad_near(b_win, s_win)
    for copy in rows_sent:
        copy.wait_recv()

    out = tn(gball[...], mixed[:, lane_at(z, wide)]).astype(BF16)
    b_wot[...] = out.reshape(group, 2, piece, wide)
    wot_near = grad_near(b_wot, s_wot)
    gv[9:10, 0:wide] = jnp.sum(dqkv[:, 0:wide].astype(F32), axis=0, keepdims=True)
    gv[10:11, 0:wide] = jnp.sum(dqkv[:, 2 * wide : 3 * wide].astype(F32), axis=0, keepdims=True)
    win_far = grad_far(win_near, b_win, s_win, t_win, r_win)
    wot_far = grad_far(wot_near, b_wot, s_wot, t_wot, r_wot)

    for copy in sents:
        copy.wait_recv()

    def block_rows(step, carry):
        at = step * ROWS
        here = pl.ds(pl.multiple_of(z * slots + at, ROWS), ROWS)
        value = first[here, :] + arrived(parts, recvs, at) + vx[5:6, :]
        out_block[here, :] = value.astype(BF16)
        return carry

    lax.fori_loop(0, slots // ROWS, block_rows, 0)
    out_block[mine, :] = jnp.where(own_live, out_block[mine, :].astype(F32), 0.0).astype(BF16)

    for copy in sent1:
        copy.wait_recv()

    def first_back(step, carry):
        at = step * ROWS
        here = pl.ds(pl.multiple_of(z * slots + at, ROWS), ROWS)
        grad = arrived(part1, recv1, at)
        normed, inv = norm_parts(tok[here, :].astype(F32))
        add_line(0, grad * normed)
        add_line(1, grad)
        scaled = grad * vx[0:1, :]
        inner = (
            scaled
            - jnp.mean(scaled, axis=-1, keepdims=True)
            - normed * jnp.mean(scaled * normed, axis=-1, keepdims=True)
        )
        value = gfirst[pl.ds(pl.multiple_of(at, ROWS), ROWS), :] + inner * inv
        out_tokens[here, :] = value.astype(BF16)
        return carry

    lax.fori_loop(0, slots // ROWS, first_back, 0)
    tail = [send(out_tokens.at[mine, :], out_tokens.at[mine, :], zpeer(k)) for k in reversed(zs)]
    tail += [send(out_block.at[mine, :], out_block.at[mine, :], zpeer(k)) for k in reversed(zs)]

    near = send(gv, vr_sib, sib)
    complete(near)
    gv[...] = gv[...] + vr_sib[...]
    far = [send(gv, vr_plane.at[k - 1], plane(k)) for k in planes]
    for copy in far:
        complete(copy)
    value = gv[...]
    for k in planes:
        value = value + vr_plane[k - 1]
    gv[...] = value
    far = [send(gv.at[0:8], vr_z.at[k - 1], zpeer(k)) for k in zs]

    grad_last(wdt_far, t_wdt, r_wdt, out_wdt)
    grad_last(wup_far, t_wup, r_wup, out_wup)
    grad_last(win_far, t_win, r_win, out_win)
    grad_last(wot_far, t_wot, r_wot, out_wot)

    for copy in far:
        copy.wait_recv()
    value = gv[0:8, :]
    for k in zs:
        value = value + vr_z[k - 1]
    out_vec[0:8, :] = value
    out_vec[8:16, :] = gv[8:16, :]
    for copy in tail:
        copy.wait_recv()
    for copy in pending:
        copy.wait_send()


def on_device(
    mesh_shape,
    tokens,
    keep_mask,
    cotangent,
    first_gain,
    first_shift,
    attend_in,
    attend_bias,
    attend_out,
    out_bias,
    second_gain,
    second_shift,
    expand_in,
    expand_bias,
    contract_out,
    contract_bias,
):
    n_dp, n_ctx, n_t = mesh_shape
    images, slots, width = tokens.shape
    piece, _, wide = attend_in.shape
    hidden = expand_in.shape[1]
    cut = expand_bias.shape[1]
    rows = images * slots
    group = n_dp * n_ctx // 2
    total = slots * n_ctx
    heads = wide // HD

    def line(values):
        values = values.reshape(-1)
        return jnp.pad(values, (0, LANES - values.shape[0]))

    lines = [
        first_gain,
        first_shift,
        out_bias,
        second_gain,
        second_shift,
        contract_bias,
        expand_bias,
        attend_bias[0],
        attend_bias[1],
    ]
    vec = jnp.stack([line(v) for v in lines])
    vec = jnp.pad(vec, ((0, ROWS - len(lines)), (0, 0)))
    sizes = (n_dp, n_ctx, n_t, images, slots, width, wide, hidden, piece, cut)
    widths = (3 * wide, wide, hidden, hidden)
    vmem = pl.BlockSpec(memory_space=pltpu.VMEM)
    scratch = [
        pltpu.VMEM((group, 2, piece, 3 * wide), BF16),
        pltpu.VMEM((group, 2, piece, n_t * wide), BF16),
        pltpu.VMEM((group, 2, piece, hidden), BF16),
        pltpu.VMEM((group, 2, piece, hidden), BF16),
        pltpu.VMEM((group, 2, ROWS, LANES), BF16),
        pltpu.VMEM((ROWS, width), F32),
        pltpu.VMEM((rows, width), F32),
        pltpu.VMEM((rows, width), BF16),
        pltpu.VMEM((images, total, 3 * wide), BF16),
        pltpu.VMEM((images, heads * slots, total), F32),
        pltpu.VMEM((images, heads * slots, total), F32),
        pltpu.VMEM((n_ctx, images * heads, total), F32),
        pltpu.VMEM((n_ctx, images * heads, total), F32),
        pltpu.VMEM((rows, n_t * wide), BF16),
        pltpu.VMEM((rows, width), F32),
        pltpu.VMEM((rows, width), BF16),
        pltpu.VMEM((rows, hidden), F32),
        pltpu.VMEM((rows, hidden), BF16),
        pltpu.VMEM((rows, hidden), BF16),
        pltpu.VMEM((rows, width), BF16),
        pltpu.VMEM((rows, width), BF16),
        pltpu.VMEM((rows, width), BF16),
        pltpu.VMEM((n_t - 1, slots, width), BF16),
        pltpu.VMEM((n_t - 1, slots, width), BF16),
        pltpu.VMEM((n_t - 1, slots, width), BF16),
        pltpu.VMEM((slots, width), F32),
        pltpu.VMEM((rows, width), BF16),
        pltpu.VMEM((rows, width), BF16),
        pltpu.VMEM((slots, n_t * wide), BF16),
        pltpu.VMEM((images, total, wide), BF16),
        pltpu.VMEM((rows, 3 * wide), BF16),
        pltpu.VMEM((ROWS, width), F32),
        pltpu.VMEM((ROWS, width), F32),
        pltpu.VMEM((group - 1, ROWS, width), F32),
        pltpu.VMEM((n_t - 1, 8, width), F32),
    ]
    scratch += [pltpu.VMEM((group, 2, piece, n), BF16) for n in widths]
    scratch += [pltpu.VMEM((group, piece, n), BF16) for n in widths]
    scratch += [pltpu.VMEM((group, piece, n), BF16) for n in widths]
    scratch += [pltpu.VMEM((group - 1, piece, n), BF16) for n in widths]
    copies = 80 + 16 * group
    scratch += [
        pltpu.SemaphoreType.DMA((copies,)),
        pltpu.SemaphoreType.DMA((copies,)),
        pltpu.SemaphoreType.DMA((8,)),
    ]
    outs = pl.pallas_call(
        functools.partial(block_kernel, sizes),
        out_shape=(
            jax.ShapeDtypeStruct((rows, width), BF16),
            jax.ShapeDtypeStruct((rows, width), BF16),
            *[jax.ShapeDtypeStruct((piece, n), F32) for n in widths],
            jax.ShapeDtypeStruct((ROWS, width), F32),
        ),
        in_specs=[vmem] * 8,
        out_specs=(vmem,) * 7,
        scratch_shapes=scratch,
        compiler_params=pltpu.CompilerParams(
            collective_id=0, has_side_effects=True, vmem_limit_bytes=62 << 20
        ),
    )(
        tokens.reshape(rows, width),
        cotangent.reshape(rows, width),
        keep_mask,
        attend_in.reshape(piece, 3 * wide),
        attend_out.T,
        expand_in,
        contract_out.T,
        vec,
    )
    block_out, tokens_grad, d_win, d_wot, d_wup, d_wdt, d_vec = outs
    shard = lax.axis_index("dp") * n_ctx + lax.axis_index("ctx")

    def own(row):
        return lax.dynamic_slice(d_vec, (row, shard * piece), (1, piece)).reshape(piece)

    def own_units(row, units):
        grid = d_vec[row, : units * HD].reshape(units, HD)
        return lax.dynamic_slice(grid, (0, shard * cut), (units, cut))

    return (
        block_out.reshape(tokens.shape),
        tokens_grad.reshape(tokens.shape),
        own(0),
        own(1),
        d_win.reshape(attend_in.shape),
        jnp.stack([own_units(9, heads), own_units(10, heads)]),
        d_wot.T,
        own(2),
        own(3),
        own(4),
        d_wup,
        own_units(8, hidden // HD),
        d_wdt.T,
        own(5),
    )


def solution(mesh):
    shape = (mesh.shape["dp"], mesh.shape["ctx"], mesh.shape["tensor"])
    vector = P(("dp", "ctx"))
    params = (
        vector,
        vector,
        P(("dp", "ctx"), None, "tensor"),
        P(None, "tensor", ("dp", "ctx")),
        P("tensor", ("dp", "ctx")),
        vector,
        vector,
        vector,
        P(("dp", "ctx"), "tensor"),
        P("tensor", ("dp", "ctx")),
        P("tensor", ("dp", "ctx")),
        vector,
    )
    rows = P("dp", "ctx", None)
    return jax.shard_map(
        functools.partial(on_device, shape),
        mesh=mesh,
        in_specs=(rows, P("dp", None), rows, *params),
        out_specs=(rows, rows, *params),
        check_vma=False,
    )
```

```python
import functools

import jax
import jax.numpy as jnp
from jax import lax
from jax.experimental import pallas as pl
from jax.experimental.pallas import tpu as pltpu
from jax.sharding import PartitionSpec as P

HD = 64
BUFFER = 64
LANES = 128
ROWS = 16
TILE = 256
BLOCK = 32
MESH = pl.DeviceIdType.MESH
F32 = jnp.float32
BF16 = jnp.bfloat16

eps = 1e-06
neg_big = -1e30
root_half = 0.7071067811865476
inv_root_two_pi = 0.3989422804014327


def flip(index, bits):
    out, bit = index, 1
    while bit <= bits:
        if bits & bit:
            out = out + bit - 2 * bit * lax.rem(lax.div(index, bit), 2)
        bit *= 2
    return out


def nn(left, right):
    return jnp.dot(left, right, preferred_element_type=F32)


def nt(left, right):
    return lax.dot_general(left, right, (((1,), (1,)), ((), ())), preferred_element_type=F32)


def tn(left, right):
    return lax.dot_general(left, right, (((0,), (0,)), ((), ())), preferred_element_type=F32)


def turned(value, ref):
    return value if value.shape == ref.shape else value.T


def norm_parts(values):
    mean = jnp.mean(values, axis=-1, keepdims=True)
    centered = values - mean
    spread = jnp.mean(centered * centered, axis=-1, keepdims=True)
    inv = lax.rsqrt(spread + eps)
    return centered * inv, inv


def block_kernel(
    sizes,
    tok_in,
    cot_in,
    keep,
    win,
    attend_out,
    wup,
    contract_out,
    first_gain,
    first_shift,
    out_bias,
    second_gain,
    second_shift,
    contract_bias,
    expand_bias,
    attend_bias,
    out_block,
    out_tokens,
    out_win,
    out_wot,
    out_wup,
    out_wdt,
    out_vec,
    tok,
    cot,
    a_out,
    c_out,
    vec,
    g_win,
    g_wot,
    g_wup,
    g_wdt,
    g_vec,
    vx,
    n1,
    h1,
    qkv,
    wq,
    wk,
    stat,
    alng,
    mixed,
    first,
    h2,
    ga,
    act,
    gi,
    part2,
    parts,
    part1,
    recv2,
    recvs,
    recv1,
    gfirst,
    gdown,
    gown,
    gm,
    do,
    dqkv,
    block_own,
    tokens_own,
    gv,
    vr_sib,
    vr_plane,
    vr_z,
    b_win,
    b_wot,
    b_wup,
    b_wdt,
    s_win,
    s_wot,
    s_wup,
    s_wdt,
    t_win,
    t_wot,
    t_wup,
    t_wdt,
    r_win,
    r_wot,
    r_wup,
    r_wdt,
    o_wot,
    z_wot,
    f_win,
    f_wot,
    f_wup,
    f_wdt,
    send_sem,
    recv_sem,
    local_sem,
):
    n_dp, n_ctx, n_t, images, slots, width, wide, hidden, piece, cut = sizes
    rows = images * slots
    total = slots * n_ctx
    heads = wide // HD
    half = n_ctx // 2
    group = n_dp * half
    scale = HD ** (-0.5)
    dp = lax.axis_index("dp")
    ctx = lax.axis_index("ctx")
    z = lax.axis_index("tensor")
    high, core = lax.div(ctx, 2), lax.rem(ctx, 2)
    me = dp * half + high
    shard = me * 2 + core
    sib = (dp, flip(ctx, 1), z)

    def plane(k):
        other = flip(me, k)
        return (lax.div(other, half), lax.rem(other, half) * 2 + core, z)

    def ctx_at(k):
        return flip(high, k) * 2 + core

    def zpeer(k):
        return (dp, ctx, flip(z, k))

    def slot_at(index):
        return pl.ds(pl.multiple_of(index * slots, ROWS), slots)

    def lane_at(index, size):
        return pl.ds(pl.multiple_of(index * size, size), size)

    own = slot_at(ctx)
    mine = slot_at(z)

    count = [0, 0]
    pending = []

    def send(src, dst, device):
        index = count[0]
        count[0] += 1
        copy = pltpu.make_async_remote_copy(
            src_ref=src,
            dst_ref=dst,
            send_sem=send_sem.at[index],
            recv_sem=recv_sem.at[index],
            device_id=device,
            device_id_type=MESH,
        )
        copy.start()
        pending.append(copy)
        return copy

    def complete(copy):
        pending[:] = [other for other in pending if other is not copy]
        copy.wait()

    def local(src, dst):
        index = count[1]
        count[1] += 1
        copy = pltpu.make_async_copy(src, dst, local_sem.at[index])
        copy.start()
        return copy

    planes = range(1, group)
    zs = range(1, n_t)

    def at_win(m, c):
        return g_win.at[:, m, c]

    def at_wot(m, c):
        return g_wot.at[m, c, :, lane_at(z, wide)]

    def at_wup(m, c):
        return g_wup.at[m, c]

    def at_wdt(m, c):
        return g_wdt.at[m, c]

    def at_vec(m, c):
        return g_vec.at[m, c]

    barrier = pltpu.get_barrier_semaphore()
    for device in [plane(k) for k in planes] + [sib] + [zpeer(k) for k in zs]:
        pl.semaphore_signal(barrier, inc=1, device_id=device, device_id_type=MESH)
    a_out_load = local(attend_out, a_out)
    tok_load = local(tok_in, tok)
    win_own = local(win, at_win(me, core))
    c_out_load = local(contract_out, c_out)
    cot_load = local(cot_in, cot)
    wup_own = local(wup, at_wup(me, core))

    vec[...] = jnp.zeros_like(vec)
    for line, ref in enumerate(
        (first_gain, first_shift, out_bias, second_gain, second_shift, contract_bias)
    ):
        vec[line : line + 1, 0:piece] = ref[...].astype(F32)
    vec[8 : 8 + cut, 0 : hidden // HD] = expand_bias[...].astype(F32)
    for j in range(2):
        vec[16 + j * heads : 16 + (j + 1) * heads, 0:cut] = attend_bias[j].astype(F32)
    g_vec[me, core] = vec[...]
    gv[...] = jnp.zeros_like(gv)
    unit_one = (
        lax.broadcasted_iota(jnp.int32, (piece, piece), 0)
        == lax.broadcasted_iota(jnp.int32, (piece, piece), 1)
    ).astype(F32)
    unit_one = unit_one.astype(BF16)
    a_out_load.wait()
    g_wot[me, core, :, lane_at(z, wide)] = nt(unit_one, a_out[...]).astype(BF16)
    pl.semaphore_wait(barrier, group + n_t - 1)

    def gather_start(src, at):
        far = [send(src, at(me, core), plane(k)) for k in planes]
        return far, send(src, at(me, core), sib)

    def gather_forward(started, at):
        out = []
        for k in planes:
            started[0][k - 1].wait_recv()
            there = at(flip(me, k), core)
            out.append(send(there, there, sib))
        return out

    def gather_finish(started, passed):
        started[1].wait_recv()
        for copy in passed:
            copy.wait_recv()

    def ctx_start(at):
        far = [send(at(ctx), at(ctx), (dp, ctx_at(k), z)) for k in range(1, half)]
        return far, send(at(ctx), at(ctx), sib)

    def ctx_forward(started, at):
        out = []
        for k in range(1, half):
            started[0][k - 1].wait_recv()
            out.append(send(at(ctx_at(k)), at(ctx_at(k)), sib))
        return out

    def ctx_finish(started, passed):
        started[1].wait_recv()
        for copy in passed:
            copy.wait_recv()

    def wot_piece(m, index):
        return g_wot.at[m, core, :, lane_at(index, wide)]

    vec_started = gather_start(vec, at_vec)
    win_started = gather_start(win, at_win)
    wot_started = gather_start(at_wot(me, core), at_wot)
    wot_z = [[send(wot_piece(me, z), wot_piece(me, z), zpeer(k)) for k in zs]]

    tok_load.wait()

    def first_norm(step, carry):
        at = pl.ds(pl.multiple_of(step * BLOCK, BLOCK), BLOCK)
        normed, _ = norm_parts(tok[at, :].astype(F32))
        n1[at, :] = normed
        return carry

    lax.fori_loop(0, rows // BLOCK, first_norm, 0)

    vec_passed = gather_forward(vec_started, at_vec)
    gather_finish(vec_started, vec_passed)
    shape = (2 * ROWS, width)
    line_id = lax.broadcasted_iota(jnp.int32, shape, 0)
    lane_id = lax.broadcasted_iota(jnp.int32, shape, 1)
    source = lax.broadcasted_iota(jnp.int32, (LANES, width), 0)
    target = lax.broadcasted_iota(jnp.int32, (LANES, width), 1)
    by_unit = jnp.where(target // HD == source, 1.0, 0.0).astype(BF16)
    for_unit = lane_id % HD - (line_id - 8)
    for_head = lane_id // HD == (line_id - 16) % heads

    def place(index, carry):
        one, two, three = carry
        shares = g_vec[lax.div(index, 2), lax.rem(index, 2)].astype(BF16)
        by_width = jnp.where(target - source == index * piece, 1.0, 0.0).astype(BF16)
        by_channel = jnp.where(target % HD - source == index * cut, 1.0, 0.0).astype(BF16)
        one = one + nn(shares, by_width)
        two = two + jnp.where(for_unit == index * cut, nn(shares, by_unit), 0.0)
        three = three + jnp.where(for_head, nn(shares, by_channel), 0.0)
        return one, two, three

    zero = jnp.zeros(shape, F32)
    one, two, three = lax.fori_loop(0, 2 * group, place, (zero, zero, zero))
    vx[0:8, :] = one[0:8]
    vx[8:9, :] = jnp.sum(two[8 : 8 + cut], axis=0, keepdims=True)
    vx[9:10, :] = jnp.sum(three[16 : 16 + heads], axis=0, keepdims=True)
    vx[10:11, :] = jnp.sum(three[16 + heads : 16 + 2 * heads], axis=0, keepdims=True)

    def first_hidden(step, carry):
        at = pl.ds(pl.multiple_of(step * BLOCK, BLOCK), BLOCK)
        h1[at, :] = (n1[at, :] * vx[0:1, :] + vx[1:2, :]).astype(BF16)
        return carry

    lax.fori_loop(0, rows // BLOCK, first_hidden, 0)

    c_out_load.wait()

    def turn(step, carry):
        at = lane_at(step, TILE)
        g_wdt[me, core, :, at] = nt(unit_one, c_out[at, :]).astype(BF16)
        return carry

    lax.fori_loop(0, hidden // TILE, turn, 0)

    lengths = BUFFER + jnp.sum(keep[...], axis=1, keepdims=True)
    slot_id = lax.broadcasted_iota(jnp.int32, (slots, 1), 0) + ctx * slots
    key_id = lax.broadcasted_iota(jnp.int32, (1, total), 1)
    head_of = lax.broadcasted_iota(jnp.int32, (slots, wide), 1) // HD
    spot = lax.broadcasted_iota(jnp.int32, (slots, total), 1) == slot_id

    def stack_heads(block):
        wider = block.astype(F32)
        return jnp.concatenate(
            [jnp.where(head_of == h, wider, 0.0).astype(BF16) for h in range(heads)], axis=0
        )

    def pick_heads(block):
        out = jnp.where(head_of == 0, block[0:slots], 0.0)
        for h in range(1, heads):
            out = jnp.where(head_of == h, block[h * slots : (h + 1) * slots], out)
        return out

    def put_rows(ref, image, column):
        for h in range(heads):
            part = jnp.where(spot, column[h * slots : (h + 1) * slots], 0.0)
            line = image * heads + h
            ref[ctx, line : line + 1, :] = jnp.sum(part, axis=0, keepdims=True)

    win_passed = gather_forward(win_started, at_win)
    win_own.wait()
    gather_finish(win_started, win_passed)

    def project(j, bias):
        out = nn(h1[...], g_win[j].reshape(width, wide))
        if bias is not None:
            out = out + vx[bias : bias + 1, 0:wide]
        qkv[:, own, j * wide : (j + 1) * wide] = out.astype(BF16).reshape(images, slots, wide)

    def at_kv(index):
        return qkv.at[:, slot_at(index), wide : 3 * wide]

    def at_q(index):
        return qkv.at[:, slot_at(index), 0:wide]

    project(1, None)
    project(2, 10)
    kv_started = ctx_start(at_kv)
    wup_started = gather_start(wup, at_wup)
    wdt_started = gather_start(at_wdt(me, core), at_wdt)
    wot_passed = []
    for k in planes:
        wot_started[0][k - 1].wait_recv()
        there = wot_piece(flip(me, k), z)
        wot_z.append([send(there, there, zpeer(j)) for j in zs])
        wot_passed.append(send(there, there, sib))
    project(0, 9)
    q_started = ctx_start(at_q)
    kv_passed = ctx_forward(kv_started, at_kv)
    ctx_finish(kv_started, kv_passed)

    def at_mixed(index, image):
        return mixed.at[image * slots : (image + 1) * slots, lane_at(index, wide)]

    mixed_sent = []
    for image in range(images):
        key_live = key_id < lengths[image : image + 1, :]
        stacked = stack_heads(qkv[image, own, 0:wide])
        scores = nt(stacked, qkv[image, :, wide : 2 * wide]) * scale
        scores = jnp.where(key_live, scores, neg_big)
        top = jnp.max(scores, axis=-1, keepdims=True)
        expo = jnp.exp(scores - top)
        whole = jnp.sum(expo, axis=-1, keepdims=True)
        probs = expo / whole
        wq[image] = probs
        put_rows(stat, image, top + jnp.log(whole))
        out = nn(probs.astype(BF16), qkv[image, :, 2 * wide : 3 * wide])
        mixed[image * slots : (image + 1) * slots, lane_at(z, wide)] = pick_heads(out).astype(BF16)
        mixed_sent.append(
            [send(at_mixed(z, image), at_mixed(z, image), zpeer(k)) for k in reversed(zs)]
        )

    def at_stat(index):
        return stat.at[index]

    stat_started = ctx_start(at_stat)

    cot_load.wait()
    row_live = []
    for image in range(images):
        row_live.append(slot_id < lengths[image : image + 1, :])
        at = slice(image * slots, (image + 1) * slots)
        gdown[at, :] = jnp.where(row_live[image], cot[at, :].astype(F32), 0.0).astype(BF16)

    gather_finish(wot_started, wot_passed)
    wot_more = []
    for order, block in enumerate(wot_z):
        for k in zs:
            block[k - 1].wait_recv()
            there = wot_piece(flip(me, order), flip(z, k))
            wot_more.append(send(there, there, sib))
    wup_passed = gather_forward(wup_started, at_wup)
    wup_own.wait()
    wdt_passed = gather_forward(wdt_started, at_wdt)
    gather_finish(wdt_started, wdt_passed)

    def down_back(step, carry):
        at = lane_at(step, TILE)
        ga[:, at] = nn(gdown[...], g_wdt[:, :, :, at].reshape(width, TILE))
        return carry

    lax.fori_loop(0, hidden // TILE, down_back, 0)

    gather_finish(wup_started, wup_passed)
    for copy in wot_more:
        copy.wait_recv()
    for copies in mixed_sent:
        for copy in copies:
            copy.wait_recv()

    some = group // (width // TILE)

    def project_out(step, carry):
        weight = g_wot[pl.ds(step * some, some)].reshape(TILE, n_t * wide)
        first[:, lane_at(step, TILE)] = nt(mixed[...], weight)
        return carry

    lax.fori_loop(0, width // TILE, project_out, 0)

    def second_norm(step, carry):
        at = pl.ds(pl.multiple_of(step * BLOCK, BLOCK), BLOCK)
        value = tok[at, :].astype(F32) + first[at, :] + vx[2:3, :]
        first[at, :] = value
        normed, _ = norm_parts(value)
        h2[at, :] = (normed * vx[3:4, :] + vx[4:5, :]).astype(BF16)
        return carry

    lax.fori_loop(0, rows // BLOCK, second_norm, 0)

    def expand(step, carry):
        at = lane_at(step, TILE)
        inner = nn(h2[...], g_wup[:, :, :, at].reshape(width, TILE)) + vx[8:9, at]
        share = 0.5 * (1.0 + lax.erf(inner * root_half))
        act[:, at] = (inner * share).astype(BF16)
        slope = share + inner * jnp.exp(-0.5 * inner * inner) * inv_root_two_pi
        grad = (ga[:, at] * slope).astype(BF16)
        gi[:, at] = grad
        gv[8:9, at] = jnp.sum(grad.astype(F32), axis=0, keepdims=True)
        return carry

    lax.fori_loop(0, hidden // TILE, expand, 0)

    def up_back(step, carry):
        weight = g_wup[pl.ds(step * some, some)].reshape(TILE, hidden)
        part2[:, lane_at(step, TILE)] = nt(gi[...], weight).astype(BF16)
        return carry

    lax.fori_loop(0, width // TILE, up_back, 0)

    def scatter(part, recv, start, size):
        return [
            send(
                part.at[pl.ds(pl.multiple_of(flip(z, k) * slots + start, ROWS), size), :],
                recv.at[k - 1, start : start + size, :],
                zpeer(k),
            )
            for k in reversed(zs)
        ]

    def arrived(part, recv, at, size):
        out = part[pl.ds(pl.multiple_of(z * slots + at, ROWS), size), :].astype(F32)
        for k in zs:
            out = out + recv[k - 1, pl.ds(pl.multiple_of(at, ROWS), size), :].astype(F32)
        return out

    sent2 = scatter(part2, recv2, 0, slots)

    def contract(step, carry):
        weight = g_wdt[pl.ds(step * some, some)].reshape(TILE, hidden)
        parts[:, lane_at(step, TILE)] = nt(act[...], weight).astype(BF16)
        return carry

    lax.fori_loop(0, width // TILE, contract, 0)
    early = 2 * ROWS
    sents = [scatter(parts, recvs, 0, early)]

    def wide_grad(buf, left, right, lanes):
        def one(step, carry):
            at = lane_at(step, TILE)
            out = tn(left[...], right[:, at]).astype(BF16)
            buf[:, :, :, at] = out.reshape(group, 2, piece, TILE)
            return carry

        lax.fori_loop(0, lanes // TILE, one, 0)

    def grad_near(buf, near):
        return send(buf.at[:, 1 - core], near, sib)

    def grad_far(copy, buf, near, both, recv):
        copy.wait_recv()

        def one(m, carry):
            both[m] = (buf[m, core].astype(F32) + near[m].astype(F32)).astype(BF16)
            return carry

        lax.fori_loop(0, group, one, 0)
        return [send(both.at[flip(me, k)], recv.at[k - 1], plane(k)) for k in reversed(planes)]

    def grad_sum(copies, both, recv):
        for copy in copies:
            copy.wait_recv()
        value = both[me].astype(F32)
        for k in planes:
            value = value + recv[k - 1].astype(F32)
        return value

    wide_grad(b_wdt, gdown, act, hidden)
    wdt_near = grad_near(b_wdt, s_wdt)
    wide_grad(b_wup, h2, gi, hidden)
    wup_near = grad_near(b_wup, s_wup)
    wdt_far = grad_far(wdt_near, b_wdt, s_wdt, t_wdt, r_wdt)

    q_passed = ctx_forward(q_started, at_q)
    stat_passed = ctx_forward(stat_started, at_stat)
    ctx_finish(q_started, q_passed)
    ctx_finish(stat_started, stat_passed)
    for image in range(images):
        stacked = stack_heads(qkv[image, own, wide : 2 * wide])
        scores = nt(stacked, qkv[image, :, 0:wide]) * scale
        for h in range(heads):
            line = image * heads + h
            level = stat[0, line : line + 1, :]
            for other in range(1, n_ctx):
                level = level + stat[other, line : line + 1, :]
            block = scores[h * slots : (h + 1) * slots]
            block = jnp.where(row_live[image], block, neg_big)
            wk[image, h * slots : (h + 1) * slots, :] = jnp.exp(block - level)

    own_live = slot_id < jnp.sum(
        jnp.where(lax.broadcasted_iota(jnp.int32, (images, 1), 0) == z, lengths, 0),
        axis=0,
        keepdims=True,
    )

    def add_line(line, value):
        gv[line : line + 1, :] += jnp.sum(value, axis=0, keepdims=True)

    def norm_back(grad, normed, inv, gain):
        scaled = grad * gain
        inner = (
            scaled
            - jnp.mean(scaled, axis=-1, keepdims=True)
            - normed * jnp.mean(scaled * normed, axis=-1, keepdims=True)
        )
        return inner * inv

    for copy in sent2:
        copy.wait_recv()

    def second_back(step, carry):
        at = step * ROWS
        here = pl.ds(pl.multiple_of(z * slots + at, ROWS), ROWS)
        grad = arrived(part2, recv2, at, ROWS)
        normed, inv = norm_parts(first[here, :])
        rows_grad = gdown[here, :].astype(F32)
        value = rows_grad + norm_back(grad, normed, inv, vx[3:4, :])
        there = pl.ds(pl.multiple_of(at, ROWS), ROWS)
        gfirst[there, :] = value
        gown[there, :] = value.astype(BF16)
        add_line(3, grad * normed)
        add_line(4, grad)
        add_line(5, rows_grad)
        add_line(2, value)
        return carry

    lax.fori_loop(0, slots // ROWS, second_back, 0)

    def mixed_back(step, carry):
        at = lane_at(step, wide)
        weight = g_wot[:, :, :, at].reshape(width, wide)
        gm[:, at] = nn(gown[...], weight).astype(BF16)
        return carry

    lax.fori_loop(0, n_t, mixed_back, 0)
    to_heads = [
        send(gm.at[:, lane_at(flip(z, k), wide)], do.at[z, own, :], zpeer(k)) for k in reversed(zs)
    ]
    sents.append(scatter(parts, recvs, early, slots - early))
    do[z, own, :] = gm[:, lane_at(z, wide)]
    def out_grad(step, carry):
        at = lane_at(step, TILE)
        out = tn(gown[...], mixed[mine, at]).astype(BF16)
        b_wot[:, :, :, at] = out.reshape(group, 2, piece, TILE)
        return carry

    lax.fori_loop(0, n_t * wide // TILE, out_grad, 0)
    wot_near = grad_near(b_wot, s_wot)

    def block_rows(start, size, copies):
        for copy in copies:
            copy.wait_recv()
        here = pl.ds(pl.multiple_of(z * slots + start, ROWS), size)
        value = first[here, :] + arrived(parts, recvs, start, size) + vx[5:6, :]
        value = jnp.where(own_live[start : start + size], value, 0.0)
        block_own[start : start + size, :] = value.astype(BF16)
        source = block_own.at[start : start + size, :]
        keep_own = local(source, out_block.at[here, :])
        return [send(source, out_block.at[here, :], zpeer(k)) for k in reversed(zs)], keep_own

    block_early, block_kept = block_rows(0, early, sents[0])
    tail = block_early
    stays = [block_kept]

    for copy in to_heads:
        copy.wait_recv()

    def at_do(index):
        return do.at[:, slot_at(index), :]

    do_started = ctx_start(at_do)

    for image in range(images):
        stacked = stack_heads(do[image, own, :])
        grad_probs = nt(stacked, qkv[image, :, 2 * wide : 3 * wide])
        weights = wq[image]
        along = jnp.sum(grad_probs * weights, axis=-1, keepdims=True)
        put_rows(alng, image, along)
        grad_scores = (weights * (grad_probs - along)).astype(BF16)
        out = pick_heads(nn(grad_scores, qkv[image, :, wide : 2 * wide])) * scale
        dqkv[image * slots : (image + 1) * slots, 0:wide] = out.astype(BF16)

    def at_along(index):
        return alng.at[index]

    along_started = ctx_start(at_along)
    wot_far = grad_far(wot_near, b_wot, s_wot, t_wot, r_wot)
    wup_far = grad_far(wup_near, b_wup, s_wup, t_wup, r_wup)
    do_passed = ctx_forward(do_started, at_do)
    along_passed = ctx_forward(along_started, at_along)
    ctx_finish(do_started, do_passed)
    ctx_finish(along_started, along_passed)

    for image in range(images):
        stacked = stack_heads(qkv[image, own, 2 * wide : 3 * wide])
        grad_probs = nt(stacked, do[image])
        weights = wk[image]
        lines = []
        for h in range(heads):
            line = image * heads + h
            level = alng[0, line : line + 1, :]
            for other in range(1, n_ctx):
                level = level + alng[other, line : line + 1, :]
            lines.append(grad_probs[h * slots : (h + 1) * slots] - level)
        grad_scores = (weights * jnp.concatenate(lines, axis=0)).astype(BF16)
        at = slice(image * slots, (image + 1) * slots)
        out = pick_heads(nn(grad_scores, qkv[image, :, 0:wide])) * scale
        dqkv[at, wide : 2 * wide] = out.astype(BF16)
        out = pick_heads(nn(weights.astype(BF16), do[image]))
        dqkv[at, 2 * wide : 3 * wide] = out.astype(BF16)

    def in_back(step, carry):
        out = None
        for j in range(3):
            weight = g_win[j, pl.ds(step * some, some)].reshape(TILE, wide)
            term = nt(dqkv[:, j * wide : (j + 1) * wide], weight)
            out = term if out is None else out + term
        part1[:, lane_at(step, TILE)] = out.astype(BF16)
        return carry

    lax.fori_loop(0, width // TILE, in_back, 0)
    sent1 = scatter(part1, recv1, 0, slots)

    block_late, block_kept = block_rows(early, slots - early, sents[1])
    tail += block_late
    stays.append(block_kept)
    for j in range(3):
        out = tn(h1[...], dqkv[:, j * wide : (j + 1) * wide]).astype(BF16)
        b_win[j] = out.reshape(group, 2, piece, wide)
    win_near = send(b_win.at[:, :, 1 - core], s_win, sib)
    gv[9:10, 0:wide] = jnp.sum(dqkv[:, 0:wide].astype(F32), axis=0, keepdims=True)
    gv[10:11, 0:wide] = jnp.sum(dqkv[:, 2 * wide : 3 * wide].astype(F32), axis=0, keepdims=True)
    f_wdt[...] = turned(grad_sum(wdt_far, t_wdt, r_wdt), f_wdt)
    stays.append(local(f_wdt, out_wdt))
    win_near.wait_recv()
    for j in range(3):
        both = b_win[j, :, pl.ds(core, 1)].reshape(group, piece, wide).astype(F32)
        t_win[:, j] = (both + s_win[j].astype(F32)).astype(BF16)
    win_far = [send(t_win.at[flip(me, k)], r_win.at[k - 1], plane(k)) for k in reversed(planes)]

    whole_rows = grad_sum(wot_far, t_wot, r_wot)
    o_wot[...] = whole_rows.astype(BF16)
    to_owner = [
        send(o_wot.at[:, lane_at(flip(z, k), wide)], z_wot.at[k - 1], zpeer(k))
        for k in reversed(zs)
    ]
    f_wup[...] = grad_sum(wup_far, t_wup, r_wup)
    stays.append(local(f_wup, out_wup))

    for copy in sent1:
        copy.wait_recv()

    def first_back(step, carry):
        at = step * ROWS
        here = pl.ds(pl.multiple_of(z * slots + at, ROWS), ROWS)
        grad = arrived(part1, recv1, at, ROWS)
        normed, inv = norm_parts(tok[here, :].astype(F32))
        there = pl.ds(pl.multiple_of(at, ROWS), ROWS)
        value = gfirst[there, :] + norm_back(grad, normed, inv, vx[0:1, :])
        tokens_own[there, :] = value.astype(BF16)
        add_line(0, grad * normed)
        add_line(1, grad)
        return carry

    lax.fori_loop(0, slots // ROWS, first_back, 0)
    tail += [send(tokens_own, out_tokens.at[mine, :], zpeer(k)) for k in reversed(zs)]
    stays.append(local(tokens_own, out_tokens.at[mine, :]))

    near = send(gv, vr_sib, sib)
    complete(near)
    gv[...] = gv[...] + vr_sib[...]
    far = [send(gv, vr_plane.at[k - 1], plane(k)) for k in planes]
    f_win[...] = grad_sum(win_far, t_win, r_win)
    stays.append(local(f_win, out_win))
    for copy in far:
        complete(copy)
    value = gv[...]
    for k in planes:
        value = value + vr_plane[k - 1]
    gv[...] = value
    lanes = lane_at(lax.div(shard * piece, LANES), LANES)
    far = [send(gv.at[0:8, lanes], vr_z.at[k - 1], zpeer(k)) for k in zs]
    for copy in to_owner:
        copy.wait_recv()
    value = o_wot[:, lane_at(z, wide)].astype(F32)
    for k in zs:
        value = value + z_wot[k - 1].astype(F32)
    f_wot[...] = turned(value, f_wot)
    stays.append(local(f_wot, out_wot))
    for copy in far:
        complete(copy)
    value = gv[0:8, lanes]
    for k in zs:
        value = value + vr_z[k - 1]
    gv[0:8, lanes] = value
    stays.append(local(gv, out_vec))
    for copy in tail:
        copy.wait_recv()
    for copy in pending:
        copy.wait_send()
    for copy in stays:
        copy.wait()


def finish_call(sizes, *refs):
    finish_kernel(sizes, *refs[:13], refs[13:19], *refs[19:])


def finish_kernel(
    sizes,
    in_block,
    in_tokens,
    in_win,
    in_wot,
    in_wup,
    in_wdt,
    in_vec,
    block,
    tokens,
    win,
    wot,
    wup,
    wdt,
    vectors,
    units,
    biases,
    sems,
):
    n_ctx, piece, cut, wide, hidden, width = sizes
    shard = lax.axis_index("dp") * n_ctx + lax.axis_index("ctx")
    pairs = [(in_block, block), (in_tokens, tokens), (in_win, win)]
    pairs += [(in_wot, wot), (in_wup, wup), (in_wdt, wdt)]
    copies = [pltpu.make_async_copy(a, b, sems.at[i]) for i, (a, b) in enumerate(pairs)]
    for copy in copies:
        copy.start()

    def exact(left, right):
        return jnp.dot(left, right, precision=lax.Precision.HIGHEST, preferred_element_type=F32)

    heads = wide // HD
    lane = lax.broadcasted_iota(jnp.int32, (width, piece), 0)
    slot = lax.broadcasted_iota(jnp.int32, (width, piece), 1)
    part = exact(in_vec[0:8, :], jnp.where(lane - slot == shard * piece, 1.0, 0.0))
    for line in range(6):
        vectors[line][...] = part[line : line + 1]
    channel = lax.broadcasted_iota(jnp.int32, (cut, hidden), 0)
    lane = lax.broadcasted_iota(jnp.int32, (cut, hidden), 1)
    chosen = jnp.where(lane % HD - channel == shard * cut, in_vec[8:9, 0:hidden], 0.0)
    lane = lax.broadcasted_iota(jnp.int32, (hidden, hidden // HD), 0)
    slot = lax.broadcasted_iota(jnp.int32, (hidden, hidden // HD), 1)
    units[...] = exact(chosen, jnp.where(lane // HD == slot, 1.0, 0.0))
    lane = lax.broadcasted_iota(jnp.int32, (wide, cut), 0)
    slot = lax.broadcasted_iota(jnp.int32, (wide, cut), 1)
    pick = jnp.where(lane % HD - slot == shard * cut, 1.0, 0.0)
    head = lax.broadcasted_iota(jnp.int32, (heads, wide), 0)
    lane = lax.broadcasted_iota(jnp.int32, (heads, wide), 1)
    for j in range(2):
        chosen = jnp.where(lane // HD == head, in_vec[9 + j : 10 + j, 0:wide], 0.0)
        biases[j] = exact(chosen, pick)
    for copy in copies:
        copy.wait()


def on_device(
    mesh_shape,
    tokens,
    keep_mask,
    cotangent,
    first_gain,
    first_shift,
    attend_in,
    attend_bias,
    attend_out,
    out_bias,
    second_gain,
    second_shift,
    expand_in,
    expand_bias,
    contract_out,
    contract_bias,
):
    n_dp, n_ctx, n_t = mesh_shape
    images, slots, width = tokens.shape
    piece, _, wide = attend_in.shape
    hidden = expand_in.shape[1]
    cut = expand_bias.shape[1]
    rows = images * slots
    group = n_dp * n_ctx // 2
    total = slots * n_ctx
    heads = wide // HD
    turn = piece % LANES == 0
    sizes = (n_dp, n_ctx, n_t, images, slots, width, wide, hidden, piece, cut)
    vmem = pl.BlockSpec(memory_space=pltpu.VMEM)
    hbm = pl.BlockSpec(memory_space=pl.ANY)
    scratch = [
        pltpu.VMEM((rows, width), BF16),
        pltpu.VMEM((rows, width), BF16),
        pltpu.VMEM((wide, piece), BF16),
        pltpu.VMEM((hidden, piece), BF16),
        pltpu.VMEM((2 * ROWS, LANES), F32),
        pltpu.VMEM((3, group, 2, piece, wide), BF16),
        pltpu.VMEM((group, 2, piece, n_t * wide), BF16),
        pltpu.VMEM((group, 2, piece, hidden), BF16),
        pltpu.VMEM((group, 2, piece, hidden), BF16),
        pltpu.VMEM((group, 2, 2 * ROWS, LANES), F32),
        pltpu.VMEM((ROWS, width), F32),
        pltpu.VMEM((rows, width), F32),
        pltpu.VMEM((rows, width), BF16),
        pltpu.VMEM((images, total, 3 * wide), BF16),
        pltpu.VMEM((images, heads * slots, total), F32),
        pltpu.VMEM((images, heads * slots, total), F32),
        pltpu.VMEM((n_ctx, images * heads, total), F32),
        pltpu.VMEM((n_ctx, images * heads, total), F32),
        pltpu.VMEM((rows, n_t * wide), BF16),
        pltpu.VMEM((rows, width), F32),
        pltpu.VMEM((rows, width), BF16),
        pltpu.VMEM((rows, hidden), F32),
        pltpu.VMEM((rows, hidden), BF16),
        pltpu.VMEM((rows, hidden), BF16),
        pltpu.VMEM((rows, width), BF16),
        pltpu.VMEM((rows, width), BF16),
        pltpu.VMEM((rows, width), BF16),
        pltpu.VMEM((n_t - 1, slots, width), BF16),
        pltpu.VMEM((n_t - 1, slots, width), BF16),
        pltpu.VMEM((n_t - 1, slots, width), BF16),
        pltpu.VMEM((slots, width), F32),
        pltpu.VMEM((rows, width), BF16),
        pltpu.VMEM((slots, width), BF16),
        pltpu.VMEM((slots, n_t * wide), BF16),
        pltpu.VMEM((images, total, wide), BF16),
        pltpu.VMEM((rows, 3 * wide), BF16),
        pltpu.VMEM((slots, width), BF16),
        pltpu.VMEM((slots, width), BF16),
        pltpu.VMEM((ROWS, width), F32),
        pltpu.VMEM((ROWS, width), F32),
        pltpu.VMEM((group - 1, ROWS, width), F32),
        pltpu.VMEM((n_t - 1, 8, LANES), F32),
        pltpu.VMEM((3, group, 2, piece, wide), BF16),
        pltpu.VMEM((group, 2, piece, n_t * wide), BF16),
        pltpu.VMEM((group, 2, piece, hidden), BF16),
        pltpu.VMEM((group, 2, piece, hidden), BF16),
        pltpu.VMEM((3, group, piece, wide), BF16),
        pltpu.VMEM((group, piece, n_t * wide), BF16),
        pltpu.VMEM((group, piece, hidden), BF16),
        pltpu.VMEM((group, piece, hidden), BF16),
        pltpu.VMEM((group, 3, piece, wide), BF16),
        pltpu.VMEM((group, piece, n_t * wide), BF16),
        pltpu.VMEM((group, piece, hidden), BF16),
        pltpu.VMEM((group, piece, hidden), BF16),
        pltpu.VMEM((group - 1, 3, piece, wide), BF16),
        pltpu.VMEM((group - 1, piece, n_t * wide), BF16),
        pltpu.VMEM((group - 1, piece, hidden), BF16),
        pltpu.VMEM((group - 1, piece, hidden), BF16),
        pltpu.VMEM((piece, n_t * wide), BF16),
        pltpu.VMEM((n_t - 1, piece, wide), BF16),
    ]
    shapes = (
        (3, piece, wide),
        (wide, piece) if turn else (piece, wide),
        (piece, hidden),
        (hidden, piece) if turn else (piece, hidden),
    )
    scratch += [pltpu.VMEM(shape, F32) for shape in shapes]
    copies = 120 + 20 * group
    scratch += [
        pltpu.SemaphoreType.DMA((copies,)),
        pltpu.SemaphoreType.DMA((copies,)),
        pltpu.SemaphoreType.DMA((24,)),
    ]
    results = [jax.ShapeDtypeStruct((rows, width), BF16)] * 2
    results += [jax.ShapeDtypeStruct(shape, F32) for shape in shapes]
    outs = pl.pallas_call(
        functools.partial(block_kernel, sizes),
        out_shape=(*results, jax.ShapeDtypeStruct((ROWS, width), F32)),
        in_specs=[hbm, hbm, vmem, hbm, hbm, hbm, hbm] + [vmem] * 8,
        out_specs=(hbm,) * 7,
        scratch_shapes=scratch,
        compiler_params=pltpu.CompilerParams(
            collective_id=0, has_side_effects=True, vmem_limit_bytes=63 << 20
        ),
    )(
        tokens.reshape(rows, width),
        cotangent.reshape(rows, width),
        keep_mask,
        jnp.transpose(attend_in, (1, 0, 2)),
        attend_out,
        expand_in,
        contract_out,
        *[
            v.reshape(1, piece)
            for v in (first_gain, first_shift, out_bias, second_gain, second_shift, contract_bias)
        ],
        expand_bias.T,
        attend_bias,
    )
    vector = jax.ShapeDtypeStruct((1, piece), F32)
    placed = pl.pallas_call(
        functools.partial(finish_call, (n_ctx, piece, cut, wide, hidden, width)),
        out_shape=(
            *results,
            *[vector] * 6,
            jax.ShapeDtypeStruct((cut, hidden // HD), F32),
            jax.ShapeDtypeStruct((2, heads, cut), F32),
        ),
        in_specs=[hbm] * 6 + [vmem],
        out_specs=(vmem,) * 14,
        scratch_shapes=[pltpu.SemaphoreType.DMA((6,))],
        compiler_params=pltpu.CompilerParams(vmem_limit_bytes=32 << 20),
    )(*outs)
    block_out, tokens_grad, d_win, d_wot, d_wup, d_wdt = placed[:6]
    vectors = [v.reshape(piece) for v in placed[6:12]]
    return (
        block_out.reshape(tokens.shape),
        tokens_grad.reshape(tokens.shape),
        vectors[0],
        vectors[1],
        jnp.transpose(d_win, (1, 0, 2)),
        placed[13],
        d_wot if turn else d_wot.T,
        vectors[2],
        vectors[3],
        vectors[4],
        d_wup,
        placed[12].T,
        d_wdt if turn else d_wdt.T,
        vectors[5],
    )


def solution(mesh):
    shape = (mesh.shape["dp"], mesh.shape["ctx"], mesh.shape["tensor"])
    vector = P(("dp", "ctx"))
    params = (
        vector,
        vector,
        P(("dp", "ctx"), None, "tensor"),
        P(None, "tensor", ("dp", "ctx")),
        P("tensor", ("dp", "ctx")),
        vector,
        vector,
        vector,
        P(("dp", "ctx"), "tensor"),
        P("tensor", ("dp", "ctx")),
        P("tensor", ("dp", "ctx")),
        vector,
    )
    rows = P("dp", "ctx", None)
    return jax.shard_map(
        functools.partial(on_device, shape),
        mesh=mesh,
        in_specs=(rows, P("dp", None), rows, *params),
        out_specs=(rows, rows, *params),
        check_vma=False,
    )
```

```python
import functools

import jax
import jax.numpy as jnp
from jax import lax
from jax.experimental import pallas as pl
from jax.experimental.pallas import tpu as pltpu
from jax.sharding import PartitionSpec as P

HD = 64
BUFFER = 64
LANES = 128
ROWS = 16
TILE = 256
BLOCK = 32
MESH = pl.DeviceIdType.MESH
F32 = jnp.float32
BF16 = jnp.bfloat16

eps = 1e-06
neg_big = -1e30
root_half = 0.7071067811865476
inv_root_two_pi = 0.3989422804014327


def flip(index, bits):
    out, bit = index, 1
    while bit <= bits:
        if bits & bit:
            out = out + bit - 2 * bit * lax.rem(lax.div(index, bit), 2)
        bit *= 2
    return out


def nn(left, right):
    return jnp.dot(left, right, preferred_element_type=F32)


def nt(left, right):
    return lax.dot_general(left, right, (((1,), (1,)), ((), ())), preferred_element_type=F32)


def tn(left, right):
    return lax.dot_general(left, right, (((0,), (0,)), ((), ())), preferred_element_type=F32)


def turned(value, ref):
    return value if value.shape == ref.shape else value.T


def norm_parts(values):
    mean = jnp.mean(values, axis=-1, keepdims=True)
    centered = values - mean
    spread = jnp.mean(centered * centered, axis=-1, keepdims=True)
    inv = lax.rsqrt(spread + eps)
    return centered * inv, inv


def block_kernel(
    sizes,
    tok_in,
    cot_in,
    keep,
    win,
    attend_out,
    wup,
    contract_out,
    first_gain,
    first_shift,
    out_bias,
    second_gain,
    second_shift,
    contract_bias,
    expand_bias,
    attend_bias,
    out_block,
    out_tokens,
    out_win,
    out_wot,
    out_wup,
    out_wdt,
    out_vec,
    tok,
    cot,
    a_out,
    c_out,
    vec,
    g_win,
    g_wot,
    g_wup,
    g_wdt,
    g_vec,
    vx,
    n1,
    h1,
    qkv,
    wq,
    wk,
    stat,
    alng,
    mixed,
    first,
    h2,
    ga,
    act,
    gi,
    part2,
    parts,
    part1,
    recv2,
    relay2,
    recvs,
    relays,
    recv1,
    relay1,
    gfirst,
    gdown,
    gown,
    gm,
    do,
    dqkv,
    block_own,
    tokens_own,
    gv,
    vr_sib,
    vr_plane,
    vr_z,
    b_win,
    b_wot,
    b_wup,
    b_wdt,
    s_win,
    s_wot,
    s_wup,
    s_wdt,
    t_win,
    t_wot,
    t_wup,
    t_wdt,
    r_win,
    r_wot,
    r_wup,
    r_wdt,
    o_wot,
    z_wot,
    f_win,
    f_wot,
    f_wup,
    f_wdt,
    send_sem,
    recv_sem,
    local_sem,
):
    n_dp, n_ctx, n_t, images, slots, width, wide, hidden, piece, cut = sizes
    rows = images * slots
    total = slots * n_ctx
    heads = wide // HD
    half = n_ctx // 2
    group = n_dp * half
    scale = HD ** (-0.5)
    dp = lax.axis_index("dp")
    ctx = lax.axis_index("ctx")
    z = lax.axis_index("tensor")
    high, core = lax.div(ctx, 2), lax.rem(ctx, 2)
    me = dp * half + high
    shard = me * 2 + core
    sib = (dp, flip(ctx, 1), z)

    def plane(k):
        other = flip(me, k)
        return (lax.div(other, half), lax.rem(other, half) * 2 + core, z)

    def ctx_at(k):
        return flip(high, k) * 2 + core

    def zpeer(k):
        return (dp, ctx, flip(z, k))

    def slot_at(index):
        return pl.ds(pl.multiple_of(index * slots, ROWS), slots)

    def lane_at(index, size):
        return pl.ds(pl.multiple_of(index * size, size), size)

    own = slot_at(ctx)
    mine = slot_at(z)

    cut_at = ROWS * ((slots // ROWS + 1) // 2)
    starts = (0, cut_at)
    sizes_of = (cut_at, slots - cut_at)
    bases = (0, images * cut_at)

    def chunk(c):
        return slice(bases[c], bases[c] + images * sizes_of[c])

    def rows_at(c, image):
        first_row = bases[c] + image * sizes_of[c]
        return pl.ds(pl.multiple_of(first_row, ROWS), sizes_of[c])

    def slot_part(c):
        return slice(starts[c], starts[c] + sizes_of[c])

    def split_rows(ref, image, lanes, value):
        for c in range(2):
            ref[rows_at(c, image), lanes] = value[slot_part(c)]

    count = [0, 0]
    pending = []

    def send(src, dst, device):
        index = count[0]
        count[0] += 1
        copy = pltpu.make_async_remote_copy(
            src_ref=src,
            dst_ref=dst,
            send_sem=send_sem.at[index],
            recv_sem=recv_sem.at[index],
            device_id=device,
            device_id_type=MESH,
        )
        copy.start()
        pending.append(copy)
        return copy

    inside = lax.rem(z - lax.div(z, 2), 2) == 1
    at_end = lax.rem(z - lax.div(z, 2), 2) == 0
    guarded = []

    def fresh():
        count[0] += 1
        return count[0] - 1

    def remote(src, dst, device, out_index, in_index):
        return pltpu.make_async_remote_copy(
            src_ref=src,
            dst_ref=dst,
            send_sem=send_sem.at[out_index],
            recv_sem=recv_sem.at[in_index],
            device_id=device,
            device_id_type=MESH,
        )

    def send_if(flag, make):
        guarded.append((flag, make))

        @pl.when(flag)
        def _():
            make().start()

    def complete(copy):
        pending[:] = [other for other in pending if other is not copy]
        copy.wait()

    def local(src, dst):
        index = count[1]
        count[1] += 1
        copy = pltpu.make_async_copy(src, dst, local_sem.at[index])
        copy.start()
        return copy

    planes = range(1, group)
    zs = range(1, n_t)

    def at_win(m, c):
        return g_win.at[:, m, c]

    def at_wot(m, c):
        return g_wot.at[m, c, :, lane_at(z, wide)]

    def at_wup(m, c):
        return g_wup.at[m, c]

    def at_wdt(m, c):
        return g_wdt.at[m, c]

    def at_vec(m, c):
        return g_vec.at[m, c]

    barrier = pltpu.get_barrier_semaphore()
    for device in [plane(k) for k in planes] + [sib] + [zpeer(k) for k in zs]:
        pl.semaphore_signal(barrier, inc=1, device_id=device, device_id_type=MESH)
    a_out_load = local(attend_out, a_out)
    def load_rows(source, ref):
        return [
            local(
                source.at[image * slots + starts[c] : image * slots + starts[c] + sizes_of[c], :],
                ref.at[rows_at(c, image), :],
            )
            for c in range(2)
            for image in range(images)
        ]

    tok_load = load_rows(tok_in, tok)
    win_own = local(win, at_win(me, core))
    c_out_load = local(contract_out, c_out)
    cot_load = load_rows(cot_in, cot)
    wup_own = local(wup, at_wup(me, core))

    vec[...] = jnp.zeros_like(vec)
    for line, ref in enumerate(
        (first_gain, first_shift, out_bias, second_gain, second_shift, contract_bias)
    ):
        vec[line : line + 1, 0:piece] = ref[...].astype(F32)
    vec[8 : 8 + cut, 0 : hidden // HD] = expand_bias[...].astype(F32)
    for j in range(2):
        vec[16 + j * heads : 16 + (j + 1) * heads, 0:cut] = attend_bias[j].astype(F32)
    g_vec[me, core] = vec[...]
    gv[...] = jnp.zeros_like(gv)
    unit_one = (
        lax.broadcasted_iota(jnp.int32, (piece, piece), 0)
        == lax.broadcasted_iota(jnp.int32, (piece, piece), 1)
    ).astype(F32)
    unit_one = unit_one.astype(BF16)
    a_out_load.wait()
    g_wot[me, core, :, lane_at(z, wide)] = nt(unit_one, a_out[...]).astype(BF16)
    pl.semaphore_wait(barrier, group + n_t - 1)

    def gather_start(src, at):
        far = [send(src, at(me, core), plane(k)) for k in planes]
        return far, send(src, at(me, core), sib)

    def gather_forward(started, at):
        out = []
        for k in planes:
            started[0][k - 1].wait_recv()
            there = at(flip(me, k), core)
            out.append(send(there, there, sib))
        return out

    def gather_finish(started, passed):
        started[1].wait_recv()
        for copy in passed:
            copy.wait_recv()

    def ctx_start(at):
        far = [send(at(ctx), at(ctx), (dp, ctx_at(k), z)) for k in range(1, half)]
        return far, send(at(ctx), at(ctx), sib)

    def ctx_forward(started, at):
        out = []
        for k in range(1, half):
            started[0][k - 1].wait_recv()
            out.append(send(at(ctx_at(k)), at(ctx_at(k)), sib))
        return out

    def ctx_finish(started, passed):
        started[1].wait_recv()
        for copy in passed:
            copy.wait_recv()

    def wot_piece(m, index):
        return g_wot.at[m, core, :, lane_at(index, wide)]

    vec_started = gather_start(vec, at_vec)
    win_started = gather_start(win, at_win)
    wot_started = gather_start(at_wot(me, core), at_wot)
    wot_z = [[send(wot_piece(me, z), wot_piece(me, z), zpeer(k)) for k in zs]]

    for copy in tok_load:
        copy.wait()

    def first_norm(step, carry):
        at = pl.ds(pl.multiple_of(step * BLOCK, BLOCK), BLOCK)
        normed, _ = norm_parts(tok[at, :].astype(F32))
        n1[at, :] = normed
        return carry

    lax.fori_loop(0, rows // BLOCK, first_norm, 0)

    vec_passed = gather_forward(vec_started, at_vec)
    gather_finish(vec_started, vec_passed)
    shape = (2 * ROWS, width)
    line_id = lax.broadcasted_iota(jnp.int32, shape, 0)
    lane_id = lax.broadcasted_iota(jnp.int32, shape, 1)
    source = lax.broadcasted_iota(jnp.int32, (LANES, width), 0)
    target = lax.broadcasted_iota(jnp.int32, (LANES, width), 1)
    by_unit = jnp.where(target // HD == source, 1.0, 0.0).astype(BF16)
    for_unit = lane_id % HD - (line_id - 8)
    for_head = lane_id // HD == (line_id - 16) % heads

    def place(index, carry):
        one, two, three = carry
        shares = g_vec[lax.div(index, 2), lax.rem(index, 2)].astype(BF16)
        by_width = jnp.where(target - source == index * piece, 1.0, 0.0).astype(BF16)
        by_channel = jnp.where(target % HD - source == index * cut, 1.0, 0.0).astype(BF16)
        one = one + nn(shares, by_width)
        two = two + jnp.where(for_unit == index * cut, nn(shares, by_unit), 0.0)
        three = three + jnp.where(for_head, nn(shares, by_channel), 0.0)
        return one, two, three

    zero = jnp.zeros(shape, F32)
    one, two, three = lax.fori_loop(0, 2 * group, place, (zero, zero, zero))
    vx[0:8, :] = one[0:8]
    vx[8:9, :] = jnp.sum(two[8 : 8 + cut], axis=0, keepdims=True)
    vx[9:10, :] = jnp.sum(three[16 : 16 + heads], axis=0, keepdims=True)
    vx[10:11, :] = jnp.sum(three[16 + heads : 16 + 2 * heads], axis=0, keepdims=True)

    def first_hidden(step, carry):
        at = pl.ds(pl.multiple_of(step * BLOCK, BLOCK), BLOCK)
        h1[at, :] = (n1[at, :] * vx[0:1, :] + vx[1:2, :]).astype(BF16)
        return carry

    lax.fori_loop(0, rows // BLOCK, first_hidden, 0)

    c_out_load.wait()

    def turn(step, carry):
        at = lane_at(step, TILE)
        g_wdt[me, core, :, at] = nt(unit_one, c_out[at, :]).astype(BF16)
        return carry

    lax.fori_loop(0, hidden // TILE, turn, 0)

    lengths = BUFFER + jnp.sum(keep[...], axis=1, keepdims=True)
    slot_id = lax.broadcasted_iota(jnp.int32, (slots, 1), 0) + ctx * slots
    key_id = lax.broadcasted_iota(jnp.int32, (1, total), 1)
    head_of = lax.broadcasted_iota(jnp.int32, (slots, wide), 1) // HD
    spot = lax.broadcasted_iota(jnp.int32, (slots, total), 1) == slot_id

    def stack_heads(block):
        wider = block.astype(F32)
        return jnp.concatenate(
            [jnp.where(head_of == h, wider, 0.0).astype(BF16) for h in range(heads)], axis=0
        )

    def pick_heads(block):
        out = jnp.where(head_of == 0, block[0:slots], 0.0)
        for h in range(1, heads):
            out = jnp.where(head_of == h, block[h * slots : (h + 1) * slots], out)
        return out

    def put_rows(ref, image, column):
        for h in range(heads):
            part = jnp.where(spot, column[h * slots : (h + 1) * slots], 0.0)
            line = image * heads + h
            ref[ctx, line : line + 1, :] = jnp.sum(part, axis=0, keepdims=True)

    win_passed = gather_forward(win_started, at_win)
    win_own.wait()
    gather_finish(win_started, win_passed)

    def project(j, bias):
        out = nn(h1[...], g_win[j].reshape(width, wide))
        if bias is not None:
            out = out + vx[bias : bias + 1, 0:wide]
        out = out.astype(BF16)
        for c in range(2):
            place_at = pl.ds(pl.multiple_of(ctx * slots + starts[c], ROWS), sizes_of[c])
            block = out[chunk(c)].reshape(images, sizes_of[c], wide)
            qkv[:, place_at, j * wide : (j + 1) * wide] = block

    def at_kv(index):
        return qkv.at[:, slot_at(index), wide : 3 * wide]

    def at_q(index):
        return qkv.at[:, slot_at(index), 0:wide]

    project(1, None)
    project(2, 10)
    kv_started = ctx_start(at_kv)
    wup_started = gather_start(wup, at_wup)
    wdt_started = gather_start(at_wdt(me, core), at_wdt)
    wot_passed = []
    for k in planes:
        wot_started[0][k - 1].wait_recv()
        there = wot_piece(flip(me, k), z)
        wot_z.append([send(there, there, zpeer(j)) for j in zs])
        wot_passed.append(send(there, there, sib))
    project(0, 9)
    q_started = ctx_start(at_q)
    kv_passed = ctx_forward(kv_started, at_kv)
    ctx_finish(kv_started, kv_passed)

    def at_mixed(index, c):
        return mixed.at[chunk(c), lane_at(index, wide)]

    for image in range(images):
        key_live = key_id < lengths[image : image + 1, :]
        stacked = stack_heads(qkv[image, own, 0:wide])
        scores = nt(stacked, qkv[image, :, wide : 2 * wide]) * scale
        scores = jnp.where(key_live, scores, neg_big)
        top = jnp.max(scores, axis=-1, keepdims=True)
        expo = jnp.exp(scores - top)
        whole = jnp.sum(expo, axis=-1, keepdims=True)
        probs = expo / whole
        wq[image] = probs
        put_rows(stat, image, top + jnp.log(whole))
        out = nn(probs.astype(BF16), qkv[image, :, 2 * wide : 3 * wide])
        split_rows(mixed, image, lane_at(z, wide), pick_heads(out).astype(BF16))
    mixed_sent = [
        [send(at_mixed(z, c), at_mixed(z, c), zpeer(k)) for k in reversed(zs)] for c in range(2)
    ]

    def at_stat(index):
        return stat.at[index]

    stat_started = ctx_start(at_stat)

    for copy in cot_load:
        copy.wait()
    row_live = []
    for image in range(images):
        row_live.append(slot_id < lengths[image : image + 1, :])
        for c in range(2):
            at = rows_at(c, image)
            live = row_live[image][slot_part(c)]
            gdown[at, :] = jnp.where(live, cot[at, :].astype(F32), 0.0).astype(BF16)

    gather_finish(wot_started, wot_passed)
    wot_more = []
    for order, block in enumerate(wot_z):
        for k in zs:
            block[k - 1].wait_recv()
            there = wot_piece(flip(me, order), flip(z, k))
            wot_more.append(send(there, there, sib))
    wup_passed = gather_forward(wup_started, at_wup)
    wup_own.wait()
    for copy in wot_more:
        copy.wait_recv()

    some = group // (width // TILE)

    def scatter(part, recv, relay, c):
        marks = [fresh() for _ in range(4)]

        def onward(j):
            return remote(
                part.at[rows_at(c, flip(z, 3 - j)), :],
                relay.at[j, slot_part(c), :],
                zpeer(1),
                marks[j],
                marks[j],
            )

        def passed(j):
            return remote(
                relay.at[j, slot_part(c), :],
                recv.at[1, slot_part(c), :],
                zpeer(2 + j),
                marks[2 + j],
                marks[2],
            )

        for j in range(2):
            send_if(at_end, functools.partial(onward, j))
        near = send(
            part.at[rows_at(c, flip(z, 1)), :], recv.at[0, slot_part(c), :], zpeer(1)
        )

        def pass_on():
            for j in range(2):

                @pl.when(inside)
                def _():
                    onward(j).wait_recv()
                    value = part[rows_at(c, flip(z, 2 + j)), :].astype(F32)
                    value = value + relay[j, slot_part(c), :].astype(F32)
                    relay[j, slot_part(c), :] = value.astype(BF16)

                send_if(inside, functools.partial(passed, j))

        def finish():
            near.wait_recv()
            passed(0).wait_recv()

        return pass_on, finish

    def spread(source, at):
        marks = [fresh() for _ in range(4)]
        near = send(source, at(z), zpeer(1))

        def far(k):
            return remote(source, at(z), zpeer(k), marks[k - 2], marks[k - 2])

        def passed(k):
            block = at(flip(z, k))
            return remote(block, block, zpeer(1), marks[k], marks[3 - k])

        send_if(at_end, functools.partial(far, 2))
        send_if(inside, functools.partial(far, 3))

        def pass_on():
            for k in (3, 2):

                @pl.when(inside)
                def _():
                    far(k).wait_recv()

                send_if(inside, functools.partial(passed, k))

        def finish():
            near.wait_recv()

            @pl.when(at_end)
            def _():
                far(2).wait_recv()
                far(3).wait_recv()

        return pass_on, finish

    def arrived(part, recv, c, at, size):
        here = pl.ds(pl.multiple_of(bases[c] + z * sizes_of[c] + at, ROWS), size)
        there = pl.ds(pl.multiple_of(starts[c] + at, ROWS), size)
        out = part[here, :].astype(F32)
        for j in range(2):
            out = out + recv[j, there, :].astype(F32)
        return out

    def attended(c):
        at_rows = chunk(c)
        for copy in mixed_sent[c]:
            copy.wait_recv()

        def project_out(step, carry):
            weight = g_wot[pl.ds(step * some, some)].reshape(TILE, n_t * wide)
            first[at_rows, lane_at(step, TILE)] = nt(mixed[at_rows, :], weight)
            return carry

        lax.fori_loop(0, width // TILE, project_out, 0)

        def second_norm(step, carry):
            at = pl.ds(pl.multiple_of(bases[c] + step * BLOCK, BLOCK), BLOCK)
            value = tok[at, :].astype(F32) + first[at, :] + vx[2:3, :]
            first[at, :] = value
            normed, _ = norm_parts(value)
            h2[at, :] = (normed * vx[3:4, :] + vx[4:5, :]).astype(BF16)
            return carry

        lax.fori_loop(0, images * sizes_of[c] // BLOCK, second_norm, 0)

    def feed_forward(c):
        at_rows = chunk(c)

        def expand(step, carry):
            at = lane_at(step, TILE)
            weight = g_wup[:, :, :, at].reshape(width, TILE)
            inner = nn(h2[at_rows, :], weight) + vx[8:9, at]
            share = 0.5 * (1.0 + lax.erf(inner * root_half))
            act[at_rows, at] = (inner * share).astype(BF16)
            slope = share + inner * jnp.exp(-0.5 * inner * inner) * inv_root_two_pi
            grad = (ga[at_rows, at] * slope).astype(BF16)
            gi[at_rows, at] = grad
            gv[8:9, at] += jnp.sum(grad.astype(F32), axis=0, keepdims=True)
            return carry

        lax.fori_loop(0, hidden // TILE, expand, 0)

        def up_back(step, carry):
            weight = g_wup[pl.ds(step * some, some)].reshape(TILE, hidden)
            part2[at_rows, lane_at(step, TILE)] = nt(gi[at_rows, :], weight).astype(BF16)
            return carry

        lax.fori_loop(0, width // TILE, up_back, 0)
        return scatter(part2, recv2, relay2, c)

    for c in range(2):
        attended(c)
    wdt_passed = gather_forward(wdt_started, at_wdt)
    gather_finish(wup_started, wup_passed)
    gather_finish(wdt_started, wdt_passed)

    def down_back(step, carry):
        at = lane_at(step, TILE)
        ga[:, at] = nn(gdown[...], g_wdt[:, :, :, at].reshape(width, TILE))
        return carry

    lax.fori_loop(0, hidden // TILE, down_back, 0)
    sent2 = [feed_forward(c) for c in range(2)]

    def contract(step, carry):
        weight = g_wdt[pl.ds(step * some, some)].reshape(TILE, hidden)
        parts[:, lane_at(step, TILE)] = nt(act[...], weight).astype(BF16)
        return carry

    lax.fori_loop(0, width // TILE, contract, 0)

    def wide_grad(buf, left, right, lanes):
        def one(step, carry):
            at = lane_at(step, TILE)
            out = tn(left[...], right[:, at]).astype(BF16)
            buf[:, :, :, at] = out.reshape(group, 2, piece, TILE)
            return carry

        lax.fori_loop(0, lanes // TILE, one, 0)

    def grad_near(buf, near):
        return send(buf.at[:, 1 - core], near, sib)

    def grad_far(copy, buf, near, both, recv):
        copy.wait_recv()

        def one(m, carry):
            both[m] = (buf[m, core].astype(F32) + near[m].astype(F32)).astype(BF16)
            return carry

        lax.fori_loop(0, group, one, 0)
        return [send(both.at[flip(me, k)], recv.at[k - 1], plane(k)) for k in reversed(planes)]

    def grad_sum(copies, both, recv):
        for copy in copies:
            copy.wait_recv()
        value = both[me].astype(F32)
        for k in planes:
            value = value + recv[k - 1].astype(F32)
        return value

    wide_grad(b_wdt, gdown, act, hidden)
    wdt_near = grad_near(b_wdt, s_wdt)
    sent2[0][0]()
    wide_grad(b_wup, h2, gi, hidden)
    wup_near = grad_near(b_wup, s_wup)
    sent2[1][0]()
    wdt_far = grad_far(wdt_near, b_wdt, s_wdt, t_wdt, r_wdt)

    q_passed = ctx_forward(q_started, at_q)
    stat_passed = ctx_forward(stat_started, at_stat)
    ctx_finish(q_started, q_passed)
    ctx_finish(stat_started, stat_passed)
    for image in range(images):
        stacked = stack_heads(qkv[image, own, wide : 2 * wide])
        scores = nt(stacked, qkv[image, :, 0:wide]) * scale
        for h in range(heads):
            line = image * heads + h
            level = stat[0, line : line + 1, :]
            for other in range(1, n_ctx):
                level = level + stat[other, line : line + 1, :]
            block = scores[h * slots : (h + 1) * slots]
            block = jnp.where(row_live[image], block, neg_big)
            wk[image, h * slots : (h + 1) * slots, :] = jnp.exp(block - level)

    own_live = slot_id < jnp.sum(
        jnp.where(lax.broadcasted_iota(jnp.int32, (images, 1), 0) == z, lengths, 0),
        axis=0,
        keepdims=True,
    )

    def add_line(line, value):
        gv[line : line + 1, :] += jnp.sum(value, axis=0, keepdims=True)

    def norm_back(grad, normed, inv, gain):
        scaled = grad * gain
        inner = (
            scaled
            - jnp.mean(scaled, axis=-1, keepdims=True)
            - normed * jnp.mean(scaled * normed, axis=-1, keepdims=True)
        )
        return inner * inv

    def second_back(c):
        sent2[c][1]()

        def one(step, carry):
            at = step * ROWS
            here = pl.ds(pl.multiple_of(bases[c] + z * sizes_of[c] + at, ROWS), ROWS)
            grad = arrived(part2, recv2, c, at, ROWS)
            normed, inv = norm_parts(first[here, :])
            rows_grad = gdown[here, :].astype(F32)
            value = rows_grad + norm_back(grad, normed, inv, vx[3:4, :])
            there = pl.ds(pl.multiple_of(starts[c] + at, ROWS), ROWS)
            gfirst[there, :] = value
            gown[there, :] = value.astype(BF16)
            add_line(3, grad * normed)
            add_line(4, grad)
            add_line(5, rows_grad)
            add_line(2, value)
            return carry

        lax.fori_loop(0, sizes_of[c] // ROWS, one, 0)

        def mixed_back(step, carry):
            at = lane_at(step, wide)
            weight = g_wot[:, :, :, at].reshape(width, wide)
            gm[slot_part(c), at] = nn(gown[slot_part(c), :], weight).astype(BF16)
            return carry

        lax.fori_loop(0, n_t, mixed_back, 0)
        place_at = pl.ds(pl.multiple_of(ctx * slots + starts[c], ROWS), sizes_of[c])
        sent = [
            send(
                gm.at[slot_part(c), lane_at(flip(z, k), wide)],
                do.at[z, place_at, :],
                zpeer(k),
            )
            for k in reversed(zs)
        ]
        do[z, place_at, :] = gm[slot_part(c), lane_at(z, wide)]
        return sent

    to_heads = [second_back(c) for c in range(2)]
    sents = [scatter(parts, recvs, relays, c) for c in range(2)]

    def out_grad(step, carry):
        at = lane_at(step, TILE)
        part = jnp.concatenate([mixed[rows_at(c, z), at] for c in range(2)], axis=0)
        out = tn(gown[...], part).astype(BF16)
        b_wot[:, :, :, at] = out.reshape(group, 2, piece, TILE)
        return carry

    lax.fori_loop(0, n_t * wide // TILE, out_grad, 0)
    wot_near = grad_near(b_wot, s_wot)

    stays = []

    def block_rows(c):
        sents[c][1]()
        value = first[rows_at(c, z), :] + arrived(parts, recvs, c, 0, sizes_of[c]) + vx[5:6, :]
        value = jnp.where(own_live[slot_part(c)], value, 0.0)
        block_own[slot_part(c), :] = value.astype(BF16)
        return to_all(block_own, out_block, c)

    def to_all(source, target, c):
        def at(index):
            here = pl.ds(pl.multiple_of(index * slots + starts[c], ROWS), sizes_of[c])
            return target.at[here, :]

        part = source.at[slot_part(c), :]
        stays.append(local(part, at(z)))
        return spread(part, at)

    def at_do(c):
        def at(index):
            first_row = index * slots + starts[c]
            return do.at[:, pl.ds(pl.multiple_of(first_row, ROWS), sizes_of[c]), :]

        return at

    do_started = []
    for c in range(2):
        for copy in to_heads[c]:
            copy.wait_recv()
        do_started.append(ctx_start(at_do(c)))

    for image in range(images):
        stacked = stack_heads(do[image, own, :])
        grad_probs = nt(stacked, qkv[image, :, 2 * wide : 3 * wide])
        weights = wq[image]
        along = jnp.sum(grad_probs * weights, axis=-1, keepdims=True)
        put_rows(alng, image, along)
        grad_scores = (weights * (grad_probs - along)).astype(BF16)
        out = pick_heads(nn(grad_scores, qkv[image, :, wide : 2 * wide])) * scale
        split_rows(dqkv, image, slice(0, wide), out.astype(BF16))

    def at_along(index):
        return alng.at[index]

    along_started = ctx_start(at_along)
    wot_far = grad_far(wot_near, b_wot, s_wot, t_wot, r_wot)
    wup_far = grad_far(wup_near, b_wup, s_wup, t_wup, r_wup)
    sents[0][0]()
    do_passed = [ctx_forward(do_started[c], at_do(c)) for c in range(2)]
    along_passed = ctx_forward(along_started, at_along)
    for c in range(2):
        ctx_finish(do_started[c], do_passed[c])
    ctx_finish(along_started, along_passed)

    for image in range(images):
        stacked = stack_heads(qkv[image, own, 2 * wide : 3 * wide])
        grad_probs = nt(stacked, do[image])
        weights = wk[image]
        lines = []
        for h in range(heads):
            line = image * heads + h
            level = alng[0, line : line + 1, :]
            for other in range(1, n_ctx):
                level = level + alng[other, line : line + 1, :]
            lines.append(grad_probs[h * slots : (h + 1) * slots] - level)
        grad_scores = (weights * jnp.concatenate(lines, axis=0)).astype(BF16)
        out = pick_heads(nn(grad_scores, qkv[image, :, 0:wide])) * scale
        split_rows(dqkv, image, slice(wide, 2 * wide), out.astype(BF16))
        out = pick_heads(nn(weights.astype(BF16), do[image]))
        split_rows(dqkv, image, slice(2 * wide, 3 * wide), out.astype(BF16))

    def in_back(c):
        at_rows = chunk(c)

        def one(step, carry):
            out = None
            for j in range(3):
                weight = g_win[j, pl.ds(step * some, some)].reshape(TILE, wide)
                term = nt(dqkv[at_rows, j * wide : (j + 1) * wide], weight)
                out = term if out is None else out + term
            part1[at_rows, lane_at(step, TILE)] = out.astype(BF16)
            return carry

        lax.fori_loop(0, width // TILE, one, 0)
        return scatter(part1, recv1, relay1, c)

    sent1 = [in_back(c) for c in range(2)]
    sents[1][0]()

    for j in range(3):
        out = tn(h1[...], dqkv[:, j * wide : (j + 1) * wide]).astype(BF16)
        b_win[j] = out.reshape(group, 2, piece, wide)
    win_near = send(b_win.at[:, :, 1 - core], s_win, sib)
    sent1[0][0]()
    tail = [block_rows(0)]
    gv[9:10, 0:wide] = jnp.sum(dqkv[:, 0:wide].astype(F32), axis=0, keepdims=True)
    gv[10:11, 0:wide] = jnp.sum(dqkv[:, 2 * wide : 3 * wide].astype(F32), axis=0, keepdims=True)
    f_wdt[...] = turned(grad_sum(wdt_far, t_wdt, r_wdt), f_wdt)
    stays.append(local(f_wdt, out_wdt))
    win_near.wait_recv()
    for j in range(3):
        both = b_win[j, :, pl.ds(core, 1)].reshape(group, piece, wide).astype(F32)
        t_win[:, j] = (both + s_win[j].astype(F32)).astype(BF16)
    win_far = [send(t_win.at[flip(me, k)], r_win.at[k - 1], plane(k)) for k in reversed(planes)]

    sent1[1][0]()
    tail.append(block_rows(1))
    whole_rows = grad_sum(wot_far, t_wot, r_wot)
    o_wot[...] = whole_rows.astype(BF16)
    to_owner = [
        send(o_wot.at[:, lane_at(flip(z, k), wide)], z_wot.at[k - 1], zpeer(k))
        for k in reversed(zs)
    ]
    f_wup[...] = grad_sum(wup_far, t_wup, r_wup)
    stays.append(local(f_wup, out_wup))

    def first_back(c):
        sent1[c][1]()

        def one(step, carry):
            at = step * ROWS
            here = pl.ds(pl.multiple_of(bases[c] + z * sizes_of[c] + at, ROWS), ROWS)
            grad = arrived(part1, recv1, c, at, ROWS)
            normed, inv = norm_parts(tok[here, :].astype(F32))
            there = pl.ds(pl.multiple_of(starts[c] + at, ROWS), ROWS)
            value = gfirst[there, :] + norm_back(grad, normed, inv, vx[0:1, :])
            tokens_own[there, :] = value.astype(BF16)
            add_line(0, grad * normed)
            add_line(1, grad)
            return carry

        lax.fori_loop(0, sizes_of[c] // ROWS, one, 0)
        return to_all(tokens_own, out_tokens, c)

    for c in range(2):
        tail[c][0]()
    for c in range(2):
        tail.append(first_back(c))

    near = send(gv, vr_sib, sib)
    tail[2][0]()
    complete(near)
    gv[...] = gv[...] + vr_sib[...]
    far = [send(gv, vr_plane.at[k - 1], plane(k)) for k in planes]
    tail[3][0]()
    f_win[...] = grad_sum(win_far, t_win, r_win)
    stays.append(local(f_win, out_win))
    for copy in far:
        complete(copy)
    value = gv[...]
    for k in planes:
        value = value + vr_plane[k - 1]
    gv[...] = value
    lanes = lane_at(lax.div(shard * piece, LANES), LANES)
    far = [send(gv.at[0:8, lanes], vr_z.at[k - 1], zpeer(k)) for k in zs]
    for copy in to_owner:
        copy.wait_recv()
    value = o_wot[:, lane_at(z, wide)].astype(F32)
    for k in zs:
        value = value + z_wot[k - 1].astype(F32)
    f_wot[...] = turned(value, f_wot)
    stays.append(local(f_wot, out_wot))
    for copy in far:
        complete(copy)
    value = gv[0:8, lanes]
    for k in zs:
        value = value + vr_z[k - 1]
    gv[0:8, lanes] = value
    stays.append(local(gv, out_vec))
    for _, finish in tail:
        finish()
    for copy in pending:
        copy.wait_send()
    for flag, make in guarded:

        @pl.when(flag)
        def _():
            make().wait_send()

    for copy in stays:
        copy.wait()


def finish_call(sizes, *refs):
    finish_kernel(sizes, *refs[:13], refs[13:19], *refs[19:])


def finish_kernel(
    sizes,
    in_block,
    in_tokens,
    in_win,
    in_wot,
    in_wup,
    in_wdt,
    in_vec,
    block,
    tokens,
    win,
    wot,
    wup,
    wdt,
    vectors,
    units,
    biases,
    sems,
):
    n_ctx, piece, cut, wide, hidden, width = sizes
    shard = lax.axis_index("dp") * n_ctx + lax.axis_index("ctx")
    pairs = [(in_block, block), (in_tokens, tokens), (in_win, win)]
    pairs += [(in_wot, wot), (in_wup, wup), (in_wdt, wdt)]
    copies = [pltpu.make_async_copy(a, b, sems.at[i]) for i, (a, b) in enumerate(pairs)]
    for copy in copies:
        copy.start()

    def exact(left, right):
        return jnp.dot(left, right, precision=lax.Precision.HIGHEST, preferred_element_type=F32)

    heads = wide // HD
    lane = lax.broadcasted_iota(jnp.int32, (width, piece), 0)
    slot = lax.broadcasted_iota(jnp.int32, (width, piece), 1)
    part = exact(in_vec[0:8, :], jnp.where(lane - slot == shard * piece, 1.0, 0.0))
    for line in range(6):
        vectors[line][...] = part[line : line + 1]
    channel = lax.broadcasted_iota(jnp.int32, (cut, hidden), 0)
    lane = lax.broadcasted_iota(jnp.int32, (cut, hidden), 1)
    chosen = jnp.where(lane % HD - channel == shard * cut, in_vec[8:9, 0:hidden], 0.0)
    lane = lax.broadcasted_iota(jnp.int32, (hidden, hidden // HD), 0)
    slot = lax.broadcasted_iota(jnp.int32, (hidden, hidden // HD), 1)
    units[...] = exact(chosen, jnp.where(lane // HD == slot, 1.0, 0.0))
    lane = lax.broadcasted_iota(jnp.int32, (wide, cut), 0)
    slot = lax.broadcasted_iota(jnp.int32, (wide, cut), 1)
    pick = jnp.where(lane % HD - slot == shard * cut, 1.0, 0.0)
    head = lax.broadcasted_iota(jnp.int32, (heads, wide), 0)
    lane = lax.broadcasted_iota(jnp.int32, (heads, wide), 1)
    for j in range(2):
        chosen = jnp.where(lane // HD == head, in_vec[9 + j : 10 + j, 0:wide], 0.0)
        biases[j] = exact(chosen, pick)
    for copy in copies:
        copy.wait()


def on_device(
    mesh_shape,
    tokens,
    keep_mask,
    cotangent,
    first_gain,
    first_shift,
    attend_in,
    attend_bias,
    attend_out,
    out_bias,
    second_gain,
    second_shift,
    expand_in,
    expand_bias,
    contract_out,
    contract_bias,
):
    n_dp, n_ctx, n_t = mesh_shape
    images, slots, width = tokens.shape
    piece, _, wide = attend_in.shape
    hidden = expand_in.shape[1]
    cut = expand_bias.shape[1]
    rows = images * slots
    group = n_dp * n_ctx // 2
    total = slots * n_ctx
    heads = wide // HD
    turn = piece % LANES == 0
    sizes = (n_dp, n_ctx, n_t, images, slots, width, wide, hidden, piece, cut)
    vmem = pl.BlockSpec(memory_space=pltpu.VMEM)
    hbm = pl.BlockSpec(memory_space=pl.ANY)
    scratch = [
        pltpu.VMEM((rows, width), BF16),
        pltpu.VMEM((rows, width), BF16),
        pltpu.VMEM((wide, piece), BF16),
        pltpu.VMEM((hidden, piece), BF16),
        pltpu.VMEM((2 * ROWS, LANES), F32),
        pltpu.VMEM((3, group, 2, piece, wide), BF16),
        pltpu.VMEM((group, 2, piece, n_t * wide), BF16),
        pltpu.VMEM((group, 2, piece, hidden), BF16),
        pltpu.VMEM((group, 2, piece, hidden), BF16),
        pltpu.VMEM((group, 2, 2 * ROWS, LANES), F32),
        pltpu.VMEM((ROWS, width), F32),
        pltpu.VMEM((rows, width), F32),
        pltpu.VMEM((rows, width), BF16),
        pltpu.VMEM((images, total, 3 * wide), BF16),
        pltpu.VMEM((images, heads * slots, total), F32),
        pltpu.VMEM((images, heads * slots, total), F32),
        pltpu.VMEM((n_ctx, images * heads, total), F32),
        pltpu.VMEM((n_ctx, images * heads, total), F32),
        pltpu.VMEM((rows, n_t * wide), BF16),
        pltpu.VMEM((rows, width), F32),
        pltpu.VMEM((rows, width), BF16),
        pltpu.VMEM((rows, hidden), F32),
        pltpu.VMEM((rows, hidden), BF16),
        pltpu.VMEM((rows, hidden), BF16),
        pltpu.VMEM((rows, width), BF16),
        pltpu.VMEM((rows, width), BF16),
        pltpu.VMEM((rows, width), BF16),
        pltpu.VMEM((2, slots, width), BF16),
        pltpu.VMEM((2, slots, width), BF16),
        pltpu.VMEM((2, slots, width), BF16),
        pltpu.VMEM((2, slots, width), BF16),
        pltpu.VMEM((2, slots, width), BF16),
        pltpu.VMEM((2, slots, width), BF16),
        pltpu.VMEM((slots, width), F32),
        pltpu.VMEM((rows, width), BF16),
        pltpu.VMEM((slots, width), BF16),
        pltpu.VMEM((slots, n_t * wide), BF16),
        pltpu.VMEM((images, total, wide), BF16),
        pltpu.VMEM((rows, 3 * wide), BF16),
        pltpu.VMEM((slots, width), BF16),
        pltpu.VMEM((slots, width), BF16),
        pltpu.VMEM((ROWS, width), F32),
        pltpu.VMEM((ROWS, width), F32),
        pltpu.VMEM((group - 1, ROWS, width), F32),
        pltpu.VMEM((n_t - 1, 8, LANES), F32),
        pltpu.VMEM((3, group, 2, piece, wide), BF16),
        pltpu.VMEM((group, 2, piece, n_t * wide), BF16),
        pltpu.VMEM((group, 2, piece, hidden), BF16),
        pltpu.VMEM((group, 2, piece, hidden), BF16),
        pltpu.VMEM((3, group, piece, wide), BF16),
        pltpu.VMEM((group, piece, n_t * wide), BF16),
        pltpu.VMEM((group, piece, hidden), BF16),
        pltpu.VMEM((group, piece, hidden), BF16),
        pltpu.VMEM((group, 3, piece, wide), BF16),
        pltpu.VMEM((group, piece, n_t * wide), BF16),
        pltpu.VMEM((group, piece, hidden), BF16),
        pltpu.VMEM((group, piece, hidden), BF16),
        pltpu.VMEM((group - 1, 3, piece, wide), BF16),
        pltpu.VMEM((group - 1, piece, n_t * wide), BF16),
        pltpu.VMEM((group - 1, piece, hidden), BF16),
        pltpu.VMEM((group - 1, piece, hidden), BF16),
        pltpu.VMEM((piece, n_t * wide), BF16),
        pltpu.VMEM((n_t - 1, piece, wide), BF16),
    ]
    shapes = (
        (3, piece, wide),
        (wide, piece) if turn else (piece, wide),
        (piece, hidden),
        (hidden, piece) if turn else (piece, hidden),
    )
    scratch += [pltpu.VMEM(shape, F32) for shape in shapes]
    copies = 160 + 20 * group
    scratch += [
        pltpu.SemaphoreType.DMA((copies,)),
        pltpu.SemaphoreType.DMA((copies,)),
        pltpu.SemaphoreType.DMA((48,)),
    ]
    results = [jax.ShapeDtypeStruct((rows, width), BF16)] * 2
    results += [jax.ShapeDtypeStruct(shape, F32) for shape in shapes]
    outs = pl.pallas_call(
        functools.partial(block_kernel, sizes),
        out_shape=(*results, jax.ShapeDtypeStruct((ROWS, width), F32)),
        in_specs=[hbm, hbm, vmem, hbm, hbm, hbm, hbm] + [vmem] * 8,
        out_specs=(hbm,) * 7,
        scratch_shapes=scratch,
        compiler_params=pltpu.CompilerParams(
            collective_id=0, has_side_effects=True, vmem_limit_bytes=63 << 20
        ),
    )(
        tokens.reshape(rows, width),
        cotangent.reshape(rows, width),
        keep_mask,
        jnp.transpose(attend_in, (1, 0, 2)),
        attend_out,
        expand_in,
        contract_out,
        *[
            v.reshape(1, piece)
            for v in (first_gain, first_shift, out_bias, second_gain, second_shift, contract_bias)
        ],
        expand_bias.T,
        attend_bias,
    )
    vector = jax.ShapeDtypeStruct((1, piece), F32)
    placed = pl.pallas_call(
        functools.partial(finish_call, (n_ctx, piece, cut, wide, hidden, width)),
        out_shape=(
            *results,
            *[vector] * 6,
            jax.ShapeDtypeStruct((cut, hidden // HD), F32),
            jax.ShapeDtypeStruct((2, heads, cut), F32),
        ),
        in_specs=[hbm] * 6 + [vmem],
        out_specs=(vmem,) * 14,
        scratch_shapes=[pltpu.SemaphoreType.DMA((6,))],
        compiler_params=pltpu.CompilerParams(vmem_limit_bytes=63 << 20),
    )(*outs)
    block_out, tokens_grad, d_win, d_wot, d_wup, d_wdt = placed[:6]
    vectors = [v.reshape(piece) for v in placed[6:12]]
    return (
        block_out.reshape(tokens.shape),
        tokens_grad.reshape(tokens.shape),
        vectors[0],
        vectors[1],
        jnp.transpose(d_win, (1, 0, 2)),
        placed[13],
        d_wot if turn else d_wot.T,
        vectors[2],
        vectors[3],
        vectors[4],
        d_wup,
        placed[12].T,
        d_wdt if turn else d_wdt.T,
        vectors[5],
    )


def solution(mesh):
    shape = (mesh.shape["dp"], mesh.shape["ctx"], mesh.shape["tensor"])
    vector = P(("dp", "ctx"))
    params = (
        vector,
        vector,
        P(("dp", "ctx"), None, "tensor"),
        P(None, "tensor", ("dp", "ctx")),
        P("tensor", ("dp", "ctx")),
        vector,
        vector,
        vector,
        P(("dp", "ctx"), "tensor"),
        P("tensor", ("dp", "ctx")),
        P("tensor", ("dp", "ctx")),
        vector,
    )
    rows = P("dp", "ctx", None)
    return jax.shard_map(
        functools.partial(on_device, shape),
        mesh=mesh,
        in_specs=(rows, P("dp", None), rows, *params),
        out_specs=(rows, rows, *params),
        check_vma=False,
    )
```

```python
import functools

import jax
import jax.numpy as jnp
from jax import lax
from jax.experimental import pallas as pl
from jax.experimental.pallas import tpu as pltpu
from jax.sharding import PartitionSpec as P

HD = 64
BUFFER = 64
LANES = 128
ROWS = 16
TILE = 256
BLOCK = 32
MESH = pl.DeviceIdType.MESH
F32 = jnp.float32
BF16 = jnp.bfloat16

eps = 1e-06
neg_big = -1e30
root_half = 0.7071067811865476
inv_root_two_pi = 0.3989422804014327


def flip(index, bits):
    out, bit = index, 1
    while bit <= bits:
        if bits & bit:
            out = out + bit - 2 * bit * lax.rem(lax.div(index, bit), 2)
        bit *= 2
    return out


def nn(left, right):
    return jnp.dot(left, right, preferred_element_type=F32)


def nt(left, right):
    return lax.dot_general(left, right, (((1,), (1,)), ((), ())), preferred_element_type=F32)


def tn(left, right):
    return lax.dot_general(left, right, (((0,), (0,)), ((), ())), preferred_element_type=F32)


def turned(value, ref):
    return value if value.shape == ref.shape else value.T


def norm_parts(values):
    mean = jnp.mean(values, axis=-1, keepdims=True)
    centered = values - mean
    spread = jnp.mean(centered * centered, axis=-1, keepdims=True)
    inv = lax.rsqrt(spread + eps)
    return centered * inv, inv


def block_kernel(
    sizes,
    tok_in,
    cot_in,
    keep,
    win,
    attend_out,
    wup,
    contract_out,
    first_gain,
    first_shift,
    out_bias,
    second_gain,
    second_shift,
    contract_bias,
    expand_bias,
    attend_bias,
    out_block,
    out_tokens,
    out_win,
    out_wot,
    out_wup,
    out_wdt,
    out_vec,
    tok,
    cot,
    a_out,
    c_out,
    vec,
    g_win,
    g_wot,
    g_wup,
    g_wdt,
    g_vec,
    vx,
    n1,
    h1,
    qkv,
    wq,
    wk,
    stat,
    alng,
    mixed,
    first,
    h2,
    ga,
    act,
    gi,
    part2,
    parts,
    part1,
    recv2,
    relay2,
    recvs,
    relays,
    recv1,
    relay1,
    gfirst,
    gdown,
    gown,
    gm,
    do,
    dqkv,
    block_own,
    tokens_own,
    gv,
    early,
    early_sib,
    early_plane,
    early_z,
    late,
    late_sib,
    late_plane,
    late_z,
    b_win,
    b_wot,
    b_wup,
    b_wdt,
    s_win,
    s_wot,
    s_wup,
    s_wdt,
    t_win,
    t_wot,
    t_wup,
    t_wdt,
    r_win,
    r_wot,
    r_wup,
    r_wdt,
    o_wot,
    z_wot,
    f_win,
    f_wot,
    f_wup,
    f_wdt,
    send_sem,
    recv_sem,
    local_sem,
):
    n_dp, n_ctx, n_t, images, slots, width, wide, hidden, piece, cut = sizes
    rows = images * slots
    total = slots * n_ctx
    heads = wide // HD
    half = n_ctx // 2
    group = n_dp * half
    scale = HD ** (-0.5)
    dp = lax.axis_index("dp")
    ctx = lax.axis_index("ctx")
    z = lax.axis_index("tensor")
    high, core = lax.div(ctx, 2), lax.rem(ctx, 2)
    me = dp * half + high
    shard = me * 2 + core
    sib = (dp, flip(ctx, 1), z)

    def plane(k):
        other = flip(me, k)
        return (lax.div(other, half), lax.rem(other, half) * 2 + core, z)

    def ctx_at(k):
        return flip(high, k) * 2 + core

    def zpeer(k):
        return (dp, ctx, flip(z, k))

    def slot_at(index):
        return pl.ds(pl.multiple_of(index * slots, ROWS), slots)

    def lane_at(index, size):
        return pl.ds(pl.multiple_of(index * size, size), size)

    own = slot_at(ctx)
    mine = slot_at(z)

    cut_at = ROWS * (slots // ROWS // 2)
    starts = (0, cut_at)
    sizes_of = (cut_at, slots - cut_at)
    bases = (0, images * cut_at)

    def chunk(c):
        return slice(bases[c], bases[c] + images * sizes_of[c])

    def rows_at(c, image):
        first_row = bases[c] + image * sizes_of[c]
        return pl.ds(pl.multiple_of(first_row, ROWS), sizes_of[c])

    def slot_part(c):
        return slice(starts[c], starts[c] + sizes_of[c])

    def split_rows(ref, image, lanes, value):
        for c in range(2):
            ref[rows_at(c, image), lanes] = value[slot_part(c)]

    count = [0, 0]
    pending = []

    def send(src, dst, device):
        index = count[0]
        count[0] += 1
        copy = pltpu.make_async_remote_copy(
            src_ref=src,
            dst_ref=dst,
            send_sem=send_sem.at[index],
            recv_sem=recv_sem.at[index],
            device_id=device,
            device_id_type=MESH,
        )
        copy.start()
        pending.append(copy)
        return copy

    inside = lax.rem(z - lax.div(z, 2), 2) == 1
    at_end = lax.rem(z - lax.div(z, 2), 2) == 0
    guarded = []

    def fresh():
        count[0] += 1
        return count[0] - 1

    def remote(src, dst, device, out_index, in_index):
        return pltpu.make_async_remote_copy(
            src_ref=src,
            dst_ref=dst,
            send_sem=send_sem.at[out_index],
            recv_sem=recv_sem.at[in_index],
            device_id=device,
            device_id_type=MESH,
        )

    def send_if(flag, make):
        guarded.append((flag, make))

        @pl.when(flag)
        def _():
            make().start()

    def complete(copy):
        pending[:] = [other for other in pending if other is not copy]
        copy.wait()

    def local(src, dst):
        index = count[1]
        count[1] += 1
        copy = pltpu.make_async_copy(src, dst, local_sem.at[index])
        copy.start()
        return copy

    planes = range(1, group)
    zs = range(1, n_t)

    def at_win_kv(m, c):
        return g_win.at[1:3, m, c]

    def at_win_q(m, c):
        return g_win.at[0:1, m, c]

    def at_wot(m, c):
        return g_wot.at[m, c, :, lane_at(z, wide)]

    def at_wup(m, c):
        return g_wup.at[m, c]

    def at_wdt(m, c):
        return g_wdt.at[m, c]

    def at_vec(m, c):
        return g_vec.at[m, c]

    barrier = pltpu.get_barrier_semaphore()
    for device in [plane(k) for k in planes] + [sib] + [zpeer(k) for k in zs]:
        pl.semaphore_signal(barrier, inc=1, device_id=device, device_id_type=MESH)
    a_out_load = local(attend_out, a_out)
    def load_rows(source, ref):
        return [
            local(
                source.at[image * slots + starts[c] : image * slots + starts[c] + sizes_of[c], :],
                ref.at[rows_at(c, image), :],
            )
            for c in range(2)
            for image in range(images)
        ]

    tok_load = load_rows(tok_in, tok)
    win_own = local(win, g_win.at[:, me, core])
    c_out_load = local(contract_out, c_out)
    cot_load = load_rows(cot_in, cot)
    wup_own = local(wup, at_wup(me, core))

    vec[...] = jnp.zeros_like(vec)
    for line, ref in enumerate(
        (first_gain, first_shift, out_bias, second_gain, second_shift, contract_bias)
    ):
        vec[line : line + 1, 0:piece] = ref[...].astype(F32)
    vec[8 : 8 + cut, 0 : hidden // HD] = expand_bias[...].astype(F32)
    for j in range(2):
        vec[16 + j * heads : 16 + (j + 1) * heads, 0:cut] = attend_bias[j].astype(F32)
    g_vec[me, core] = vec[...]
    gv[...] = jnp.zeros_like(gv)
    unit_one = (
        lax.broadcasted_iota(jnp.int32, (piece, piece), 0)
        == lax.broadcasted_iota(jnp.int32, (piece, piece), 1)
    ).astype(F32)
    unit_one = unit_one.astype(BF16)
    a_out_load.wait()
    g_wot[me, core, :, lane_at(z, wide)] = nt(unit_one, a_out[...]).astype(BF16)
    pl.semaphore_wait(barrier, group + n_t - 1)

    def gather_start(src, at):
        far = [send(src, at(me, core), plane(k)) for k in planes]
        return far, send(src, at(me, core), sib)

    def gather_forward(started, at):
        out = []
        for k in planes:
            started[0][k - 1].wait_recv()
            there = at(flip(me, k), core)
            out.append(send(there, there, sib))
        return out

    def gather_finish(started, passed):
        started[1].wait_recv()
        for copy in passed:
            copy.wait_recv()

    relayed = group == 4 and piece % (2 * ROWS) == 0

    def relay_start(src, at):
        if not relayed:
            return gather_start(src, at)
        far = [send(src, at(me, core), plane(k)) for k in (1, 2)]
        return far, send(src, at(me, core), sib)

    def relay_forward(started, at):
        if not relayed:
            return gather_forward(started, at), []
        out, halves = [], []
        for k in (1, 2):
            started[0][k - 1].wait_recv()
            there = at(flip(me, k), core)
            part = there.at[pl.ds((k - 1) * (piece // 2), piece // 2)]
            halves.append(send(part, part, plane(3 - k)))
            out.append(send(there, there, sib))
        return out, halves

    def relay_last(halves, at):
        if not halves:
            return []
        for copy in halves:
            copy.wait_recv()
        there = at(flip(me, 3), core)
        return [send(there, there, sib)]

    def ctx_start(at):
        far = [send(at(ctx), at(ctx), (dp, ctx_at(k), z)) for k in range(1, half)]
        return far, send(at(ctx), at(ctx), sib)

    def ctx_forward(started, at):
        out = []
        for k in range(1, half):
            started[0][k - 1].wait_recv()
            out.append(send(at(ctx_at(k)), at(ctx_at(k)), sib))
        return out

    def ctx_finish(started, passed):
        started[1].wait_recv()
        for copy in passed:
            copy.wait_recv()

    def wot_piece(m, index):
        return g_wot.at[m, core, :, lane_at(index, wide)]

    vec_started = gather_start(vec, at_vec)
    kv_win_started = gather_start(win.at[1:3], at_win_kv)
    q_win_started = gather_start(win.at[0:1], at_win_q)
    wot_started = gather_start(at_wot(me, core), at_wot)
    wot_z = [[send(wot_piece(me, z), wot_piece(me, z), zpeer(k)) for k in zs]]

    for copy in tok_load:
        copy.wait()

    def first_norm(step, carry):
        at = pl.ds(pl.multiple_of(step * BLOCK, BLOCK), BLOCK)
        normed, _ = norm_parts(tok[at, :].astype(F32))
        n1[at, :] = normed
        return carry

    lax.fori_loop(0, rows // BLOCK, first_norm, 0)

    vec_passed = gather_forward(vec_started, at_vec)
    gather_finish(vec_started, vec_passed)
    shape = (2 * ROWS, width)
    line_id = lax.broadcasted_iota(jnp.int32, shape, 0)
    lane_id = lax.broadcasted_iota(jnp.int32, shape, 1)
    source = lax.broadcasted_iota(jnp.int32, (LANES, width), 0)
    target = lax.broadcasted_iota(jnp.int32, (LANES, width), 1)
    by_unit = jnp.where(target // HD == source, 1.0, 0.0).astype(BF16)
    for_unit = lane_id % HD - (line_id - 8)
    for_head = lane_id // HD == (line_id - 16) % heads

    def place(index, carry):
        one, two, three = carry
        shares = g_vec[lax.div(index, 2), lax.rem(index, 2)].astype(BF16)
        by_width = jnp.where(target - source == index * piece, 1.0, 0.0).astype(BF16)
        by_channel = jnp.where(target % HD - source == index * cut, 1.0, 0.0).astype(BF16)
        one = one + nn(shares, by_width)
        two = two + jnp.where(for_unit == index * cut, nn(shares, by_unit), 0.0)
        three = three + jnp.where(for_head, nn(shares, by_channel), 0.0)
        return one, two, three

    zero = jnp.zeros(shape, F32)
    one, two, three = lax.fori_loop(0, 2 * group, place, (zero, zero, zero))
    vx[0:8, :] = one[0:8]
    vx[8:9, :] = jnp.sum(two[8 : 8 + cut], axis=0, keepdims=True)
    vx[9:10, :] = jnp.sum(three[16 : 16 + heads], axis=0, keepdims=True)
    vx[10:11, :] = jnp.sum(three[16 + heads : 16 + 2 * heads], axis=0, keepdims=True)

    def first_hidden(step, carry):
        at = pl.ds(pl.multiple_of(step * BLOCK, BLOCK), BLOCK)
        h1[at, :] = (n1[at, :] * vx[0:1, :] + vx[1:2, :]).astype(BF16)
        return carry

    lax.fori_loop(0, rows // BLOCK, first_hidden, 0)

    c_out_load.wait()

    def turn(step, carry):
        at = lane_at(step, TILE)
        g_wdt[me, core, :, at] = nt(unit_one, c_out[at, :]).astype(BF16)
        return carry

    lax.fori_loop(0, hidden // TILE, turn, 0)

    lengths = BUFFER + jnp.sum(keep[...], axis=1, keepdims=True)
    slot_id = lax.broadcasted_iota(jnp.int32, (slots, 1), 0) + ctx * slots
    key_id = lax.broadcasted_iota(jnp.int32, (1, total), 1)
    head_of = lax.broadcasted_iota(jnp.int32, (slots, wide), 1) // HD
    spot = lax.broadcasted_iota(jnp.int32, (slots, total), 1) == slot_id

    def stack_heads(block):
        wider = block.astype(F32)
        return jnp.concatenate(
            [jnp.where(head_of == h, wider, 0.0).astype(BF16) for h in range(heads)], axis=0
        )

    def pick_heads(block):
        out = jnp.where(head_of == 0, block[0:slots], 0.0)
        for h in range(1, heads):
            out = jnp.where(head_of == h, block[h * slots : (h + 1) * slots], out)
        return out

    def put_rows(ref, image, column):
        for h in range(heads):
            part = jnp.where(spot, column[h * slots : (h + 1) * slots], 0.0)
            line = image * heads + h
            ref[ctx, line : line + 1, :] = jnp.sum(part, axis=0, keepdims=True)

    win_passed = gather_forward(kv_win_started, at_win_kv)
    win_own.wait()
    gather_finish(kv_win_started, win_passed)

    def project(j, bias):
        out = nn(h1[...], g_win[j].reshape(width, wide))
        if bias is not None:
            out = out + vx[bias : bias + 1, 0:wide]
        out = out.astype(BF16)
        for c in range(2):
            place_at = pl.ds(pl.multiple_of(ctx * slots + starts[c], ROWS), sizes_of[c])
            block = out[chunk(c)].reshape(images, sizes_of[c], wide)
            qkv[:, place_at, j * wide : (j + 1) * wide] = block

    def at_kv(images_of):
        def at(index):
            return qkv.at[images_of, slot_at(index), wide : 3 * wide]

        return at

    def at_q(index):
        return qkv.at[:, slot_at(index), 0:wide]

    project(1, None)
    project(2, 10)
    middle = images // 2
    image_parts = (slice(0, middle), slice(middle, images))
    kv_started = [ctx_start(at_kv(part)) for part in image_parts]
    wup_started = relay_start(wup, at_wup)
    wdt_started = relay_start(at_wdt(me, core), at_wdt)
    win_passed = gather_forward(q_win_started, at_win_q)
    gather_finish(q_win_started, win_passed)
    project(0, 9)
    q_started = ctx_start(at_q)
    wot_passed = []
    for k in planes:
        wot_started[0][k - 1].wait_recv()
        there = wot_piece(flip(me, k), z)
        wot_z.append([send(there, there, zpeer(j)) for j in zs])
        wot_passed.append(send(there, there, sib))

    def at_mixed(index, c):
        return mixed.at[chunk(c), lane_at(index, wide)]

    for image in range(images):
        for part in range(2):
            if image == image_parts[part].start:
                kv_at = at_kv(image_parts[part])
                kv_passed = ctx_forward(kv_started[part], kv_at)
                ctx_finish(kv_started[part], kv_passed)
        key_live = key_id < lengths[image : image + 1, :]
        stacked = stack_heads(qkv[image, own, 0:wide])
        scores = nt(stacked, qkv[image, :, wide : 2 * wide]) * scale
        scores = jnp.where(key_live, scores, neg_big)
        top = jnp.max(scores, axis=-1, keepdims=True)
        expo = jnp.exp(scores - top)
        whole = jnp.sum(expo, axis=-1, keepdims=True)
        probs = expo / whole
        wq[image] = probs
        put_rows(stat, image, top + jnp.log(whole))
        out = nn(probs.astype(BF16), qkv[image, :, 2 * wide : 3 * wide])
        split_rows(mixed, image, lane_at(z, wide), pick_heads(out).astype(BF16))
    mixed_sent = [
        [send(at_mixed(z, c), at_mixed(z, c), zpeer(k)) for k in reversed(zs)] for c in range(2)
    ]

    def at_stat(index):
        return stat.at[index]

    stat_started = ctx_start(at_stat)

    for copy in cot_load:
        copy.wait()
    row_live = []
    for image in range(images):
        row_live.append(slot_id < lengths[image : image + 1, :])
        for c in range(2):
            at = rows_at(c, image)
            live = row_live[image][slot_part(c)]
            gdown[at, :] = jnp.where(live, cot[at, :].astype(F32), 0.0).astype(BF16)

    wup_passed, wup_halves = relay_forward(wup_started, at_wup)
    gather_finish(wot_started, wot_passed)
    wot_more = []
    for order, block in enumerate(wot_z):
        for k in zs:
            block[k - 1].wait_recv()
            there = wot_piece(flip(me, order), flip(z, k))
            wot_more.append(send(there, there, sib))
    wup_own.wait()
    wdt_passed, wdt_halves = relay_forward(wdt_started, at_wdt)
    wup_passed += relay_last(wup_halves, at_wup)
    for copy in wot_more:
        copy.wait_recv()

    some = group // (width // TILE)

    def scatter(part, recv, relay, c):
        marks = [fresh() for _ in range(5)]

        def onward(j):
            return remote(
                part.at[rows_at(c, flip(z, 3 - j)), :],
                relay.at[j, slot_part(c), :],
                zpeer(1),
                marks[j],
                marks[j],
            )

        def passed(j):
            return remote(
                relay.at[j, slot_part(c), :],
                recv.at[1, slot_part(c), :],
                zpeer(2 + j),
                marks[2 + j],
                marks[2],
            )

        for j in range(2):
            send_if(at_end, functools.partial(onward, j))
        near = []

        def send_near():
            source = part.at[rows_at(c, flip(z, 1)), :]
            near.append(send(source, recv.at[0, slot_part(c), :], zpeer(1)))

        def pass_on():
            for j in range(2):

                @pl.when(inside)
                def _():
                    onward(j).wait_recv()
                    value = part[rows_at(c, flip(z, 2 + j)), :].astype(F32)
                    value = value + relay[j, slot_part(c), :].astype(F32)
                    relay[j, slot_part(c), :] = value.astype(BF16)

                send_if(inside, functools.partial(passed, j))

        def finish():
            near[0].wait_recv()
            passed(0).wait_recv()

        return pass_on, finish, send_near

    def spread(source, at):
        marks = [fresh() for _ in range(4)]
        near = send(source, at(z), zpeer(1))

        def far(k):
            return remote(source, at(z), zpeer(k), marks[k - 2], marks[k - 2])

        def passed(k):
            block = at(flip(z, k))
            return remote(block, block, zpeer(1), marks[k], marks[3 - k])

        send_if(at_end, functools.partial(far, 2))
        send_if(inside, functools.partial(far, 3))

        def pass_on():
            for k in (3, 2):

                @pl.when(inside)
                def _():
                    far(k).wait_recv()

                send_if(inside, functools.partial(passed, k))

        def finish():
            near.wait_recv()

            @pl.when(at_end)
            def _():
                far(2).wait_recv()
                far(3).wait_recv()

        return pass_on, finish

    def arrived(part, recv, c, at, size):
        here = pl.ds(pl.multiple_of(bases[c] + z * sizes_of[c] + at, ROWS), size)
        there = pl.ds(pl.multiple_of(starts[c] + at, ROWS), size)
        out = part[here, :].astype(F32)
        for j in range(2):
            out = out + recv[j, there, :].astype(F32)
        return out

    def attended(c):
        at_rows = chunk(c)
        for copy in mixed_sent[c]:
            copy.wait_recv()

        def project_out(step, carry):
            weight = g_wot[pl.ds(step * some, some)].reshape(TILE, n_t * wide)
            first[at_rows, lane_at(step, TILE)] = nt(mixed[at_rows, :], weight)
            return carry

        lax.fori_loop(0, width // TILE, project_out, 0)

        for row in range(bases[c], bases[c] + images * sizes_of[c], ROWS):
            at = slice(row, row + ROWS)
            value = tok[at, :].astype(F32) + first[at, :] + vx[2:3, :]
            first[at, :] = value
            normed, _ = norm_parts(value)
            h2[at, :] = (normed * vx[3:4, :] + vx[4:5, :]).astype(BF16)

    def feed_forward(c):
        at_rows = chunk(c)

        def expand(step, carry):
            at = lane_at(step, TILE)
            weight = g_wup[:, :, :, at].reshape(width, TILE)
            inner = nn(h2[at_rows, :], weight) + vx[8:9, at]
            share = 0.5 * (1.0 + lax.erf(inner * root_half))
            act[at_rows, at] = (inner * share).astype(BF16)
            slope = share + inner * jnp.exp(-0.5 * inner * inner) * inv_root_two_pi
            grad = (ga[at_rows, at] * slope).astype(BF16)
            gi[at_rows, at] = grad
            gv[8:9, at] += jnp.sum(grad.astype(F32), axis=0, keepdims=True)
            return carry

        lax.fori_loop(0, hidden // TILE, expand, 0)

        def up_back(step, carry):
            weight = g_wup[pl.ds(step * some, some)].reshape(TILE, hidden)
            part2[at_rows, lane_at(step, TILE)] = nt(gi[at_rows, :], weight).astype(BF16)
            return carry

        lax.fori_loop(0, width // TILE, up_back, 0)
        return scatter(part2, recv2, relay2, c)

    attended(0)
    wdt_passed += relay_last(wdt_halves, at_wdt)
    gather_finish(wup_started, wup_passed)
    gather_finish(wdt_started, wdt_passed)

    def down_back(c):
        at_rows = chunk(c)

        def one(step, carry):
            at = lane_at(step, TILE)
            weight = g_wdt[:, :, :, at].reshape(width, TILE)
            ga[at_rows, at] = nn(gdown[at_rows, :], weight)
            return carry

        lax.fori_loop(0, hidden // TILE, one, 0)

    down_back(0)
    sent2 = [feed_forward(0)]
    sent2[0][2]()
    down_back(1)
    attended(1)
    sent2.append(feed_forward(1))
    sent2[1][2]()

    def contract(step, carry):
        weight = g_wdt[pl.ds(step * some, some)].reshape(TILE, hidden)
        parts[:, lane_at(step, TILE)] = nt(act[...], weight).astype(BF16)
        return carry

    lax.fori_loop(0, width // TILE, contract, 0)
    sents = [scatter(parts, recvs, relays, 0)]
    sents[0][2]()

    def wide_grad(buf, left, right, lanes):
        def one(step, carry):
            at = lane_at(step, TILE)
            out = tn(left[...], right[:, at]).astype(BF16)
            buf[:, :, :, at] = out.reshape(group, 2, piece, TILE)
            return carry

        lax.fori_loop(0, lanes // TILE, one, 0)

    def grad_near(buf, near):
        return send(buf.at[:, 1 - core], near, sib)

    def grad_far(copy, buf, near, both, recv):
        copy.wait_recv()

        def one(m, carry):
            both[m] = (buf[m, core].astype(F32) + near[m].astype(F32)).astype(BF16)
            return carry

        lax.fori_loop(0, group, one, 0)
        return [send(both.at[flip(me, k)], recv.at[k - 1], plane(k)) for k in reversed(planes)]

    def grad_sum(copies, both, recv):
        for copy in copies:
            copy.wait_recv()
        value = both[me].astype(F32)
        for k in planes:
            value = value + recv[k - 1].astype(F32)
        return value

    wide_grad(b_wdt, gdown, act, hidden)
    wdt_near = grad_near(b_wdt, s_wdt)
    sent2[0][0]()
    wide_grad(b_wup, h2, gi, hidden)
    wup_near = grad_near(b_wup, s_wup)
    sent2[1][0]()
    wdt_far = grad_far(wdt_near, b_wdt, s_wdt, t_wdt, r_wdt)

    q_passed = ctx_forward(q_started, at_q)
    stat_passed = ctx_forward(stat_started, at_stat)
    ctx_finish(q_started, q_passed)
    ctx_finish(stat_started, stat_passed)
    for image in range(images):
        stacked = stack_heads(qkv[image, own, wide : 2 * wide])
        scores = nt(stacked, qkv[image, :, 0:wide]) * scale
        for h in range(heads):
            line = image * heads + h
            level = stat[0, line : line + 1, :]
            for other in range(1, n_ctx):
                level = level + stat[other, line : line + 1, :]
            block = scores[h * slots : (h + 1) * slots]
            block = jnp.where(row_live[image], block, neg_big)
            wk[image, h * slots : (h + 1) * slots, :] = jnp.exp(block - level)

    own_live = slot_id < jnp.sum(
        jnp.where(lax.broadcasted_iota(jnp.int32, (images, 1), 0) == z, lengths, 0),
        axis=0,
        keepdims=True,
    )

    def norm_back(grad, normed, inv, gain):
        scaled = grad * gain
        inner = (
            scaled
            - jnp.mean(scaled, axis=-1, keepdims=True)
            - normed * jnp.mean(scaled * normed, axis=-1, keepdims=True)
        )
        return inner * inv

    def second_back(c):
        sent2[c][1]()

        sums = [0.0, 0.0, 0.0, 0.0]
        for at in range(0, sizes_of[c], ROWS):
            here = pl.ds(pl.multiple_of(bases[c] + z * sizes_of[c] + at, ROWS), ROWS)
            grad = arrived(part2, recv2, c, at, ROWS)
            normed, inv = norm_parts(first[here, :])
            rows_grad = gdown[here, :].astype(F32)
            value = rows_grad + norm_back(grad, normed, inv, vx[3:4, :])
            there = slice(starts[c] + at, starts[c] + at + ROWS)
            gfirst[there, :] = value
            gown[there, :] = value.astype(BF16)
            terms = (value, grad * normed, grad, rows_grad)
            sums = [old + jnp.sum(term, axis=0, keepdims=True) for old, term in zip(sums, terms)]
        for line, value in enumerate(sums):
            gv[2 + line : 3 + line, :] += value

        def mixed_back(step, carry):
            at = lane_at(step, wide)
            weight = g_wot[:, :, :, at].reshape(width, wide)
            gm[slot_part(c), at] = nn(gown[slot_part(c), :], weight).astype(BF16)
            return carry

        lax.fori_loop(0, n_t, mixed_back, 0)
        place_at = pl.ds(pl.multiple_of(ctx * slots + starts[c], ROWS), sizes_of[c])
        sent = [
            send(
                gm.at[slot_part(c), lane_at(flip(z, k), wide)],
                do.at[z, place_at, :],
                zpeer(k),
            )
            for k in reversed(zs)
        ]
        do[z, place_at, :] = gm[slot_part(c), lane_at(z, wide)]
        return sent

    to_heads = [second_back(c) for c in range(2)]

    per = width // LANES

    def pack(ref, row, value):
        for i in range(value.shape[1] // LANES):
            ref[row + i : row + i + 1, :] = value[:, i * LANES : (i + 1) * LANES]

    def unpack(ref, row, size):
        return jnp.concatenate([ref[row + i : row + i + 1, :] for i in range(size // LANES)], axis=1)

    for line in range(4):
        pack(early, line * per, gv[2 + line : 3 + line, :])
    pack(early, 4 * per, gv[8:9, 0:hidden])

    def vector_z(ref, recv, size):
        return [send(ref.at[0:size], recv.at[k - 1], zpeer(k)) for k in reversed(zs)]

    def vector_near(copies, ref, recv, size, near):
        for copy in copies:
            complete(copy)
        value = ref[0:size]
        for k in zs:
            value = value + recv[k - 1]
        ref[0:size] = value
        return send(ref, near, sib)

    def vector_far(copy, ref, near, recv):
        complete(copy)
        ref[...] = ref[...] + near[...]
        return [send(ref, recv.at[k - 1], plane(k)) for k in planes]

    def vector_last(copies, ref, recv):
        for copy in copies:
            complete(copy)
        value = ref[...]
        for k in planes:
            value = value + recv[k - 1]
        ref[...] = value

    vector_copies = vector_z(early, early_z, 4 * per)
    sents.append(scatter(parts, recvs, relays, 1))
    sents[1][2]()
    sents[0][0]()

    def out_grad(step, carry):
        at = lane_at(step, TILE)
        part = jnp.concatenate([mixed[rows_at(c, z), at] for c in range(2)], axis=0)
        out = tn(gown[...], part).astype(BF16)
        b_wot[:, :, :, at] = out.reshape(group, 2, piece, TILE)
        return carry

    lax.fori_loop(0, n_t * wide // TILE, out_grad, 0)
    wot_near = grad_near(b_wot, s_wot)

    stays = []

    def block_rows(c):
        sents[c][1]()
        value = first[rows_at(c, z), :] + arrived(parts, recvs, c, 0, sizes_of[c]) + vx[5:6, :]
        value = jnp.where(own_live[slot_part(c)], value, 0.0)
        block_own[slot_part(c), :] = value.astype(BF16)
        return to_all(block_own, out_block, c)

    def to_all(source, target, c):
        def at(index):
            here = pl.ds(pl.multiple_of(index * slots + starts[c], ROWS), sizes_of[c])
            return target.at[here, :]

        part = source.at[slot_part(c), :]
        stays.append(local(part, at(z)))
        return spread(part, at)

    def at_do(c):
        def at(index):
            first_row = index * slots + starts[c]
            return do.at[:, pl.ds(pl.multiple_of(first_row, ROWS), sizes_of[c]), :]

        return at

    do_started = []
    for c in range(2):
        for copy in to_heads[c]:
            copy.wait_recv()
        do_started.append(ctx_start(at_do(c)))

    for image in range(images):
        stacked = stack_heads(do[image, own, :])
        grad_probs = nt(stacked, qkv[image, :, 2 * wide : 3 * wide])
        weights = wq[image]
        along = jnp.sum(grad_probs * weights, axis=-1, keepdims=True)
        put_rows(alng, image, along)
        grad_scores = (weights * (grad_probs - along)).astype(BF16)
        out = pick_heads(nn(grad_scores, qkv[image, :, wide : 2 * wide])) * scale
        split_rows(dqkv, image, slice(0, wide), out.astype(BF16))

    def at_along(index):
        return alng.at[index]

    along_started = ctx_start(at_along)
    vector_copy = vector_near(vector_copies, early, early_z, 4 * per, early_sib)
    wot_far = grad_far(wot_near, b_wot, s_wot, t_wot, r_wot)
    early_far = vector_far(vector_copy, early, early_sib, early_plane)
    wup_far = grad_far(wup_near, b_wup, s_wup, t_wup, r_wup)
    sents[1][0]()
    do_passed = [ctx_forward(do_started[c], at_do(c)) for c in range(2)]
    along_passed = ctx_forward(along_started, at_along)
    for c in range(2):
        ctx_finish(do_started[c], do_passed[c])
    ctx_finish(along_started, along_passed)

    for image in range(images):
        stacked = stack_heads(qkv[image, own, 2 * wide : 3 * wide])
        grad_probs = nt(stacked, do[image])
        weights = wk[image]
        lines = []
        for h in range(heads):
            line = image * heads + h
            level = alng[0, line : line + 1, :]
            for other in range(1, n_ctx):
                level = level + alng[other, line : line + 1, :]
            lines.append(grad_probs[h * slots : (h + 1) * slots] - level)
        grad_scores = (weights * jnp.concatenate(lines, axis=0)).astype(BF16)
        out = pick_heads(nn(grad_scores, qkv[image, :, 0:wide])) * scale
        split_rows(dqkv, image, slice(wide, 2 * wide), out.astype(BF16))
        out = pick_heads(nn(weights.astype(BF16), do[image]))
        split_rows(dqkv, image, slice(2 * wide, 3 * wide), out.astype(BF16))

    def in_back(c):
        at_rows = chunk(c)

        def one(step, carry):
            out = None
            for j in range(3):
                weight = g_win[j, pl.ds(step * some, some)].reshape(TILE, wide)
                term = nt(dqkv[at_rows, j * wide : (j + 1) * wide], weight)
                out = term if out is None else out + term
            part1[at_rows, lane_at(step, TILE)] = out.astype(BF16)
            return carry

        lax.fori_loop(0, width // TILE, one, 0)
        return scatter(part1, recv1, relay1, c)

    tail = [block_rows(0)]
    sent1 = [in_back(c) for c in range(2)]
    for c in range(2):
        sent1[c][2]()
    tail.append(block_rows(1))

    for j in range(3):
        out = tn(h1[...], dqkv[:, j * wide : (j + 1) * wide]).astype(BF16)
        b_win[j] = out.reshape(group, 2, piece, wide)
    win_near = send(b_win.at[:, :, 1 - core], s_win, sib)
    sent1[0][0]()
    late[2 * per :, :] = jnp.zeros((late.shape[0] - 2 * per, LANES), F32)
    for j, start in enumerate((0, 2 * wide)):
        value = jnp.sum(dqkv[:, start : start + wide].astype(F32), axis=0, keepdims=True)
        pack(late, 2 * per + j * (wide // LANES), value)
    f_wdt[...] = turned(grad_sum(wdt_far, t_wdt, r_wdt), f_wdt)
    stays.append(local(f_wdt, out_wdt))
    win_near.wait_recv()
    for j in range(3):
        both = b_win[j, :, pl.ds(core, 1)].reshape(group, piece, wide).astype(F32)
        t_win[:, j] = (both + s_win[j].astype(F32)).astype(BF16)
    win_far = [send(t_win.at[flip(me, k)], r_win.at[k - 1], plane(k)) for k in reversed(planes)]

    sent1[1][0]()
    whole_rows = grad_sum(wot_far, t_wot, r_wot)
    o_wot[...] = whole_rows.astype(BF16)
    to_owner = [
        send(o_wot.at[:, lane_at(flip(z, k), wide)], z_wot.at[k - 1], zpeer(k))
        for k in reversed(zs)
    ]

    def first_back(c):
        sent1[c][1]()

        sums = [0.0, 0.0]
        for at in range(0, sizes_of[c], ROWS):
            here = pl.ds(pl.multiple_of(bases[c] + z * sizes_of[c] + at, ROWS), ROWS)
            grad = arrived(part1, recv1, c, at, ROWS)
            normed, inv = norm_parts(tok[here, :].astype(F32))
            there = slice(starts[c] + at, starts[c] + at + ROWS)
            value = gfirst[there, :] + norm_back(grad, normed, inv, vx[0:1, :])
            tokens_own[there, :] = value.astype(BF16)
            terms = (grad * normed, grad)
            sums = [old + jnp.sum(term, axis=0, keepdims=True) for old, term in zip(sums, terms)]
        return sums

    for c in range(2):
        tail[c][0]()
    sums = first_back(0)
    tail.append(to_all(tokens_own, out_tokens, 0))
    for line, (one, two) in enumerate(zip(sums, first_back(1))):
        pack(late, line * per, one + two)
    vector_copies = vector_z(late, late_z, 2 * per)
    tail.append(to_all(tokens_own, out_tokens, 1))
    f_wup[...] = grad_sum(wup_far, t_wup, r_wup)
    stays.append(local(f_wup, out_wup))
    vector_last(early_far, early, early_plane)
    tail[2][0]()
    vector_copy = vector_near(vector_copies, late, late_z, 2 * per, late_sib)
    tail[3][0]()
    late_far = vector_far(vector_copy, late, late_sib, late_plane)
    f_win[...] = grad_sum(win_far, t_win, r_win)
    stays.append(local(f_win, out_win))
    for copy in to_owner:
        copy.wait_recv()
    value = o_wot[:, lane_at(z, wide)].astype(F32)
    for k in zs:
        value = value + z_wot[k - 1].astype(F32)
    f_wot[...] = turned(value, f_wot)
    stays.append(local(f_wot, out_wot))
    vector_last(late_far, late, late_plane)
    for line in range(2):
        gv[line : line + 1, :] = unpack(late, line * per, width)
        row = 2 * per + line * (wide // LANES)
        gv[9 + line : 10 + line, 0:wide] = unpack(late, row, wide)
    for line in range(4):
        gv[2 + line : 3 + line, :] = unpack(early, line * per, width)
    gv[8:9, 0:hidden] = unpack(early, 4 * per, hidden)
    stays.append(local(gv, out_vec))
    for passing in tail:
        passing[1]()
    for copy in pending:
        copy.wait_send()
    for flag, make in guarded:

        @pl.when(flag)
        def _():
            make().wait_send()

    for copy in stays:
        copy.wait()


def finish_call(sizes, *refs):
    finish_kernel(sizes, *refs[:13], refs[13:19], *refs[19:21], refs[21:27], refs[27])


def finish_kernel(
    sizes,
    in_block,
    in_tokens,
    in_win,
    in_wot,
    in_wup,
    in_wdt,
    in_vec,
    block,
    tokens,
    win,
    wot,
    wup,
    wdt,
    vectors,
    units,
    biases,
    held,
    sems,
):
    n_ctx, piece, cut, wide, hidden, width = sizes
    shard = lax.axis_index("dp") * n_ctx + lax.axis_index("ctx")
    pairs = [(in_block, block), (in_tokens, tokens), (in_win, win)]
    pairs += [(in_wot, wot), (in_wup, wup), (in_wdt, wdt)]
    ins = [pltpu.make_async_copy(a, h, sems.at[0, i]) for i, ((a, _), h) in enumerate(zip(pairs, held))]
    outs = [pltpu.make_async_copy(h, b, sems.at[1, i]) for i, ((_, b), h) in enumerate(zip(pairs, held))]
    for copy in ins:
        copy.start()
    for into, out_of in zip(ins, outs):
        into.wait()
        out_of.start()

    def exact(left, right):
        parts, rest = [], left
        for _ in range(3):
            parts.append(rest.astype(BF16).astype(F32))
            rest = rest - parts[-1]
        count = left.shape[0]
        product = nn(jnp.concatenate(parts, axis=0).astype(BF16), right.astype(BF16))
        return product[0:count] + product[count : 2 * count] + product[2 * count :]

    heads = wide // HD
    lane = lax.broadcasted_iota(jnp.int32, (width, piece), 0)
    slot = lax.broadcasted_iota(jnp.int32, (width, piece), 1)
    part = exact(in_vec[0:8, :], jnp.where(lane - slot == shard * piece, 1.0, 0.0))
    for line in range(6):
        vectors[line][...] = part[line : line + 1]
    channel = lax.broadcasted_iota(jnp.int32, (cut, hidden), 0)
    lane = lax.broadcasted_iota(jnp.int32, (cut, hidden), 1)
    chosen = jnp.where(lane % HD - channel == shard * cut, in_vec[8:9, 0:hidden], 0.0)
    lane = lax.broadcasted_iota(jnp.int32, (hidden, hidden // HD), 0)
    slot = lax.broadcasted_iota(jnp.int32, (hidden, hidden // HD), 1)
    units[...] = exact(chosen, jnp.where(lane // HD == slot, 1.0, 0.0))
    lane = lax.broadcasted_iota(jnp.int32, (wide, cut), 0)
    slot = lax.broadcasted_iota(jnp.int32, (wide, cut), 1)
    pick = jnp.where(lane % HD - slot == shard * cut, 1.0, 0.0)
    head = lax.broadcasted_iota(jnp.int32, (heads, wide), 0)
    lane = lax.broadcasted_iota(jnp.int32, (heads, wide), 1)
    for j in range(2):
        chosen = jnp.where(lane // HD == head, in_vec[9 + j : 10 + j, 0:wide], 0.0)
        biases[j] = exact(chosen, pick)
    for copy in outs:
        copy.wait()


def on_device(
    mesh_shape,
    tokens,
    keep_mask,
    cotangent,
    first_gain,
    first_shift,
    attend_in,
    attend_bias,
    attend_out,
    out_bias,
    second_gain,
    second_shift,
    expand_in,
    expand_bias,
    contract_out,
    contract_bias,
):
    n_dp, n_ctx, n_t = mesh_shape
    images, slots, width = tokens.shape
    piece, _, wide = attend_in.shape
    hidden = expand_in.shape[1]
    cut = expand_bias.shape[1]
    rows = images * slots
    group = n_dp * n_ctx // 2
    total = slots * n_ctx
    heads = wide // HD
    turn = piece % LANES == 0
    per = width // LANES
    early_rows = 4 * per + hidden // LANES
    late_rows = 2 * per + 8 * ((2 * wide // LANES + 7) // 8)
    sizes = (n_dp, n_ctx, n_t, images, slots, width, wide, hidden, piece, cut)
    vmem = pl.BlockSpec(memory_space=pltpu.VMEM)
    hbm = pl.BlockSpec(memory_space=pl.ANY)
    scratch = [
        pltpu.VMEM((rows, width), BF16),
        pltpu.VMEM((rows, width), BF16),
        pltpu.VMEM((wide, piece), BF16),
        pltpu.VMEM((hidden, piece), BF16),
        pltpu.VMEM((2 * ROWS, LANES), F32),
        pltpu.VMEM((3, group, 2, piece, wide), BF16),
        pltpu.VMEM((group, 2, piece, n_t * wide), BF16),
        pltpu.VMEM((group, 2, piece, hidden), BF16),
        pltpu.VMEM((group, 2, piece, hidden), BF16),
        pltpu.VMEM((group, 2, 2 * ROWS, LANES), F32),
        pltpu.VMEM((ROWS, width), F32),
        pltpu.VMEM((rows, width), F32),
        pltpu.VMEM((rows, width), BF16),
        pltpu.VMEM((images, total, 3 * wide), BF16),
        pltpu.VMEM((images, heads * slots, total), F32),
        pltpu.VMEM((images, heads * slots, total), F32),
        pltpu.VMEM((n_ctx, images * heads, total), F32),
        pltpu.VMEM((n_ctx, images * heads, total), F32),
        pltpu.VMEM((rows, n_t * wide), BF16),
        pltpu.VMEM((rows, width), F32),
        pltpu.VMEM((rows, width), BF16),
        pltpu.VMEM((rows, hidden), F32),
        pltpu.VMEM((rows, hidden), BF16),
        pltpu.VMEM((rows, hidden), BF16),
        pltpu.VMEM((rows, width), BF16),
        pltpu.VMEM((rows, width), BF16),
        pltpu.VMEM((rows, width), BF16),
        pltpu.VMEM((2, slots, width), BF16),
        pltpu.VMEM((2, slots, width), BF16),
        pltpu.VMEM((2, slots, width), BF16),
        pltpu.VMEM((2, slots, width), BF16),
        pltpu.VMEM((2, slots, width), BF16),
        pltpu.VMEM((2, slots, width), BF16),
        pltpu.VMEM((slots, width), F32),
        pltpu.VMEM((rows, width), BF16),
        pltpu.VMEM((slots, width), BF16),
        pltpu.VMEM((slots, n_t * wide), BF16),
        pltpu.VMEM((images, total, wide), BF16),
        pltpu.VMEM((rows, 3 * wide), BF16),
        pltpu.VMEM((slots, width), BF16),
        pltpu.VMEM((slots, width), BF16),
        pltpu.VMEM((ROWS, width), F32),
        pltpu.VMEM((early_rows, LANES), F32),
        pltpu.VMEM((early_rows, LANES), F32),
        pltpu.VMEM((group - 1, early_rows, LANES), F32),
        pltpu.VMEM((n_t - 1, 4 * per, LANES), F32),
        pltpu.VMEM((late_rows, LANES), F32),
        pltpu.VMEM((late_rows, LANES), F32),
        pltpu.VMEM((group - 1, late_rows, LANES), F32),
        pltpu.VMEM((n_t - 1, 2 * per, LANES), F32),
        pltpu.VMEM((3, group, 2, piece, wide), BF16),
        pltpu.VMEM((group, 2, piece, n_t * wide), BF16),
        pltpu.VMEM((group, 2, piece, hidden), BF16),
        pltpu.VMEM((group, 2, piece, hidden), BF16),
        pltpu.VMEM((3, group, piece, wide), BF16),
        pltpu.VMEM((group, piece, n_t * wide), BF16),
        pltpu.VMEM((group, piece, hidden), BF16),
        pltpu.VMEM((group, piece, hidden), BF16),
        pltpu.VMEM((group, 3, piece, wide), BF16),
        pltpu.VMEM((group, piece, n_t * wide), BF16),
        pltpu.VMEM((group, piece, hidden), BF16),
        pltpu.VMEM((group, piece, hidden), BF16),
        pltpu.VMEM((group - 1, 3, piece, wide), BF16),
        pltpu.VMEM((group - 1, piece, n_t * wide), BF16),
        pltpu.VMEM((group - 1, piece, hidden), BF16),
        pltpu.VMEM((group - 1, piece, hidden), BF16),
        pltpu.VMEM((piece, n_t * wide), BF16),
        pltpu.VMEM((n_t - 1, piece, wide), BF16),
    ]
    shapes = (
        (3, piece, wide),
        (wide, piece) if turn else (piece, wide),
        (piece, hidden),
        (hidden, piece) if turn else (piece, hidden),
    )
    scratch += [pltpu.VMEM(shape, F32) for shape in shapes]
    copies = 160 + 20 * group
    scratch += [
        pltpu.SemaphoreType.DMA((copies,)),
        pltpu.SemaphoreType.DMA((copies,)),
        pltpu.SemaphoreType.DMA((48,)),
    ]
    results = [jax.ShapeDtypeStruct((rows, width), BF16)] * 2
    results += [jax.ShapeDtypeStruct(shape, F32) for shape in shapes]
    outs = pl.pallas_call(
        functools.partial(block_kernel, sizes),
        out_shape=(*results, jax.ShapeDtypeStruct((ROWS, width), F32)),
        in_specs=[hbm, hbm, vmem, hbm, hbm, hbm, hbm] + [vmem] * 8,
        out_specs=(hbm,) * 7,
        scratch_shapes=scratch,
        compiler_params=pltpu.CompilerParams(
            collective_id=0, has_side_effects=True, vmem_limit_bytes=63 << 20
        ),
    )(
        tokens.reshape(rows, width),
        cotangent.reshape(rows, width),
        keep_mask,
        jnp.transpose(attend_in, (1, 0, 2)),
        attend_out,
        expand_in,
        contract_out,
        *[
            v.reshape(1, piece)
            for v in (first_gain, first_shift, out_bias, second_gain, second_shift, contract_bias)
        ],
        expand_bias.T,
        attend_bias,
    )
    vector = jax.ShapeDtypeStruct((1, piece), F32)
    placed = pl.pallas_call(
        functools.partial(finish_call, (n_ctx, piece, cut, wide, hidden, width)),
        out_shape=(
            *results,
            *[vector] * 6,
            jax.ShapeDtypeStruct((cut, hidden // HD), F32),
            jax.ShapeDtypeStruct((2, heads, cut), F32),
        ),
        in_specs=[hbm] * 6 + [vmem],
        out_specs=(hbm,) * 6 + (vmem,) * 8,
        scratch_shapes=[pltpu.VMEM(r.shape, r.dtype) for r in results]
        + [pltpu.SemaphoreType.DMA((2, 6))],
        compiler_params=pltpu.CompilerParams(vmem_limit_bytes=63 << 20),
    )(*outs)
    block_out, tokens_grad, d_win, d_wot, d_wup, d_wdt = placed[:6]
    vectors = [v.reshape(piece) for v in placed[6:12]]
    return (
        block_out.reshape(tokens.shape),
        tokens_grad.reshape(tokens.shape),
        vectors[0],
        vectors[1],
        jnp.transpose(d_win, (1, 0, 2)),
        placed[13],
        d_wot if turn else d_wot.T,
        vectors[2],
        vectors[3],
        vectors[4],
        d_wup,
        placed[12].T,
        d_wdt if turn else d_wdt.T,
        vectors[5],
    )


def solution(mesh):
    shape = (mesh.shape["dp"], mesh.shape["ctx"], mesh.shape["tensor"])
    vector = P(("dp", "ctx"))
    params = (
        vector,
        vector,
        P(("dp", "ctx"), None, "tensor"),
        P(None, "tensor", ("dp", "ctx")),
        P("tensor", ("dp", "ctx")),
        vector,
        vector,
        vector,
        P(("dp", "ctx"), "tensor"),
        P("tensor", ("dp", "ctx")),
        P("tensor", ("dp", "ctx")),
        vector,
    )
    rows = P("dp", "ctx", None)
    return jax.shard_map(
        functools.partial(on_device, shape),
        mesh=mesh,
        in_specs=(rows, P("dp", None), rows, *params),
        out_specs=(rows, rows, *params),
        check_vma=False,
    )
```

```python
import functools

import jax
import jax.numpy as jnp
from jax import lax
from jax.experimental import pallas as pl
from jax.experimental.pallas import tpu as pltpu
from jax.sharding import PartitionSpec as P

HD = 64
BUFFER = 64
LANES = 128
ROWS = 16
TILE = 256
BLOCK = 32
MESH = pl.DeviceIdType.MESH
F32 = jnp.float32
BF16 = jnp.bfloat16

eps = 1e-06
neg_big = -1e30
root_half = 0.7071067811865476
inv_root_two_pi = 0.3989422804014327


def flip(index, bits):
    out, bit = index, 1
    while bit <= bits:
        if bits & bit:
            out = out + bit - 2 * bit * lax.rem(lax.div(index, bit), 2)
        bit *= 2
    return out


def nn(left, right):
    return jnp.dot(left, right, preferred_element_type=F32)


def nt(left, right):
    return lax.dot_general(left, right, (((1,), (1,)), ((), ())), preferred_element_type=F32)


def tn(left, right):
    return lax.dot_general(left, right, (((0,), (0,)), ((), ())), preferred_element_type=F32)


def turned(value, ref):
    return value if value.shape == ref.shape else value.T


def norm_parts(values):
    mean = jnp.mean(values, axis=-1, keepdims=True)
    centered = values - mean
    spread = jnp.mean(centered * centered, axis=-1, keepdims=True)
    inv = lax.rsqrt(spread + eps)
    return centered * inv, inv


def block_kernel(
    sizes,
    tok_in,
    cot_in,
    keep,
    win,
    attend_out,
    wup,
    contract_out,
    first_gain,
    first_shift,
    out_bias,
    second_gain,
    second_shift,
    contract_bias,
    expand_bias,
    attend_bias,
    out_block,
    out_tokens,
    out_win,
    out_wot,
    out_wup,
    out_wdt,
    out_vec,
    tok,
    cot,
    a_out,
    c_out,
    vec,
    g_win,
    g_wot,
    g_wup,
    g_wdt,
    g_vec,
    vx,
    n1,
    h1,
    qkv,
    wq,
    wk,
    stat,
    alng,
    mixed,
    first,
    h2,
    ga,
    act,
    gi,
    part2,
    parts,
    part1,
    recv2,
    relay2,
    recvs,
    relays,
    recv1,
    relay1,
    gfirst,
    gdown,
    gown,
    gm,
    do,
    dqkv,
    block_own,
    tokens_own,
    gv,
    early,
    early_sib,
    early_plane,
    early_z,
    late,
    late_sib,
    late_plane,
    late_z,
    b_win,
    b_wot,
    b_wup,
    b_wdt,
    s_win,
    s_wot,
    s_wup,
    s_wdt,
    t_win,
    t_wot,
    t_wup,
    t_wdt,
    r_win,
    r_wot,
    r_wup,
    r_wdt,
    o_wot,
    z_wot,
    f_win,
    f_wot,
    f_wup,
    f_wdt,
    send_sem,
    recv_sem,
    local_sem,
):
    n_dp, n_ctx, n_t, images, slots, width, wide, hidden, piece, cut = sizes
    rows = images * slots
    total = slots * n_ctx
    heads = wide // HD
    half = n_ctx // 2
    group = n_dp * half
    scale = HD ** (-0.5)
    dp = lax.axis_index("dp")
    ctx = lax.axis_index("ctx")
    z = lax.axis_index("tensor")
    high, core = lax.div(ctx, 2), lax.rem(ctx, 2)
    me = dp * half + high
    shard = me * 2 + core
    sib = (dp, flip(ctx, 1), z)

    def plane(k):
        other = flip(me, k)
        return (lax.div(other, half), lax.rem(other, half) * 2 + core, z)

    def ctx_at(k):
        return flip(high, k) * 2 + core

    def zpeer(k):
        return (dp, ctx, flip(z, k))

    def slot_at(index):
        return pl.ds(pl.multiple_of(index * slots, ROWS), slots)

    def lane_at(index, size):
        return pl.ds(pl.multiple_of(index * size, size), size)

    own = slot_at(ctx)
    mine = slot_at(z)

    cut_at = ROWS * (slots // ROWS // 2)
    starts = (0, cut_at)
    sizes_of = (cut_at, slots - cut_at)
    bases = (0, images * cut_at)

    def chunk(c):
        return slice(bases[c], bases[c] + images * sizes_of[c])

    def rows_at(c, image):
        first_row = bases[c] + image * sizes_of[c]
        return pl.ds(pl.multiple_of(first_row, ROWS), sizes_of[c])

    def slot_part(c):
        return slice(starts[c], starts[c] + sizes_of[c])

    def split_rows(ref, image, lanes, value):
        for c in range(2):
            ref[rows_at(c, image), lanes] = value[slot_part(c)]

    count = [0, 0]
    stays = []
    pending = []

    def send(src, dst, device):
        index = count[0]
        count[0] += 1
        copy = pltpu.make_async_remote_copy(
            src_ref=src,
            dst_ref=dst,
            send_sem=send_sem.at[index],
            recv_sem=recv_sem.at[index],
            device_id=device,
            device_id_type=MESH,
        )
        copy.start()
        pending.append(copy)
        return copy

    inside = lax.rem(z - lax.div(z, 2), 2) == 1
    at_end = lax.rem(z - lax.div(z, 2), 2) == 0
    guarded = []

    def fresh():
        count[0] += 1
        return count[0] - 1

    def remote(src, dst, device, out_index, in_index):
        return pltpu.make_async_remote_copy(
            src_ref=src,
            dst_ref=dst,
            send_sem=send_sem.at[out_index],
            recv_sem=recv_sem.at[in_index],
            device_id=device,
            device_id_type=MESH,
        )

    def send_if(flag, makes):
        guarded.append((flag, makes))

        @pl.when(flag)
        def _():
            for make in makes:
                make().start()

    def complete(copy):
        pending[:] = [other for other in pending if other is not copy]
        copy.wait()

    def local(src, dst):
        index = count[1]
        count[1] += 1
        copy = pltpu.make_async_copy(src, dst, local_sem.at[index])
        copy.start()
        return copy

    planes = range(1, group)
    zs = range(1, n_t)

    def at_win_kv(m, c):
        return g_win.at[1:3, m, c]

    def at_win_q(m, c):
        return g_win.at[0:1, m, c]

    def at_wot(m, c):
        return g_wot.at[m, c, :, lane_at(z, wide)]

    def at_wup(m, c):
        return g_wup.at[m, c]

    def at_wdt(m, c):
        return g_wdt.at[m, c]

    def at_vec(m, c):
        return g_vec.at[m, c]

    barrier = pltpu.get_barrier_semaphore()
    for device in [plane(k) for k in planes] + [sib] + [zpeer(k) for k in zs]:
        pl.semaphore_signal(barrier, inc=1, device_id=device, device_id_type=MESH)
    a_out_load = local(attend_out, a_out)
    def load_rows(source, ref):
        return [
            local(
                source.at[image * slots + starts[c] : image * slots + starts[c] + sizes_of[c], :],
                ref.at[rows_at(c, image), :],
            )
            for c in range(2)
            for image in range(images)
        ]

    tok_load = load_rows(tok_in, tok)
    win_own = local(win, g_win.at[:, me, core])
    c_out_load = local(contract_out, c_out)
    cot_load = load_rows(cot_in, cot)
    wup_own = local(wup, at_wup(me, core))

    vec[...] = jnp.zeros_like(vec)
    for line, ref in enumerate(
        (first_gain, first_shift, out_bias, second_gain, second_shift, contract_bias)
    ):
        vec[line : line + 1, 0:piece] = ref[...].astype(F32)
    vec[8 : 8 + cut, 0 : hidden // HD] = expand_bias[...].astype(F32)
    for j in range(2):
        vec[16 + j * heads : 16 + (j + 1) * heads, 0:cut] = attend_bias[j].astype(F32)
    g_vec[me, core] = vec[...]
    gv[...] = jnp.zeros_like(gv)
    unit_one = (
        lax.broadcasted_iota(jnp.int32, (piece, piece), 0)
        == lax.broadcasted_iota(jnp.int32, (piece, piece), 1)
    ).astype(F32)
    unit_one = unit_one.astype(BF16)
    a_out_load.wait()
    g_wot[me, core, :, lane_at(z, wide)] = nt(unit_one, a_out[...]).astype(BF16)
    pl.semaphore_wait(barrier, group + n_t - 1)

    def gather_start(src, at):
        far = [send(src, at(me, core), plane(k)) for k in planes]
        return far, send(src, at(me, core), sib)

    def gather_forward(started, at):
        out = []
        for k in planes:
            started[0][k - 1].wait_recv()
            there = at(flip(me, k), core)
            out.append(send(there, there, sib))
        return out

    def gather_finish(started, passed):
        started[1].wait_recv()
        for copy in passed:
            copy.wait_recv()

    relayed = group == 4 and piece % (2 * ROWS) == 0

    def relay_start(src, at):
        if not relayed:
            return gather_start(src, at)
        far = [send(src, at(me, core), plane(k)) for k in (1, 2)]
        return far, send(src, at(me, core), sib)

    def relay_forward(started, at):
        if not relayed:
            return gather_forward(started, at), []
        out, halves = [], []
        for k in (1, 2):
            started[0][k - 1].wait_recv()
            there = at(flip(me, k), core)
            part = there.at[pl.ds((k - 1) * (piece // 2), piece // 2)]
            halves.append(send(part, part, plane(3 - k)))
            out.append(send(there, there, sib))
        return out, halves

    def relay_last(halves, at):
        if not halves:
            return []
        for copy in halves:
            copy.wait_recv()
        there = at(flip(me, 3), core)
        return [send(there, there, sib)]

    def ctx_start(at):
        far = [send(at(ctx), at(ctx), (dp, ctx_at(k), z)) for k in range(1, half)]
        return far, send(at(ctx), at(ctx), sib)

    def ctx_forward(started, at):
        out = []
        for k in range(1, half):
            started[0][k - 1].wait_recv()
            out.append(send(at(ctx_at(k)), at(ctx_at(k)), sib))
        return out

    def ctx_finish(started, passed):
        started[1].wait_recv()
        for copy in passed:
            copy.wait_recv()

    def wot_piece(m, index):
        return g_wot.at[m, core, :, lane_at(index, wide)]

    vec_started = gather_start(vec, at_vec)
    wot_own = at_wot(me, core)
    wot_far = [send(wot_own, wot_own, plane(k)) for k in planes if k < 3]
    kv_win_started = gather_start(win.at[1:3], at_win_kv)
    wot_far += [send(wot_own, wot_own, plane(k)) for k in planes if k >= 3]
    wot_started = (wot_far, send(wot_own, wot_own, sib))
    q_win_started = gather_start(win.at[0:1], at_win_q)
    wot_z = [[send(wot_piece(me, z), wot_piece(me, z), zpeer(k)) for k in zs]]

    for copy in tok_load:
        copy.wait()

    def first_norm(step, carry):
        at = pl.ds(pl.multiple_of(step * BLOCK, BLOCK), BLOCK)
        normed, _ = norm_parts(tok[at, :].astype(F32))
        n1[at, :] = normed
        return carry

    lax.fori_loop(0, rows // BLOCK, first_norm, 0)

    vec_passed = gather_forward(vec_started, at_vec)
    gather_finish(vec_started, vec_passed)
    shape = (2 * ROWS, width)
    line_id = lax.broadcasted_iota(jnp.int32, shape, 0)
    lane_id = lax.broadcasted_iota(jnp.int32, shape, 1)
    source = lax.broadcasted_iota(jnp.int32, (LANES, width), 0)
    target = lax.broadcasted_iota(jnp.int32, (LANES, width), 1)
    by_unit = jnp.where(target // HD == source, 1.0, 0.0).astype(BF16)
    for_unit = lane_id % HD - (line_id - 8)
    for_head = lane_id // HD == (line_id - 16) % heads

    def place(index, carry):
        one, two, three = carry
        shares = g_vec[lax.div(index, 2), lax.rem(index, 2)].astype(BF16)
        by_width = jnp.where(target - source == index * piece, 1.0, 0.0).astype(BF16)
        by_channel = jnp.where(target % HD - source == index * cut, 1.0, 0.0).astype(BF16)
        one = one + nn(shares, by_width)
        two = two + jnp.where(for_unit == index * cut, nn(shares, by_unit), 0.0)
        three = three + jnp.where(for_head, nn(shares, by_channel), 0.0)
        return one, two, three

    zero = jnp.zeros(shape, F32)
    one, two, three = lax.fori_loop(0, 2 * group, place, (zero, zero, zero))
    vx[0:8, :] = one[0:8]
    vx[8:9, :] = jnp.sum(two[8 : 8 + cut], axis=0, keepdims=True)
    vx[9:10, :] = jnp.sum(three[16 : 16 + heads], axis=0, keepdims=True)
    vx[10:11, :] = jnp.sum(three[16 + heads : 16 + 2 * heads], axis=0, keepdims=True)

    def first_hidden(step, carry):
        at = pl.ds(pl.multiple_of(step * BLOCK, BLOCK), BLOCK)
        h1[at, :] = (n1[at, :] * vx[0:1, :] + vx[1:2, :]).astype(BF16)
        return carry

    lax.fori_loop(0, rows // BLOCK, first_hidden, 0)

    wot_passed = []

    def wot_onward(k):
        wot_started[0][k - 1].wait_recv()
        there = wot_piece(flip(me, k), z)
        wot_z.append([send(there, there, zpeer(j)) for j in reversed(zs)][::-1])
        wot_passed.append(send(there, there, sib))

    for k in planes:
        if k < 3:
            wot_onward(k)

    c_out_load.wait()

    def turn(step, carry):
        at = lane_at(step, TILE)
        g_wdt[me, core, :, at] = nt(unit_one, c_out[at, :]).astype(BF16)
        return carry

    lax.fori_loop(0, hidden // TILE, turn, 0)

    lengths = BUFFER + jnp.sum(keep[...], axis=1, keepdims=True)
    slot_id = lax.broadcasted_iota(jnp.int32, (slots, 1), 0) + ctx * slots
    key_id = lax.broadcasted_iota(jnp.int32, (1, total), 1)
    head_of = lax.broadcasted_iota(jnp.int32, (slots, wide), 1) // HD
    spot = lax.broadcasted_iota(jnp.int32, (slots, total), 1) == slot_id

    def stack_heads(block):
        wider = block.astype(F32)
        return jnp.concatenate(
            [jnp.where(head_of == h, wider, 0.0).astype(BF16) for h in range(heads)], axis=0
        )

    def pick_heads(block):
        out = jnp.where(head_of == 0, block[0:slots], 0.0)
        for h in range(1, heads):
            out = jnp.where(head_of == h, block[h * slots : (h + 1) * slots], out)
        return out

    def put_rows(ref, image, column):
        for h in range(heads):
            part = jnp.where(spot, column[h * slots : (h + 1) * slots], 0.0)
            line = image * heads + h
            ref[ctx, line : line + 1, :] = jnp.sum(part, axis=0, keepdims=True)

    win_passed = gather_forward(kv_win_started, at_win_kv)
    win_own.wait()
    gather_finish(kv_win_started, win_passed)

    def project(j, bias):
        out = nn(h1[...], g_win[j].reshape(width, wide))
        if bias is not None:
            out = out + vx[bias : bias + 1, 0:wide]
        out = out.astype(BF16)
        for c in range(2):
            place_at = pl.ds(pl.multiple_of(ctx * slots + starts[c], ROWS), sizes_of[c])
            block = out[chunk(c)].reshape(images, sizes_of[c], wide)
            qkv[:, place_at, j * wide : (j + 1) * wide] = block

    def at_kv(images_of):
        def at(index):
            return qkv.at[images_of, slot_at(index), wide : 3 * wide]

        return at

    def at_q(index):
        return qkv.at[:, slot_at(index), 0:wide]

    project(1, None)
    project(2, 10)
    middle = images // 2
    image_parts = (slice(0, middle), slice(middle, images))
    kv_started = [ctx_start(at_kv(part)) for part in image_parts]
    wup_started = relay_start(wup, at_wup)
    wdt_started = relay_start(at_wdt(me, core), at_wdt)
    for k in planes:
        if k >= 3:
            wot_onward(k)
    win_passed = gather_forward(q_win_started, at_win_q)
    gather_finish(q_win_started, win_passed)
    project(0, 9)

    def at_mixed(index, c, part):
        first_row = bases[c] + part.start * sizes_of[c]
        last_row = bases[c] + part.stop * sizes_of[c]
        return mixed.at[first_row:last_row, lane_at(index, wide)]

    mixed_sent = [[], []]
    for image in range(images):
        for part in range(2):
            if image == image_parts[part].start:
                kv_at = at_kv(image_parts[part])
                kv_passed = ctx_forward(kv_started[part], kv_at)
                ctx_finish(kv_started[part], kv_passed)
        key_live = key_id < lengths[image : image + 1, :]
        stacked = stack_heads(qkv[image, own, 0:wide])
        scores = nt(stacked, qkv[image, :, wide : 2 * wide]) * scale
        scores = jnp.where(key_live, scores, neg_big)
        top = jnp.max(scores, axis=-1, keepdims=True)
        expo = jnp.exp(scores - top)
        whole = jnp.sum(expo, axis=-1, keepdims=True)
        probs = expo / whole
        wq[image] = probs
        put_rows(stat, image, top + jnp.log(whole))
        out = nn(probs.astype(BF16), qkv[image, :, 2 * wide : 3 * wide])
        split_rows(mixed, image, lane_at(z, wide), pick_heads(out).astype(BF16))
        for part in image_parts:
            if image == part.stop - 1:
                for c in range(2):
                    there = at_mixed(z, c, part)
                    mixed_sent[c] += [send(there, there, zpeer(k)) for k in reversed(zs)]

    def at_stat(index):
        return stat.at[index]

    for copy in cot_load:
        copy.wait()
    row_live = []
    for image in range(images):
        row_live.append(slot_id < lengths[image : image + 1, :])
        for c in range(2):
            at = rows_at(c, image)
            live = row_live[image][slot_part(c)]
            gdown[at, :] = jnp.where(live, cot[at, :].astype(F32), 0.0).astype(BF16)

    wup_passed, wup_halves = relay_forward(wup_started, at_wup)
    gather_finish(wot_started, wot_passed)
    wot_more = []
    for order, block in enumerate(wot_z):
        for k in zs:
            block[k - 1].wait_recv()
            there = wot_piece(flip(me, order), flip(z, k))
            wot_more.append(send(there, there, sib))
    wup_own.wait()
    wdt_passed, wdt_halves = relay_forward(wdt_started, at_wdt)
    q_started = ctx_start(at_q)
    stat_started = ctx_start(at_stat)
    wup_passed += relay_last(wup_halves, at_wup)
    for copy in wot_more:
        copy.wait_recv()

    some = group // (width // TILE)

    def pieces(c):
        return range(0, sizes_of[c], ROWS)

    def block_at(c, index, at):
        first_row = bases[c] + index * sizes_of[c] + at
        return pl.ds(pl.multiple_of(first_row, ROWS), ROWS)

    def slots_at(c, at):
        return slice(starts[c] + at, starts[c] + at + ROWS)

    def scatter(part, recv, relay, c):
        marks = {at: [fresh() for _ in range(4)] for at in pieces(c)}

        def onward(j, at):
            return remote(
                part.at[block_at(c, flip(z, 3 - j), at), :],
                relay.at[j, slots_at(c, at), :],
                zpeer(1),
                marks[at][j],
                marks[at][j],
            )

        def passed(j, at):
            return remote(
                relay.at[j, slots_at(c, at), :],
                recv.at[1, slots_at(c, at), :],
                zpeer(2 + j),
                marks[at][2 + j],
                marks[at][2],
            )

        both = [(at, j) for at in pieces(c) for j in range(2)]
        send_if(at_end, [functools.partial(onward, j, at) for at, j in both])
        near = []

        def send_near():
            source = part.at[rows_at(c, flip(z, 1)), :]
            near.append(send(source, recv.at[0, slot_part(c), :], zpeer(1)))

        def pass_on():
            guarded.append((inside, [functools.partial(passed, j, at) for at, j in both]))

            @pl.when(inside)
            def _():
                for at, j in both:
                    onward(j, at).wait_recv()
                    value = part[block_at(c, flip(z, 2 + j), at), :].astype(F32)
                    value = value + relay[j, slots_at(c, at), :].astype(F32)
                    relay[j, slots_at(c, at), :] = value.astype(BF16)
                    passed(j, at).start()

        def finish():
            near[0].wait_recv()
            for at in pieces(c):
                passed(0, at).wait_recv()

        return pass_on, finish, send_near

    def to_all(source, target, c):
        marks = {at: [fresh() for _ in range(4)] for at in pieces(c)}

        def block(index):
            first_row = index * slots + starts[c]
            return target.at[pl.ds(pl.multiple_of(first_row, ROWS), sizes_of[c]), :]

        def piece_of(index, at):
            first_row = index * slots + starts[c] + at
            return target.at[pl.ds(pl.multiple_of(first_row, ROWS), ROWS), :]

        def far(k, at):
            mark = marks[at][k - 2]
            return remote(source.at[slots_at(c, at), :], piece_of(z, at), zpeer(k), mark, mark)

        def passed(k, at):
            there = piece_of(flip(z, k), at)
            return remote(there, there, zpeer(1), marks[at][k], marks[at][3 - k])

        send_if(at_end, [functools.partial(far, 2, at) for at in pieces(c)])
        send_if(inside, [functools.partial(far, 3, at) for at in pieces(c)])
        own_part = source.at[slot_part(c), :]
        near = send(own_part, block(z), zpeer(1))
        stays.append(local(own_part, block(z)))
        both = [(k, at) for at in pieces(c) for k in (3, 2)]

        def pass_on():
            guarded.append((inside, [functools.partial(passed, k, at) for k, at in both]))

            @pl.when(inside)
            def _():
                for k, at in both:
                    far(k, at).wait_recv()
                    passed(k, at).start()

        def finish():
            near.wait_recv()

            @pl.when(at_end)
            def _():
                for k, at in both:
                    far(k, at).wait_recv()

        return pass_on, finish

    def arrived(part, recv, c, at, size):
        here = pl.ds(pl.multiple_of(bases[c] + z * sizes_of[c] + at, ROWS), size)
        there = pl.ds(pl.multiple_of(starts[c] + at, ROWS), size)
        out = part[here, :].astype(F32)
        for j in range(2):
            out = out + recv[j, there, :].astype(F32)
        return out

    def attended(c):
        at_rows = chunk(c)
        for copy in mixed_sent[c]:
            copy.wait_recv()

        def project_out(step, carry):
            weight = g_wot[pl.ds(step * some, some)].reshape(TILE, n_t * wide)
            first[at_rows, lane_at(step, TILE)] = nt(mixed[at_rows, :], weight)
            return carry

        lax.fori_loop(0, width // TILE, project_out, 0)

        for row in range(bases[c], bases[c] + images * sizes_of[c], ROWS):
            at = slice(row, row + ROWS)
            value = tok[at, :].astype(F32) + first[at, :] + vx[2:3, :]
            first[at, :] = value
            normed, _ = norm_parts(value)
            h2[at, :] = (normed * vx[3:4, :] + vx[4:5, :]).astype(BF16)

    def feed_forward(c):
        at_rows = chunk(c)

        def expand(step, carry):
            at = lane_at(step, TILE)
            weight = g_wup[:, :, :, at].reshape(width, TILE)
            inner = nn(h2[at_rows, :], weight) + vx[8:9, at]
            share = 0.5 * (1.0 + lax.erf(inner * root_half))
            act[at_rows, at] = (inner * share).astype(BF16)
            slope = share + inner * jnp.exp(-0.5 * inner * inner) * inv_root_two_pi
            grad = (ga[at_rows, at] * slope).astype(BF16)
            gi[at_rows, at] = grad
            gv[8:9, at] += jnp.sum(grad.astype(F32), axis=0, keepdims=True)
            return carry

        lax.fori_loop(0, hidden // TILE, expand, 0)

        def up_back(step, carry):
            weight = g_wup[pl.ds(step * some, some)].reshape(TILE, hidden)
            part2[at_rows, lane_at(step, TILE)] = nt(gi[at_rows, :], weight).astype(BF16)
            return carry

        lax.fori_loop(0, width // TILE, up_back, 0)
        return scatter(part2, recv2, relay2, c)

    attended(0)
    wdt_passed += relay_last(wdt_halves, at_wdt)
    gather_finish(wup_started, wup_passed)
    gather_finish(wdt_started, wdt_passed)

    def down_back(c):
        at_rows = chunk(c)

        def one(step, carry):
            at = lane_at(step, TILE)
            weight = g_wdt[:, :, :, at].reshape(width, TILE)
            ga[at_rows, at] = nn(gdown[at_rows, :], weight)
            return carry

        lax.fori_loop(0, hidden // TILE, one, 0)

    down_back(0)
    sent2 = [feed_forward(0)]
    sent2[0][2]()
    down_back(1)
    attended(1)
    sent2.append(feed_forward(1))
    sent2[1][2]()
    sent2[0][0]()

    def contract(step, carry):
        weight = g_wdt[pl.ds(step * some, some)].reshape(TILE, hidden)
        parts[:, lane_at(step, TILE)] = nt(act[...], weight).astype(BF16)
        return carry

    lax.fori_loop(0, width // TILE, contract, 0)
    sents = []
    for c in range(2):
        sents.append(scatter(parts, recvs, relays, c))
        sents[c][2]()

    def wide_grad(buf, left, right, lanes):
        def one(step, carry):
            at = lane_at(step, TILE)
            out = tn(left[...], right[:, at]).astype(BF16)
            buf[:, :, :, at] = out.reshape(group, 2, piece, TILE)
            return carry

        lax.fori_loop(0, lanes // TILE, one, 0)

    def grad_near(buf, near):
        return send(buf.at[:, 1 - core], near, sib)

    def grad_far(copy, buf, near, both, recv):
        copy.wait_recv()

        def one(m, carry):
            both[m] = (buf[m, core].astype(F32) + near[m].astype(F32)).astype(BF16)
            return carry

        lax.fori_loop(0, group, one, 0)
        return [send(both.at[flip(me, k)], recv.at[k - 1], plane(k)) for k in reversed(planes)]

    def grad_sum(copies, both, recv):
        for copy in copies:
            copy.wait_recv()
        value = both[me].astype(F32)
        for k in planes:
            value = value + recv[k - 1].astype(F32)
        return value

    wide_grad(b_wdt, gdown, act, hidden)
    wdt_near = grad_near(b_wdt, s_wdt)
    sent2[1][0]()
    wide_grad(b_wup, h2, gi, hidden)
    wup_near = grad_near(b_wup, s_wup)
    wdt_far = grad_far(wdt_near, b_wdt, s_wdt, t_wdt, r_wdt)

    q_passed = ctx_forward(q_started, at_q)
    stat_passed = ctx_forward(stat_started, at_stat)
    ctx_finish(q_started, q_passed)
    ctx_finish(stat_started, stat_passed)
    for image in range(images):
        stacked = stack_heads(qkv[image, own, wide : 2 * wide])
        scores = nt(stacked, qkv[image, :, 0:wide]) * scale
        for h in range(heads):
            line = image * heads + h
            level = stat[0, line : line + 1, :]
            for other in range(1, n_ctx):
                level = level + stat[other, line : line + 1, :]
            block = scores[h * slots : (h + 1) * slots]
            block = jnp.where(row_live[image], block, neg_big)
            wk[image, h * slots : (h + 1) * slots, :] = jnp.exp(block - level)

    own_live = slot_id < jnp.sum(
        jnp.where(lax.broadcasted_iota(jnp.int32, (images, 1), 0) == z, lengths, 0),
        axis=0,
        keepdims=True,
    )

    def norm_back(grad, normed, inv, gain):
        scaled = grad * gain
        inner = (
            scaled
            - jnp.mean(scaled, axis=-1, keepdims=True)
            - normed * jnp.mean(scaled * normed, axis=-1, keepdims=True)
        )
        return inner * inv

    def second_back(c):
        sent2[c][1]()

        sums = [0.0, 0.0, 0.0, 0.0]
        for at in range(0, sizes_of[c], ROWS):
            here = pl.ds(pl.multiple_of(bases[c] + z * sizes_of[c] + at, ROWS), ROWS)
            grad = arrived(part2, recv2, c, at, ROWS)
            normed, inv = norm_parts(first[here, :])
            rows_grad = gdown[here, :].astype(F32)
            value = rows_grad + norm_back(grad, normed, inv, vx[3:4, :])
            there = slice(starts[c] + at, starts[c] + at + ROWS)
            gfirst[there, :] = value
            gown[there, :] = value.astype(BF16)
            terms = (value, grad * normed, grad, rows_grad)
            sums = [old + jnp.sum(term, axis=0, keepdims=True) for old, term in zip(sums, terms)]
        for line, value in enumerate(sums):
            gv[2 + line : 3 + line, :] += value

        def mixed_back(step, carry):
            at = lane_at(step, wide)
            weight = g_wot[:, :, :, at].reshape(width, wide)
            gm[slot_part(c), at] = nn(gown[slot_part(c), :], weight).astype(BF16)
            return carry

        lax.fori_loop(0, n_t, mixed_back, 0)
        place_at = pl.ds(pl.multiple_of(ctx * slots + starts[c], ROWS), sizes_of[c])
        sent = [
            send(
                gm.at[slot_part(c), lane_at(flip(z, k), wide)],
                do.at[z, place_at, :],
                zpeer(k),
            )
            for k in reversed(zs)
        ]
        do[z, place_at, :] = gm[slot_part(c), lane_at(z, wide)]
        return sent

    to_heads = [second_back(0)]
    sents[0][0]()
    to_heads.append(second_back(1))
    sents[1][0]()

    per = width // LANES

    def pack(ref, row, value):
        for i in range(value.shape[1] // LANES):
            ref[row + i : row + i + 1, :] = value[:, i * LANES : (i + 1) * LANES]

    def unpack(ref, row, size):
        return jnp.concatenate([ref[row + i : row + i + 1, :] for i in range(size // LANES)], axis=1)

    for line in range(4):
        pack(early, line * per, gv[2 + line : 3 + line, :])
    pack(early, 4 * per, gv[8:9, 0:hidden])

    def vector_z(ref, recv, size):
        return [send(ref.at[0:size], recv.at[k - 1], zpeer(k)) for k in reversed(zs)]

    def vector_near(copies, ref, recv, size, near):
        for copy in copies:
            complete(copy)
        value = ref[0:size]
        for k in zs:
            value = value + recv[k - 1]
        ref[0:size] = value
        return send(ref, near, sib)

    def vector_far(copy, ref, near, recv):
        complete(copy)
        ref[...] = ref[...] + near[...]
        return [send(ref, recv.at[k - 1], plane(k)) for k in planes]

    def vector_last(copies, ref, recv):
        for copy in copies:
            complete(copy)
        value = ref[...]
        for k in planes:
            value = value + recv[k - 1]
        ref[...] = value

    vector_copies = vector_z(early, early_z, 4 * per)

    def out_grad(step, carry):
        at = lane_at(step, TILE)
        part = jnp.concatenate([mixed[rows_at(c, z), at] for c in range(2)], axis=0)
        out = tn(gown[...], part).astype(BF16)
        b_wot[:, :, :, at] = out.reshape(group, 2, piece, TILE)
        return carry

    lax.fori_loop(0, n_t * wide // TILE, out_grad, 0)
    wot_near = grad_near(b_wot, s_wot)


    def block_rows(c):
        sents[c][1]()
        value = first[rows_at(c, z), :] + arrived(parts, recvs, c, 0, sizes_of[c]) + vx[5:6, :]
        value = jnp.where(own_live[slot_part(c)], value, 0.0)
        block_own[slot_part(c), :] = value.astype(BF16)
        return to_all(block_own, out_block, c)

    def at_do(c):
        def at(index):
            first_row = index * slots + starts[c]
            return do.at[:, pl.ds(pl.multiple_of(first_row, ROWS), sizes_of[c]), :]

        return at

    tail = [block_rows(0)]
    do_started = []
    for c in range(2):
        for copy in to_heads[c]:
            copy.wait_recv()
        do_started.append(ctx_start(at_do(c)))

    for image in range(images):
        stacked = stack_heads(do[image, own, :])
        grad_probs = nt(stacked, qkv[image, :, 2 * wide : 3 * wide])
        weights = wq[image]
        along = jnp.sum(grad_probs * weights, axis=-1, keepdims=True)
        put_rows(alng, image, along)
        grad_scores = (weights * (grad_probs - along)).astype(BF16)
        out = pick_heads(nn(grad_scores, qkv[image, :, wide : 2 * wide])) * scale
        split_rows(dqkv, image, slice(0, wide), out.astype(BF16))

    def at_along(index):
        return alng.at[index]

    along_started = ctx_start(at_along)
    vector_copy = vector_near(vector_copies, early, early_z, 4 * per, early_sib)
    tail[0][0]()
    tail.append(block_rows(1))
    wot_grad_far = grad_far(wot_near, b_wot, s_wot, t_wot, r_wot)
    early_far = vector_far(vector_copy, early, early_sib, early_plane)
    do_passed = [ctx_forward(do_started[c], at_do(c)) for c in range(2)]
    along_passed = ctx_forward(along_started, at_along)
    for c in range(2):
        ctx_finish(do_started[c], do_passed[c])
    ctx_finish(along_started, along_passed)

    for image in range(images):
        stacked = stack_heads(qkv[image, own, 2 * wide : 3 * wide])
        grad_probs = nt(stacked, do[image])
        weights = wk[image]
        lines = []
        for h in range(heads):
            line = image * heads + h
            level = alng[0, line : line + 1, :]
            for other in range(1, n_ctx):
                level = level + alng[other, line : line + 1, :]
            lines.append(grad_probs[h * slots : (h + 1) * slots] - level)
        grad_scores = (weights * jnp.concatenate(lines, axis=0)).astype(BF16)
        out = pick_heads(nn(grad_scores, qkv[image, :, 0:wide])) * scale
        split_rows(dqkv, image, slice(wide, 2 * wide), out.astype(BF16))
        out = pick_heads(nn(weights.astype(BF16), do[image]))
        split_rows(dqkv, image, slice(2 * wide, 3 * wide), out.astype(BF16))

    def in_back(c):
        at_rows = chunk(c)

        def one(step, carry):
            out = None
            for j in range(3):
                weight = g_win[j, pl.ds(step * some, some)].reshape(TILE, wide)
                term = nt(dqkv[at_rows, j * wide : (j + 1) * wide], weight)
                out = term if out is None else out + term
            part1[at_rows, lane_at(step, TILE)] = out.astype(BF16)
            return carry

        lax.fori_loop(0, width // TILE, one, 0)
        return scatter(part1, recv1, relay1, c)

    sent1 = [in_back(c) for c in range(2)]
    for c in range(2):
        sent1[c][2]()
    tail[1][0]()
    wup_far = grad_far(wup_near, b_wup, s_wup, t_wup, r_wup)

    for j in range(3):
        out = tn(h1[...], dqkv[:, j * wide : (j + 1) * wide]).astype(BF16)
        b_win[j] = out.reshape(group, 2, piece, wide)
    win_near = send(b_win.at[:, :, 1 - core], s_win, sib)
    sent1[0][0]()
    late[2 * per :, :] = jnp.zeros((late.shape[0] - 2 * per, LANES), F32)
    for j, start in enumerate((0, 2 * wide)):
        value = jnp.sum(dqkv[:, start : start + wide].astype(F32), axis=0, keepdims=True)
        pack(late, 2 * per + j * (wide // LANES), value)
    f_wdt[...] = turned(grad_sum(wdt_far, t_wdt, r_wdt), f_wdt)
    stays.append(local(f_wdt, out_wdt))
    win_near.wait_recv()
    for j in range(3):
        both = b_win[j, :, pl.ds(core, 1)].reshape(group, piece, wide).astype(F32)
        t_win[:, j] = (both + s_win[j].astype(F32)).astype(BF16)
    win_far = [send(t_win.at[flip(me, k)], r_win.at[k - 1], plane(k)) for k in reversed(planes)]

    sent1[1][0]()
    whole_rows = grad_sum(wot_grad_far, t_wot, r_wot)
    o_wot[...] = whole_rows.astype(BF16)
    to_owner = [
        send(o_wot.at[:, lane_at(flip(z, k), wide)], z_wot.at[k - 1], zpeer(k))
        for k in reversed(zs)
    ]

    def first_back(c):
        sent1[c][1]()

        sums = [0.0, 0.0]
        for at in range(0, sizes_of[c], ROWS):
            here = pl.ds(pl.multiple_of(bases[c] + z * sizes_of[c] + at, ROWS), ROWS)
            grad = arrived(part1, recv1, c, at, ROWS)
            normed, inv = norm_parts(tok[here, :].astype(F32))
            there = slice(starts[c] + at, starts[c] + at + ROWS)
            value = gfirst[there, :] + norm_back(grad, normed, inv, vx[0:1, :])
            tokens_own[there, :] = value.astype(BF16)
            terms = (grad * normed, grad)
            sums = [old + jnp.sum(term, axis=0, keepdims=True) for old, term in zip(sums, terms)]
        return sums

    sums = first_back(0)
    tail.append(to_all(tokens_own, out_tokens, 0))
    for line, (one, two) in enumerate(zip(sums, first_back(1))):
        pack(late, line * per, one + two)
    vector_copies = vector_z(late, late_z, 2 * per)
    tail.append(to_all(tokens_own, out_tokens, 1))
    f_wup[...] = grad_sum(wup_far, t_wup, r_wup)
    stays.append(local(f_wup, out_wup))
    vector_last(early_far, early, early_plane)
    tail[2][0]()
    vector_copy = vector_near(vector_copies, late, late_z, 2 * per, late_sib)
    tail[3][0]()
    late_far = vector_far(vector_copy, late, late_sib, late_plane)
    f_win[...] = grad_sum(win_far, t_win, r_win)
    stays.append(local(f_win, out_win))
    for copy in to_owner:
        copy.wait_recv()
    value = o_wot[:, lane_at(z, wide)].astype(F32)
    for k in zs:
        value = value + z_wot[k - 1].astype(F32)
    f_wot[...] = turned(value, f_wot)
    stays.append(local(f_wot, out_wot))
    vector_last(late_far, late, late_plane)
    for line in range(2):
        gv[line : line + 1, :] = unpack(late, line * per, width)
        row = 2 * per + line * (wide // LANES)
        gv[9 + line : 10 + line, 0:wide] = unpack(late, row, wide)
    for line in range(4):
        gv[2 + line : 3 + line, :] = unpack(early, line * per, width)
    gv[8:9, 0:hidden] = unpack(early, 4 * per, hidden)
    stays.append(local(gv, out_vec))
    for passing in tail:
        passing[1]()
    for copy in pending:
        copy.wait_send()
    for flag, makes in guarded:

        @pl.when(flag)
        def _():
            for make in makes:
                make().wait_send()

    for copy in stays:
        copy.wait()


def finish_kernel(sizes, *refs):
    n_ctx, piece, cut, wide, hidden, width = sizes
    sources, results, held = refs[:6], refs[7:13], refs[21:27]
    smalls, own, vec, sems = refs[13:21], refs[27:35], refs[35], refs[36]
    shard = lax.axis_index("dp") * n_ctx + lax.axis_index("ctx")
    load = pltpu.make_async_copy(refs[6], vec, sems.at[2, 0])
    load.start()
    ins, outs = [], []
    for i in range(6):
        ins.append(pltpu.make_async_copy(sources[i], held[i], sems.at[0, i]))
        outs.append(pltpu.make_async_copy(held[i], results[i], sems.at[1, i]))
    for copy in ins:
        copy.start()

    def exact(left, right):
        parts, rest = [], left
        for _ in range(3):
            parts.append(rest.astype(BF16).astype(F32))
            rest = rest - parts[-1]
        count = left.shape[0]
        product = nn(jnp.concatenate(parts, axis=0).astype(BF16), right.astype(BF16))
        return product[0:count] + product[count : 2 * count] + product[2 * count :]

    heads = wide // HD
    lane = lax.broadcasted_iota(jnp.int32, (width, piece), 0)
    slot = lax.broadcasted_iota(jnp.int32, (width, piece), 1)
    one = jnp.where(lane - slot == shard * piece, 1.0, 0.0)
    lane = lax.broadcasted_iota(jnp.int32, (hidden, hidden // HD), 0)
    slot = lax.broadcasted_iota(jnp.int32, (hidden, hidden // HD), 1)
    by_unit = jnp.where(lane // HD == slot, 1.0, 0.0)
    load.wait()
    part = exact(vec[0:8, :], one)
    for line in range(6):
        own[line][...] = part[line : line + 1]
    channel = lax.broadcasted_iota(jnp.int32, (cut, hidden), 0)
    lane = lax.broadcasted_iota(jnp.int32, (cut, hidden), 1)
    chosen = jnp.where(lane % HD - channel == shard * cut, vec[8:9, 0:hidden], 0.0)
    own[6][...] = exact(chosen, by_unit)
    lane = lax.broadcasted_iota(jnp.int32, (wide, cut), 0)
    slot = lax.broadcasted_iota(jnp.int32, (wide, cut), 1)
    pick = jnp.where(lane % HD - slot == shard * cut, 1.0, 0.0)
    head = lax.broadcasted_iota(jnp.int32, (heads, wide), 0)
    lane = lax.broadcasted_iota(jnp.int32, (heads, wide), 1)
    for j in range(2):
        chosen = jnp.where(lane // HD == head, vec[9 + j : 10 + j, 0:wide], 0.0)
        own[7][j] = exact(chosen, pick)
    for i in range(8):
        outs.append(pltpu.make_async_copy(own[i], smalls[i], sems.at[2, 1 + i]))
        outs[-1].start()
    for i in range(6):
        ins[i].wait()
        outs[i].start()
    for copy in outs:
        copy.wait()


def on_device(
    mesh_shape,
    tokens,
    keep_mask,
    cotangent,
    first_gain,
    first_shift,
    attend_in,
    attend_bias,
    attend_out,
    out_bias,
    second_gain,
    second_shift,
    expand_in,
    expand_bias,
    contract_out,
    contract_bias,
):
    n_dp, n_ctx, n_t = mesh_shape
    images, slots, width = tokens.shape
    piece, _, wide = attend_in.shape
    hidden = expand_in.shape[1]
    cut = expand_bias.shape[1]
    rows = images * slots
    group = n_dp * n_ctx // 2
    total = slots * n_ctx
    heads = wide // HD
    turn = piece % LANES == 0
    per = width // LANES
    early_rows = 4 * per + hidden // LANES
    late_rows = 2 * per + 8 * ((2 * wide // LANES + 7) // 8)
    sizes = (n_dp, n_ctx, n_t, images, slots, width, wide, hidden, piece, cut)
    vmem = pl.BlockSpec(memory_space=pltpu.VMEM)
    hbm = pl.BlockSpec(memory_space=pl.ANY)
    scratch = [
        pltpu.VMEM((rows, width), BF16),
        pltpu.VMEM((rows, width), BF16),
        pltpu.VMEM((wide, piece), BF16),
        pltpu.VMEM((hidden, piece), BF16),
        pltpu.VMEM((2 * ROWS, LANES), F32),
        pltpu.VMEM((3, group, 2, piece, wide), BF16),
        pltpu.VMEM((group, 2, piece, n_t * wide), BF16),
        pltpu.VMEM((group, 2, piece, hidden), BF16),
        pltpu.VMEM((group, 2, piece, hidden), BF16),
        pltpu.VMEM((group, 2, 2 * ROWS, LANES), F32),
        pltpu.VMEM((ROWS, width), F32),
        pltpu.VMEM((rows, width), F32),
        pltpu.VMEM((rows, width), BF16),
        pltpu.VMEM((images, total, 3 * wide), BF16),
        pltpu.VMEM((images, heads * slots, total), F32),
        pltpu.VMEM((images, heads * slots, total), F32),
        pltpu.VMEM((n_ctx, images * heads, total), F32),
        pltpu.VMEM((n_ctx, images * heads, total), F32),
        pltpu.VMEM((rows, n_t * wide), BF16),
        pltpu.VMEM((rows, width), F32),
        pltpu.VMEM((rows, width), BF16),
        pltpu.VMEM((rows, hidden), F32),
        pltpu.VMEM((rows, hidden), BF16),
        pltpu.VMEM((rows, hidden), BF16),
        pltpu.VMEM((rows, width), BF16),
        pltpu.VMEM((rows, width), BF16),
        pltpu.VMEM((rows, width), BF16),
        pltpu.VMEM((2, slots, width), BF16),
        pltpu.VMEM((2, slots, width), BF16),
        pltpu.VMEM((2, slots, width), BF16),
        pltpu.VMEM((2, slots, width), BF16),
        pltpu.VMEM((2, slots, width), BF16),
        pltpu.VMEM((2, slots, width), BF16),
        pltpu.VMEM((slots, width), F32),
        pltpu.VMEM((rows, width), BF16),
        pltpu.VMEM((slots, width), BF16),
        pltpu.VMEM((slots, n_t * wide), BF16),
        pltpu.VMEM((images, total, wide), BF16),
        pltpu.VMEM((rows, 3 * wide), BF16),
        pltpu.VMEM((slots, width), BF16),
        pltpu.VMEM((slots, width), BF16),
        pltpu.VMEM((ROWS, width), F32),
        pltpu.VMEM((early_rows, LANES), F32),
        pltpu.VMEM((early_rows, LANES), F32),
        pltpu.VMEM((group - 1, early_rows, LANES), F32),
        pltpu.VMEM((n_t - 1, 4 * per, LANES), F32),
        pltpu.VMEM((late_rows, LANES), F32),
        pltpu.VMEM((late_rows, LANES), F32),
        pltpu.VMEM((group - 1, late_rows, LANES), F32),
        pltpu.VMEM((n_t - 1, 2 * per, LANES), F32),
        pltpu.VMEM((3, group, 2, piece, wide), BF16),
        pltpu.VMEM((group, 2, piece, n_t * wide), BF16),
        pltpu.VMEM((group, 2, piece, hidden), BF16),
        pltpu.VMEM((group, 2, piece, hidden), BF16),
        pltpu.VMEM((3, group, piece, wide), BF16),
        pltpu.VMEM((group, piece, n_t * wide), BF16),
        pltpu.VMEM((group, piece, hidden), BF16),
        pltpu.VMEM((group, piece, hidden), BF16),
        pltpu.VMEM((group, 3, piece, wide), BF16),
        pltpu.VMEM((group, piece, n_t * wide), BF16),
        pltpu.VMEM((group, piece, hidden), BF16),
        pltpu.VMEM((group, piece, hidden), BF16),
        pltpu.VMEM((group - 1, 3, piece, wide), BF16),
        pltpu.VMEM((group - 1, piece, n_t * wide), BF16),
        pltpu.VMEM((group - 1, piece, hidden), BF16),
        pltpu.VMEM((group - 1, piece, hidden), BF16),
        pltpu.VMEM((piece, n_t * wide), BF16),
        pltpu.VMEM((n_t - 1, piece, wide), BF16),
    ]
    shapes = (
        (3, piece, wide),
        (wide, piece) if turn else (piece, wide),
        (piece, hidden),
        (hidden, piece) if turn else (piece, hidden),
    )
    scratch += [pltpu.VMEM(shape, F32) for shape in shapes]
    copies = 260 + 20 * group
    scratch += [
        pltpu.SemaphoreType.DMA((copies,)),
        pltpu.SemaphoreType.DMA((copies,)),
        pltpu.SemaphoreType.DMA((48,)),
    ]
    results = [jax.ShapeDtypeStruct((rows, width), BF16)] * 2
    results += [jax.ShapeDtypeStruct(shape, F32) for shape in shapes]
    outs = pl.pallas_call(
        functools.partial(block_kernel, sizes),
        out_shape=(*results, jax.ShapeDtypeStruct((ROWS, width), F32)),
        in_specs=[hbm, hbm, vmem, hbm, hbm, hbm, hbm] + [vmem] * 8,
        out_specs=(hbm,) * 7,
        scratch_shapes=scratch,
        compiler_params=pltpu.CompilerParams(
            collective_id=0, has_side_effects=True, vmem_limit_bytes=63 << 20
        ),
    )(
        tokens.reshape(rows, width),
        cotangent.reshape(rows, width),
        keep_mask,
        jnp.transpose(attend_in, (1, 0, 2)),
        attend_out,
        expand_in,
        contract_out,
        *[
            v.reshape(1, piece)
            for v in (first_gain, first_shift, out_bias, second_gain, second_shift, contract_bias)
        ],
        expand_bias.T,
        attend_bias,
    )
    vector = jax.ShapeDtypeStruct((1, piece), F32)
    small = [vector] * 6 + [
        jax.ShapeDtypeStruct((cut, hidden // HD), F32),
        jax.ShapeDtypeStruct((2, heads, cut), F32),
    ]
    placed = pl.pallas_call(
        functools.partial(finish_kernel, (n_ctx, piece, cut, wide, hidden, width)),
        out_shape=(*results, *small),
        in_specs=[hbm] * 7,
        out_specs=(hbm,) * 14,
        scratch_shapes=[pltpu.VMEM(r.shape, r.dtype) for r in (*results, *small)]
        + [pltpu.VMEM((ROWS, width), F32), pltpu.SemaphoreType.DMA((3, 9))],
        compiler_params=pltpu.CompilerParams(vmem_limit_bytes=63 << 20),
    )(*outs)
    block_out, tokens_grad, d_win, d_wot, d_wup, d_wdt = placed[:6]
    vectors = [v.reshape(piece) for v in placed[6:12]]
    return (
        block_out.reshape(tokens.shape),
        tokens_grad.reshape(tokens.shape),
        vectors[0],
        vectors[1],
        jnp.transpose(d_win, (1, 0, 2)),
        placed[13],
        d_wot if turn else d_wot.T,
        vectors[2],
        vectors[3],
        vectors[4],
        d_wup,
        placed[12].T,
        d_wdt if turn else d_wdt.T,
        vectors[5],
    )


def solution(mesh):
    shape = (mesh.shape["dp"], mesh.shape["ctx"], mesh.shape["tensor"])
    vector = P(("dp", "ctx"))
    params = (
        vector,
        vector,
        P(("dp", "ctx"), None, "tensor"),
        P(None, "tensor", ("dp", "ctx")),
        P("tensor", ("dp", "ctx")),
        vector,
        vector,
        vector,
        P(("dp", "ctx"), "tensor"),
        P("tensor", ("dp", "ctx")),
        P("tensor", ("dp", "ctx")),
        vector,
    )
    rows = P("dp", "ctx", None)
    return jax.shard_map(
        functools.partial(on_device, shape),
        mesh=mesh,
        in_specs=(rows, P("dp", None), rows, *params),
        out_specs=(rows, rows, *params),
        check_vma=False,
    )
```

```python
import functools

import jax
import jax.numpy as jnp
from jax import lax
from jax.experimental import pallas as pl
from jax.experimental.pallas import tpu as pltpu
from jax.sharding import PartitionSpec as P

HD = 64
BUFFER = 64
LANES = 128
ROWS = 16
TILE = 256
BLOCK = 32
MESH = pl.DeviceIdType.MESH
F32 = jnp.float32
BF16 = jnp.bfloat16

eps = 1e-06
neg_big = -1e30
root_half = 0.7071067811865476
inv_root_two_pi = 0.3989422804014327


def flip(index, bits):
    out, bit = index, 1
    while bit <= bits:
        if bits & bit:
            out = out + bit - 2 * bit * lax.rem(lax.div(index, bit), 2)
        bit *= 2
    return out


def nn(left, right):
    return jnp.dot(left, right, preferred_element_type=F32)


def nt(left, right):
    return lax.dot_general(left, right, (((1,), (1,)), ((), ())), preferred_element_type=F32)


def tn(left, right):
    return lax.dot_general(left, right, (((0,), (0,)), ((), ())), preferred_element_type=F32)


def turned(value, ref):
    return value if value.shape == ref.shape else value.T


def norm_parts(values):
    mean = jnp.mean(values, axis=-1, keepdims=True)
    centered = values - mean
    spread = jnp.mean(centered * centered, axis=-1, keepdims=True)
    inv = lax.rsqrt(spread + eps)
    return centered * inv, inv


def block_kernel(
    sizes,
    tok_in,
    cot_in,
    keep,
    win,
    attend_out,
    wup,
    contract_out,
    first_gain,
    first_shift,
    out_bias,
    second_gain,
    second_shift,
    contract_bias,
    expand_bias,
    attend_bias,
    out_block,
    out_tokens,
    out_win,
    out_wot,
    out_wup,
    out_wdt,
    out_vec,
    tok,
    cot,
    a_out,
    c_out,
    vec,
    g_win,
    g_wot,
    g_wup,
    g_wdt,
    g_vec,
    vx,
    n1,
    h1,
    qkv,
    wq,
    wk,
    stat,
    alng,
    mixed,
    first,
    h2,
    ga,
    act,
    gi,
    part2,
    parts,
    part1,
    recv2,
    relay2,
    recvs,
    relays,
    recv1,
    relay1,
    gfirst,
    gdown,
    gown,
    gm,
    do,
    dqkv,
    block_own,
    tokens_own,
    gv,
    early,
    early_sib,
    early_plane,
    early_z,
    late,
    late_sib,
    late_plane,
    late_z,
    b_win,
    b_wot,
    b_wup,
    b_wdt,
    s_win,
    s_wot,
    s_wup,
    s_wdt,
    t_win,
    t_wot,
    t_wup,
    t_wdt,
    r_win,
    r_wot,
    r_wup,
    r_wdt,
    o_wot,
    z_wot,
    f_win,
    f_wot,
    f_wup,
    f_wdt,
    send_sem,
    recv_sem,
    local_sem,
):
    n_dp, n_ctx, n_t, images, slots, width, wide, hidden, piece, cut = sizes
    rows = images * slots
    total = slots * n_ctx
    heads = wide // HD
    half = n_ctx // 2
    group = n_dp * half
    scale = HD ** (-0.5)
    dp = lax.axis_index("dp")
    ctx = lax.axis_index("ctx")
    z = lax.axis_index("tensor")
    high, core = lax.div(ctx, 2), lax.rem(ctx, 2)
    me = dp * half + high
    shard = me * 2 + core
    sib = (dp, flip(ctx, 1), z)

    def plane(k):
        other = flip(me, k)
        return (lax.div(other, half), lax.rem(other, half) * 2 + core, z)

    def ctx_at(k):
        return flip(high, k) * 2 + core

    def zpeer(k):
        return (dp, ctx, flip(z, k))

    def slot_at(index):
        return pl.ds(pl.multiple_of(index * slots, ROWS), slots)

    def lane_at(index, size):
        return pl.ds(pl.multiple_of(index * size, size), size)

    own = slot_at(ctx)
    mine = slot_at(z)

    cut_at = ROWS * (slots // ROWS // 2)
    starts = (0, cut_at)
    sizes_of = (cut_at, slots - cut_at)
    bases = (0, images * cut_at)

    def chunk(c):
        return slice(bases[c], bases[c] + images * sizes_of[c])

    def rows_at(c, image):
        first_row = bases[c] + image * sizes_of[c]
        return pl.ds(pl.multiple_of(first_row, ROWS), sizes_of[c])

    def slot_part(c):
        return slice(starts[c], starts[c] + sizes_of[c])

    def split_rows(ref, image, lanes, value):
        for c in range(2):
            ref[rows_at(c, image), lanes] = value[slot_part(c)]

    count = [0, 0]
    stays = []
    pending = []

    def send(src, dst, device):
        index = count[0]
        count[0] += 1
        copy = pltpu.make_async_remote_copy(
            src_ref=src,
            dst_ref=dst,
            send_sem=send_sem.at[index],
            recv_sem=recv_sem.at[index],
            device_id=device,
            device_id_type=MESH,
        )
        copy.start()
        pending.append(copy)
        return copy

    inside = lax.rem(z - lax.div(z, 2), 2) == 1
    at_end = lax.rem(z - lax.div(z, 2), 2) == 0
    guarded = []

    def fresh():
        count[0] += 1
        return count[0] - 1

    def remote(src, dst, device, out_index, in_index):
        return pltpu.make_async_remote_copy(
            src_ref=src,
            dst_ref=dst,
            send_sem=send_sem.at[out_index],
            recv_sem=recv_sem.at[in_index],
            device_id=device,
            device_id_type=MESH,
        )

    def send_if(flag, makes):
        guarded.append((flag, makes))

        @pl.when(flag)
        def _():
            for make in makes:
                make().start()

    def complete(copy):
        pending[:] = [other for other in pending if other is not copy]
        copy.wait()

    def local(src, dst):
        index = count[1]
        count[1] += 1
        copy = pltpu.make_async_copy(src, dst, local_sem.at[index])
        copy.start()
        return copy

    planes = range(1, group)
    zs = range(1, n_t)

    def at_win_kv(m, c):
        return g_win.at[1:3, m, c]

    def at_win_q(m, c):
        return g_win.at[0:1, m, c]

    def at_wot(m, c):
        return g_wot.at[m, c, :, lane_at(z, wide)]

    def at_wup(m, c):
        return g_wup.at[m, c]

    def at_wdt(m, c):
        return g_wdt.at[m, c]

    def at_vec(m, c):
        return g_vec.at[m, c]

    barrier = pltpu.get_barrier_semaphore()
    for device in [plane(k) for k in planes] + [sib] + [zpeer(k) for k in zs]:
        pl.semaphore_signal(barrier, inc=1, device_id=device, device_id_type=MESH)
    a_out_load = local(attend_out, a_out)
    def load_rows(source, ref):
        return [
            local(
                source.at[image * slots + starts[c] : image * slots + starts[c] + sizes_of[c], :],
                ref.at[rows_at(c, image), :],
            )
            for c in range(2)
            for image in range(images)
        ]

    tok_load = load_rows(tok_in, tok)
    win_own = local(win, g_win.at[:, me, core])
    c_out_load = local(contract_out, c_out)
    cot_load = load_rows(cot_in, cot)
    wup_own = local(wup, at_wup(me, core))

    vec[...] = jnp.zeros_like(vec)
    for line, ref in enumerate(
        (first_gain, first_shift, out_bias, second_gain, second_shift, contract_bias)
    ):
        vec[line : line + 1, 0:piece] = ref[...].astype(F32)
    vec[8 : 8 + cut, 0 : hidden // HD] = expand_bias[...].astype(F32)
    for j in range(2):
        vec[16 + j * heads : 16 + (j + 1) * heads, 0:cut] = attend_bias[j].astype(F32)
    g_vec[me, core] = vec[...]
    gv[...] = jnp.zeros_like(gv)
    unit_one = (
        lax.broadcasted_iota(jnp.int32, (piece, piece), 0)
        == lax.broadcasted_iota(jnp.int32, (piece, piece), 1)
    ).astype(F32)
    unit_one = unit_one.astype(BF16)
    a_out_load.wait()
    g_wot[me, core, :, lane_at(z, wide)] = nt(unit_one, a_out[...]).astype(BF16)
    pl.semaphore_wait(barrier, group + n_t - 1)

    def gather_start(src, at):
        far = [send(src, at(me, core), plane(k)) for k in planes]
        return far, send(src, at(me, core), sib)

    def gather_forward(started, at):
        out = []
        for k in planes:
            started[0][k - 1].wait_recv()
            there = at(flip(me, k), core)
            out.append(send(there, there, sib))
        return out

    def gather_finish(started, passed):
        started[1].wait_recv()
        for copy in passed:
            copy.wait_recv()

    relayed = group == 4 and piece % (2 * ROWS) == 0

    def relay_start(src, at):
        if not relayed:
            return gather_start(src, at)
        far = [send(src, at(me, core), plane(k)) for k in (1, 2)]
        return far, send(src, at(me, core), sib)

    def relay_forward(started, at):
        if not relayed:
            return gather_forward(started, at), []
        out, halves = [], []
        for k in (1, 2):
            started[0][k - 1].wait_recv()
            there = at(flip(me, k), core)
            part = there.at[pl.ds((k - 1) * (piece // 2), piece // 2)]
            halves.append(send(part, part, plane(3 - k)))
            out.append(send(there, there, sib))
        return out, halves

    def relay_last(halves, at):
        if not halves:
            return []
        for copy in halves:
            copy.wait_recv()
        there = at(flip(me, 3), core)
        return [send(there, there, sib)]

    def ctx_start(at):
        far = [send(at(ctx), at(ctx), (dp, ctx_at(k), z)) for k in range(1, half)]
        return far, send(at(ctx), at(ctx), sib)

    def ctx_forward(started, at):
        out = []
        for k in range(1, half):
            started[0][k - 1].wait_recv()
            out.append(send(at(ctx_at(k)), at(ctx_at(k)), sib))
        return out

    def ctx_finish(started, passed):
        started[1].wait_recv()
        for copy in passed:
            copy.wait_recv()

    def wot_piece(m, index):
        return g_wot.at[m, core, :, lane_at(index, wide)]

    vec_started = gather_start(vec, at_vec)
    wot_own = at_wot(me, core)
    wot_far = [send(wot_own, wot_own, plane(k)) for k in planes if k < 3]
    kv_win_started = gather_start(win.at[1:3], at_win_kv)
    wot_far += [send(wot_own, wot_own, plane(k)) for k in planes if k >= 3]
    wot_started = (wot_far, send(wot_own, wot_own, sib))
    q_win_started = gather_start(win.at[0:1], at_win_q)
    wot_z = [[send(wot_piece(me, z), wot_piece(me, z), zpeer(k)) for k in zs]]

    for copy in tok_load:
        copy.wait()

    def first_norm(step, carry):
        at = pl.ds(pl.multiple_of(step * BLOCK, BLOCK), BLOCK)
        normed, _ = norm_parts(tok[at, :].astype(F32))
        n1[at, :] = normed
        return carry

    lax.fori_loop(0, rows // BLOCK, first_norm, 0)

    vec_passed = gather_forward(vec_started, at_vec)
    gather_finish(vec_started, vec_passed)
    shape = (2 * ROWS, width)
    line_id = lax.broadcasted_iota(jnp.int32, shape, 0)
    lane_id = lax.broadcasted_iota(jnp.int32, shape, 1)
    source = lax.broadcasted_iota(jnp.int32, (LANES, width), 0)
    target = lax.broadcasted_iota(jnp.int32, (LANES, width), 1)
    by_unit = jnp.where(target // HD == source, 1.0, 0.0).astype(BF16)
    for_unit = lane_id % HD - (line_id - 8)
    for_head = lane_id // HD == (line_id - 16) % heads

    def place(index, carry):
        one, two, three = carry
        shares = g_vec[lax.div(index, 2), lax.rem(index, 2)].astype(BF16)
        by_width = jnp.where(target - source == index * piece, 1.0, 0.0).astype(BF16)
        by_channel = jnp.where(target % HD - source == index * cut, 1.0, 0.0).astype(BF16)
        one = one + nn(shares, by_width)
        two = two + jnp.where(for_unit == index * cut, nn(shares, by_unit), 0.0)
        three = three + jnp.where(for_head, nn(shares, by_channel), 0.0)
        return one, two, three

    zero = jnp.zeros(shape, F32)
    one, two, three = lax.fori_loop(0, 2 * group, place, (zero, zero, zero))
    vx[0:8, :] = one[0:8]
    vx[8:9, :] = jnp.sum(two[8 : 8 + cut], axis=0, keepdims=True)
    vx[9:10, :] = jnp.sum(three[16 : 16 + heads], axis=0, keepdims=True)
    vx[10:11, :] = jnp.sum(three[16 + heads : 16 + 2 * heads], axis=0, keepdims=True)

    def first_hidden(step, carry):
        at = pl.ds(pl.multiple_of(step * BLOCK, BLOCK), BLOCK)
        h1[at, :] = (n1[at, :] * vx[0:1, :] + vx[1:2, :]).astype(BF16)
        return carry

    lax.fori_loop(0, rows // BLOCK, first_hidden, 0)

    wot_passed = []

    def wot_onward(k):
        wot_started[0][k - 1].wait_recv()
        there = wot_piece(flip(me, k), z)
        wot_z.append([send(there, there, zpeer(j)) for j in reversed(zs)][::-1])
        wot_passed.append(send(there, there, sib))

    for k in planes:
        if k < 3:
            wot_onward(k)

    c_out_load.wait()

    def turn(step, carry):
        at = lane_at(step, TILE)
        g_wdt[me, core, :, at] = nt(unit_one, c_out[at, :]).astype(BF16)
        return carry

    lax.fori_loop(0, hidden // TILE, turn, 0)

    lengths = BUFFER + jnp.sum(keep[...], axis=1, keepdims=True)
    slot_id = lax.broadcasted_iota(jnp.int32, (slots, 1), 0) + ctx * slots
    key_id = lax.broadcasted_iota(jnp.int32, (1, total), 1)
    head_of = lax.broadcasted_iota(jnp.int32, (slots, wide), 1) // HD
    spot = lax.broadcasted_iota(jnp.int32, (slots, total), 1) == slot_id

    def stack_heads(block):
        wider = block.astype(F32)
        return jnp.concatenate(
            [jnp.where(head_of == h, wider, 0.0).astype(BF16) for h in range(heads)], axis=0
        )

    def pick_heads(block):
        out = jnp.where(head_of == 0, block[0:slots], 0.0)
        for h in range(1, heads):
            out = jnp.where(head_of == h, block[h * slots : (h + 1) * slots], out)
        return out

    def put_rows(ref, image, column):
        for h in range(heads):
            part = jnp.where(spot, column[h * slots : (h + 1) * slots], 0.0)
            line = image * heads + h
            ref[ctx, line : line + 1, :] = jnp.sum(part, axis=0, keepdims=True)

    win_passed = gather_forward(kv_win_started, at_win_kv)
    win_own.wait()
    gather_finish(kv_win_started, win_passed)

    def project(j, bias):
        out = nn(h1[...], g_win[j].reshape(width, wide))
        if bias is not None:
            out = out + vx[bias : bias + 1, 0:wide]
        out = out.astype(BF16)
        for c in range(2):
            place_at = pl.ds(pl.multiple_of(ctx * slots + starts[c], ROWS), sizes_of[c])
            block = out[chunk(c)].reshape(images, sizes_of[c], wide)
            qkv[:, place_at, j * wide : (j + 1) * wide] = block

    def at_kv(images_of):
        def at(index):
            return qkv.at[images_of, slot_at(index), wide : 3 * wide]

        return at

    def at_q(index):
        return qkv.at[:, slot_at(index), 0:wide]

    project(1, None)
    project(2, 10)
    middle = images // 2
    image_parts = (slice(0, middle), slice(middle, images))
    kv_started = [ctx_start(at_kv(part)) for part in image_parts]
    wup_started = relay_start(wup, at_wup)
    wdt_started = relay_start(at_wdt(me, core), at_wdt)
    for k in planes:
        if k >= 3:
            wot_onward(k)
    win_passed = gather_forward(q_win_started, at_win_q)
    gather_finish(q_win_started, win_passed)
    project(0, 9)

    def at_mixed(index, c, part):
        first_row = bases[c] + part.start * sizes_of[c]
        last_row = bases[c] + part.stop * sizes_of[c]
        return mixed.at[first_row:last_row, lane_at(index, wide)]

    mixed_sent = [[], []]
    for image in range(images):
        for part in range(2):
            if image == image_parts[part].start:
                kv_at = at_kv(image_parts[part])
                kv_passed = ctx_forward(kv_started[part], kv_at)
                ctx_finish(kv_started[part], kv_passed)
        key_live = key_id < lengths[image : image + 1, :]
        stacked = stack_heads(qkv[image, own, 0:wide])
        scores = nt(stacked, qkv[image, :, wide : 2 * wide]) * scale
        scores = jnp.where(key_live, scores, neg_big)
        top = jnp.max(scores, axis=-1, keepdims=True)
        expo = jnp.exp(scores - top)
        whole = jnp.sum(expo, axis=-1, keepdims=True)
        probs = expo / whole
        wq[image] = probs
        put_rows(stat, image, top + jnp.log(whole))
        out = nn(probs.astype(BF16), qkv[image, :, 2 * wide : 3 * wide])
        split_rows(mixed, image, lane_at(z, wide), pick_heads(out).astype(BF16))
        for part in image_parts:
            if image == part.stop - 1:
                for c in range(2):
                    there = at_mixed(z, c, part)
                    mixed_sent[c] += [send(there, there, zpeer(k)) for k in reversed(zs)]

    def at_stat(index):
        return stat.at[index]

    for copy in cot_load:
        copy.wait()
    row_live = []
    for image in range(images):
        row_live.append(slot_id < lengths[image : image + 1, :])
        for c in range(2):
            at = rows_at(c, image)
            live = row_live[image][slot_part(c)]
            gdown[at, :] = jnp.where(live, cot[at, :].astype(F32), 0.0).astype(BF16)

    wup_passed, wup_halves = relay_forward(wup_started, at_wup)
    gather_finish(wot_started, wot_passed)
    wot_more = []
    for order, block in enumerate(wot_z):
        for k in zs:
            block[k - 1].wait_recv()
            there = wot_piece(flip(me, order), flip(z, k))
            wot_more.append(send(there, there, sib))
    wup_own.wait()
    wdt_passed, wdt_halves = relay_forward(wdt_started, at_wdt)
    q_started = ctx_start(at_q)
    stat_started = ctx_start(at_stat)
    wup_passed += relay_last(wup_halves, at_wup)
    for copy in wot_more:
        copy.wait_recv()

    some = group // (width // TILE)

    def pieces(c):
        return range(0, sizes_of[c], ROWS)

    def block_at(c, index, at):
        first_row = bases[c] + index * sizes_of[c] + at
        return pl.ds(pl.multiple_of(first_row, ROWS), ROWS)

    def slots_at(c, at):
        return slice(starts[c] + at, starts[c] + at + ROWS)

    def scatter(part, recv, relay, c):
        marks = {at: [fresh() for _ in range(4)] for at in pieces(c)}

        def onward(j, at):
            return remote(
                part.at[block_at(c, flip(z, 3 - j), at), :],
                relay.at[j, slots_at(c, at), :],
                zpeer(1),
                marks[at][j],
                marks[at][j],
            )

        def passed(j, at):
            return remote(
                relay.at[j, slots_at(c, at), :],
                recv.at[1, slots_at(c, at), :],
                zpeer(2 + j),
                marks[at][2 + j],
                marks[at][2],
            )

        both = [(at, j) for at in pieces(c) for j in range(2)]
        send_if(at_end, [functools.partial(onward, j, at) for at, j in both])
        near = []

        def send_near():
            source = part.at[rows_at(c, flip(z, 1)), :]
            near.append(send(source, recv.at[0, slot_part(c), :], zpeer(1)))

        def pass_on():
            guarded.append((inside, [functools.partial(passed, j, at) for at, j in both]))

            @pl.when(inside)
            def _():
                for at, j in both:
                    onward(j, at).wait_recv()
                    value = part[block_at(c, flip(z, 2 + j), at), :].astype(F32)
                    value = value + relay[j, slots_at(c, at), :].astype(F32)
                    relay[j, slots_at(c, at), :] = value.astype(BF16)
                    passed(j, at).start()

        def finish(some_pieces=None):
            if some_pieces is None or 0 in some_pieces:
                near[0].wait_recv()
            for at in some_pieces or pieces(c):
                passed(0, at).wait_recv()

        return pass_on, finish, send_near

    def to_all(source, target, c):
        marks = {at: [fresh() for _ in range(4)] for at in pieces(c)}

        def piece_of(index, at):
            first_row = index * slots + starts[c] + at
            return target.at[pl.ds(pl.multiple_of(first_row, ROWS), ROWS), :]

        def far(k, at):
            mark = marks[at][k - 2]
            return remote(source.at[slots_at(c, at), :], piece_of(z, at), zpeer(k), mark, mark)

        def passed(k, at):
            there = piece_of(flip(z, k), at)
            return remote(there, there, zpeer(1), marks[at][k], marks[at][3 - k])

        nears = []

        def start(at):
            own_part = source.at[slots_at(c, at), :]
            send_if(at_end, [functools.partial(far, 2, at)])
            send_if(inside, [functools.partial(far, 3, at)])
            nears.append(send(own_part, piece_of(z, at), zpeer(1)))
            stays.append(local(own_part, piece_of(z, at)))

        both = [(k, at) for at in pieces(c) for k in (3, 2)]

        def pass_on():
            guarded.append((inside, [functools.partial(passed, k, at) for k, at in both]))

            @pl.when(inside)
            def _():
                for k, at in both:
                    far(k, at).wait_recv()
                    passed(k, at).start()

        def finish():
            for copy in nears:
                copy.wait_recv()

            @pl.when(at_end)
            def _():
                for k, at in both:
                    far(k, at).wait_recv()

        return pass_on, finish, start

    def arrived(part, recv, c, at, size):
        here = pl.ds(pl.multiple_of(bases[c] + z * sizes_of[c] + at, ROWS), size)
        there = pl.ds(pl.multiple_of(starts[c] + at, ROWS), size)
        out = part[here, :].astype(F32)
        for j in range(2):
            out = out + recv[j, there, :].astype(F32)
        return out

    def attended(c):
        at_rows = chunk(c)
        for copy in mixed_sent[c]:
            copy.wait_recv()

        def project_out(step, carry):
            weight = g_wot[pl.ds(step * some, some)].reshape(TILE, n_t * wide)
            first[at_rows, lane_at(step, TILE)] = nt(mixed[at_rows, :], weight)
            return carry

        lax.fori_loop(0, width // TILE, project_out, 0)

        for row in range(bases[c], bases[c] + images * sizes_of[c], ROWS):
            at = slice(row, row + ROWS)
            value = tok[at, :].astype(F32) + first[at, :] + vx[2:3, :]
            first[at, :] = value
            normed, _ = norm_parts(value)
            h2[at, :] = (normed * vx[3:4, :] + vx[4:5, :]).astype(BF16)

    def feed_forward(c):
        at_rows = chunk(c)

        def expand(step, carry):
            at = lane_at(step, TILE)
            weight = g_wup[:, :, :, at].reshape(width, TILE)
            inner = nn(h2[at_rows, :], weight) + vx[8:9, at]
            share = 0.5 * (1.0 + lax.erf(inner * root_half))
            act[at_rows, at] = (inner * share).astype(BF16)
            slope = share + inner * jnp.exp(-0.5 * inner * inner) * inv_root_two_pi
            grad = (ga[at_rows, at] * slope).astype(BF16)
            gi[at_rows, at] = grad
            gv[8:9, at] += jnp.sum(grad.astype(F32), axis=0, keepdims=True)
            return carry

        lax.fori_loop(0, hidden // TILE, expand, 0)

        def up_back(step, carry):
            weight = g_wup[pl.ds(step * some, some)].reshape(TILE, hidden)
            part2[at_rows, lane_at(step, TILE)] = nt(gi[at_rows, :], weight).astype(BF16)
            return carry

        lax.fori_loop(0, width // TILE, up_back, 0)
        return scatter(part2, recv2, relay2, c)

    attended(0)
    wdt_passed += relay_last(wdt_halves, at_wdt)
    gather_finish(wup_started, wup_passed)
    gather_finish(wdt_started, wdt_passed)

    def down_back(c):
        at_rows = chunk(c)

        def one(step, carry):
            at = lane_at(step, TILE)
            weight = g_wdt[:, :, :, at].reshape(width, TILE)
            ga[at_rows, at] = nn(gdown[at_rows, :], weight)
            return carry

        lax.fori_loop(0, hidden // TILE, one, 0)

    down_back(0)
    sent2 = [feed_forward(0)]
    sent2[0][2]()
    down_back(1)
    attended(1)
    sent2.append(feed_forward(1))
    sent2[1][2]()
    sent2[0][0]()

    def contract(step, carry):
        weight = g_wdt[pl.ds(step * some, some)].reshape(TILE, hidden)
        parts[:, lane_at(step, TILE)] = nt(act[...], weight).astype(BF16)
        return carry

    lax.fori_loop(0, width // TILE, contract, 0)
    sents = []
    for c in range(2):
        sents.append(scatter(parts, recvs, relays, c))
        sents[c][2]()

    def wide_grad(buf, left, right, lanes):
        def one(step, carry):
            at = lane_at(step, TILE)
            out = tn(left[...], right[:, at]).astype(BF16)
            buf[:, :, :, at] = out.reshape(group, 2, piece, TILE)
            return carry

        lax.fori_loop(0, lanes // TILE, one, 0)

    def grad_near(buf, near):
        return send(buf.at[:, 1 - core], near, sib)

    def grad_far(copy, buf, near, both, recv):
        copy.wait_recv()

        def one(m, carry):
            both[m] = (buf[m, core].astype(F32) + near[m].astype(F32)).astype(BF16)
            return carry

        lax.fori_loop(0, group, one, 0)
        return [send(both.at[flip(me, k)], recv.at[k - 1], plane(k)) for k in reversed(planes)]

    def grad_halves(copy, buf, near, both, recv):
        if not relayed:
            return grad_far(copy, buf, near, both, recv)
        copy.wait_recv()

        def one(m, carry):
            both[m] = (buf[m, core].astype(F32) + near[m].astype(F32)).astype(BF16)
            return carry

        lax.fori_loop(0, group, one, 0)
        part = piece // 2
        corner = flip(me, 3)
        return [
            send(both.at[corner, 0:part], recv.at[2, 0:part], plane(1)),
            send(both.at[corner, part:piece], recv.at[2, part:piece], plane(2)),
        ]

    def grad_onward(copies, both, recv):
        if not relayed:
            return copies
        part = piece // 2
        for k, at in ((2, slice(0, part)), (1, slice(part, piece))):
            copies[2 - k].wait_recv()
            other = flip(me, k)
            value = both[other, at].astype(F32) + recv[2, at].astype(F32)
            both[other, at] = value.astype(BF16)
        return [send(both.at[flip(me, k)], recv.at[k - 1], plane(k)) for k in (1, 2)]

    def grad_sum(copies, both, recv):
        for copy in copies:
            copy.wait_recv()
        value = both[me].astype(F32)
        for k in range(len(copies)):
            value = value + recv[k].astype(F32)
        return value

    wide_grad(b_wdt, gdown, act, hidden)
    wdt_near = grad_near(b_wdt, s_wdt)
    sent2[1][0]()
    wide_grad(b_wup, h2, gi, hidden)
    wup_near = grad_near(b_wup, s_wup)
    wdt_far = grad_far(wdt_near, b_wdt, s_wdt, t_wdt, r_wdt)

    q_passed = ctx_forward(q_started, at_q)
    stat_passed = ctx_forward(stat_started, at_stat)
    ctx_finish(q_started, q_passed)
    ctx_finish(stat_started, stat_passed)
    for image in range(images):
        stacked = stack_heads(qkv[image, own, wide : 2 * wide])
        scores = nt(stacked, qkv[image, :, 0:wide]) * scale
        for h in range(heads):
            line = image * heads + h
            level = stat[0, line : line + 1, :]
            for other in range(1, n_ctx):
                level = level + stat[other, line : line + 1, :]
            block = scores[h * slots : (h + 1) * slots]
            block = jnp.where(row_live[image], block, neg_big)
            wk[image, h * slots : (h + 1) * slots, :] = jnp.exp(block - level)

    own_live = slot_id < jnp.sum(
        jnp.where(lax.broadcasted_iota(jnp.int32, (images, 1), 0) == z, lengths, 0),
        axis=0,
        keepdims=True,
    )

    def norm_back(grad, normed, inv, gain):
        scaled = grad * gain
        inner = (
            scaled
            - jnp.mean(scaled, axis=-1, keepdims=True)
            - normed * jnp.mean(scaled * normed, axis=-1, keepdims=True)
        )
        return inner * inv

    def second_back(c):
        sent2[c][1]()

        sums = [0.0, 0.0, 0.0, 0.0]
        for at in range(0, sizes_of[c], ROWS):
            here = pl.ds(pl.multiple_of(bases[c] + z * sizes_of[c] + at, ROWS), ROWS)
            grad = arrived(part2, recv2, c, at, ROWS)
            normed, inv = norm_parts(first[here, :])
            rows_grad = gdown[here, :].astype(F32)
            value = rows_grad + norm_back(grad, normed, inv, vx[3:4, :])
            there = slice(starts[c] + at, starts[c] + at + ROWS)
            gfirst[there, :] = value
            gown[there, :] = value.astype(BF16)
            terms = (value, grad * normed, grad, rows_grad)
            sums = [old + jnp.sum(term, axis=0, keepdims=True) for old, term in zip(sums, terms)]
        for line, value in enumerate(sums):
            gv[2 + line : 3 + line, :] += value

        def mixed_back(step, carry):
            at = lane_at(step, wide)
            weight = g_wot[:, :, :, at].reshape(width, wide)
            gm[slot_part(c), at] = nn(gown[slot_part(c), :], weight).astype(BF16)
            return carry

        lax.fori_loop(0, n_t, mixed_back, 0)
        place_at = pl.ds(pl.multiple_of(ctx * slots + starts[c], ROWS), sizes_of[c])
        sent = [
            send(
                gm.at[slot_part(c), lane_at(flip(z, k), wide)],
                do.at[z, place_at, :],
                zpeer(k),
            )
            for k in reversed(zs)
        ]
        do[z, place_at, :] = gm[slot_part(c), lane_at(z, wide)]
        return sent

    to_heads = [second_back(0)]
    sents[0][0]()
    to_heads.append(second_back(1))
    sents[1][0]()

    per = width // LANES

    def pack(ref, row, value):
        for i in range(value.shape[1] // LANES):
            ref[row + i : row + i + 1, :] = value[:, i * LANES : (i + 1) * LANES]

    def unpack(ref, row, size):
        return jnp.concatenate([ref[row + i : row + i + 1, :] for i in range(size // LANES)], axis=1)

    for line in range(4):
        pack(early, line * per, gv[2 + line : 3 + line, :])
    pack(early, 4 * per, gv[8:9, 0:hidden])

    def vector_z(ref, recv, size):
        return [send(ref.at[0:size], recv.at[k - 1], zpeer(k)) for k in reversed(zs)]

    def vector_near(copies, ref, recv, size, near):
        for copy in copies:
            complete(copy)
        value = ref[0:size]
        for k in zs:
            value = value + recv[k - 1]
        ref[0:size] = value
        return send(ref, near, sib)

    def vector_far(copy, ref, near, recv):
        complete(copy)
        ref[...] = ref[...] + near[...]
        return [send(ref, recv.at[k - 1], plane(k)) for k in planes]

    def vector_last(copies, ref, recv):
        for copy in copies:
            complete(copy)
        value = ref[...]
        for k in planes:
            value = value + recv[k - 1]
        ref[...] = value

    vector_copies = vector_z(early, early_z, 4 * per)

    def out_grad(step, carry):
        at = lane_at(step, TILE)
        part = jnp.concatenate([mixed[rows_at(c, z), at] for c in range(2)], axis=0)
        out = tn(gown[...], part).astype(BF16)
        b_wot[:, :, :, at] = out.reshape(group, 2, piece, TILE)
        return carry

    lax.fori_loop(0, n_t * wide // TILE, out_grad, 0)
    wot_near = grad_near(b_wot, s_wot)


    def block_rows(c):
        sents[c][1]()
        value = first[rows_at(c, z), :] + arrived(parts, recvs, c, 0, sizes_of[c]) + vx[5:6, :]
        value = jnp.where(own_live[slot_part(c)], value, 0.0)
        block_own[slot_part(c), :] = value.astype(BF16)
        passing = to_all(block_own, out_block, c)
        for at in pieces(c):
            passing[2](at)
        return passing

    def at_do(c):
        def at(index):
            first_row = index * slots + starts[c]
            return do.at[:, pl.ds(pl.multiple_of(first_row, ROWS), sizes_of[c]), :]

        return at

    tail = [block_rows(0)]
    do_started = []
    for c in range(2):
        for copy in to_heads[c]:
            copy.wait_recv()
        do_started.append(ctx_start(at_do(c)))

    for image in range(images):
        stacked = stack_heads(do[image, own, :])
        grad_probs = nt(stacked, qkv[image, :, 2 * wide : 3 * wide])
        weights = wq[image]
        along = jnp.sum(grad_probs * weights, axis=-1, keepdims=True)
        put_rows(alng, image, along)
        grad_scores = (weights * (grad_probs - along)).astype(BF16)
        out = pick_heads(nn(grad_scores, qkv[image, :, wide : 2 * wide])) * scale
        split_rows(dqkv, image, slice(0, wide), out.astype(BF16))

    def at_along(index):
        return alng.at[index]

    along_started = ctx_start(at_along)
    vector_copy = vector_near(vector_copies, early, early_z, 4 * per, early_sib)
    tail[0][0]()
    tail.append(block_rows(1))
    wot_grad_far = grad_halves(wot_near, b_wot, s_wot, t_wot, r_wot)
    early_far = vector_far(vector_copy, early, early_sib, early_plane)
    do_passed = [ctx_forward(do_started[c], at_do(c)) for c in range(2)]
    along_passed = ctx_forward(along_started, at_along)
    for c in range(2):
        ctx_finish(do_started[c], do_passed[c])
    ctx_finish(along_started, along_passed)

    for image in range(images):
        stacked = stack_heads(qkv[image, own, 2 * wide : 3 * wide])
        grad_probs = nt(stacked, do[image])
        weights = wk[image]
        lines = []
        for h in range(heads):
            line = image * heads + h
            level = alng[0, line : line + 1, :]
            for other in range(1, n_ctx):
                level = level + alng[other, line : line + 1, :]
            lines.append(grad_probs[h * slots : (h + 1) * slots] - level)
        grad_scores = (weights * jnp.concatenate(lines, axis=0)).astype(BF16)
        out = pick_heads(nn(grad_scores, qkv[image, :, 0:wide])) * scale
        split_rows(dqkv, image, slice(wide, 2 * wide), out.astype(BF16))
        out = pick_heads(nn(weights.astype(BF16), do[image]))
        split_rows(dqkv, image, slice(2 * wide, 3 * wide), out.astype(BF16))

    def in_back(c):
        at_rows = chunk(c)

        def one(step, carry):
            out = None
            for j in range(3):
                weight = g_win[j, pl.ds(step * some, some)].reshape(TILE, wide)
                term = nt(dqkv[at_rows, j * wide : (j + 1) * wide], weight)
                out = term if out is None else out + term
            part1[at_rows, lane_at(step, TILE)] = out.astype(BF16)
            return carry

        lax.fori_loop(0, width // TILE, one, 0)
        return scatter(part1, recv1, relay1, c)

    sent1 = [in_back(c) for c in range(2)]
    for c in range(2):
        sent1[c][2]()
    sums = [0.0, 0.0]
    for row in range(0, rows, 2 * BLOCK):
        term = part1[row : row + 2 * BLOCK, :].astype(F32)
        weighted = term * n1[row : row + 2 * BLOCK, :]
        sums[0] = sums[0] + jnp.sum(weighted, axis=0, keepdims=True)
        sums[1] = sums[1] + jnp.sum(term, axis=0, keepdims=True)
    for line, value in enumerate(sums):
        pack(late, line * per, value)
    late[2 * per :, :] = jnp.zeros((late.shape[0] - 2 * per, LANES), F32)
    for j, start in enumerate((0, 2 * wide)):
        value = jnp.sum(dqkv[:, start : start + wide].astype(F32), axis=0, keepdims=True)
        pack(late, 2 * per + j * (wide // LANES), value)
    vector_copies = vector_z(late, late_z, 2 * per)
    tail[1][0]()
    wup_far = grad_halves(wup_near, b_wup, s_wup, t_wup, r_wup)
    wot_grad_far = grad_onward(wot_grad_far, t_wot, r_wot)

    for j in range(3):
        out = tn(h1[...], dqkv[:, j * wide : (j + 1) * wide]).astype(BF16)
        b_win[j] = out.reshape(group, 2, piece, wide)
    win_near = send(b_win.at[:, :, 1 - core], s_win, sib)
    sent1[0][0]()
    wup_far = grad_onward(wup_far, t_wup, r_wup)
    f_wdt[...] = turned(grad_sum(wdt_far, t_wdt, r_wdt), f_wdt)
    stays.append(local(f_wdt, out_wdt))
    win_near.wait_recv()
    for j in range(3):
        both = b_win[j, :, pl.ds(core, 1)].reshape(group, piece, wide).astype(F32)
        t_win[:, j] = (both + s_win[j].astype(F32)).astype(BF16)
    win_far = [send(t_win.at[flip(me, k)], r_win.at[k - 1], plane(k)) for k in reversed(planes)]

    sent1[1][0]()
    def first_back(c, at):
        sent1[c][1]((at,))
        normed, inv = norm_parts(tok[block_at(c, z, at), :].astype(F32))
        grad = arrived(part1, recv1, c, at, ROWS)
        there = slots_at(c, at)
        value = gfirst[there, :] + norm_back(grad, normed, inv, vx[0:1, :])
        tokens_own[there, :] = value.astype(BF16)
        tail[2 + c][2](at)

    tail += [to_all(tokens_own, out_tokens, c) for c in range(2)]
    for at in pieces(0):
        first_back(0, at)
    for at in pieces(1)[:-1]:
        first_back(1, at)
    tail[2][0]()
    first_back(1, pieces(1)[-1])
    whole_rows = grad_sum(wot_grad_far, t_wot, r_wot)
    o_wot[...] = whole_rows.astype(BF16)
    to_owner = [
        send(o_wot.at[:, lane_at(flip(z, k), wide)], z_wot.at[k - 1], zpeer(k))
        for k in reversed(zs)
    ]

    vector_copy = vector_near(vector_copies, late, late_z, 2 * per, late_sib)
    tail[3][0]()
    late_far = vector_far(vector_copy, late, late_sib, late_plane)
    f_wup[...] = grad_sum(wup_far, t_wup, r_wup)
    stays.append(local(f_wup, out_wup))
    vector_last(early_far, early, early_plane)
    f_win[...] = grad_sum(win_far, t_win, r_win)
    stays.append(local(f_win, out_win))
    for copy in to_owner:
        copy.wait_recv()
    value = o_wot[:, lane_at(z, wide)].astype(F32)
    for k in zs:
        value = value + z_wot[k - 1].astype(F32)
    f_wot[...] = turned(value, f_wot)
    stays.append(local(f_wot, out_wot))
    vector_last(late_far, late, late_plane)
    for line in range(2):
        gv[line : line + 1, :] = unpack(late, line * per, width)
        row = 2 * per + line * (wide // LANES)
        gv[9 + line : 10 + line, 0:wide] = unpack(late, row, wide)
    for line in range(4):
        gv[2 + line : 3 + line, :] = unpack(early, line * per, width)
    gv[8:9, 0:hidden] = unpack(early, 4 * per, hidden)
    stays.append(local(gv, out_vec))
    for passing in tail:
        passing[1]()
    for copy in pending:
        copy.wait_send()
    for flag, makes in guarded:

        @pl.when(flag)
        def _():
            for make in makes:
                make().wait_send()

    for copy in stays:
        copy.wait()


def finish_kernel(sizes, *refs):
    n_ctx, piece, cut, wide, hidden, width = sizes
    sources, results, held = refs[:6], refs[7:13], refs[21:27]
    smalls, own, vec, sems = refs[13:21], refs[27:35], refs[35], refs[36]
    shard = lax.axis_index("dp") * n_ctx + lax.axis_index("ctx")
    load = pltpu.make_async_copy(refs[6], vec, sems.at[2, 0])
    load.start()
    ins, outs = [], []
    for i in range(6):
        ins.append(pltpu.make_async_copy(sources[i], held[i], sems.at[0, i]))
        outs.append(pltpu.make_async_copy(held[i], results[i], sems.at[1, i]))
    for copy in ins:
        copy.start()

    def exact(left, right):
        parts, rest = [], left
        for _ in range(3):
            parts.append(rest.astype(BF16).astype(F32))
            rest = rest - parts[-1]
        count = left.shape[0]
        product = nn(jnp.concatenate(parts, axis=0).astype(BF16), right.astype(BF16))
        return product[0:count] + product[count : 2 * count] + product[2 * count :]

    heads = wide // HD
    lane = lax.broadcasted_iota(jnp.int32, (width, piece), 0)
    slot = lax.broadcasted_iota(jnp.int32, (width, piece), 1)
    one = jnp.where(lane - slot == shard * piece, 1.0, 0.0)
    lane = lax.broadcasted_iota(jnp.int32, (hidden, hidden // HD), 0)
    slot = lax.broadcasted_iota(jnp.int32, (hidden, hidden // HD), 1)
    by_unit = jnp.where(lane // HD == slot, 1.0, 0.0)
    load.wait()
    part = exact(vec[0:8, :], one)
    for line in range(6):
        own[line][...] = part[line : line + 1]
    channel = lax.broadcasted_iota(jnp.int32, (cut, hidden), 0)
    lane = lax.broadcasted_iota(jnp.int32, (cut, hidden), 1)
    chosen = jnp.where(lane % HD - channel == shard * cut, vec[8:9, 0:hidden], 0.0)
    own[6][...] = exact(chosen, by_unit)
    lane = lax.broadcasted_iota(jnp.int32, (wide, cut), 0)
    slot = lax.broadcasted_iota(jnp.int32, (wide, cut), 1)
    pick = jnp.where(lane % HD - slot == shard * cut, 1.0, 0.0)
    head = lax.broadcasted_iota(jnp.int32, (heads, wide), 0)
    lane = lax.broadcasted_iota(jnp.int32, (heads, wide), 1)
    for j in range(2):
        chosen = jnp.where(lane // HD == head, vec[9 + j : 10 + j, 0:wide], 0.0)
        own[7][j] = exact(chosen, pick)
    for i in range(8):
        outs.append(pltpu.make_async_copy(own[i], smalls[i], sems.at[2, 1 + i]))
        outs[-1].start()
    for i in range(6):
        ins[i].wait()
        outs[i].start()
    for copy in outs:
        copy.wait()


def on_device(
    mesh_shape,
    tokens,
    keep_mask,
    cotangent,
    first_gain,
    first_shift,
    attend_in,
    attend_bias,
    attend_out,
    out_bias,
    second_gain,
    second_shift,
    expand_in,
    expand_bias,
    contract_out,
    contract_bias,
):
    n_dp, n_ctx, n_t = mesh_shape
    images, slots, width = tokens.shape
    piece, _, wide = attend_in.shape
    hidden = expand_in.shape[1]
    cut = expand_bias.shape[1]
    rows = images * slots
    group = n_dp * n_ctx // 2
    total = slots * n_ctx
    heads = wide // HD
    turn = piece % LANES == 0
    per = width // LANES
    early_rows = 4 * per + hidden // LANES
    late_rows = 2 * per + 8 * ((2 * wide // LANES + 7) // 8)
    sizes = (n_dp, n_ctx, n_t, images, slots, width, wide, hidden, piece, cut)
    vmem = pl.BlockSpec(memory_space=pltpu.VMEM)
    hbm = pl.BlockSpec(memory_space=pl.ANY)
    scratch = [
        pltpu.VMEM((rows, width), BF16),
        pltpu.VMEM((rows, width), BF16),
        pltpu.VMEM((wide, piece), BF16),
        pltpu.VMEM((hidden, piece), BF16),
        pltpu.VMEM((2 * ROWS, LANES), F32),
        pltpu.VMEM((3, group, 2, piece, wide), BF16),
        pltpu.VMEM((group, 2, piece, n_t * wide), BF16),
        pltpu.VMEM((group, 2, piece, hidden), BF16),
        pltpu.VMEM((group, 2, piece, hidden), BF16),
        pltpu.VMEM((group, 2, 2 * ROWS, LANES), F32),
        pltpu.VMEM((ROWS, width), F32),
        pltpu.VMEM((rows, width), F32),
        pltpu.VMEM((rows, width), BF16),
        pltpu.VMEM((images, total, 3 * wide), BF16),
        pltpu.VMEM((images, heads * slots, total), F32),
        pltpu.VMEM((images, heads * slots, total), F32),
        pltpu.VMEM((n_ctx, images * heads, total), F32),
        pltpu.VMEM((n_ctx, images * heads, total), F32),
        pltpu.VMEM((rows, n_t * wide), BF16),
        pltpu.VMEM((rows, width), F32),
        pltpu.VMEM((rows, width), BF16),
        pltpu.VMEM((rows, hidden), F32),
        pltpu.VMEM((rows, hidden), BF16),
        pltpu.VMEM((rows, hidden), BF16),
        pltpu.VMEM((rows, width), BF16),
        pltpu.VMEM((rows, width), BF16),
        pltpu.VMEM((rows, width), BF16),
        pltpu.VMEM((2, slots, width), BF16),
        pltpu.VMEM((2, slots, width), BF16),
        pltpu.VMEM((2, slots, width), BF16),
        pltpu.VMEM((2, slots, width), BF16),
        pltpu.VMEM((2, slots, width), BF16),
        pltpu.VMEM((2, slots, width), BF16),
        pltpu.VMEM((slots, width), F32),
        pltpu.VMEM((rows, width), BF16),
        pltpu.VMEM((slots, width), BF16),
        pltpu.VMEM((slots, n_t * wide), BF16),
        pltpu.VMEM((images, total, wide), BF16),
        pltpu.VMEM((rows, 3 * wide), BF16),
        pltpu.VMEM((slots, width), BF16),
        pltpu.VMEM((slots, width), BF16),
        pltpu.VMEM((ROWS, width), F32),
        pltpu.VMEM((early_rows, LANES), F32),
        pltpu.VMEM((early_rows, LANES), F32),
        pltpu.VMEM((group - 1, early_rows, LANES), F32),
        pltpu.VMEM((n_t - 1, 4 * per, LANES), F32),
        pltpu.VMEM((late_rows, LANES), F32),
        pltpu.VMEM((late_rows, LANES), F32),
        pltpu.VMEM((group - 1, late_rows, LANES), F32),
        pltpu.VMEM((n_t - 1, 2 * per, LANES), F32),
        pltpu.VMEM((3, group, 2, piece, wide), BF16),
        pltpu.VMEM((group, 2, piece, n_t * wide), BF16),
        pltpu.VMEM((group, 2, piece, hidden), BF16),
        pltpu.VMEM((group, 2, piece, hidden), BF16),
        pltpu.VMEM((3, group, piece, wide), BF16),
        pltpu.VMEM((group, piece, n_t * wide), BF16),
        pltpu.VMEM((group, piece, hidden), BF16),
        pltpu.VMEM((group, piece, hidden), BF16),
        pltpu.VMEM((group, 3, piece, wide), BF16),
        pltpu.VMEM((group, piece, n_t * wide), BF16),
        pltpu.VMEM((group, piece, hidden), BF16),
        pltpu.VMEM((group, piece, hidden), BF16),
        pltpu.VMEM((group - 1, 3, piece, wide), BF16),
        pltpu.VMEM((group - 1, piece, n_t * wide), BF16),
        pltpu.VMEM((group - 1, piece, hidden), BF16),
        pltpu.VMEM((group - 1, piece, hidden), BF16),
        pltpu.VMEM((piece, n_t * wide), BF16),
        pltpu.VMEM((n_t - 1, piece, wide), BF16),
    ]
    shapes = (
        (3, piece, wide),
        (wide, piece) if turn else (piece, wide),
        (piece, hidden),
        (hidden, piece) if turn else (piece, hidden),
    )
    scratch += [pltpu.VMEM(shape, F32) for shape in shapes]
    copies = 260 + 20 * group
    scratch += [
        pltpu.SemaphoreType.DMA((copies,)),
        pltpu.SemaphoreType.DMA((copies,)),
        pltpu.SemaphoreType.DMA((48,)),
    ]
    results = [jax.ShapeDtypeStruct((rows, width), BF16)] * 2
    results += [jax.ShapeDtypeStruct(shape, F32) for shape in shapes]
    outs = pl.pallas_call(
        functools.partial(block_kernel, sizes),
        out_shape=(*results, jax.ShapeDtypeStruct((ROWS, width), F32)),
        in_specs=[hbm, hbm, vmem, hbm, hbm, hbm, hbm] + [vmem] * 8,
        out_specs=(hbm,) * 7,
        scratch_shapes=scratch,
        compiler_params=pltpu.CompilerParams(
            collective_id=0, has_side_effects=True, vmem_limit_bytes=63 << 20
        ),
    )(
        tokens.reshape(rows, width),
        cotangent.reshape(rows, width),
        keep_mask,
        jnp.transpose(attend_in, (1, 0, 2)),
        attend_out,
        expand_in,
        contract_out,
        *[
            v.reshape(1, piece)
            for v in (first_gain, first_shift, out_bias, second_gain, second_shift, contract_bias)
        ],
        expand_bias.T,
        attend_bias,
    )
    vector = jax.ShapeDtypeStruct((1, piece), F32)
    small = [vector] * 6 + [
        jax.ShapeDtypeStruct((cut, hidden // HD), F32),
        jax.ShapeDtypeStruct((2, heads, cut), F32),
    ]
    placed = pl.pallas_call(
        functools.partial(finish_kernel, (n_ctx, piece, cut, wide, hidden, width)),
        out_shape=(*results, *small),
        in_specs=[hbm] * 7,
        out_specs=(hbm,) * 14,
        scratch_shapes=[pltpu.VMEM(r.shape, r.dtype) for r in (*results, *small)]
        + [pltpu.VMEM((ROWS, width), F32), pltpu.SemaphoreType.DMA((3, 9))],
        compiler_params=pltpu.CompilerParams(vmem_limit_bytes=63 << 20),
    )(*outs)
    block_out, tokens_grad, d_win, d_wot, d_wup, d_wdt = placed[:6]
    vectors = [v.reshape(piece) for v in placed[6:12]]
    return (
        block_out.reshape(tokens.shape),
        tokens_grad.reshape(tokens.shape),
        vectors[0],
        vectors[1],
        jnp.transpose(d_win, (1, 0, 2)),
        placed[13],
        d_wot if turn else d_wot.T,
        vectors[2],
        vectors[3],
        vectors[4],
        d_wup,
        placed[12].T,
        d_wdt if turn else d_wdt.T,
        vectors[5],
    )


def solution(mesh):
    shape = (mesh.shape["dp"], mesh.shape["ctx"], mesh.shape["tensor"])
    vector = P(("dp", "ctx"))
    params = (
        vector,
        vector,
        P(("dp", "ctx"), None, "tensor"),
        P(None, "tensor", ("dp", "ctx")),
        P("tensor", ("dp", "ctx")),
        vector,
        vector,
        vector,
        P(("dp", "ctx"), "tensor"),
        P("tensor", ("dp", "ctx")),
        P("tensor", ("dp", "ctx")),
        vector,
    )
    rows = P("dp", "ctx", None)
    return jax.shard_map(
        functools.partial(on_device, shape),
        mesh=mesh,
        in_specs=(rows, P("dp", None), rows, *params),
        out_specs=(rows, rows, *params),
        check_vma=False,
    )
```

```python
import functools

import jax
import jax.numpy as jnp
from jax import lax
from jax.experimental import pallas as pl
from jax.experimental.pallas import tpu as pltpu
from jax.sharding import PartitionSpec as P

HD = 64
BUFFER = 64
LANES = 128
ROWS = 16
TILE = 256
BLOCK = 32
MESH = pl.DeviceIdType.MESH
F32 = jnp.float32
BF16 = jnp.bfloat16

eps = 1e-06
neg_big = -1e30
root_half = 0.7071067811865476
inv_root_two_pi = 0.3989422804014327


def flip(index, bits):
    out, bit = index, 1
    while bit <= bits:
        if bits & bit:
            out = out + bit - 2 * bit * lax.rem(lax.div(index, bit), 2)
        bit *= 2
    return out


def nn(left, right):
    return jnp.dot(left, right, preferred_element_type=F32)


def nt(left, right):
    return lax.dot_general(left, right, (((1,), (1,)), ((), ())), preferred_element_type=F32)


def tn(left, right):
    return lax.dot_general(left, right, (((0,), (0,)), ((), ())), preferred_element_type=F32)


def steps(count, body):
    if count > 8:
        lax.fori_loop(0, count, body, 0)
        return
    for step in range(count):
        body(step, 0)


def turned(value, ref):
    return value if value.shape == ref.shape else value.T


def norm_parts(values):
    mean = jnp.mean(values, axis=-1, keepdims=True)
    centered = values - mean
    spread = jnp.mean(centered * centered, axis=-1, keepdims=True)
    inv = lax.rsqrt(spread + eps)
    return centered * inv, inv


def block_kernel(
    sizes,
    tok_in,
    cot_in,
    keep,
    win,
    attend_out,
    wup,
    contract_out,
    first_gain,
    first_shift,
    out_bias,
    second_gain,
    second_shift,
    contract_bias,
    expand_bias,
    attend_bias,
    out_block,
    out_tokens,
    out_win,
    out_wot,
    out_wup,
    out_wdt,
    out_vec,
    tok,
    cot,
    a_out,
    c_out,
    vec,
    g_win,
    g_wot,
    g_wup,
    g_wdt,
    g_vec,
    vx,
    n1,
    h1,
    qkv,
    wq,
    wk,
    stat,
    alng,
    mixed,
    first,
    h2,
    ga,
    act,
    gi,
    part2,
    parts,
    part1,
    recv2,
    relay2,
    recvs,
    relays,
    recv1,
    relay1,
    gfirst,
    gdown,
    gown,
    gm,
    do,
    dqkv,
    block_own,
    tokens_own,
    gv,
    early,
    early_sib,
    early_plane,
    early_z,
    late,
    late_sib,
    late_plane,
    late_z,
    b_win,
    b_wot,
    b_wup,
    b_wdt,
    s_win,
    s_wot,
    s_wup,
    s_wdt,
    t_win,
    t_wot,
    t_wup,
    t_wdt,
    r_win,
    r_wot,
    r_wup,
    r_wdt,
    o_wot,
    z_wot,
    f_win,
    f_wot,
    f_wup,
    f_wdt,
    send_sem,
    recv_sem,
    local_sem,
):
    n_dp, n_ctx, n_t, images, slots, width, wide, hidden, piece, cut = sizes
    rows = images * slots
    total = slots * n_ctx
    heads = wide // HD
    half = n_ctx // 2
    group = n_dp * half
    scale = HD ** (-0.5)
    dp = lax.axis_index("dp")
    ctx = lax.axis_index("ctx")
    z = lax.axis_index("tensor")
    high, core = lax.div(ctx, 2), lax.rem(ctx, 2)
    me = dp * half + high
    shard = me * 2 + core
    sib = (dp, flip(ctx, 1), z)

    def plane(k):
        other = flip(me, k)
        return (lax.div(other, half), lax.rem(other, half) * 2 + core, z)

    def ctx_at(k):
        return flip(high, k) * 2 + core

    def zpeer(k):
        return (dp, ctx, flip(z, k))

    def slot_at(index):
        return pl.ds(pl.multiple_of(index * slots, ROWS), slots)

    def lane_at(index, size):
        return pl.ds(pl.multiple_of(index * size, size), size)

    own = slot_at(ctx)
    mine = slot_at(z)

    cut_at = ROWS * (slots // ROWS // 2)
    starts = (0, cut_at)
    sizes_of = (cut_at, slots - cut_at)
    bases = (0, images * cut_at)

    def chunk(c):
        return slice(bases[c], bases[c] + images * sizes_of[c])

    def rows_at(c, image):
        first_row = bases[c] + image * sizes_of[c]
        return pl.ds(pl.multiple_of(first_row, ROWS), sizes_of[c])

    def slot_part(c):
        return slice(starts[c], starts[c] + sizes_of[c])

    def split_rows(ref, image, lanes, value):
        for c in range(2):
            ref[rows_at(c, image), lanes] = value[slot_part(c)]

    count = [0, 0]
    stays = []
    pending = []

    def send(src, dst, device):
        index = count[0]
        count[0] += 1
        copy = pltpu.make_async_remote_copy(
            src_ref=src,
            dst_ref=dst,
            send_sem=send_sem.at[index],
            recv_sem=recv_sem.at[index],
            device_id=device,
            device_id_type=MESH,
        )
        copy.start()
        pending.append(copy)
        return copy

    inside = lax.rem(z - lax.div(z, 2), 2) == 1
    at_end = lax.rem(z - lax.div(z, 2), 2) == 0
    guarded = []

    def fresh():
        count[0] += 1
        return count[0] - 1

    def remote(src, dst, device, out_index, in_index):
        return pltpu.make_async_remote_copy(
            src_ref=src,
            dst_ref=dst,
            send_sem=send_sem.at[out_index],
            recv_sem=recv_sem.at[in_index],
            device_id=device,
            device_id_type=MESH,
        )

    def send_if(flag, makes):
        guarded.append((flag, makes))

        @pl.when(flag)
        def _():
            for make in makes:
                make().start()

    def complete(copy):
        pending[:] = [other for other in pending if other is not copy]
        copy.wait()

    def local(src, dst):
        index = count[1]
        count[1] += 1
        copy = pltpu.make_async_copy(src, dst, local_sem.at[index])
        copy.start()
        return copy

    planes = range(1, group)
    zs = range(1, n_t)

    def at_win_kv(m, c):
        return g_win.at[1:3, m, c]

    def at_win_q(m, c):
        return g_win.at[0:1, m, c]

    def at_wot(m, c):
        return g_wot.at[m, c, :, lane_at(z, wide)]

    def at_wup(m, c):
        return g_wup.at[m, c]

    def at_wdt(m, c):
        return g_wdt.at[m, c]

    def at_vec(m, c):
        return g_vec.at[m, c]

    barrier = pltpu.get_barrier_semaphore()
    for device in [plane(k) for k in planes] + [sib] + [zpeer(k) for k in zs]:
        pl.semaphore_signal(barrier, inc=1, device_id=device, device_id_type=MESH)
    a_out_load = local(attend_out, a_out)
    def load_rows(source, ref):
        return [
            local(
                source.at[image * slots + starts[c] : image * slots + starts[c] + sizes_of[c], :],
                ref.at[rows_at(c, image), :],
            )
            for c in range(2)
            for image in range(images)
        ]

    tok_load = load_rows(tok_in, tok)
    win_own = local(win, g_win.at[:, me, core])
    c_out_load = local(contract_out, c_out)
    cot_load = load_rows(cot_in, cot)
    wup_own = local(wup, at_wup(me, core))

    vec[...] = jnp.zeros_like(vec)
    for line, ref in enumerate(
        (first_gain, first_shift, out_bias, second_gain, second_shift, contract_bias)
    ):
        vec[line : line + 1, 0:piece] = ref[...].astype(F32)
    vec[8 : 8 + cut, 0 : hidden // HD] = expand_bias[...].astype(F32)
    for j in range(2):
        vec[16 + j * heads : 16 + (j + 1) * heads, 0:cut] = attend_bias[j].astype(F32)
    g_vec[me, core] = vec[...]
    gv[...] = jnp.zeros_like(gv)
    unit_one = (
        lax.broadcasted_iota(jnp.int32, (piece, piece), 0)
        == lax.broadcasted_iota(jnp.int32, (piece, piece), 1)
    ).astype(F32)
    unit_one = unit_one.astype(BF16)
    a_out_load.wait()
    g_wot[me, core, :, lane_at(z, wide)] = nt(unit_one, a_out[...]).astype(BF16)
    pl.semaphore_wait(barrier, group + n_t - 1)

    def gather_start(src, at):
        far = [send(src, at(me, core), plane(k)) for k in planes]
        return far, send(src, at(me, core), sib)

    def gather_forward(started, at):
        out = []
        for k in planes:
            started[0][k - 1].wait_recv()
            there = at(flip(me, k), core)
            out.append(send(there, there, sib))
        return out

    def gather_finish(started, passed):
        started[1].wait_recv()
        for copy in passed:
            copy.wait_recv()

    relayed = group == 4 and piece % (2 * ROWS) == 0

    def relay_start(src, at):
        if not relayed:
            return gather_start(src, at)
        far = [send(src, at(me, core), plane(k)) for k in (1, 2)]
        return far, send(src, at(me, core), sib)

    def relay_forward(started, at):
        if not relayed:
            return gather_forward(started, at), []
        out, halves = [], []
        for k in (1, 2):
            started[0][k - 1].wait_recv()
            there = at(flip(me, k), core)
            part = there.at[pl.ds((k - 1) * (piece // 2), piece // 2)]
            halves.append(send(part, part, plane(3 - k)))
            out.append(send(there, there, sib))
        return out, halves

    def relay_last(halves, at):
        if not halves:
            return []
        for copy in halves:
            copy.wait_recv()
        there = at(flip(me, 3), core)
        return [send(there, there, sib)]

    def ctx_start(at):
        far = [send(at(ctx), at(ctx), (dp, ctx_at(k), z)) for k in range(1, half)]
        return far, send(at(ctx), at(ctx), sib)

    def ctx_forward(started, at):
        out = []
        for k in range(1, half):
            started[0][k - 1].wait_recv()
            out.append(send(at(ctx_at(k)), at(ctx_at(k)), sib))
        return out

    def ctx_finish(started, passed):
        started[1].wait_recv()
        for copy in passed:
            copy.wait_recv()

    def wot_piece(m, index):
        return g_wot.at[m, core, :, lane_at(index, wide)]

    vec_started = gather_start(vec, at_vec)
    wot_own = at_wot(me, core)
    wot_far = [send(wot_own, wot_own, plane(k)) for k in planes if k < 3]
    kv_win_started = gather_start(win.at[1:3], at_win_kv)
    wot_far += [send(wot_own, wot_own, plane(k)) for k in planes if k >= 3]
    wot_started = (wot_far, send(wot_own, wot_own, sib))
    q_win_started = gather_start(win.at[0:1], at_win_q)
    wot_z = [[send(wot_piece(me, z), wot_piece(me, z), zpeer(k)) for k in zs]]

    for copy in tok_load:
        copy.wait()

    def first_norm(step, carry):
        at = pl.ds(pl.multiple_of(step * BLOCK, BLOCK), BLOCK)
        normed, _ = norm_parts(tok[at, :].astype(F32))
        n1[at, :] = normed
        return carry

    lax.fori_loop(0, rows // BLOCK, first_norm, 0)

    vec_passed = gather_forward(vec_started, at_vec)
    gather_finish(vec_started, vec_passed)
    shape = (2 * ROWS, width)
    line_id = lax.broadcasted_iota(jnp.int32, shape, 0)
    lane_id = lax.broadcasted_iota(jnp.int32, shape, 1)
    source = lax.broadcasted_iota(jnp.int32, (LANES, width), 0)
    target = lax.broadcasted_iota(jnp.int32, (LANES, width), 1)
    by_unit = jnp.where(target // HD == source, 1.0, 0.0).astype(BF16)
    for_unit = lane_id % HD - (line_id - 8)
    for_head = lane_id // HD == (line_id - 16) % heads

    def place(index, carry):
        one, two, three = carry
        shares = g_vec[lax.div(index, 2), lax.rem(index, 2)].astype(BF16)
        by_width = jnp.where(target - source == index * piece, 1.0, 0.0).astype(BF16)
        by_channel = jnp.where(target % HD - source == index * cut, 1.0, 0.0).astype(BF16)
        one = one + nn(shares, by_width)
        two = two + jnp.where(for_unit == index * cut, nn(shares, by_unit), 0.0)
        three = three + jnp.where(for_head, nn(shares, by_channel), 0.0)
        return one, two, three

    zero = jnp.zeros(shape, F32)
    one, two, three = lax.fori_loop(0, 2 * group, place, (zero, zero, zero))
    vx[0:8, :] = one[0:8]
    vx[8:9, :] = jnp.sum(two[8 : 8 + cut], axis=0, keepdims=True)
    vx[9:10, :] = jnp.sum(three[16 : 16 + heads], axis=0, keepdims=True)
    vx[10:11, :] = jnp.sum(three[16 + heads : 16 + 2 * heads], axis=0, keepdims=True)

    def first_hidden(step, carry):
        at = pl.ds(pl.multiple_of(step * BLOCK, BLOCK), BLOCK)
        h1[at, :] = (n1[at, :] * vx[0:1, :] + vx[1:2, :]).astype(BF16)
        return carry

    lax.fori_loop(0, rows // BLOCK, first_hidden, 0)

    wot_passed = []

    def wot_onward(k):
        wot_started[0][k - 1].wait_recv()
        there = wot_piece(flip(me, k), z)
        wot_z.append([send(there, there, zpeer(j)) for j in reversed(zs)][::-1])
        wot_passed.append(send(there, there, sib))

    for k in planes:
        if k < 3:
            wot_onward(k)

    c_out_load.wait()

    def turn(step, carry):
        at = lane_at(step, TILE)
        g_wdt[me, core, :, at] = nt(unit_one, c_out[at, :]).astype(BF16)
        return carry

    steps(hidden // TILE, turn)

    lengths = BUFFER + jnp.sum(keep[...], axis=1, keepdims=True)
    slot_id = lax.broadcasted_iota(jnp.int32, (slots, 1), 0) + ctx * slots
    key_id = lax.broadcasted_iota(jnp.int32, (1, total), 1)
    head_of = lax.broadcasted_iota(jnp.int32, (slots, wide), 1) // HD
    spot = lax.broadcasted_iota(jnp.int32, (slots, total), 1) == slot_id

    def stack_heads(block):
        wider = block.astype(F32)
        return jnp.concatenate(
            [jnp.where(head_of == h, wider, 0.0).astype(BF16) for h in range(heads)], axis=0
        )

    def pick_heads(block):
        out = jnp.where(head_of == 0, block[0:slots], 0.0)
        for h in range(1, heads):
            out = jnp.where(head_of == h, block[h * slots : (h + 1) * slots], out)
        return out

    def put_rows(ref, image, column):
        for h in range(heads):
            part = jnp.where(spot, column[h * slots : (h + 1) * slots], 0.0)
            line = image * heads + h
            ref[ctx, line : line + 1, :] = jnp.sum(part, axis=0, keepdims=True)

    win_passed = gather_forward(kv_win_started, at_win_kv)
    win_own.wait()
    gather_finish(kv_win_started, win_passed)

    def project(j, bias):
        out = nn(h1[...], g_win[j].reshape(width, wide))
        if bias is not None:
            out = out + vx[bias : bias + 1, 0:wide]
        out = out.astype(BF16)
        for c in range(2):
            place_at = pl.ds(pl.multiple_of(ctx * slots + starts[c], ROWS), sizes_of[c])
            block = out[chunk(c)].reshape(images, sizes_of[c], wide)
            qkv[:, place_at, j * wide : (j + 1) * wide] = block

    def at_kv(images_of):
        def at(index):
            return qkv.at[images_of, slot_at(index), wide : 3 * wide]

        return at

    def at_q(index):
        return qkv.at[:, slot_at(index), 0:wide]

    project(1, None)
    project(2, 10)
    middle = images // 2
    image_parts = (slice(0, middle), slice(middle, images))
    kv_started = [ctx_start(at_kv(part)) for part in image_parts]
    wup_started = relay_start(wup, at_wup)
    wdt_started = relay_start(at_wdt(me, core), at_wdt)
    for k in planes:
        if k >= 3:
            wot_onward(k)
    win_passed = gather_forward(q_win_started, at_win_q)
    gather_finish(q_win_started, win_passed)
    project(0, 9)

    def at_mixed(index, c, part):
        first_row = bases[c] + part.start * sizes_of[c]
        last_row = bases[c] + part.stop * sizes_of[c]
        return mixed.at[first_row:last_row, lane_at(index, wide)]

    mixed_sent = [[], []]
    for image in range(images):
        for part in range(2):
            if image == image_parts[part].start:
                kv_at = at_kv(image_parts[part])
                kv_passed = ctx_forward(kv_started[part], kv_at)
                ctx_finish(kv_started[part], kv_passed)
        key_live = key_id < lengths[image : image + 1, :]
        stacked = stack_heads(qkv[image, own, 0:wide])
        scores = nt(stacked, qkv[image, :, wide : 2 * wide]) * scale
        scores = jnp.where(key_live, scores, neg_big)
        top = jnp.max(scores, axis=-1, keepdims=True)
        expo = jnp.exp(scores - top)
        whole = jnp.sum(expo, axis=-1, keepdims=True)
        probs = expo / whole
        wq[image] = probs
        put_rows(stat, image, top + jnp.log(whole))
        out = nn(probs.astype(BF16), qkv[image, :, 2 * wide : 3 * wide])
        split_rows(mixed, image, lane_at(z, wide), pick_heads(out).astype(BF16))
        for part in image_parts:
            if image == part.stop - 1:
                for c in range(2):
                    there = at_mixed(z, c, part)
                    mixed_sent[c] += [send(there, there, zpeer(k)) for k in reversed(zs)]

    def at_stat(index):
        return stat.at[index]

    for copy in cot_load:
        copy.wait()
    row_live = []
    for image in range(images):
        row_live.append(slot_id < lengths[image : image + 1, :])
        for c in range(2):
            at = rows_at(c, image)
            live = row_live[image][slot_part(c)]
            gdown[at, :] = jnp.where(live, cot[at, :].astype(F32), 0.0).astype(BF16)

    wup_passed, wup_halves = relay_forward(wup_started, at_wup)
    gather_finish(wot_started, wot_passed)
    wot_more = []
    for order, block in enumerate(wot_z):
        for k in zs:
            block[k - 1].wait_recv()
            there = wot_piece(flip(me, order), flip(z, k))
            wot_more.append(send(there, there, sib))
    wup_own.wait()
    wdt_passed, wdt_halves = relay_forward(wdt_started, at_wdt)
    q_started = ctx_start(at_q)
    stat_started = ctx_start(at_stat)
    wup_passed += relay_last(wup_halves, at_wup)
    for copy in wot_more:
        copy.wait_recv()

    some = group // (width // TILE)

    def pieces(c):
        return range(0, sizes_of[c], ROWS)

    def block_at(c, index, at):
        first_row = bases[c] + index * sizes_of[c] + at
        return pl.ds(pl.multiple_of(first_row, ROWS), ROWS)

    def slots_at(c, at):
        return slice(starts[c] + at, starts[c] + at + ROWS)

    def scatter(part, recv, relay, c):
        marks = {at: [fresh() for _ in range(4)] for at in pieces(c)}

        def onward(j, at):
            return remote(
                part.at[block_at(c, flip(z, 3 - j), at), :],
                relay.at[j, slots_at(c, at), :],
                zpeer(1),
                marks[at][j],
                marks[at][j],
            )

        def passed(j, at):
            return remote(
                relay.at[j, slots_at(c, at), :],
                recv.at[1, slots_at(c, at), :],
                zpeer(2 + j),
                marks[at][2 + j],
                marks[at][2],
            )

        both = [(at, j) for at in pieces(c) for j in range(2)]
        send_if(at_end, [functools.partial(onward, j, at) for at, j in both])
        near = []

        def send_near():
            source = part.at[rows_at(c, flip(z, 1)), :]
            near.append(send(source, recv.at[0, slot_part(c), :], zpeer(1)))

        def pass_on():
            guarded.append((inside, [functools.partial(passed, j, at) for at, j in both]))

            @pl.when(inside)
            def _():
                for at, j in both:
                    onward(j, at).wait_recv()
                    value = part[block_at(c, flip(z, 2 + j), at), :].astype(F32)
                    value = value + relay[j, slots_at(c, at), :].astype(F32)
                    relay[j, slots_at(c, at), :] = value.astype(BF16)
                    passed(j, at).start()

        def finish(some_pieces=None):
            if some_pieces is None or 0 in some_pieces:
                near[0].wait_recv()
            for at in some_pieces or pieces(c):
                passed(0, at).wait_recv()

        return pass_on, finish, send_near

    def to_all(source, target, c):
        marks = {at: [fresh() for _ in range(4)] for at in pieces(c)}

        def piece_of(index, at):
            first_row = index * slots + starts[c] + at
            return target.at[pl.ds(pl.multiple_of(first_row, ROWS), ROWS), :]

        def far(k, at):
            mark = marks[at][k - 2]
            return remote(source.at[slots_at(c, at), :], piece_of(z, at), zpeer(k), mark, mark)

        def passed(k, at):
            there = piece_of(flip(z, k), at)
            return remote(there, there, zpeer(1), marks[at][k], marks[at][3 - k])

        nears = []

        def start(at):
            own_part = source.at[slots_at(c, at), :]
            send_if(at_end, [functools.partial(far, 2, at)])
            send_if(inside, [functools.partial(far, 3, at)])
            nears.append(send(own_part, piece_of(z, at), zpeer(1)))
            stays.append(local(own_part, piece_of(z, at)))

        both = [(k, at) for at in pieces(c) for k in (3, 2)]

        def pass_on():
            guarded.append((inside, [functools.partial(passed, k, at) for k, at in both]))

            @pl.when(inside)
            def _():
                for k, at in both:
                    far(k, at).wait_recv()
                    passed(k, at).start()

        def finish():
            for copy in nears:
                copy.wait_recv()

            @pl.when(at_end)
            def _():
                for k, at in both:
                    far(k, at).wait_recv()

        return pass_on, finish, start

    def arrived(part, recv, c, at, size):
        here = pl.ds(pl.multiple_of(bases[c] + z * sizes_of[c] + at, ROWS), size)
        there = pl.ds(pl.multiple_of(starts[c] + at, ROWS), size)
        out = part[here, :].astype(F32)
        for j in range(2):
            out = out + recv[j, there, :].astype(F32)
        return out

    def attended(c):
        at_rows = chunk(c)
        for copy in mixed_sent[c]:
            copy.wait_recv()

        def project_out(step, carry):
            weight = g_wot[pl.ds(step * some, some)].reshape(TILE, n_t * wide)
            first[at_rows, lane_at(step, TILE)] = nt(mixed[at_rows, :], weight)
            return carry

        steps(width // TILE, project_out)

        for row in range(bases[c], bases[c] + images * sizes_of[c], ROWS):
            at = slice(row, row + ROWS)
            value = tok[at, :].astype(F32) + first[at, :] + vx[2:3, :]
            first[at, :] = value
            normed, _ = norm_parts(value)
            h2[at, :] = (normed * vx[3:4, :] + vx[4:5, :]).astype(BF16)

    def feed_forward(c):
        at_rows = chunk(c)

        def expand(step, carry):
            at = lane_at(step, TILE)
            weight = g_wup[:, :, :, at].reshape(width, TILE)
            inner = nn(h2[at_rows, :], weight) + vx[8:9, at]
            share = 0.5 * (1.0 + lax.erf(inner * root_half))
            act[at_rows, at] = (inner * share).astype(BF16)
            slope = share + inner * jnp.exp(-0.5 * inner * inner) * inv_root_two_pi
            grad = (ga[at_rows, at] * slope).astype(BF16)
            gi[at_rows, at] = grad
            gv[8:9, at] += jnp.sum(grad.astype(F32), axis=0, keepdims=True)
            return carry

        steps(hidden // TILE, expand)

        def up_back(step, carry):
            weight = g_wup[pl.ds(step * some, some)].reshape(TILE, hidden)
            part2[at_rows, lane_at(step, TILE)] = nt(gi[at_rows, :], weight).astype(BF16)
            return carry

        steps(width // TILE, up_back)
        return scatter(part2, recv2, relay2, c)

    attended(0)
    wdt_passed += relay_last(wdt_halves, at_wdt)
    gather_finish(wup_started, wup_passed)
    gather_finish(wdt_started, wdt_passed)

    def down_back(c):
        at_rows = chunk(c)

        def one(step, carry):
            at = lane_at(step, TILE)
            weight = g_wdt[:, :, :, at].reshape(width, TILE)
            ga[at_rows, at] = nn(gdown[at_rows, :], weight)
            return carry

        steps(hidden // TILE, one)

    down_back(0)
    sent2 = [feed_forward(0)]
    sent2[0][2]()
    down_back(1)
    attended(1)
    sent2.append(feed_forward(1))
    sent2[1][2]()
    sent2[0][0]()

    def contract(step, carry):
        weight = g_wdt[pl.ds(step * some, some)].reshape(TILE, hidden)
        parts[:, lane_at(step, TILE)] = nt(act[...], weight).astype(BF16)
        return carry

    steps(width // TILE, contract)
    sents = []
    for c in range(2):
        sents.append(scatter(parts, recvs, relays, c))
        sents[c][2]()

    def wide_grad(buf, left, right, lanes):
        def one(step, carry):
            at = lane_at(step, TILE)
            out = tn(left[...], right[:, at]).astype(BF16)
            buf[:, :, :, at] = out.reshape(group, 2, piece, TILE)
            return carry

        steps(lanes // TILE, one)

    def grad_near(buf, near):
        return send(buf.at[:, 1 - core], near, sib)

    def grad_far(copy, buf, near, both, recv):
        copy.wait_recv()

        def one(m, carry):
            both[m] = (buf[m, core].astype(F32) + near[m].astype(F32)).astype(BF16)
            return carry

        steps(group, one)
        return [send(both.at[flip(me, k)], recv.at[k - 1], plane(k)) for k in reversed(planes)]

    def grad_halves(copy, buf, near, both, recv):
        if not relayed:
            return grad_far(copy, buf, near, both, recv)
        copy.wait_recv()

        def one(m, carry):
            both[m] = (buf[m, core].astype(F32) + near[m].astype(F32)).astype(BF16)
            return carry

        steps(group, one)
        part = piece // 2
        corner = flip(me, 3)
        return [
            send(both.at[corner, 0:part], recv.at[2, 0:part], plane(1)),
            send(both.at[corner, part:piece], recv.at[2, part:piece], plane(2)),
        ]

    def grad_onward(copies, both, recv):
        if not relayed:
            return copies
        part = piece // 2
        for k, at in ((2, slice(0, part)), (1, slice(part, piece))):
            copies[2 - k].wait_recv()
            other = flip(me, k)
            value = both[other, at].astype(F32) + recv[2, at].astype(F32)
            both[other, at] = value.astype(BF16)
        return [send(both.at[flip(me, k)], recv.at[k - 1], plane(k)) for k in (1, 2)]

    def grad_sum(copies, both, recv):
        for copy in copies:
            copy.wait_recv()
        value = both[me].astype(F32)
        for k in range(len(copies)):
            value = value + recv[k].astype(F32)
        return value

    wide_grad(b_wdt, gdown, act, hidden)
    wdt_near = grad_near(b_wdt, s_wdt)
    sent2[1][0]()
    wide_grad(b_wup, h2, gi, hidden)
    wup_near = grad_near(b_wup, s_wup)
    wdt_far = grad_far(wdt_near, b_wdt, s_wdt, t_wdt, r_wdt)

    q_passed = ctx_forward(q_started, at_q)
    stat_passed = ctx_forward(stat_started, at_stat)
    ctx_finish(q_started, q_passed)
    ctx_finish(stat_started, stat_passed)
    for image in range(images):
        stacked = stack_heads(qkv[image, own, wide : 2 * wide])
        scores = nt(stacked, qkv[image, :, 0:wide]) * scale
        for h in range(heads):
            line = image * heads + h
            level = stat[0, line : line + 1, :]
            for other in range(1, n_ctx):
                level = level + stat[other, line : line + 1, :]
            block = scores[h * slots : (h + 1) * slots]
            block = jnp.where(row_live[image], block, neg_big)
            wk[image, h * slots : (h + 1) * slots, :] = jnp.exp(block - level)

    own_live = slot_id < jnp.sum(
        jnp.where(lax.broadcasted_iota(jnp.int32, (images, 1), 0) == z, lengths, 0),
        axis=0,
        keepdims=True,
    )

    def norm_back(grad, normed, inv, gain):
        scaled = grad * gain
        inner = (
            scaled
            - jnp.mean(scaled, axis=-1, keepdims=True)
            - normed * jnp.mean(scaled * normed, axis=-1, keepdims=True)
        )
        return inner * inv

    def second_back(c):
        sent2[c][1]()

        sums = [0.0, 0.0, 0.0, 0.0]
        for at in range(0, sizes_of[c], ROWS):
            here = pl.ds(pl.multiple_of(bases[c] + z * sizes_of[c] + at, ROWS), ROWS)
            grad = arrived(part2, recv2, c, at, ROWS)
            normed, inv = norm_parts(first[here, :])
            rows_grad = gdown[here, :].astype(F32)
            value = rows_grad + norm_back(grad, normed, inv, vx[3:4, :])
            there = slice(starts[c] + at, starts[c] + at + ROWS)
            gfirst[there, :] = value
            gown[there, :] = value.astype(BF16)
            terms = (value, grad * normed, grad, rows_grad)
            sums = [old + jnp.sum(term, axis=0, keepdims=True) for old, term in zip(sums, terms)]
        for line, value in enumerate(sums):
            gv[2 + line : 3 + line, :] += value

        def mixed_back(step, carry):
            at = lane_at(step, wide)
            weight = g_wot[:, :, :, at].reshape(width, wide)
            gm[slot_part(c), at] = nn(gown[slot_part(c), :], weight).astype(BF16)
            return carry

        steps(n_t, mixed_back)
        place_at = pl.ds(pl.multiple_of(ctx * slots + starts[c], ROWS), sizes_of[c])
        sent = [
            send(
                gm.at[slot_part(c), lane_at(flip(z, k), wide)],
                do.at[z, place_at, :],
                zpeer(k),
            )
            for k in reversed(zs)
        ]
        do[z, place_at, :] = gm[slot_part(c), lane_at(z, wide)]
        return sent

    to_heads = [second_back(0)]
    sents[0][0]()
    to_heads.append(second_back(1))
    sents[1][0]()

    per = width // LANES

    def pack(ref, row, value):
        for i in range(value.shape[1] // LANES):
            ref[row + i : row + i + 1, :] = value[:, i * LANES : (i + 1) * LANES]

    def unpack(ref, row, size):
        return jnp.concatenate([ref[row + i : row + i + 1, :] for i in range(size // LANES)], axis=1)

    for line in range(4):
        pack(early, line * per, gv[2 + line : 3 + line, :])
    pack(early, 4 * per, gv[8:9, 0:hidden])

    def vector_z(ref, recv, size):
        return [send(ref.at[0:size], recv.at[k - 1], zpeer(k)) for k in reversed(zs)]

    def vector_near(copies, ref, recv, size, near):
        for copy in copies:
            complete(copy)
        value = ref[0:size]
        for k in zs:
            value = value + recv[k - 1]
        ref[0:size] = value
        return send(ref, near, sib)

    def vector_far(copy, ref, near, recv):
        complete(copy)
        ref[...] = ref[...] + near[...]
        return [send(ref, recv.at[k - 1], plane(k)) for k in planes]

    def vector_last(copies, ref, recv):
        for copy in copies:
            complete(copy)
        value = ref[...]
        for k in planes:
            value = value + recv[k - 1]
        ref[...] = value

    vector_copies = vector_z(early, early_z, 4 * per)

    def out_grad(step, carry):
        at = lane_at(step, TILE)
        part = jnp.concatenate([mixed[rows_at(c, z), at] for c in range(2)], axis=0)
        out = tn(gown[...], part).astype(BF16)
        b_wot[:, :, :, at] = out.reshape(group, 2, piece, TILE)
        return carry

    steps(n_t * wide // TILE, out_grad)
    wot_near = grad_near(b_wot, s_wot)


    def block_rows(c):
        sents[c][1]()
        value = first[rows_at(c, z), :] + arrived(parts, recvs, c, 0, sizes_of[c]) + vx[5:6, :]
        value = jnp.where(own_live[slot_part(c)], value, 0.0)
        block_own[slot_part(c), :] = value.astype(BF16)
        passing = to_all(block_own, out_block, c)
        for at in pieces(c):
            passing[2](at)
        return passing

    def at_do(c):
        def at(index):
            first_row = index * slots + starts[c]
            return do.at[:, pl.ds(pl.multiple_of(first_row, ROWS), sizes_of[c]), :]

        return at

    tail = [block_rows(0)]
    do_started = []
    for c in range(2):
        for copy in to_heads[c]:
            copy.wait_recv()
        do_started.append(ctx_start(at_do(c)))

    for image in range(images):
        stacked = stack_heads(do[image, own, :])
        grad_probs = nt(stacked, qkv[image, :, 2 * wide : 3 * wide])
        weights = wq[image]
        along = jnp.sum(grad_probs * weights, axis=-1, keepdims=True)
        put_rows(alng, image, along)
        grad_scores = (weights * (grad_probs - along)).astype(BF16)
        out = pick_heads(nn(grad_scores, qkv[image, :, wide : 2 * wide])) * scale
        split_rows(dqkv, image, slice(0, wide), out.astype(BF16))

    def at_along(index):
        return alng.at[index]

    along_started = ctx_start(at_along)
    vector_copy = vector_near(vector_copies, early, early_z, 4 * per, early_sib)
    tail[0][0]()
    tail.append(block_rows(1))
    wot_grad_far = grad_halves(wot_near, b_wot, s_wot, t_wot, r_wot)
    early_far = vector_far(vector_copy, early, early_sib, early_plane)
    do_passed = [ctx_forward(do_started[c], at_do(c)) for c in range(2)]
    along_passed = ctx_forward(along_started, at_along)
    for c in range(2):
        ctx_finish(do_started[c], do_passed[c])
    ctx_finish(along_started, along_passed)

    for image in range(images):
        stacked = stack_heads(qkv[image, own, 2 * wide : 3 * wide])
        grad_probs = nt(stacked, do[image])
        weights = wk[image]
        lines = []
        for h in range(heads):
            line = image * heads + h
            level = alng[0, line : line + 1, :]
            for other in range(1, n_ctx):
                level = level + alng[other, line : line + 1, :]
            lines.append(grad_probs[h * slots : (h + 1) * slots] - level)
        grad_scores = (weights * jnp.concatenate(lines, axis=0)).astype(BF16)
        out = pick_heads(nn(grad_scores, qkv[image, :, 0:wide])) * scale
        split_rows(dqkv, image, slice(wide, 2 * wide), out.astype(BF16))
        out = pick_heads(nn(weights.astype(BF16), do[image]))
        split_rows(dqkv, image, slice(2 * wide, 3 * wide), out.astype(BF16))

    def in_back(c):
        at_rows = chunk(c)

        def one(step, carry):
            out = None
            for j in range(3):
                weight = g_win[j, pl.ds(step * some, some)].reshape(TILE, wide)
                term = nt(dqkv[at_rows, j * wide : (j + 1) * wide], weight)
                out = term if out is None else out + term
            part1[at_rows, lane_at(step, TILE)] = out.astype(BF16)
            return carry

        steps(width // TILE, one)
        return scatter(part1, recv1, relay1, c)

    sent1 = [in_back(c) for c in range(2)]
    for c in range(2):
        sent1[c][2]()
    sums = [0.0, 0.0]
    for row in range(0, rows, 2 * BLOCK):
        term = part1[row : row + 2 * BLOCK, :].astype(F32)
        weighted = term * n1[row : row + 2 * BLOCK, :]
        sums[0] = sums[0] + jnp.sum(weighted, axis=0, keepdims=True)
        sums[1] = sums[1] + jnp.sum(term, axis=0, keepdims=True)
    for line, value in enumerate(sums):
        pack(late, line * per, value)
    late[2 * per :, :] = jnp.zeros((late.shape[0] - 2 * per, LANES), F32)
    for j, start in enumerate((0, 2 * wide)):
        value = jnp.sum(dqkv[:, start : start + wide].astype(F32), axis=0, keepdims=True)
        pack(late, 2 * per + j * (wide // LANES), value)
    vector_copies = vector_z(late, late_z, 2 * per)
    tail[1][0]()
    wup_far = grad_halves(wup_near, b_wup, s_wup, t_wup, r_wup)
    wot_grad_far = grad_onward(wot_grad_far, t_wot, r_wot)

    for j in range(3):
        out = tn(h1[...], dqkv[:, j * wide : (j + 1) * wide]).astype(BF16)
        b_win[j] = out.reshape(group, 2, piece, wide)
    win_near = send(b_win.at[:, :, 1 - core], s_win, sib)
    sent1[0][0]()
    wup_far = grad_onward(wup_far, t_wup, r_wup)
    f_wdt[...] = turned(grad_sum(wdt_far, t_wdt, r_wdt), f_wdt)
    stays.append(local(f_wdt, out_wdt))
    win_near.wait_recv()
    for j in range(3):
        both = b_win[j, :, pl.ds(core, 1)].reshape(group, piece, wide).astype(F32)
        t_win[:, j] = (both + s_win[j].astype(F32)).astype(BF16)
    win_far = [send(t_win.at[flip(me, k)], r_win.at[k - 1], plane(k)) for k in reversed(planes)]

    sent1[1][0]()
    def first_back(c, at):
        sent1[c][1]((at,))
        normed, inv = norm_parts(tok[block_at(c, z, at), :].astype(F32))
        grad = arrived(part1, recv1, c, at, ROWS)
        there = slots_at(c, at)
        value = gfirst[there, :] + norm_back(grad, normed, inv, vx[0:1, :])
        tokens_own[there, :] = value.astype(BF16)
        tail[2 + c][2](at)

    tail += [to_all(tokens_own, out_tokens, c) for c in range(2)]
    for at in pieces(0):
        first_back(0, at)
    for at in pieces(1)[:-1]:
        first_back(1, at)
    tail[2][0]()
    first_back(1, pieces(1)[-1])
    whole_rows = grad_sum(wot_grad_far, t_wot, r_wot)
    o_wot[...] = whole_rows.astype(BF16)
    to_owner = [
        send(o_wot.at[:, lane_at(flip(z, k), wide)], z_wot.at[k - 1], zpeer(k))
        for k in reversed(zs)
    ]

    vector_copy = vector_near(vector_copies, late, late_z, 2 * per, late_sib)
    tail[3][0]()
    late_far = vector_far(vector_copy, late, late_sib, late_plane)
    f_wup[...] = grad_sum(wup_far, t_wup, r_wup)
    stays.append(local(f_wup, out_wup))
    vector_last(early_far, early, early_plane)
    f_win[...] = grad_sum(win_far, t_win, r_win)
    stays.append(local(f_win, out_win))
    for copy in to_owner:
        copy.wait_recv()
    value = o_wot[:, lane_at(z, wide)].astype(F32)
    for k in zs:
        value = value + z_wot[k - 1].astype(F32)
    f_wot[...] = turned(value, f_wot)
    stays.append(local(f_wot, out_wot))
    vector_last(late_far, late, late_plane)
    for line in range(2):
        gv[line : line + 1, :] = unpack(late, line * per, width)
        row = 2 * per + line * (wide // LANES)
        gv[9 + line : 10 + line, 0:wide] = unpack(late, row, wide)
    for line in range(4):
        gv[2 + line : 3 + line, :] = unpack(early, line * per, width)
    gv[8:9, 0:hidden] = unpack(early, 4 * per, hidden)
    stays.append(local(gv, out_vec))
    for passing in tail:
        passing[1]()
    for copy in pending:
        copy.wait_send()
    for flag, makes in guarded:

        @pl.when(flag)
        def _():
            for make in makes:
                make().wait_send()

    for copy in stays:
        copy.wait()


def finish_kernel(sizes, *refs):
    n_ctx, piece, cut, wide, hidden, width = sizes
    sources, results, held = refs[:6], refs[7:13], refs[21:27]
    smalls, own, vec, sems = refs[13:21], refs[27:35], refs[35], refs[36]
    shard = lax.axis_index("dp") * n_ctx + lax.axis_index("ctx")
    load = pltpu.make_async_copy(refs[6], vec, sems.at[2, 0])
    load.start()
    ins, outs = [], []
    for i in range(6):
        ins.append(pltpu.make_async_copy(sources[i], held[i], sems.at[0, i]))
        outs.append(pltpu.make_async_copy(held[i], results[i], sems.at[1, i]))
    for copy in ins:
        copy.start()

    def exact(left, right):
        parts, rest = [], left
        for _ in range(3):
            parts.append(rest.astype(BF16).astype(F32))
            rest = rest - parts[-1]
        count = left.shape[0]
        product = nn(jnp.concatenate(parts, axis=0).astype(BF16), right.astype(BF16))
        return product[0:count] + product[count : 2 * count] + product[2 * count :]

    heads = wide // HD
    lane = lax.broadcasted_iota(jnp.int32, (width, piece), 0)
    slot = lax.broadcasted_iota(jnp.int32, (width, piece), 1)
    one = jnp.where(lane - slot == shard * piece, 1.0, 0.0)
    lane = lax.broadcasted_iota(jnp.int32, (hidden, hidden // HD), 0)
    slot = lax.broadcasted_iota(jnp.int32, (hidden, hidden // HD), 1)
    by_unit = jnp.where(lane // HD == slot, 1.0, 0.0)
    load.wait()
    part = exact(vec[0:8, :], one)
    for line in range(6):
        own[line][...] = part[line : line + 1]
    channel = lax.broadcasted_iota(jnp.int32, (cut, hidden), 0)
    lane = lax.broadcasted_iota(jnp.int32, (cut, hidden), 1)
    chosen = jnp.where(lane % HD - channel == shard * cut, vec[8:9, 0:hidden], 0.0)
    own[6][...] = exact(chosen, by_unit)
    lane = lax.broadcasted_iota(jnp.int32, (wide, cut), 0)
    slot = lax.broadcasted_iota(jnp.int32, (wide, cut), 1)
    pick = jnp.where(lane % HD - slot == shard * cut, 1.0, 0.0)
    head = lax.broadcasted_iota(jnp.int32, (heads, wide), 0)
    lane = lax.broadcasted_iota(jnp.int32, (heads, wide), 1)
    for j in range(2):
        chosen = jnp.where(lane // HD == head, vec[9 + j : 10 + j, 0:wide], 0.0)
        own[7][j] = exact(chosen, pick)
    for i in range(8):
        outs.append(pltpu.make_async_copy(own[i], smalls[i], sems.at[2, 1 + i]))
        outs[-1].start()
    for i in range(6):
        ins[i].wait()
        outs[i].start()
    for copy in outs:
        copy.wait()


def on_device(
    mesh_shape,
    tokens,
    keep_mask,
    cotangent,
    first_gain,
    first_shift,
    attend_in,
    attend_bias,
    attend_out,
    out_bias,
    second_gain,
    second_shift,
    expand_in,
    expand_bias,
    contract_out,
    contract_bias,
):
    n_dp, n_ctx, n_t = mesh_shape
    images, slots, width = tokens.shape
    piece, _, wide = attend_in.shape
    hidden = expand_in.shape[1]
    cut = expand_bias.shape[1]
    rows = images * slots
    group = n_dp * n_ctx // 2
    total = slots * n_ctx
    heads = wide // HD
    turn = piece % LANES == 0
    per = width // LANES
    early_rows = 4 * per + hidden // LANES
    late_rows = 2 * per + 8 * ((2 * wide // LANES + 7) // 8)
    sizes = (n_dp, n_ctx, n_t, images, slots, width, wide, hidden, piece, cut)
    vmem = pl.BlockSpec(memory_space=pltpu.VMEM)
    hbm = pl.BlockSpec(memory_space=pl.ANY)
    scratch = [
        pltpu.VMEM((rows, width), BF16),
        pltpu.VMEM((rows, width), BF16),
        pltpu.VMEM((wide, piece), BF16),
        pltpu.VMEM((hidden, piece), BF16),
        pltpu.VMEM((2 * ROWS, LANES), F32),
        pltpu.VMEM((3, group, 2, piece, wide), BF16),
        pltpu.VMEM((group, 2, piece, n_t * wide), BF16),
        pltpu.VMEM((group, 2, piece, hidden), BF16),
        pltpu.VMEM((group, 2, piece, hidden), BF16),
        pltpu.VMEM((group, 2, 2 * ROWS, LANES), F32),
        pltpu.VMEM((ROWS, width), F32),
        pltpu.VMEM((rows, width), F32),
        pltpu.VMEM((rows, width), BF16),
        pltpu.VMEM((images, total, 3 * wide), BF16),
        pltpu.VMEM((images, heads * slots, total), F32),
        pltpu.VMEM((images, heads * slots, total), F32),
        pltpu.VMEM((n_ctx, images * heads, total), F32),
        pltpu.VMEM((n_ctx, images * heads, total), F32),
        pltpu.VMEM((rows, n_t * wide), BF16),
        pltpu.VMEM((rows, width), F32),
        pltpu.VMEM((rows, width), BF16),
        pltpu.VMEM((rows, hidden), F32),
        pltpu.VMEM((rows, hidden), BF16),
        pltpu.VMEM((rows, hidden), BF16),
        pltpu.VMEM((rows, width), BF16),
        pltpu.VMEM((rows, width), BF16),
        pltpu.VMEM((rows, width), BF16),
        pltpu.VMEM((2, slots, width), BF16),
        pltpu.VMEM((2, slots, width), BF16),
        pltpu.VMEM((2, slots, width), BF16),
        pltpu.VMEM((2, slots, width), BF16),
        pltpu.VMEM((2, slots, width), BF16),
        pltpu.VMEM((2, slots, width), BF16),
        pltpu.VMEM((slots, width), F32),
        pltpu.VMEM((rows, width), BF16),
        pltpu.VMEM((slots, width), BF16),
        pltpu.VMEM((slots, n_t * wide), BF16),
        pltpu.VMEM((images, total, wide), BF16),
        pltpu.VMEM((rows, 3 * wide), BF16),
        pltpu.VMEM((slots, width), BF16),
        pltpu.VMEM((slots, width), BF16),
        pltpu.VMEM((ROWS, width), F32),
        pltpu.VMEM((early_rows, LANES), F32),
        pltpu.VMEM((early_rows, LANES), F32),
        pltpu.VMEM((group - 1, early_rows, LANES), F32),
        pltpu.VMEM((n_t - 1, 4 * per, LANES), F32),
        pltpu.VMEM((late_rows, LANES), F32),
        pltpu.VMEM((late_rows, LANES), F32),
        pltpu.VMEM((group - 1, late_rows, LANES), F32),
        pltpu.VMEM((n_t - 1, 2 * per, LANES), F32),
        pltpu.VMEM((3, group, 2, piece, wide), BF16),
        pltpu.VMEM((group, 2, piece, n_t * wide), BF16),
        pltpu.VMEM((group, 2, piece, hidden), BF16),
        pltpu.VMEM((group, 2, piece, hidden), BF16),
        pltpu.VMEM((3, group, piece, wide), BF16),
        pltpu.VMEM((group, piece, n_t * wide), BF16),
        pltpu.VMEM((group, piece, hidden), BF16),
        pltpu.VMEM((group, piece, hidden), BF16),
        pltpu.VMEM((group, 3, piece, wide), BF16),
        pltpu.VMEM((group, piece, n_t * wide), BF16),
        pltpu.VMEM((group, piece, hidden), BF16),
        pltpu.VMEM((group, piece, hidden), BF16),
        pltpu.VMEM((group - 1, 3, piece, wide), BF16),
        pltpu.VMEM((group - 1, piece, n_t * wide), BF16),
        pltpu.VMEM((group - 1, piece, hidden), BF16),
        pltpu.VMEM((group - 1, piece, hidden), BF16),
        pltpu.VMEM((piece, n_t * wide), BF16),
        pltpu.VMEM((n_t - 1, piece, wide), BF16),
    ]
    shapes = (
        (3, piece, wide),
        (wide, piece) if turn else (piece, wide),
        (piece, hidden),
        (hidden, piece) if turn else (piece, hidden),
    )
    scratch += [pltpu.VMEM(shape, F32) for shape in shapes]
    copies = 260 + 20 * group
    scratch += [
        pltpu.SemaphoreType.DMA((copies,)),
        pltpu.SemaphoreType.DMA((copies,)),
        pltpu.SemaphoreType.DMA((48,)),
    ]
    results = [jax.ShapeDtypeStruct((rows, width), BF16)] * 2
    results += [jax.ShapeDtypeStruct(shape, F32) for shape in shapes]
    outs = pl.pallas_call(
        functools.partial(block_kernel, sizes),
        out_shape=(*results, jax.ShapeDtypeStruct((ROWS, width), F32)),
        in_specs=[hbm, hbm, vmem, hbm, hbm, hbm, hbm] + [vmem] * 8,
        out_specs=(hbm,) * 7,
        scratch_shapes=scratch,
        compiler_params=pltpu.CompilerParams(
            collective_id=0, has_side_effects=True, vmem_limit_bytes=63 << 20
        ),
    )(
        tokens.reshape(rows, width),
        cotangent.reshape(rows, width),
        keep_mask,
        jnp.transpose(attend_in, (1, 0, 2)),
        attend_out,
        expand_in,
        contract_out,
        *[
            v.reshape(1, piece)
            for v in (first_gain, first_shift, out_bias, second_gain, second_shift, contract_bias)
        ],
        expand_bias.T,
        attend_bias,
    )
    vector = jax.ShapeDtypeStruct((1, piece), F32)
    small = [vector] * 6 + [
        jax.ShapeDtypeStruct((cut, hidden // HD), F32),
        jax.ShapeDtypeStruct((2, heads, cut), F32),
    ]
    placed = pl.pallas_call(
        functools.partial(finish_kernel, (n_ctx, piece, cut, wide, hidden, width)),
        out_shape=(*results, *small),
        in_specs=[hbm] * 7,
        out_specs=(hbm,) * 14,
        scratch_shapes=[pltpu.VMEM(r.shape, r.dtype) for r in (*results, *small)]
        + [pltpu.VMEM((ROWS, width), F32), pltpu.SemaphoreType.DMA((3, 9))],
        compiler_params=pltpu.CompilerParams(vmem_limit_bytes=63 << 20),
    )(*outs)
    block_out, tokens_grad, d_win, d_wot, d_wup, d_wdt = placed[:6]
    vectors = [v.reshape(piece) for v in placed[6:12]]
    return (
        block_out.reshape(tokens.shape),
        tokens_grad.reshape(tokens.shape),
        vectors[0],
        vectors[1],
        jnp.transpose(d_win, (1, 0, 2)),
        placed[13],
        d_wot if turn else d_wot.T,
        vectors[2],
        vectors[3],
        vectors[4],
        d_wup,
        placed[12].T,
        d_wdt if turn else d_wdt.T,
        vectors[5],
    )


def solution(mesh):
    shape = (mesh.shape["dp"], mesh.shape["ctx"], mesh.shape["tensor"])
    vector = P(("dp", "ctx"))
    params = (
        vector,
        vector,
        P(("dp", "ctx"), None, "tensor"),
        P(None, "tensor", ("dp", "ctx")),
        P("tensor", ("dp", "ctx")),
        vector,
        vector,
        vector,
        P(("dp", "ctx"), "tensor"),
        P("tensor", ("dp", "ctx")),
        P("tensor", ("dp", "ctx")),
        vector,
    )
    rows = P("dp", "ctx", None)
    return jax.shard_map(
        functools.partial(on_device, shape),
        mesh=mesh,
        in_specs=(rows, P("dp", None), rows, *params),
        out_specs=(rows, rows, *params),
        check_vma=False,
    )
```

```python
import functools

import jax
import jax.numpy as jnp
from jax import lax
from jax.experimental import pallas as pl
from jax.experimental.pallas import tpu as pltpu
from jax.sharding import PartitionSpec as P

HD = 64
BUFFER = 64
LANES = 128
ROWS = 16
TILE = 256
BLOCK = 32
MESH = pl.DeviceIdType.MESH
F32 = jnp.float32
BF16 = jnp.bfloat16

eps = 1e-06
neg_big = -1e30
root_half = 0.7071067811865476
inv_root_two_pi = 0.3989422804014327


def flip(index, bits):
    out, bit = index, 1
    while bit <= bits:
        if bits & bit:
            out = out + bit - 2 * bit * lax.rem(lax.div(index, bit), 2)
        bit *= 2
    return out


def nn(left, right):
    return jnp.dot(left, right, preferred_element_type=F32)


def nt(left, right):
    return lax.dot_general(left, right, (((1,), (1,)), ((), ())), preferred_element_type=F32)


def tn(left, right):
    return lax.dot_general(left, right, (((0,), (0,)), ((), ())), preferred_element_type=F32)


def steps(count, body):
    if count > 8:
        lax.fori_loop(0, count, body, 0)
        return
    for step in range(count):
        body(step, 0)


def turned(value, ref):
    return value if value.shape == ref.shape else value.T


def norm_parts(values):
    mean = jnp.mean(values, axis=-1, keepdims=True)
    centered = values - mean
    spread = jnp.mean(centered * centered, axis=-1, keepdims=True)
    inv = lax.rsqrt(spread + eps)
    return centered * inv, inv


def block_kernel(
    sizes,
    tok_in,
    cot_in,
    keep,
    win,
    attend_out,
    wup,
    contract_out,
    first_gain,
    first_shift,
    out_bias,
    second_gain,
    second_shift,
    contract_bias,
    expand_bias,
    attend_bias,
    out_block,
    out_tokens,
    out_win,
    out_wot,
    out_wup,
    out_wdt,
    out_vec,
    tok,
    cot,
    a_out,
    c_out,
    vec,
    g_win,
    g_wot,
    g_wup,
    g_wdt,
    g_vec,
    vx,
    n1,
    h1,
    qkv,
    wq,
    wk,
    stat,
    alng,
    mixed,
    first,
    h2,
    ga,
    act,
    gi,
    part2,
    parts,
    part1,
    recv2,
    relay2,
    recvs,
    relays,
    recv1,
    relay1,
    gfirst,
    gdown,
    gown,
    gm,
    do,
    dqkv,
    block_own,
    tokens_own,
    gv,
    early,
    early_sib,
    early_plane,
    early_z,
    late,
    late_sib,
    late_plane,
    late_z,
    b_win,
    b_wot,
    b_wup,
    b_wdt,
    s_win,
    s_wot,
    s_wup,
    s_wdt,
    t_win,
    t_wot,
    t_wup,
    t_wdt,
    r_win,
    r_wot,
    r_wup,
    r_wdt,
    o_wot,
    z_wot,
    f_win,
    f_wot,
    f_wup,
    f_wdt,
    send_sem,
    recv_sem,
    local_sem,
):
    n_dp, n_ctx, n_t, images, slots, width, wide, hidden, piece, cut = sizes
    rows = images * slots
    total = slots * n_ctx
    heads = wide // HD
    half = n_ctx // 2
    group = n_dp * half
    scale = HD ** (-0.5)
    dp = lax.axis_index("dp")
    ctx = lax.axis_index("ctx")
    z = lax.axis_index("tensor")
    high, core = lax.div(ctx, 2), lax.rem(ctx, 2)
    me = dp * half + high
    shard = me * 2 + core
    sib = (dp, flip(ctx, 1), z)

    def plane(k):
        other = flip(me, k)
        return (lax.div(other, half), lax.rem(other, half) * 2 + core, z)

    def ctx_at(k):
        return flip(high, k) * 2 + core

    def zpeer(k):
        return (dp, ctx, flip(z, k))

    def slot_at(index):
        return pl.ds(pl.multiple_of(index * slots, ROWS), slots)

    def lane_at(index, size):
        return pl.ds(pl.multiple_of(index * size, size), size)

    own = slot_at(ctx)
    mine = slot_at(z)

    cut_at = ROWS * (slots // ROWS // 2)
    starts = (0, cut_at)
    sizes_of = (cut_at, slots - cut_at)
    bases = (0, images * cut_at)

    def chunk(c):
        return slice(bases[c], bases[c] + images * sizes_of[c])

    def rows_at(c, image):
        first_row = bases[c] + image * sizes_of[c]
        return pl.ds(pl.multiple_of(first_row, ROWS), sizes_of[c])

    def slot_part(c):
        return slice(starts[c], starts[c] + sizes_of[c])

    def split_rows(ref, image, lanes, value):
        for c in range(2):
            ref[rows_at(c, image), lanes] = value[slot_part(c)]

    count = [0, 0]
    stays = []
    pending = []

    def send(src, dst, device):
        index = count[0]
        count[0] += 1
        copy = pltpu.make_async_remote_copy(
            src_ref=src,
            dst_ref=dst,
            send_sem=send_sem.at[index],
            recv_sem=recv_sem.at[index],
            device_id=device,
            device_id_type=MESH,
        )
        copy.start()
        pending.append(copy)
        return copy

    inside = lax.rem(z - lax.div(z, 2), 2) == 1
    at_end = lax.rem(z - lax.div(z, 2), 2) == 0
    guarded = []

    def fresh():
        count[0] += 1
        return count[0] - 1

    def remote(src, dst, device, out_index, in_index):
        return pltpu.make_async_remote_copy(
            src_ref=src,
            dst_ref=dst,
            send_sem=send_sem.at[out_index],
            recv_sem=recv_sem.at[in_index],
            device_id=device,
            device_id_type=MESH,
        )

    def send_if(flag, makes):
        guarded.append((flag, makes))

        @pl.when(flag)
        def _():
            for make in makes:
                make().start()

    def complete(copy):
        pending[:] = [other for other in pending if other is not copy]
        copy.wait()

    def local(src, dst):
        index = count[1]
        count[1] += 1
        copy = pltpu.make_async_copy(src, dst, local_sem.at[index])
        copy.start()
        return copy

    planes = range(1, group)
    zs = range(1, n_t)

    def at_win_kv(m, c):
        return g_win.at[1:3, m, c]

    def at_win_q(m, c):
        return g_win.at[0:1, m, c]

    def at_wot(m, c):
        return g_wot.at[m, c, :, lane_at(z, wide)]

    def at_wup(m, c):
        return g_wup.at[m, c]

    def at_wdt(m, c):
        return g_wdt.at[m, c]

    def at_vec(m, c):
        return g_vec.at[m, c]

    barrier = pltpu.get_barrier_semaphore()
    for device in [plane(k) for k in planes] + [sib] + [zpeer(k) for k in zs]:
        pl.semaphore_signal(barrier, inc=1, device_id=device, device_id_type=MESH)
    a_out_load = local(attend_out, a_out)
    def load_rows(source, ref):
        return [
            local(
                source.at[image * slots + starts[c] : image * slots + starts[c] + sizes_of[c], :],
                ref.at[rows_at(c, image), :],
            )
            for c in range(2)
            for image in range(images)
        ]

    tok_load = load_rows(tok_in, tok)
    win_own = local(win, g_win.at[:, me, core])
    c_out_load = local(contract_out, c_out)
    cot_load = load_rows(cot_in, cot)
    wup_own = local(wup, at_wup(me, core))

    vec[...] = jnp.zeros_like(vec)
    for line, ref in enumerate(
        (first_gain, first_shift, out_bias, second_gain, second_shift, contract_bias)
    ):
        vec[line : line + 1, 0:piece] = ref[...].astype(F32)
    vec[8 : 8 + cut, 0 : hidden // HD] = expand_bias[...].astype(F32)
    for j in range(2):
        vec[16 + j * heads : 16 + (j + 1) * heads, 0:cut] = attend_bias[j].astype(F32)
    g_vec[me, core] = vec[...]
    gv[...] = jnp.zeros_like(gv)
    unit_one = (
        lax.broadcasted_iota(jnp.int32, (piece, piece), 0)
        == lax.broadcasted_iota(jnp.int32, (piece, piece), 1)
    ).astype(F32)
    unit_one = unit_one.astype(BF16)
    a_out_load.wait()
    g_wot[me, core, :, lane_at(z, wide)] = nt(unit_one, a_out[...]).astype(BF16)
    pl.semaphore_wait(barrier, group + n_t - 1)

    def gather_start(src, at):
        far = [send(src, at(me, core), plane(k)) for k in planes]
        return far, send(src, at(me, core), sib)

    def gather_forward(started, at):
        out = []
        for k in planes:
            started[0][k - 1].wait_recv()
            there = at(flip(me, k), core)
            out.append(send(there, there, sib))
        return out

    def gather_finish(started, passed):
        started[1].wait_recv()
        for copy in passed:
            copy.wait_recv()

    relayed = group == 4 and piece % (2 * ROWS) == 0

    def relay_start(src, at):
        if not relayed:
            return gather_start(src, at)
        far = [send(src, at(me, core), plane(k)) for k in (1, 2)]
        return far, send(src, at(me, core), sib)

    def relay_forward(started, at):
        if not relayed:
            return gather_forward(started, at), []
        out, halves = [], []
        for k in (1, 2):
            started[0][k - 1].wait_recv()
            there = at(flip(me, k), core)
            part = there.at[pl.ds((k - 1) * (piece // 2), piece // 2)]
            halves.append(send(part, part, plane(3 - k)))
            out.append(send(there, there, sib))
        return out, halves

    def relay_last(halves, at):
        if not halves:
            return []
        for copy in halves:
            copy.wait_recv()
        there = at(flip(me, 3), core)
        return [send(there, there, sib)]

    def ctx_start(at):
        far = [send(at(ctx), at(ctx), (dp, ctx_at(k), z)) for k in range(1, half)]
        return far, send(at(ctx), at(ctx), sib)

    def ctx_forward(started, at):
        out = []
        for k in range(1, half):
            started[0][k - 1].wait_recv()
            out.append(send(at(ctx_at(k)), at(ctx_at(k)), sib))
        return out

    def ctx_finish(started, passed):
        started[1].wait_recv()
        for copy in passed:
            copy.wait_recv()

    def wot_piece(m, index):
        return g_wot.at[m, core, :, lane_at(index, wide)]

    vec_started = gather_start(vec, at_vec)
    wot_own = at_wot(me, core)
    wot_far = [send(wot_own, wot_own, plane(k)) for k in planes if k < 3]
    kv_win_started = gather_start(win.at[1:3], at_win_kv)
    wot_far += [send(wot_own, wot_own, plane(k)) for k in planes if k >= 3]
    wot_started = (wot_far, send(wot_own, wot_own, sib))
    q_win_started = gather_start(win.at[0:1], at_win_q)
    wot_z = [[send(wot_piece(me, z), wot_piece(me, z), zpeer(k)) for k in zs]]

    for copy in tok_load:
        copy.wait()

    def first_norm(step, carry):
        at = pl.ds(pl.multiple_of(step * BLOCK, BLOCK), BLOCK)
        normed, _ = norm_parts(tok[at, :].astype(F32))
        n1[at, :] = normed
        return carry

    lax.fori_loop(0, rows // BLOCK, first_norm, 0)

    vec_passed = gather_forward(vec_started, at_vec)
    gather_finish(vec_started, vec_passed)
    shape = (2 * ROWS, width)
    line_id = lax.broadcasted_iota(jnp.int32, shape, 0)
    lane_id = lax.broadcasted_iota(jnp.int32, shape, 1)
    source = lax.broadcasted_iota(jnp.int32, (LANES, width), 0)
    target = lax.broadcasted_iota(jnp.int32, (LANES, width), 1)
    by_unit = jnp.where(target // HD == source, 1.0, 0.0).astype(BF16)
    for_unit = lane_id % HD - (line_id - 8)
    for_head = lane_id // HD == (line_id - 16) % heads

    def place(index, carry):
        one, two, three = carry
        shares = g_vec[lax.div(index, 2), lax.rem(index, 2)].astype(BF16)
        by_width = jnp.where(target - source == index * piece, 1.0, 0.0).astype(BF16)
        by_channel = jnp.where(target % HD - source == index * cut, 1.0, 0.0).astype(BF16)
        one = one + nn(shares, by_width)
        two = two + jnp.where(for_unit == index * cut, nn(shares, by_unit), 0.0)
        three = three + jnp.where(for_head, nn(shares, by_channel), 0.0)
        return one, two, three

    zero = jnp.zeros(shape, F32)
    one, two, three = lax.fori_loop(0, 2 * group, place, (zero, zero, zero))
    vx[0:8, :] = one[0:8]
    vx[8:9, :] = jnp.sum(two[8 : 8 + cut], axis=0, keepdims=True)
    vx[9:10, :] = jnp.sum(three[16 : 16 + heads], axis=0, keepdims=True)
    vx[10:11, :] = jnp.sum(three[16 + heads : 16 + 2 * heads], axis=0, keepdims=True)

    def first_hidden(step, carry):
        at = pl.ds(pl.multiple_of(step * BLOCK, BLOCK), BLOCK)
        h1[at, :] = (n1[at, :] * vx[0:1, :] + vx[1:2, :]).astype(BF16)
        return carry

    lax.fori_loop(0, rows // BLOCK, first_hidden, 0)

    wot_passed = []

    def wot_onward(k):
        wot_started[0][k - 1].wait_recv()
        there = wot_piece(flip(me, k), z)
        wot_z.append([send(there, there, zpeer(j)) for j in reversed(zs)][::-1])
        wot_passed.append(send(there, there, sib))

    for k in planes:
        if k < 3:
            wot_onward(k)

    c_out_load.wait()

    def turn(step, carry):
        at = lane_at(step, TILE)
        g_wdt[me, core, :, at] = nt(unit_one, c_out[at, :]).astype(BF16)
        return carry

    steps(hidden // TILE, turn)

    lengths = BUFFER + jnp.sum(keep[...], axis=1, keepdims=True)
    slot_id = lax.broadcasted_iota(jnp.int32, (slots, 1), 0) + ctx * slots
    key_id = lax.broadcasted_iota(jnp.int32, (1, total), 1)
    head_of = lax.broadcasted_iota(jnp.int32, (slots, wide), 1) // HD
    spot = lax.broadcasted_iota(jnp.int32, (slots, total), 1) == slot_id

    def stack_heads(block):
        wider = block.astype(F32)
        return jnp.concatenate(
            [jnp.where(head_of == h, wider, 0.0).astype(BF16) for h in range(heads)], axis=0
        )

    def pick_heads(block):
        out = jnp.where(head_of == 0, block[0:slots], 0.0)
        for h in range(1, heads):
            out = jnp.where(head_of == h, block[h * slots : (h + 1) * slots], out)
        return out

    def put_rows(ref, image, column):
        for h in range(heads):
            part = jnp.where(spot, column[h * slots : (h + 1) * slots], 0.0)
            line = image * heads + h
            ref[ctx, line : line + 1, :] = jnp.sum(part, axis=0, keepdims=True)

    win_passed = gather_forward(kv_win_started, at_win_kv)
    win_own.wait()
    gather_finish(kv_win_started, win_passed)

    def project(j, bias):
        out = nn(h1[...], g_win[j].reshape(width, wide))
        if bias is not None:
            out = out + vx[bias : bias + 1, 0:wide]
        out = out.astype(BF16)
        for c in range(2):
            place_at = pl.ds(pl.multiple_of(ctx * slots + starts[c], ROWS), sizes_of[c])
            block = out[chunk(c)].reshape(images, sizes_of[c], wide)
            qkv[:, place_at, j * wide : (j + 1) * wide] = block

    def at_kv(images_of):
        def at(index):
            return qkv.at[images_of, slot_at(index), wide : 3 * wide]

        return at

    def at_q(index):
        return qkv.at[:, slot_at(index), 0:wide]

    project(1, None)
    project(2, 10)
    middle = images // 2
    image_parts = (slice(0, middle), slice(middle, images))
    kv_started = [ctx_start(at_kv(part)) for part in image_parts]
    wup_started = relay_start(wup, at_wup)
    wdt_started = relay_start(at_wdt(me, core), at_wdt)
    for k in planes:
        if k >= 3:
            wot_onward(k)
    win_passed = gather_forward(q_win_started, at_win_q)
    gather_finish(q_win_started, win_passed)
    project(0, 9)

    def at_mixed(index, c, part):
        first_row = bases[c] + part.start * sizes_of[c]
        last_row = bases[c] + part.stop * sizes_of[c]
        return mixed.at[first_row:last_row, lane_at(index, wide)]

    mixed_sent = [[], []]
    for image in range(images):
        for part in range(2):
            if image == image_parts[part].start:
                kv_at = at_kv(image_parts[part])
                kv_passed = ctx_forward(kv_started[part], kv_at)
                ctx_finish(kv_started[part], kv_passed)
        key_live = key_id < lengths[image : image + 1, :]
        stacked = stack_heads(qkv[image, own, 0:wide])
        scores = nt(stacked, qkv[image, :, wide : 2 * wide]) * scale
        scores = jnp.where(key_live, scores, neg_big)
        top = jnp.max(scores, axis=-1, keepdims=True)
        expo = jnp.exp(scores - top)
        whole = jnp.sum(expo, axis=-1, keepdims=True)
        probs = expo / whole
        wq[image] = probs
        put_rows(stat, image, top + jnp.log(whole))
        out = nn(probs.astype(BF16), qkv[image, :, 2 * wide : 3 * wide])
        split_rows(mixed, image, lane_at(z, wide), pick_heads(out).astype(BF16))
        for part in image_parts:
            if image == part.stop - 1:
                for c in range(2):
                    there = at_mixed(z, c, part)
                    mixed_sent[c] += [send(there, there, zpeer(k)) for k in reversed(zs)]

    def at_stat(index):
        return stat.at[index]

    for copy in cot_load:
        copy.wait()
    row_live = []
    for image in range(images):
        row_live.append(slot_id < lengths[image : image + 1, :])
        for c in range(2):
            at = rows_at(c, image)
            live = row_live[image][slot_part(c)]
            gdown[at, :] = jnp.where(live, cot[at, :].astype(F32), 0.0).astype(BF16)

    wup_passed, wup_halves = relay_forward(wup_started, at_wup)
    gather_finish(wot_started, wot_passed)
    wot_more = []
    for order, block in enumerate(wot_z):
        for k in zs:
            block[k - 1].wait_recv()
            there = wot_piece(flip(me, order), flip(z, k))
            wot_more.append(send(there, there, sib))
    wup_own.wait()
    wdt_passed, wdt_halves = relay_forward(wdt_started, at_wdt)
    q_started = ctx_start(at_q)
    stat_started = ctx_start(at_stat)
    wup_passed += relay_last(wup_halves, at_wup)
    for copy in wot_more:
        copy.wait_recv()

    some = group // (width // TILE)

    def pieces(c):
        return range(0, sizes_of[c], ROWS)

    def block_at(c, index, at):
        first_row = bases[c] + index * sizes_of[c] + at
        return pl.ds(pl.multiple_of(first_row, ROWS), ROWS)

    def slots_at(c, at):
        return slice(starts[c] + at, starts[c] + at + ROWS)

    def scatter(part, recv, relay, c):
        marks = {at: [fresh() for _ in range(4)] for at in pieces(c)}

        def onward(j, at):
            return remote(
                part.at[block_at(c, flip(z, 3 - j), at), :],
                relay.at[j, slots_at(c, at), :],
                zpeer(1),
                marks[at][j],
                marks[at][j],
            )

        def passed(j, at):
            return remote(
                relay.at[j, slots_at(c, at), :],
                recv.at[1, slots_at(c, at), :],
                zpeer(2 + j),
                marks[at][2 + j],
                marks[at][2],
            )

        both = [(at, j) for at in pieces(c) for j in range(2)]
        send_if(at_end, [functools.partial(onward, j, at) for at, j in both])
        near = []

        def send_near():
            source = part.at[rows_at(c, flip(z, 1)), :]
            near.append(send(source, recv.at[0, slot_part(c), :], zpeer(1)))

        def pass_on():
            guarded.append((inside, [functools.partial(passed, j, at) for at, j in both]))

            @pl.when(inside)
            def _():
                for at, j in both:
                    onward(j, at).wait_recv()
                    value = part[block_at(c, flip(z, 2 + j), at), :].astype(F32)
                    value = value + relay[j, slots_at(c, at), :].astype(F32)
                    relay[j, slots_at(c, at), :] = value.astype(BF16)
                    passed(j, at).start()

        def finish(some_pieces=None):
            if some_pieces is None or 0 in some_pieces:
                near[0].wait_recv()
            for at in some_pieces or pieces(c):
                passed(0, at).wait_recv()

        return pass_on, finish, send_near

    def to_all(source, target, c):
        marks = {at: [fresh() for _ in range(4)] for at in pieces(c)}

        def piece_of(index, at):
            first_row = index * slots + starts[c] + at
            return target.at[pl.ds(pl.multiple_of(first_row, ROWS), ROWS), :]

        def far(k, at):
            mark = marks[at][k - 2]
            return remote(source.at[slots_at(c, at), :], piece_of(z, at), zpeer(k), mark, mark)

        def passed(k, at):
            there = piece_of(flip(z, k), at)
            return remote(there, there, zpeer(1), marks[at][k], marks[at][3 - k])

        nears = []

        def start(at):
            own_part = source.at[slots_at(c, at), :]
            send_if(at_end, [functools.partial(far, 2, at)])
            send_if(inside, [functools.partial(far, 3, at)])
            nears.append(send(own_part, piece_of(z, at), zpeer(1)))
            stays.append(local(own_part, piece_of(z, at)))

        both = [(k, at) for at in pieces(c) for k in (3, 2)]

        def pass_on():
            guarded.append((inside, [functools.partial(passed, k, at) for k, at in both]))

            @pl.when(inside)
            def _():
                for k, at in both:
                    far(k, at).wait_recv()
                    passed(k, at).start()

        def finish():
            for copy in nears:
                copy.wait_recv()

            @pl.when(at_end)
            def _():
                for k, at in both:
                    far(k, at).wait_recv()

        return pass_on, finish, start

    def arrived(part, recv, c, at, size):
        here = pl.ds(pl.multiple_of(bases[c] + z * sizes_of[c] + at, ROWS), size)
        there = pl.ds(pl.multiple_of(starts[c] + at, ROWS), size)
        out = part[here, :].astype(F32)
        for j in range(2):
            out = out + recv[j, there, :].astype(F32)
        return out

    def attended(c):
        at_rows = chunk(c)
        for copy in mixed_sent[c]:
            copy.wait_recv()

        def project_out(step, carry):
            weight = g_wot[pl.ds(step * some, some)].reshape(TILE, n_t * wide)
            first[at_rows, lane_at(step, TILE)] = nt(mixed[at_rows, :], weight)
            return carry

        steps(width // TILE, project_out)

        for row in range(bases[c], bases[c] + images * sizes_of[c], ROWS):
            at = slice(row, row + ROWS)
            value = tok[at, :].astype(F32) + first[at, :] + vx[2:3, :]
            first[at, :] = value
            normed, _ = norm_parts(value)
            h2[at, :] = (normed * vx[3:4, :] + vx[4:5, :]).astype(BF16)

    def feed_forward(c):
        at_rows = chunk(c)

        def expand(step, carry):
            at = lane_at(step, TILE)
            weight = g_wup[:, :, :, at].reshape(width, TILE)
            inner = nn(h2[at_rows, :], weight) + vx[8:9, at]
            share = 0.5 * (1.0 + lax.erf(inner * root_half))
            act[at_rows, at] = (inner * share).astype(BF16)
            slope = share + inner * jnp.exp(-0.5 * inner * inner) * inv_root_two_pi
            grad = (ga[at_rows, at] * slope).astype(BF16)
            gi[at_rows, at] = grad
            gv[8:9, at] += jnp.sum(grad.astype(F32), axis=0, keepdims=True)
            return carry

        steps(hidden // TILE, expand)

        def up_back(step, carry):
            weight = g_wup[pl.ds(step * some, some)].reshape(TILE, hidden)
            part2[at_rows, lane_at(step, TILE)] = nt(gi[at_rows, :], weight).astype(BF16)
            return carry

        steps(width // TILE, up_back)
        return scatter(part2, recv2, relay2, c)

    attended(0)
    wdt_passed += relay_last(wdt_halves, at_wdt)
    gather_finish(wup_started, wup_passed)
    gather_finish(wdt_started, wdt_passed)

    def down_back(c):
        at_rows = chunk(c)

        def one(step, carry):
            at = lane_at(step, TILE)
            weight = g_wdt[:, :, :, at].reshape(width, TILE)
            ga[at_rows, at] = nn(gdown[at_rows, :], weight)
            return carry

        steps(hidden // TILE, one)

    down_back(0)
    sent2 = [feed_forward(0)]
    sent2[0][2]()
    down_back(1)
    attended(1)
    sent2.append(feed_forward(1))
    sent2[1][2]()
    sent2[0][0]()

    def contract(step, carry):
        weight = g_wdt[pl.ds(step * some, some)].reshape(TILE, hidden)
        parts[:, lane_at(step, TILE)] = nt(act[...], weight).astype(BF16)
        return carry

    steps(width // TILE, contract)
    sents = []
    for c in range(2):
        sents.append(scatter(parts, recvs, relays, c))
        sents[c][2]()

    def wide_grad(buf, left, right, lanes):
        def one(step, carry):
            at = lane_at(step, TILE)
            out = tn(left[...], right[:, at]).astype(BF16)
            buf[:, :, :, at] = out.reshape(group, 2, piece, TILE)
            return carry

        steps(lanes // TILE, one)

    def grad_near(buf, near):
        return send(buf.at[:, 1 - core], near, sib)

    def grad_far(copy, buf, near, both, recv):
        copy.wait_recv()

        def one(m, carry):
            both[m] = (buf[m, core].astype(F32) + near[m].astype(F32)).astype(BF16)
            return carry

        steps(group, one)
        return [send(both.at[flip(me, k)], recv.at[k - 1], plane(k)) for k in reversed(planes)]

    def grad_halves(copy, buf, near, both, recv):
        if not relayed:
            return grad_far(copy, buf, near, both, recv)
        copy.wait_recv()

        def one(m, carry):
            both[m] = (buf[m, core].astype(F32) + near[m].astype(F32)).astype(BF16)
            return carry

        steps(group, one)
        part = piece // 2
        corner = flip(me, 3)
        return [
            send(both.at[corner, 0:part], recv.at[2, 0:part], plane(1)),
            send(both.at[corner, part:piece], recv.at[2, part:piece], plane(2)),
        ]

    def grad_onward(copies, both, recv):
        if not relayed:
            return copies
        part = piece // 2
        for k, at in ((2, slice(0, part)), (1, slice(part, piece))):
            copies[2 - k].wait_recv()
            other = flip(me, k)
            value = both[other, at].astype(F32) + recv[2, at].astype(F32)
            both[other, at] = value.astype(BF16)
        return [send(both.at[flip(me, k)], recv.at[k - 1], plane(k)) for k in (1, 2)]

    def grad_sum(copies, both, recv):
        for copy in copies:
            copy.wait_recv()
        value = both[me].astype(F32)
        for k in range(len(copies)):
            value = value + recv[k].astype(F32)
        return value

    wide_grad(b_wdt, gdown, act, hidden)
    wdt_near = grad_near(b_wdt, s_wdt)
    sent2[1][0]()
    wide_grad(b_wup, h2, gi, hidden)
    wup_near = grad_near(b_wup, s_wup)
    wdt_far = grad_far(wdt_near, b_wdt, s_wdt, t_wdt, r_wdt)

    own_live = slot_id < jnp.sum(
        jnp.where(lax.broadcasted_iota(jnp.int32, (images, 1), 0) == z, lengths, 0),
        axis=0,
        keepdims=True,
    )

    def norm_back(grad, normed, inv, gain):
        scaled = grad * gain
        inner = (
            scaled
            - jnp.mean(scaled, axis=-1, keepdims=True)
            - normed * jnp.mean(scaled * normed, axis=-1, keepdims=True)
        )
        return inner * inv

    def second_back(c):
        sent2[c][1]()

        sums = [0.0, 0.0, 0.0, 0.0]
        for at in range(0, sizes_of[c], ROWS):
            here = pl.ds(pl.multiple_of(bases[c] + z * sizes_of[c] + at, ROWS), ROWS)
            grad = arrived(part2, recv2, c, at, ROWS)
            normed, inv = norm_parts(first[here, :])
            rows_grad = gdown[here, :].astype(F32)
            value = rows_grad + norm_back(grad, normed, inv, vx[3:4, :])
            there = slice(starts[c] + at, starts[c] + at + ROWS)
            gfirst[there, :] = value
            gown[there, :] = value.astype(BF16)
            terms = (value, grad * normed, grad, rows_grad)
            sums = [old + jnp.sum(term, axis=0, keepdims=True) for old, term in zip(sums, terms)]
        for line, value in enumerate(sums):
            gv[2 + line : 3 + line, :] += value

        def mixed_back(step, carry):
            at = lane_at(step, wide)
            weight = g_wot[:, :, :, at].reshape(width, wide)
            gm[slot_part(c), at] = nn(gown[slot_part(c), :], weight).astype(BF16)
            return carry

        steps(n_t, mixed_back)
        place_at = pl.ds(pl.multiple_of(ctx * slots + starts[c], ROWS), sizes_of[c])
        sent = [
            send(
                gm.at[slot_part(c), lane_at(flip(z, k), wide)],
                do.at[z, place_at, :],
                zpeer(k),
            )
            for k in reversed(zs)
        ]
        do[z, place_at, :] = gm[slot_part(c), lane_at(z, wide)]
        return sent

    to_heads = [second_back(0)]
    sents[0][0]()
    to_heads.append(second_back(1))
    sents[1][0]()

    per = width // LANES

    def pack(ref, row, value):
        for i in range(value.shape[1] // LANES):
            ref[row + i : row + i + 1, :] = value[:, i * LANES : (i + 1) * LANES]

    def unpack(ref, row, size):
        return jnp.concatenate([ref[row + i : row + i + 1, :] for i in range(size // LANES)], axis=1)

    for line in range(4):
        pack(early, line * per, gv[2 + line : 3 + line, :])
    pack(early, 4 * per, gv[8:9, 0:hidden])

    def vector_z(ref, recv, size):
        return [send(ref.at[0:size], recv.at[k - 1], zpeer(k)) for k in reversed(zs)]

    def vector_near(copies, ref, recv, size, near):
        for copy in copies:
            complete(copy)
        value = ref[0:size]
        for k in zs:
            value = value + recv[k - 1]
        ref[0:size] = value
        return send(ref, near, sib)

    def vector_far(copy, ref, near, recv):
        complete(copy)
        ref[...] = ref[...] + near[...]
        return [send(ref, recv.at[k - 1], plane(k)) for k in planes]

    def vector_last(copies, ref, recv):
        for copy in copies:
            complete(copy)
        value = ref[...]
        for k in planes:
            value = value + recv[k - 1]
        ref[...] = value

    vector_copies = vector_z(early, early_z, 4 * per)

    def out_grad(step, carry):
        at = lane_at(step, TILE)
        part = jnp.concatenate([mixed[rows_at(c, z), at] for c in range(2)], axis=0)
        out = tn(gown[...], part).astype(BF16)
        b_wot[:, :, :, at] = out.reshape(group, 2, piece, TILE)
        return carry

    steps(n_t * wide // TILE, out_grad)
    wot_near = grad_near(b_wot, s_wot)
    q_passed = ctx_forward(q_started, at_q)
    stat_passed = ctx_forward(stat_started, at_stat)
    ctx_finish(q_started, q_passed)
    ctx_finish(stat_started, stat_passed)
    for image in range(images):
        stacked = stack_heads(qkv[image, own, wide : 2 * wide])
        scores = nt(stacked, qkv[image, :, 0:wide]) * scale
        for h in range(heads):
            line = image * heads + h
            level = stat[0, line : line + 1, :]
            for other in range(1, n_ctx):
                level = level + stat[other, line : line + 1, :]
            block = scores[h * slots : (h + 1) * slots]
            block = jnp.where(row_live[image], block, neg_big)
            wk[image, h * slots : (h + 1) * slots, :] = jnp.exp(block - level)


    def block_rows(c):
        sents[c][1]()
        value = first[rows_at(c, z), :] + arrived(parts, recvs, c, 0, sizes_of[c]) + vx[5:6, :]
        value = jnp.where(own_live[slot_part(c)], value, 0.0)
        block_own[slot_part(c), :] = value.astype(BF16)
        passing = to_all(block_own, out_block, c)
        for at in pieces(c):
            passing[2](at)
        return passing

    def at_do(c):
        def at(index):
            first_row = index * slots + starts[c]
            return do.at[:, pl.ds(pl.multiple_of(first_row, ROWS), sizes_of[c]), :]

        return at

    tail = [block_rows(0)]
    do_started = []
    for c in range(2):
        for copy in to_heads[c]:
            copy.wait_recv()
        do_started.append(ctx_start(at_do(c)))

    for image in range(images):
        stacked = stack_heads(do[image, own, :])
        grad_probs = nt(stacked, qkv[image, :, 2 * wide : 3 * wide])
        weights = wq[image]
        along = jnp.sum(grad_probs * weights, axis=-1, keepdims=True)
        put_rows(alng, image, along)
        grad_scores = (weights * (grad_probs - along)).astype(BF16)
        out = pick_heads(nn(grad_scores, qkv[image, :, wide : 2 * wide])) * scale
        split_rows(dqkv, image, slice(0, wide), out.astype(BF16))

    def at_along(index):
        return alng.at[index]

    along_started = ctx_start(at_along)
    vector_copy = vector_near(vector_copies, early, early_z, 4 * per, early_sib)
    tail[0][0]()
    tail.append(block_rows(1))
    wot_grad_far = grad_halves(wot_near, b_wot, s_wot, t_wot, r_wot)
    early_far = vector_far(vector_copy, early, early_sib, early_plane)
    do_passed = [ctx_forward(do_started[c], at_do(c)) for c in range(2)]
    along_passed = ctx_forward(along_started, at_along)
    for c in range(2):
        ctx_finish(do_started[c], do_passed[c])
    ctx_finish(along_started, along_passed)

    for image in range(images):
        stacked = stack_heads(qkv[image, own, 2 * wide : 3 * wide])
        grad_probs = nt(stacked, do[image])
        weights = wk[image]
        lines = []
        for h in range(heads):
            line = image * heads + h
            level = alng[0, line : line + 1, :]
            for other in range(1, n_ctx):
                level = level + alng[other, line : line + 1, :]
            lines.append(grad_probs[h * slots : (h + 1) * slots] - level)
        grad_scores = (weights * jnp.concatenate(lines, axis=0)).astype(BF16)
        out = pick_heads(nn(grad_scores, qkv[image, :, 0:wide])) * scale
        split_rows(dqkv, image, slice(wide, 2 * wide), out.astype(BF16))
        out = pick_heads(nn(weights.astype(BF16), do[image]))
        split_rows(dqkv, image, slice(2 * wide, 3 * wide), out.astype(BF16))

    def in_back(c):
        at_rows = chunk(c)

        def one(step, carry):
            out = None
            for j in range(3):
                weight = g_win[j, pl.ds(step * some, some)].reshape(TILE, wide)
                term = nt(dqkv[at_rows, j * wide : (j + 1) * wide], weight)
                out = term if out is None else out + term
            part1[at_rows, lane_at(step, TILE)] = out.astype(BF16)
            return carry

        steps(width // TILE, one)
        return scatter(part1, recv1, relay1, c)

    sent1 = [in_back(c) for c in range(2)]
    for c in range(2):
        sent1[c][2]()
    sums = [0.0, 0.0]
    for row in range(0, rows, 2 * BLOCK):
        term = part1[row : row + 2 * BLOCK, :].astype(F32)
        weighted = term * n1[row : row + 2 * BLOCK, :]
        sums[0] = sums[0] + jnp.sum(weighted, axis=0, keepdims=True)
        sums[1] = sums[1] + jnp.sum(term, axis=0, keepdims=True)
    for line, value in enumerate(sums):
        pack(late, line * per, value)
    late[2 * per :, :] = jnp.zeros((late.shape[0] - 2 * per, LANES), F32)
    for j, start in enumerate((0, 2 * wide)):
        value = jnp.sum(dqkv[:, start : start + wide].astype(F32), axis=0, keepdims=True)
        pack(late, 2 * per + j * (wide // LANES), value)
    vector_copies = vector_z(late, late_z, 2 * per)
    tail[1][0]()
    wup_far = grad_halves(wup_near, b_wup, s_wup, t_wup, r_wup)
    wot_grad_far = grad_onward(wot_grad_far, t_wot, r_wot)

    for j in range(3):
        out = tn(h1[...], dqkv[:, j * wide : (j + 1) * wide]).astype(BF16)
        b_win[j] = out.reshape(group, 2, piece, wide)
    win_near = send(b_win.at[:, :, 1 - core], s_win, sib)
    sent1[0][0]()
    wup_far = grad_onward(wup_far, t_wup, r_wup)
    f_wdt[...] = turned(grad_sum(wdt_far, t_wdt, r_wdt), f_wdt)
    stays.append(local(f_wdt, out_wdt))
    win_near.wait_recv()
    for j in range(3):
        both = b_win[j, :, pl.ds(core, 1)].reshape(group, piece, wide).astype(F32)
        t_win[:, j] = (both + s_win[j].astype(F32)).astype(BF16)
    win_far = [send(t_win.at[flip(me, k)], r_win.at[k - 1], plane(k)) for k in reversed(planes)]

    sent1[1][0]()
    def first_back(c, at):
        sent1[c][1]((at,))
        normed, inv = norm_parts(tok[block_at(c, z, at), :].astype(F32))
        grad = arrived(part1, recv1, c, at, ROWS)
        there = slots_at(c, at)
        value = gfirst[there, :] + norm_back(grad, normed, inv, vx[0:1, :])
        tokens_own[there, :] = value.astype(BF16)
        tail[2 + c][2](at)

    tail += [to_all(tokens_own, out_tokens, c) for c in range(2)]
    for at in pieces(0):
        first_back(0, at)
    for at in pieces(1)[:-1]:
        first_back(1, at)
    tail[2][0]()
    first_back(1, pieces(1)[-1])
    whole_rows = grad_sum(wot_grad_far, t_wot, r_wot)
    o_wot[...] = whole_rows.astype(BF16)
    to_owner = [
        send(o_wot.at[:, lane_at(flip(z, k), wide)], z_wot.at[k - 1], zpeer(k))
        for k in reversed(zs)
    ]

    vector_copy = vector_near(vector_copies, late, late_z, 2 * per, late_sib)
    tail[3][0]()
    late_far = vector_far(vector_copy, late, late_sib, late_plane)
    f_wup[...] = grad_sum(wup_far, t_wup, r_wup)
    stays.append(local(f_wup, out_wup))
    vector_last(early_far, early, early_plane)
    f_win[...] = grad_sum(win_far, t_win, r_win)
    stays.append(local(f_win, out_win))
    for copy in to_owner:
        copy.wait_recv()
    value = o_wot[:, lane_at(z, wide)].astype(F32)
    for k in zs:
        value = value + z_wot[k - 1].astype(F32)
    f_wot[...] = turned(value, f_wot)
    stays.append(local(f_wot, out_wot))
    vector_last(late_far, late, late_plane)
    for line in range(2):
        gv[line : line + 1, :] = unpack(late, line * per, width)
        row = 2 * per + line * (wide // LANES)
        gv[9 + line : 10 + line, 0:wide] = unpack(late, row, wide)
    for line in range(4):
        gv[2 + line : 3 + line, :] = unpack(early, line * per, width)
    gv[8:9, 0:hidden] = unpack(early, 4 * per, hidden)
    stays.append(local(gv, out_vec))
    for passing in tail:
        passing[1]()
    for copy in pending:
        copy.wait_send()
    for flag, makes in guarded:

        @pl.when(flag)
        def _():
            for make in makes:
                make().wait_send()

    for copy in stays:
        copy.wait()


def finish_kernel(sizes, *refs):
    n_ctx, piece, cut, wide, hidden, width = sizes
    sources, results, held = refs[:6], refs[7:13], refs[21:27]
    smalls, own, vec, sems = refs[13:21], refs[27:35], refs[35], refs[36]
    shard = lax.axis_index("dp") * n_ctx + lax.axis_index("ctx")
    load = pltpu.make_async_copy(refs[6], vec, sems.at[2, 0])
    load.start()
    ins, outs = [], []
    for i in range(6):
        ins.append(pltpu.make_async_copy(sources[i], held[i], sems.at[0, i]))
        outs.append(pltpu.make_async_copy(held[i], results[i], sems.at[1, i]))
    for copy in ins:
        copy.start()

    def exact(left, right):
        parts, rest = [], left
        for _ in range(3):
            parts.append(rest.astype(BF16).astype(F32))
            rest = rest - parts[-1]
        count = left.shape[0]
        product = nn(jnp.concatenate(parts, axis=0).astype(BF16), right.astype(BF16))
        return product[0:count] + product[count : 2 * count] + product[2 * count :]

    heads = wide // HD
    lane = lax.broadcasted_iota(jnp.int32, (width, piece), 0)
    slot = lax.broadcasted_iota(jnp.int32, (width, piece), 1)
    one = jnp.where(lane - slot == shard * piece, 1.0, 0.0)
    lane = lax.broadcasted_iota(jnp.int32, (hidden, hidden // HD), 0)
    slot = lax.broadcasted_iota(jnp.int32, (hidden, hidden // HD), 1)
    by_unit = jnp.where(lane // HD == slot, 1.0, 0.0)
    load.wait()
    part = exact(vec[0:8, :], one)
    for line in range(6):
        own[line][...] = part[line : line + 1]
    channel = lax.broadcasted_iota(jnp.int32, (cut, hidden), 0)
    lane = lax.broadcasted_iota(jnp.int32, (cut, hidden), 1)
    chosen = jnp.where(lane % HD - channel == shard * cut, vec[8:9, 0:hidden], 0.0)
    own[6][...] = exact(chosen, by_unit)
    lane = lax.broadcasted_iota(jnp.int32, (wide, cut), 0)
    slot = lax.broadcasted_iota(jnp.int32, (wide, cut), 1)
    pick = jnp.where(lane % HD - slot == shard * cut, 1.0, 0.0)
    head = lax.broadcasted_iota(jnp.int32, (heads, wide), 0)
    lane = lax.broadcasted_iota(jnp.int32, (heads, wide), 1)
    for j in range(2):
        chosen = jnp.where(lane // HD == head, vec[9 + j : 10 + j, 0:wide], 0.0)
        own[7][j] = exact(chosen, pick)
    for i in range(8):
        outs.append(pltpu.make_async_copy(own[i], smalls[i], sems.at[2, 1 + i]))
        outs[-1].start()
    for i in range(6):
        ins[i].wait()
        outs[i].start()
    for copy in outs:
        copy.wait()


def on_device(
    mesh_shape,
    tokens,
    keep_mask,
    cotangent,
    first_gain,
    first_shift,
    attend_in,
    attend_bias,
    attend_out,
    out_bias,
    second_gain,
    second_shift,
    expand_in,
    expand_bias,
    contract_out,
    contract_bias,
):
    n_dp, n_ctx, n_t = mesh_shape
    images, slots, width = tokens.shape
    piece, _, wide = attend_in.shape
    hidden = expand_in.shape[1]
    cut = expand_bias.shape[1]
    rows = images * slots
    group = n_dp * n_ctx // 2
    total = slots * n_ctx
    heads = wide // HD
    turn = piece % LANES == 0
    per = width // LANES
    early_rows = 4 * per + hidden // LANES
    late_rows = 2 * per + 8 * ((2 * wide // LANES + 7) // 8)
    sizes = (n_dp, n_ctx, n_t, images, slots, width, wide, hidden, piece, cut)
    vmem = pl.BlockSpec(memory_space=pltpu.VMEM)
    hbm = pl.BlockSpec(memory_space=pl.ANY)
    scratch = [
        pltpu.VMEM((rows, width), BF16),
        pltpu.VMEM((rows, width), BF16),
        pltpu.VMEM((wide, piece), BF16),
        pltpu.VMEM((hidden, piece), BF16),
        pltpu.VMEM((2 * ROWS, LANES), F32),
        pltpu.VMEM((3, group, 2, piece, wide), BF16),
        pltpu.VMEM((group, 2, piece, n_t * wide), BF16),
        pltpu.VMEM((group, 2, piece, hidden), BF16),
        pltpu.VMEM((group, 2, piece, hidden), BF16),
        pltpu.VMEM((group, 2, 2 * ROWS, LANES), F32),
        pltpu.VMEM((ROWS, width), F32),
        pltpu.VMEM((rows, width), F32),
        pltpu.VMEM((rows, width), BF16),
        pltpu.VMEM((images, total, 3 * wide), BF16),
        pltpu.VMEM((images, heads * slots, total), F32),
        pltpu.VMEM((images, heads * slots, total), F32),
        pltpu.VMEM((n_ctx, images * heads, total), F32),
        pltpu.VMEM((n_ctx, images * heads, total), F32),
        pltpu.VMEM((rows, n_t * wide), BF16),
        pltpu.VMEM((rows, width), F32),
        pltpu.VMEM((rows, width), BF16),
        pltpu.VMEM((rows, hidden), F32),
        pltpu.VMEM((rows, hidden), BF16),
        pltpu.VMEM((rows, hidden), BF16),
        pltpu.VMEM((rows, width), BF16),
        pltpu.VMEM((rows, width), BF16),
        pltpu.VMEM((rows, width), BF16),
        pltpu.VMEM((2, slots, width), BF16),
        pltpu.VMEM((2, slots, width), BF16),
        pltpu.VMEM((2, slots, width), BF16),
        pltpu.VMEM((2, slots, width), BF16),
        pltpu.VMEM((2, slots, width), BF16),
        pltpu.VMEM((2, slots, width), BF16),
        pltpu.VMEM((slots, width), F32),
        pltpu.VMEM((rows, width), BF16),
        pltpu.VMEM((slots, width), BF16),
        pltpu.VMEM((slots, n_t * wide), BF16),
        pltpu.VMEM((images, total, wide), BF16),
        pltpu.VMEM((rows, 3 * wide), BF16),
        pltpu.VMEM((slots, width), BF16),
        pltpu.VMEM((slots, width), BF16),
        pltpu.VMEM((ROWS, width), F32),
        pltpu.VMEM((early_rows, LANES), F32),
        pltpu.VMEM((early_rows, LANES), F32),
        pltpu.VMEM((group - 1, early_rows, LANES), F32),
        pltpu.VMEM((n_t - 1, 4 * per, LANES), F32),
        pltpu.VMEM((late_rows, LANES), F32),
        pltpu.VMEM((late_rows, LANES), F32),
        pltpu.VMEM((group - 1, late_rows, LANES), F32),
        pltpu.VMEM((n_t - 1, 2 * per, LANES), F32),
        pltpu.VMEM((3, group, 2, piece, wide), BF16),
        pltpu.VMEM((group, 2, piece, n_t * wide), BF16),
        pltpu.VMEM((group, 2, piece, hidden), BF16),
        pltpu.VMEM((group, 2, piece, hidden), BF16),
        pltpu.VMEM((3, group, piece, wide), BF16),
        pltpu.VMEM((group, piece, n_t * wide), BF16),
        pltpu.VMEM((group, piece, hidden), BF16),
        pltpu.VMEM((group, piece, hidden), BF16),
        pltpu.VMEM((group, 3, piece, wide), BF16),
        pltpu.VMEM((group, piece, n_t * wide), BF16),
        pltpu.VMEM((group, piece, hidden), BF16),
        pltpu.VMEM((group, piece, hidden), BF16),
        pltpu.VMEM((group - 1, 3, piece, wide), BF16),
        pltpu.VMEM((group - 1, piece, n_t * wide), BF16),
        pltpu.VMEM((group - 1, piece, hidden), BF16),
        pltpu.VMEM((group - 1, piece, hidden), BF16),
        pltpu.VMEM((piece, n_t * wide), BF16),
        pltpu.VMEM((n_t - 1, piece, wide), BF16),
    ]
    shapes = (
        (3, piece, wide),
        (wide, piece) if turn else (piece, wide),
        (piece, hidden),
        (hidden, piece) if turn else (piece, hidden),
    )
    scratch += [pltpu.VMEM(shape, F32) for shape in shapes]
    copies = 260 + 20 * group
    scratch += [
        pltpu.SemaphoreType.DMA((copies,)),
        pltpu.SemaphoreType.DMA((copies,)),
        pltpu.SemaphoreType.DMA((48,)),
    ]
    results = [jax.ShapeDtypeStruct((rows, width), BF16)] * 2
    results += [jax.ShapeDtypeStruct(shape, F32) for shape in shapes]
    outs = pl.pallas_call(
        functools.partial(block_kernel, sizes),
        out_shape=(*results, jax.ShapeDtypeStruct((ROWS, width), F32)),
        in_specs=[hbm, hbm, vmem, hbm, hbm, hbm, hbm] + [vmem] * 8,
        out_specs=(hbm,) * 7,
        scratch_shapes=scratch,
        compiler_params=pltpu.CompilerParams(
            collective_id=0, has_side_effects=True, vmem_limit_bytes=63 << 20
        ),
    )(
        tokens.reshape(rows, width),
        cotangent.reshape(rows, width),
        keep_mask,
        jnp.transpose(attend_in, (1, 0, 2)),
        attend_out,
        expand_in,
        contract_out,
        *[
            v.reshape(1, piece)
            for v in (first_gain, first_shift, out_bias, second_gain, second_shift, contract_bias)
        ],
        expand_bias.T,
        attend_bias,
    )
    vector = jax.ShapeDtypeStruct((1, piece), F32)
    small = [vector] * 6 + [
        jax.ShapeDtypeStruct((cut, hidden // HD), F32),
        jax.ShapeDtypeStruct((2, heads, cut), F32),
    ]
    placed = pl.pallas_call(
        functools.partial(finish_kernel, (n_ctx, piece, cut, wide, hidden, width)),
        out_shape=(*results, *small),
        in_specs=[hbm] * 7,
        out_specs=(hbm,) * 14,
        scratch_shapes=[pltpu.VMEM(r.shape, r.dtype) for r in (*results, *small)]
        + [pltpu.VMEM((ROWS, width), F32), pltpu.SemaphoreType.DMA((3, 9))],
        compiler_params=pltpu.CompilerParams(vmem_limit_bytes=63 << 20),
    )(*outs)
    block_out, tokens_grad, d_win, d_wot, d_wup, d_wdt = placed[:6]
    vectors = [v.reshape(piece) for v in placed[6:12]]
    return (
        block_out.reshape(tokens.shape),
        tokens_grad.reshape(tokens.shape),
        vectors[0],
        vectors[1],
        jnp.transpose(d_win, (1, 0, 2)),
        placed[13],
        d_wot if turn else d_wot.T,
        vectors[2],
        vectors[3],
        vectors[4],
        d_wup,
        placed[12].T,
        d_wdt if turn else d_wdt.T,
        vectors[5],
    )


def solution(mesh):
    shape = (mesh.shape["dp"], mesh.shape["ctx"], mesh.shape["tensor"])
    vector = P(("dp", "ctx"))
    params = (
        vector,
        vector,
        P(("dp", "ctx"), None, "tensor"),
        P(None, "tensor", ("dp", "ctx")),
        P("tensor", ("dp", "ctx")),
        vector,
        vector,
        vector,
        P(("dp", "ctx"), "tensor"),
        P("tensor", ("dp", "ctx")),
        P("tensor", ("dp", "ctx")),
        vector,
    )
    rows = P("dp", "ctx", None)
    return jax.shard_map(
        functools.partial(on_device, shape),
        mesh=mesh,
        in_specs=(rows, P("dp", None), rows, *params),
        out_specs=(rows, rows, *params),
        check_vma=False,
    )
```

```python
import functools

import jax
import jax.numpy as jnp
from jax import lax
from jax.experimental import pallas as pl
from jax.experimental.pallas import tpu as pltpu
from jax.sharding import PartitionSpec as P

HD = 64
BUFFER = 64
LANES = 128
ROWS = 16
TILE = 256
BLOCK = 32
MESH = pl.DeviceIdType.MESH
F32 = jnp.float32
BF16 = jnp.bfloat16

eps = 1e-06
neg_big = -1e30
root_half = 0.7071067811865476
inv_root_two_pi = 0.3989422804014327


def flip(index, bits):
    out, bit = index, 1
    while bit <= bits:
        if bits & bit:
            out = out + bit - 2 * bit * lax.rem(lax.div(index, bit), 2)
        bit *= 2
    return out


def nn(left, right):
    return jnp.dot(left, right, preferred_element_type=F32)


def nt(left, right):
    return lax.dot_general(left, right, (((1,), (1,)), ((), ())), preferred_element_type=F32)


def tn(left, right):
    return lax.dot_general(left, right, (((0,), (0,)), ((), ())), preferred_element_type=F32)


def steps(count, body):
    if count > 8:
        lax.fori_loop(0, count, body, 0)
        return
    for step in range(count):
        body(step, 0)


def turned(value, ref):
    return value if value.shape == ref.shape else value.T


def norm_parts(values):
    mean = jnp.mean(values, axis=-1, keepdims=True)
    centered = values - mean
    spread = jnp.mean(centered * centered, axis=-1, keepdims=True)
    inv = lax.rsqrt(spread + eps)
    return centered * inv, inv


def block_kernel(
    sizes,
    tok_in,
    cot_in,
    keep,
    win,
    attend_out,
    wup,
    contract_out,
    first_gain,
    first_shift,
    out_bias,
    second_gain,
    second_shift,
    contract_bias,
    expand_bias,
    attend_bias,
    out_block,
    out_tokens,
    out_win,
    out_wot,
    out_wup,
    out_wdt,
    out_vec,
    tok,
    cot,
    a_out,
    c_out,
    vec,
    g_win,
    g_wot,
    g_wup,
    g_wdt,
    g_vec,
    vx,
    n1,
    h1,
    qkv,
    wq,
    wk,
    stat,
    alng,
    mixed,
    first,
    h2,
    ga,
    act,
    gi,
    part2,
    parts,
    part1,
    recv2,
    relay2,
    recvs,
    relays,
    recv1,
    relay1,
    gfirst,
    gdown,
    gown,
    gm,
    do,
    dqkv,
    block_own,
    tokens_own,
    gv,
    early,
    early_sib,
    early_plane,
    early_z,
    late,
    late_sib,
    late_plane,
    late_z,
    b_win,
    b_wot,
    b_wup,
    b_wdt,
    s_win,
    s_wot,
    s_wup,
    s_wdt,
    t_win,
    t_wot,
    t_wup,
    t_wdt,
    r_win,
    r_wot,
    r_wup,
    r_wdt,
    o_wot,
    z_wot,
    f_win,
    f_wot,
    f_wup,
    f_wdt,
    send_sem,
    recv_sem,
    local_sem,
):
    n_dp, n_ctx, n_t, images, slots, width, wide, hidden, piece, cut = sizes
    rows = images * slots
    total = slots * n_ctx
    heads = wide // HD
    half = n_ctx // 2
    group = n_dp * half
    scale = HD ** (-0.5)
    dp = lax.axis_index("dp")
    ctx = lax.axis_index("ctx")
    z = lax.axis_index("tensor")
    high, core = lax.div(ctx, 2), lax.rem(ctx, 2)
    me = dp * half + high
    shard = me * 2 + core
    sib = (dp, flip(ctx, 1), z)

    def plane(k):
        other = flip(me, k)
        return (lax.div(other, half), lax.rem(other, half) * 2 + core, z)

    def ctx_at(k):
        return flip(high, k) * 2 + core

    def zpeer(k):
        return (dp, ctx, flip(z, k))

    def slot_at(index):
        return pl.ds(pl.multiple_of(index * slots, ROWS), slots)

    def lane_at(index, size):
        return pl.ds(pl.multiple_of(index * size, size), size)

    own = slot_at(ctx)
    mine = slot_at(z)

    cut_at = ROWS * (slots // ROWS // 2)
    starts = (0, cut_at)
    sizes_of = (cut_at, slots - cut_at)
    bases = (0, images * cut_at)

    def chunk(c):
        return slice(bases[c], bases[c] + images * sizes_of[c])

    def rows_at(c, image):
        first_row = bases[c] + image * sizes_of[c]
        return pl.ds(pl.multiple_of(first_row, ROWS), sizes_of[c])

    def slot_part(c):
        return slice(starts[c], starts[c] + sizes_of[c])

    def split_rows(ref, image, lanes, value):
        for c in range(2):
            ref[rows_at(c, image), lanes] = value[slot_part(c)]

    count = [0, 0]
    stays = []
    pending = []

    def send(src, dst, device):
        index = count[0]
        count[0] += 1
        copy = pltpu.make_async_remote_copy(
            src_ref=src,
            dst_ref=dst,
            send_sem=send_sem.at[index],
            recv_sem=recv_sem.at[index],
            device_id=device,
            device_id_type=MESH,
        )
        copy.start()
        pending.append(copy)
        return copy

    inside = lax.rem(z - lax.div(z, 2), 2) == 1
    at_end = lax.rem(z - lax.div(z, 2), 2) == 0
    guarded = []

    def fresh():
        count[0] += 1
        return count[0] - 1

    def remote(src, dst, device, out_index, in_index):
        return pltpu.make_async_remote_copy(
            src_ref=src,
            dst_ref=dst,
            send_sem=send_sem.at[out_index],
            recv_sem=recv_sem.at[in_index],
            device_id=device,
            device_id_type=MESH,
        )

    def send_if(flag, makes):
        guarded.append((flag, makes))

        @pl.when(flag)
        def _():
            for make in makes:
                make().start()

    def complete(copy):
        pending[:] = [other for other in pending if other is not copy]
        copy.wait()

    def local(src, dst):
        index = count[1]
        count[1] += 1
        copy = pltpu.make_async_copy(src, dst, local_sem.at[index])
        copy.start()
        return copy

    planes = range(1, group)
    zs = range(1, n_t)

    def at_win_kv(m, c):
        return g_win.at[1:3, m, c]

    def at_win_q(m, c):
        return g_win.at[0:1, m, c]

    def at_wot(m, c):
        return g_wot.at[m, c, :, lane_at(z, wide)]

    def at_wup(m, c):
        return g_wup.at[m, c]

    def at_wdt(m, c):
        return g_wdt.at[m, c]

    def at_vec(m, c):
        return g_vec.at[m, c]

    barrier = pltpu.get_barrier_semaphore()
    for device in [plane(k) for k in planes] + [sib] + [zpeer(k) for k in zs]:
        pl.semaphore_signal(barrier, inc=1, device_id=device, device_id_type=MESH)
    a_out_load = local(attend_out, a_out)
    def load_rows(source, ref):
        return [
            local(
                source.at[image * slots + starts[c] : image * slots + starts[c] + sizes_of[c], :],
                ref.at[rows_at(c, image), :],
            )
            for c in range(2)
            for image in range(images)
        ]

    tok_load = load_rows(tok_in, tok)
    win_own = local(win, g_win.at[:, me, core])
    c_out_load = local(contract_out, c_out)
    cot_load = load_rows(cot_in, cot)
    wup_own = local(wup, at_wup(me, core))

    vec[...] = jnp.zeros_like(vec)
    for line, ref in enumerate(
        (first_gain, first_shift, out_bias, second_gain, second_shift, contract_bias)
    ):
        vec[line : line + 1, 0:piece] = ref[...].astype(F32)
    vec[8 : 8 + cut, 0 : hidden // HD] = expand_bias[...].astype(F32)
    for j in range(2):
        vec[16 + j * heads : 16 + (j + 1) * heads, 0:cut] = attend_bias[j].astype(F32)
    g_vec[me, core] = vec[...]
    gv[...] = jnp.zeros_like(gv)
    unit_one = (
        lax.broadcasted_iota(jnp.int32, (piece, piece), 0)
        == lax.broadcasted_iota(jnp.int32, (piece, piece), 1)
    ).astype(F32)
    unit_one = unit_one.astype(BF16)
    a_out_load.wait()
    g_wot[me, core, :, lane_at(z, wide)] = nt(unit_one, a_out[...]).astype(BF16)
    pl.semaphore_wait(barrier, group + n_t - 1)

    def gather_start(src, at):
        far = [send(src, at(me, core), plane(k)) for k in planes]
        return far, send(src, at(me, core), sib)

    def gather_forward(started, at):
        out = []
        for k in planes:
            started[0][k - 1].wait_recv()
            there = at(flip(me, k), core)
            out.append(send(there, there, sib))
        return out

    def gather_finish(started, passed):
        started[1].wait_recv()
        for copy in passed:
            copy.wait_recv()

    relayed = group == 4 and piece % (2 * ROWS) == 0

    def relay_start(src, at):
        if not relayed:
            return gather_start(src, at)
        far = [send(src, at(me, core), plane(k)) for k in (1, 2)]
        return far, send(src, at(me, core), sib)

    def relay_forward(started, at):
        if not relayed:
            return gather_forward(started, at), []
        out, halves = [], []
        for k in (1, 2):
            started[0][k - 1].wait_recv()
            there = at(flip(me, k), core)
            part = there.at[pl.ds((k - 1) * (piece // 2), piece // 2)]
            halves.append(send(part, part, plane(3 - k)))
            out.append(send(there, there, sib))
        return out, halves

    def relay_last(halves, at):
        if not halves:
            return []
        for copy in halves:
            copy.wait_recv()
        there = at(flip(me, 3), core)
        return [send(there, there, sib)]

    def ctx_start(at):
        far = [send(at(ctx), at(ctx), (dp, ctx_at(k), z)) for k in range(1, half)]
        return far, send(at(ctx), at(ctx), sib)

    def ctx_forward(started, at):
        out = []
        for k in range(1, half):
            started[0][k - 1].wait_recv()
            out.append(send(at(ctx_at(k)), at(ctx_at(k)), sib))
        return out

    def ctx_finish(started, passed):
        started[1].wait_recv()
        for copy in passed:
            copy.wait_recv()

    def wot_piece(m, index):
        return g_wot.at[m, core, :, lane_at(index, wide)]

    vec_started = gather_start(vec, at_vec)
    wot_own = at_wot(me, core)
    wot_far = [send(wot_own, wot_own, plane(k)) for k in planes if k < 3]
    kv_win_started = gather_start(win.at[1:3], at_win_kv)
    wot_far += [send(wot_own, wot_own, plane(k)) for k in planes if k >= 3]
    wot_started = (wot_far, send(wot_own, wot_own, sib))
    q_win_started = gather_start(win.at[0:1], at_win_q)
    wot_z = [[send(wot_piece(me, z), wot_piece(me, z), zpeer(k)) for k in zs]]

    for copy in tok_load:
        copy.wait()

    def first_norm(step, carry):
        at = pl.ds(pl.multiple_of(step * BLOCK, BLOCK), BLOCK)
        normed, _ = norm_parts(tok[at, :].astype(F32))
        n1[at, :] = normed
        return carry

    lax.fori_loop(0, rows // BLOCK, first_norm, 0)

    vec_passed = gather_forward(vec_started, at_vec)
    gather_finish(vec_started, vec_passed)
    shape = (2 * ROWS, width)
    line_id = lax.broadcasted_iota(jnp.int32, shape, 0)
    lane_id = lax.broadcasted_iota(jnp.int32, shape, 1)
    source = lax.broadcasted_iota(jnp.int32, (LANES, width), 0)
    target = lax.broadcasted_iota(jnp.int32, (LANES, width), 1)
    by_unit = jnp.where(target // HD == source, 1.0, 0.0).astype(BF16)
    for_unit = lane_id % HD - (line_id - 8)
    for_head = lane_id // HD == (line_id - 16) % heads

    def place(index, carry):
        one, two, three = carry
        shares = g_vec[lax.div(index, 2), lax.rem(index, 2)].astype(BF16)
        by_width = jnp.where(target - source == index * piece, 1.0, 0.0).astype(BF16)
        by_channel = jnp.where(target % HD - source == index * cut, 1.0, 0.0).astype(BF16)
        one = one + nn(shares, by_width)
        two = two + jnp.where(for_unit == index * cut, nn(shares, by_unit), 0.0)
        three = three + jnp.where(for_head, nn(shares, by_channel), 0.0)
        return one, two, three

    zero = jnp.zeros(shape, F32)
    one, two, three = lax.fori_loop(0, 2 * group, place, (zero, zero, zero))
    vx[0:8, :] = one[0:8]
    vx[8:9, :] = jnp.sum(two[8 : 8 + cut], axis=0, keepdims=True)
    vx[9:10, :] = jnp.sum(three[16 : 16 + heads], axis=0, keepdims=True)
    vx[10:11, :] = jnp.sum(three[16 + heads : 16 + 2 * heads], axis=0, keepdims=True)

    def first_hidden(step, carry):
        at = pl.ds(pl.multiple_of(step * BLOCK, BLOCK), BLOCK)
        h1[at, :] = (n1[at, :] * vx[0:1, :] + vx[1:2, :]).astype(BF16)
        return carry

    lax.fori_loop(0, rows // BLOCK, first_hidden, 0)

    wot_passed = []

    def wot_onward(k):
        wot_started[0][k - 1].wait_recv()
        there = wot_piece(flip(me, k), z)
        wot_z.append([send(there, there, zpeer(j)) for j in reversed(zs)][::-1])
        wot_passed.append(send(there, there, sib))

    for k in planes:
        if k < 3:
            wot_onward(k)

    c_out_load.wait()

    def turn(step, carry):
        at = lane_at(step, TILE)
        g_wdt[me, core, :, at] = nt(unit_one, c_out[at, :]).astype(BF16)
        return carry

    steps(hidden // TILE, turn)

    lengths = BUFFER + jnp.sum(keep[...], axis=1, keepdims=True)
    slot_id = lax.broadcasted_iota(jnp.int32, (slots, 1), 0) + ctx * slots
    key_id = lax.broadcasted_iota(jnp.int32, (1, total), 1)
    head_of = lax.broadcasted_iota(jnp.int32, (slots, wide), 1) // HD
    spot = lax.broadcasted_iota(jnp.int32, (slots, total), 1) == slot_id

    def stack_heads(block):
        wider = block.astype(F32)
        return jnp.concatenate(
            [jnp.where(head_of == h, wider, 0.0).astype(BF16) for h in range(heads)], axis=0
        )

    def pick_heads(block):
        out = jnp.where(head_of == 0, block[0:slots], 0.0)
        for h in range(1, heads):
            out = jnp.where(head_of == h, block[h * slots : (h + 1) * slots], out)
        return out

    def put_rows(ref, image, column):
        for h in range(heads):
            part = jnp.where(spot, column[h * slots : (h + 1) * slots], 0.0)
            line = image * heads + h
            ref[ctx, line : line + 1, :] = jnp.sum(part, axis=0, keepdims=True)

    win_passed = gather_forward(kv_win_started, at_win_kv)
    win_own.wait()
    gather_finish(kv_win_started, win_passed)

    def project(j, bias):
        out = nn(h1[...], g_win[j].reshape(width, wide))
        if bias is not None:
            out = out + vx[bias : bias + 1, 0:wide]
        out = out.astype(BF16)
        for c in range(2):
            place_at = pl.ds(pl.multiple_of(ctx * slots + starts[c], ROWS), sizes_of[c])
            block = out[chunk(c)].reshape(images, sizes_of[c], wide)
            qkv[:, place_at, j * wide : (j + 1) * wide] = block

    def at_kv(images_of):
        def at(index):
            return qkv.at[images_of, slot_at(index), wide : 3 * wide]

        return at

    def at_q(index):
        return qkv.at[:, slot_at(index), 0:wide]

    project(1, None)
    project(2, 10)
    middle = images // 2
    image_parts = (slice(0, middle), slice(middle, images))
    kv_started = [ctx_start(at_kv(part)) for part in image_parts]
    wup_started = relay_start(wup, at_wup)
    wdt_started = relay_start(at_wdt(me, core), at_wdt)
    for k in planes:
        if k >= 3:
            wot_onward(k)
    win_passed = gather_forward(q_win_started, at_win_q)
    gather_finish(q_win_started, win_passed)
    project(0, 9)

    def at_mixed(index, c, part):
        first_row = bases[c] + part.start * sizes_of[c]
        last_row = bases[c] + part.stop * sizes_of[c]
        return mixed.at[first_row:last_row, lane_at(index, wide)]

    mixed_sent = [[], []]
    for image in range(images):
        for part in range(2):
            if image == image_parts[part].start:
                kv_at = at_kv(image_parts[part])
                kv_passed = ctx_forward(kv_started[part], kv_at)
                ctx_finish(kv_started[part], kv_passed)
        key_live = key_id < lengths[image : image + 1, :]
        stacked = stack_heads(qkv[image, own, 0:wide])
        scores = nt(stacked, qkv[image, :, wide : 2 * wide]) * scale
        scores = jnp.where(key_live, scores, neg_big)
        top = jnp.max(scores, axis=-1, keepdims=True)
        expo = jnp.exp(scores - top)
        whole = jnp.sum(expo, axis=-1, keepdims=True)
        probs = expo / whole
        wq[image] = probs
        put_rows(stat, image, top + jnp.log(whole))
        out = nn(probs.astype(BF16), qkv[image, :, 2 * wide : 3 * wide])
        split_rows(mixed, image, lane_at(z, wide), pick_heads(out).astype(BF16))
        for part, order in zip(image_parts, ((0,), (0, 1))):
            if image == part.stop - 1:
                for c in order:
                    whole_part = slice(0, images) if c == 1 else part
                    there = at_mixed(z, c, whole_part)
                    mixed_sent[c] += [send(there, there, zpeer(k)) for k in reversed(zs)]

    def at_stat(index):
        return stat.at[index]

    for copy in cot_load:
        copy.wait()
    row_live = []
    for image in range(images):
        row_live.append(slot_id < lengths[image : image + 1, :])
        for c in range(2):
            at = rows_at(c, image)
            live = row_live[image][slot_part(c)]
            gdown[at, :] = jnp.where(live, cot[at, :].astype(F32), 0.0).astype(BF16)

    wup_passed, wup_halves = relay_forward(wup_started, at_wup)
    gather_finish(wot_started, wot_passed)
    wot_more = []
    for order, block in enumerate(wot_z):
        for k in zs:
            block[k - 1].wait_recv()
            there = wot_piece(flip(me, order), flip(z, k))
            wot_more.append(send(there, there, sib))
    wup_own.wait()
    wdt_passed, wdt_halves = relay_forward(wdt_started, at_wdt)
    q_started = ctx_start(at_q)
    stat_started = ctx_start(at_stat)
    wup_passed += relay_last(wup_halves, at_wup)
    for copy in wot_more:
        copy.wait_recv()

    some = group // (width // TILE)

    def pieces(c):
        return range(0, sizes_of[c], ROWS)

    def block_at(c, index, at):
        first_row = bases[c] + index * sizes_of[c] + at
        return pl.ds(pl.multiple_of(first_row, ROWS), ROWS)

    def slots_at(c, at):
        return slice(starts[c] + at, starts[c] + at + ROWS)

    def scatter(part, recv, relay, c):
        marks = {at: [fresh() for _ in range(4)] for at in pieces(c)}

        def onward(j, at):
            return remote(
                part.at[block_at(c, flip(z, 3 - j), at), :],
                relay.at[j, slots_at(c, at), :],
                zpeer(1),
                marks[at][j],
                marks[at][j],
            )

        def passed(j, at):
            return remote(
                relay.at[j, slots_at(c, at), :],
                recv.at[1, slots_at(c, at), :],
                zpeer(2 + j),
                marks[at][2 + j],
                marks[at][2],
            )

        both = [(at, j) for at in pieces(c) for j in range(2)]
        send_if(at_end, [functools.partial(onward, j, at) for at, j in both])
        near = []

        def send_near():
            source = part.at[rows_at(c, flip(z, 1)), :]
            near.append(send(source, recv.at[0, slot_part(c), :], zpeer(1)))

        def pass_on():
            guarded.append((inside, [functools.partial(passed, j, at) for at, j in both]))

            @pl.when(inside)
            def _():
                for at, j in both:
                    onward(j, at).wait_recv()
                    value = part[block_at(c, flip(z, 2 + j), at), :].astype(F32)
                    value = value + relay[j, slots_at(c, at), :].astype(F32)
                    relay[j, slots_at(c, at), :] = value.astype(BF16)
                    passed(j, at).start()

        def finish(some_pieces=None):
            if some_pieces is None or 0 in some_pieces:
                near[0].wait_recv()
            for at in some_pieces or pieces(c):
                passed(0, at).wait_recv()

        return pass_on, finish, send_near

    def to_all(source, target, c):
        marks = {at: [fresh() for _ in range(4)] for at in pieces(c)}

        def piece_of(index, at):
            first_row = index * slots + starts[c] + at
            return target.at[pl.ds(pl.multiple_of(first_row, ROWS), ROWS), :]

        def far(k, at):
            mark = marks[at][k - 2]
            return remote(source.at[slots_at(c, at), :], piece_of(z, at), zpeer(k), mark, mark)

        def passed(k, at):
            there = piece_of(flip(z, k), at)
            return remote(there, there, zpeer(1), marks[at][k], marks[at][3 - k])

        nears = []

        def start(at):
            own_part = source.at[slots_at(c, at), :]
            send_if(at_end, [functools.partial(far, 2, at)])
            send_if(inside, [functools.partial(far, 3, at)])
            nears.append(send(own_part, piece_of(z, at), zpeer(1)))
            stays.append(local(own_part, piece_of(z, at)))

        both = [(k, at) for at in pieces(c) for k in (3, 2)]

        def pass_on():
            guarded.append((inside, [functools.partial(passed, k, at) for k, at in both]))

            @pl.when(inside)
            def _():
                for k, at in both:
                    far(k, at).wait_recv()
                    passed(k, at).start()

        def finish():
            for copy in nears:
                copy.wait_recv()

            @pl.when(at_end)
            def _():
                for k, at in both:
                    far(k, at).wait_recv()

        return pass_on, finish, start

    def arrived(part, recv, c, at, size):
        here = pl.ds(pl.multiple_of(bases[c] + z * sizes_of[c] + at, ROWS), size)
        there = pl.ds(pl.multiple_of(starts[c] + at, ROWS), size)
        out = part[here, :].astype(F32)
        for j in range(2):
            out = out + recv[j, there, :].astype(F32)
        return out

    def attended(c):
        at_rows = chunk(c)
        for copy in mixed_sent[c]:
            copy.wait_recv()

        def project_out(step, carry):
            weight = g_wot[pl.ds(step * some, some)].reshape(TILE, n_t * wide)
            first[at_rows, lane_at(step, TILE)] = nt(mixed[at_rows, :], weight)
            return carry

        steps(width // TILE, project_out)

        for row in range(bases[c], bases[c] + images * sizes_of[c], ROWS):
            at = slice(row, row + ROWS)
            value = tok[at, :].astype(F32) + first[at, :] + vx[2:3, :]
            first[at, :] = value
            normed, _ = norm_parts(value)
            h2[at, :] = (normed * vx[3:4, :] + vx[4:5, :]).astype(BF16)

    def feed_forward(c):
        at_rows = chunk(c)

        def expand(step, carry):
            at = lane_at(step, TILE)
            weight = g_wup[:, :, :, at].reshape(width, TILE)
            inner = nn(h2[at_rows, :], weight) + vx[8:9, at]
            share = 0.5 * (1.0 + lax.erf(inner * root_half))
            act[at_rows, at] = (inner * share).astype(BF16)
            slope = share + inner * jnp.exp(-0.5 * inner * inner) * inv_root_two_pi
            grad = (ga[at_rows, at] * slope).astype(BF16)
            gi[at_rows, at] = grad
            gv[8:9, at] += jnp.sum(grad.astype(F32), axis=0, keepdims=True)
            return carry

        steps(hidden // TILE, expand)

        def up_back(step, carry):
            weight = g_wup[pl.ds(step * some, some)].reshape(TILE, hidden)
            part2[at_rows, lane_at(step, TILE)] = nt(gi[at_rows, :], weight).astype(BF16)
            return carry

        steps(width // TILE, up_back)
        return scatter(part2, recv2, relay2, c)

    attended(0)
    wdt_passed += relay_last(wdt_halves, at_wdt)
    gather_finish(wup_started, wup_passed)
    gather_finish(wdt_started, wdt_passed)

    def down_back(c):
        at_rows = chunk(c)

        def one(step, carry):
            at = lane_at(step, TILE)
            weight = g_wdt[:, :, :, at].reshape(width, TILE)
            ga[at_rows, at] = nn(gdown[at_rows, :], weight)
            return carry

        steps(hidden // TILE, one)

    down_back(0)
    sent2 = [feed_forward(0)]
    sent2[0][2]()
    down_back(1)
    attended(1)
    sent2.append(feed_forward(1))
    sent2[1][2]()
    sent2[0][0]()

    def contract(step, carry):
        weight = g_wdt[pl.ds(step * some, some)].reshape(TILE, hidden)
        parts[:, lane_at(step, TILE)] = nt(act[...], weight).astype(BF16)
        return carry

    steps(width // TILE, contract)
    sents = []
    for c in range(2):
        sents.append(scatter(parts, recvs, relays, c))
        sents[c][2]()

    def wide_grad(buf, left, right, lanes):
        def one(step, carry):
            at = lane_at(step, TILE)
            out = tn(left[...], right[:, at]).astype(BF16)
            buf[:, :, :, at] = out.reshape(group, 2, piece, TILE)
            return carry

        steps(lanes // TILE, one)

    def grad_near(buf, near):
        return send(buf.at[:, 1 - core], near, sib)

    def grad_far(copy, buf, near, both, recv):
        copy.wait_recv()

        def one(m, carry):
            both[m] = (buf[m, core].astype(F32) + near[m].astype(F32)).astype(BF16)
            return carry

        steps(group, one)
        return [send(both.at[flip(me, k)], recv.at[k - 1], plane(k)) for k in reversed(planes)]

    def grad_halves(copy, buf, near, both, recv):
        if not relayed:
            return grad_far(copy, buf, near, both, recv)
        copy.wait_recv()

        def one(m, carry):
            both[m] = (buf[m, core].astype(F32) + near[m].astype(F32)).astype(BF16)
            return carry

        steps(group, one)
        part = piece // 2
        corner = flip(me, 3)
        return [
            send(both.at[corner, 0:part], recv.at[2, 0:part], plane(1)),
            send(both.at[corner, part:piece], recv.at[2, part:piece], plane(2)),
        ]

    def grad_onward(copies, both, recv):
        if not relayed:
            return copies
        part = piece // 2
        for k, at in ((2, slice(0, part)), (1, slice(part, piece))):
            copies[2 - k].wait_recv()
            other = flip(me, k)
            value = both[other, at].astype(F32) + recv[2, at].astype(F32)
            both[other, at] = value.astype(BF16)
        return [send(both.at[flip(me, k)], recv.at[k - 1], plane(k)) for k in (1, 2)]

    def grad_sum(copies, both, recv):
        for copy in copies:
            copy.wait_recv()
        value = both[me].astype(F32)
        for k in range(len(copies)):
            value = value + recv[k].astype(F32)
        return value

    wide_grad(b_wdt, gdown, act, hidden)
    wdt_near = grad_near(b_wdt, s_wdt)
    sent2[1][0]()
    wide_grad(b_wup, h2, gi, hidden)
    wup_near = grad_near(b_wup, s_wup)
    wdt_far = grad_far(wdt_near, b_wdt, s_wdt, t_wdt, r_wdt)

    own_live = slot_id < jnp.sum(
        jnp.where(lax.broadcasted_iota(jnp.int32, (images, 1), 0) == z, lengths, 0),
        axis=0,
        keepdims=True,
    )

    def norm_back(grad, normed, inv, gain):
        scaled = grad * gain
        inner = (
            scaled
            - jnp.mean(scaled, axis=-1, keepdims=True)
            - normed * jnp.mean(scaled * normed, axis=-1, keepdims=True)
        )
        return inner * inv

    def second_back(c):
        sent2[c][1]()

        sums = [0.0, 0.0, 0.0, 0.0]
        for at in range(0, sizes_of[c], ROWS):
            here = pl.ds(pl.multiple_of(bases[c] + z * sizes_of[c] + at, ROWS), ROWS)
            grad = arrived(part2, recv2, c, at, ROWS)
            normed, inv = norm_parts(first[here, :])
            rows_grad = gdown[here, :].astype(F32)
            value = rows_grad + norm_back(grad, normed, inv, vx[3:4, :])
            there = slice(starts[c] + at, starts[c] + at + ROWS)
            gfirst[there, :] = value
            gown[there, :] = value.astype(BF16)
            terms = (value, grad * normed, grad, rows_grad)
            sums = [old + jnp.sum(term, axis=0, keepdims=True) for old, term in zip(sums, terms)]
        for line, value in enumerate(sums):
            gv[2 + line : 3 + line, :] += value

        def mixed_back(step, carry):
            at = lane_at(step, wide)
            weight = g_wot[:, :, :, at].reshape(width, wide)
            gm[slot_part(c), at] = nn(gown[slot_part(c), :], weight).astype(BF16)
            return carry

        steps(n_t, mixed_back)
        place_at = pl.ds(pl.multiple_of(ctx * slots + starts[c], ROWS), sizes_of[c])
        sent = [
            send(
                gm.at[slot_part(c), lane_at(flip(z, k), wide)],
                do.at[z, place_at, :],
                zpeer(k),
            )
            for k in reversed(zs)
        ]
        do[z, place_at, :] = gm[slot_part(c), lane_at(z, wide)]
        return sent

    to_heads = [second_back(0)]
    sents[0][0]()
    to_heads.append(second_back(1))
    sents[1][0]()

    per = width // LANES

    def pack(ref, row, value):
        for i in range(value.shape[1] // LANES):
            ref[row + i : row + i + 1, :] = value[:, i * LANES : (i + 1) * LANES]

    def unpack(ref, row, size):
        return jnp.concatenate([ref[row + i : row + i + 1, :] for i in range(size // LANES)], axis=1)

    for line in range(4):
        pack(early, line * per, gv[2 + line : 3 + line, :])
    pack(early, 4 * per, gv[8:9, 0:hidden])

    def vector_z(ref, recv, size):
        return [send(ref.at[0:size], recv.at[k - 1], zpeer(k)) for k in reversed(zs)]

    def vector_near(copies, ref, recv, size, near):
        for copy in copies:
            complete(copy)
        value = ref[0:size]
        for k in zs:
            value = value + recv[k - 1]
        ref[0:size] = value
        return send(ref, near, sib)

    def vector_far(copy, ref, near, recv):
        complete(copy)
        ref[...] = ref[...] + near[...]
        return [send(ref, recv.at[k - 1], plane(k)) for k in planes]

    def vector_last(copies, ref, recv):
        for copy in copies:
            complete(copy)
        value = ref[...]
        for k in planes:
            value = value + recv[k - 1]
        ref[...] = value

    vector_copies = vector_z(early, early_z, 4 * per)

    def out_grad(step, carry):
        at = lane_at(step, TILE)
        part = jnp.concatenate([mixed[rows_at(c, z), at] for c in range(2)], axis=0)
        out = tn(gown[...], part).astype(BF16)
        b_wot[:, :, :, at] = out.reshape(group, 2, piece, TILE)
        return carry

    steps(n_t * wide // TILE, out_grad)
    wot_near = grad_near(b_wot, s_wot)
    q_passed = ctx_forward(q_started, at_q)
    stat_passed = ctx_forward(stat_started, at_stat)
    ctx_finish(q_started, q_passed)
    ctx_finish(stat_started, stat_passed)
    for image in range(images):
        stacked = stack_heads(qkv[image, own, wide : 2 * wide])
        scores = nt(stacked, qkv[image, :, 0:wide]) * scale
        for h in range(heads):
            line = image * heads + h
            level = stat[0, line : line + 1, :]
            for other in range(1, n_ctx):
                level = level + stat[other, line : line + 1, :]
            block = scores[h * slots : (h + 1) * slots]
            block = jnp.where(row_live[image], block, neg_big)
            wk[image, h * slots : (h + 1) * slots, :] = jnp.exp(block - level)


    def block_rows(c):
        sents[c][1]()
        value = first[rows_at(c, z), :] + arrived(parts, recvs, c, 0, sizes_of[c]) + vx[5:6, :]
        value = jnp.where(own_live[slot_part(c)], value, 0.0)
        block_own[slot_part(c), :] = value.astype(BF16)
        passing = to_all(block_own, out_block, c)
        for at in pieces(c):
            passing[2](at)
        return passing

    def at_do(c):
        def at(index):
            first_row = index * slots + starts[c]
            return do.at[:, pl.ds(pl.multiple_of(first_row, ROWS), sizes_of[c]), :]

        return at

    tail = [block_rows(0)]
    do_started = []
    for c in range(2):
        for copy in to_heads[c]:
            copy.wait_recv()
        do_started.append(ctx_start(at_do(c)))

    for image in range(images):
        stacked = stack_heads(do[image, own, :])
        grad_probs = nt(stacked, qkv[image, :, 2 * wide : 3 * wide])
        weights = wq[image]
        along = jnp.sum(grad_probs * weights, axis=-1, keepdims=True)
        put_rows(alng, image, along)
        grad_scores = (weights * (grad_probs - along)).astype(BF16)
        out = pick_heads(nn(grad_scores, qkv[image, :, wide : 2 * wide])) * scale
        split_rows(dqkv, image, slice(0, wide), out.astype(BF16))

    def at_along(index):
        return alng.at[index]

    along_started = ctx_start(at_along)
    vector_copy = vector_near(vector_copies, early, early_z, 4 * per, early_sib)
    tail[0][0]()
    tail.append(block_rows(1))
    wot_grad_far = grad_halves(wot_near, b_wot, s_wot, t_wot, r_wot)
    early_far = vector_far(vector_copy, early, early_sib, early_plane)
    do_passed = [ctx_forward(do_started[c], at_do(c)) for c in range(2)]
    along_passed = ctx_forward(along_started, at_along)
    for c in range(2):
        ctx_finish(do_started[c], do_passed[c])
    ctx_finish(along_started, along_passed)

    for image in range(images):
        stacked = stack_heads(qkv[image, own, 2 * wide : 3 * wide])
        grad_probs = nt(stacked, do[image])
        weights = wk[image]
        lines = []
        for h in range(heads):
            line = image * heads + h
            level = alng[0, line : line + 1, :]
            for other in range(1, n_ctx):
                level = level + alng[other, line : line + 1, :]
            lines.append(grad_probs[h * slots : (h + 1) * slots] - level)
        grad_scores = (weights * jnp.concatenate(lines, axis=0)).astype(BF16)
        out = pick_heads(nn(grad_scores, qkv[image, :, 0:wide])) * scale
        split_rows(dqkv, image, slice(wide, 2 * wide), out.astype(BF16))
        out = pick_heads(nn(weights.astype(BF16), do[image]))
        split_rows(dqkv, image, slice(2 * wide, 3 * wide), out.astype(BF16))

    def in_back(c):
        at_rows = chunk(c)

        def one(step, carry):
            out = None
            for j in range(3):
                weight = g_win[j, pl.ds(step * some, some)].reshape(TILE, wide)
                term = nt(dqkv[at_rows, j * wide : (j + 1) * wide], weight)
                out = term if out is None else out + term
            part1[at_rows, lane_at(step, TILE)] = out.astype(BF16)
            return carry

        steps(width // TILE, one)
        return scatter(part1, recv1, relay1, c)

    sent1 = [in_back(c) for c in range(2)]
    for c in range(2):
        sent1[c][2]()
    sums = [0.0, 0.0]
    for row in range(0, rows, 2 * BLOCK):
        term = part1[row : row + 2 * BLOCK, :].astype(F32)
        weighted = term * n1[row : row + 2 * BLOCK, :]
        sums[0] = sums[0] + jnp.sum(weighted, axis=0, keepdims=True)
        sums[1] = sums[1] + jnp.sum(term, axis=0, keepdims=True)
    for line, value in enumerate(sums):
        pack(late, line * per, value)
    late[2 * per :, :] = jnp.zeros((late.shape[0] - 2 * per, LANES), F32)
    for j, start in enumerate((0, 2 * wide)):
        value = jnp.sum(dqkv[:, start : start + wide].astype(F32), axis=0, keepdims=True)
        pack(late, 2 * per + j * (wide // LANES), value)
    vector_copies = vector_z(late, late_z, 2 * per)
    tail[1][0]()
    wup_far = grad_halves(wup_near, b_wup, s_wup, t_wup, r_wup)
    wot_grad_far = grad_onward(wot_grad_far, t_wot, r_wot)

    for j in range(3):
        out = tn(h1[...], dqkv[:, j * wide : (j + 1) * wide]).astype(BF16)
        b_win[j] = out.reshape(group, 2, piece, wide)
    win_near = send(b_win.at[:, :, 1 - core], s_win, sib)
    sent1[0][0]()
    wup_far = grad_onward(wup_far, t_wup, r_wup)
    win_near.wait_recv()
    for j in range(3):
        both = b_win[j, :, pl.ds(core, 1)].reshape(group, piece, wide).astype(F32)
        t_win[:, j] = (both + s_win[j].astype(F32)).astype(BF16)
    win_far = [send(t_win.at[flip(me, k)], r_win.at[k - 1], plane(k)) for k in reversed(planes)]

    sent1[1][0]()
    def first_back(c, at):
        sent1[c][1]((at,))
        normed, inv = norm_parts(tok[block_at(c, z, at), :].astype(F32))
        grad = arrived(part1, recv1, c, at, ROWS)
        there = slots_at(c, at)
        value = gfirst[there, :] + norm_back(grad, normed, inv, vx[0:1, :])
        tokens_own[there, :] = value.astype(BF16)
        tail[2 + c][2](at)

    tail += [to_all(tokens_own, out_tokens, c) for c in range(2)]
    for at in pieces(0):
        first_back(0, at)
    for at in pieces(1)[:-1]:
        first_back(1, at)
    tail[2][0]()
    first_back(1, pieces(1)[-1])
    whole_rows = grad_sum(wot_grad_far, t_wot, r_wot)
    o_wot[...] = whole_rows.astype(BF16)
    to_owner = [
        send(o_wot.at[:, lane_at(flip(z, k), wide)], z_wot.at[k - 1], zpeer(k))
        for k in reversed(zs)
    ]

    vector_copy = vector_near(vector_copies, late, late_z, 2 * per, late_sib)
    tail[3][0]()
    late_far = vector_far(vector_copy, late, late_sib, late_plane)
    f_wdt[...] = turned(grad_sum(wdt_far, t_wdt, r_wdt), f_wdt)
    stays.append(local(f_wdt, out_wdt))
    f_wup[...] = grad_sum(wup_far, t_wup, r_wup)
    stays.append(local(f_wup, out_wup))
    vector_last(early_far, early, early_plane)
    f_win[...] = grad_sum(win_far, t_win, r_win)
    stays.append(local(f_win, out_win))
    for copy in to_owner:
        copy.wait_recv()
    value = o_wot[:, lane_at(z, wide)].astype(F32)
    for k in zs:
        value = value + z_wot[k - 1].astype(F32)
    f_wot[...] = turned(value, f_wot)
    stays.append(local(f_wot, out_wot))
    vector_last(late_far, late, late_plane)
    for line in range(2):
        gv[line : line + 1, :] = unpack(late, line * per, width)
        row = 2 * per + line * (wide // LANES)
        gv[9 + line : 10 + line, 0:wide] = unpack(late, row, wide)
    for line in range(4):
        gv[2 + line : 3 + line, :] = unpack(early, line * per, width)
    gv[8:9, 0:hidden] = unpack(early, 4 * per, hidden)
    stays.append(local(gv, out_vec))
    for passing in tail:
        passing[1]()
    for copy in pending:
        copy.wait_send()
    for flag, makes in guarded:

        @pl.when(flag)
        def _():
            for make in makes:
                make().wait_send()

    for copy in stays:
        copy.wait()


def finish_kernel(sizes, *refs):
    n_ctx, piece, cut, wide, hidden, width = sizes
    sources, results, held = refs[:6], refs[7:13], refs[21:27]
    smalls, own, vec, sems = refs[13:21], refs[27:35], refs[35], refs[36]
    shard = lax.axis_index("dp") * n_ctx + lax.axis_index("ctx")
    load = pltpu.make_async_copy(refs[6], vec, sems.at[2, 0])
    load.start()
    ins, outs = [], []
    for i in range(6):
        ins.append(pltpu.make_async_copy(sources[i], held[i], sems.at[0, i]))
        outs.append(pltpu.make_async_copy(held[i], results[i], sems.at[1, i]))
    for copy in ins:
        copy.start()

    def exact(left, right):
        parts, rest = [], left
        for _ in range(3):
            parts.append(rest.astype(BF16).astype(F32))
            rest = rest - parts[-1]
        count = left.shape[0]
        product = nn(jnp.concatenate(parts, axis=0).astype(BF16), right.astype(BF16))
        return product[0:count] + product[count : 2 * count] + product[2 * count :]

    heads = wide // HD
    lane = lax.broadcasted_iota(jnp.int32, (width, piece), 0)
    slot = lax.broadcasted_iota(jnp.int32, (width, piece), 1)
    one = jnp.where(lane - slot == shard * piece, 1.0, 0.0)
    lane = lax.broadcasted_iota(jnp.int32, (hidden, hidden // HD), 0)
    slot = lax.broadcasted_iota(jnp.int32, (hidden, hidden // HD), 1)
    by_unit = jnp.where(lane // HD == slot, 1.0, 0.0)
    load.wait()
    part = exact(vec[0:8, :], one)
    for line in range(6):
        own[line][...] = part[line : line + 1]
    channel = lax.broadcasted_iota(jnp.int32, (cut, hidden), 0)
    lane = lax.broadcasted_iota(jnp.int32, (cut, hidden), 1)
    chosen = jnp.where(lane % HD - channel == shard * cut, vec[8:9, 0:hidden], 0.0)
    own[6][...] = exact(chosen, by_unit)
    lane = lax.broadcasted_iota(jnp.int32, (wide, cut), 0)
    slot = lax.broadcasted_iota(jnp.int32, (wide, cut), 1)
    pick = jnp.where(lane % HD - slot == shard * cut, 1.0, 0.0)
    head = lax.broadcasted_iota(jnp.int32, (heads, wide), 0)
    lane = lax.broadcasted_iota(jnp.int32, (heads, wide), 1)
    for j in range(2):
        chosen = jnp.where(lane // HD == head, vec[9 + j : 10 + j, 0:wide], 0.0)
        own[7][j] = exact(chosen, pick)
    for i in range(8):
        outs.append(pltpu.make_async_copy(own[i], smalls[i], sems.at[2, 1 + i]))
        outs[-1].start()
    for i in range(6):
        ins[i].wait()
        outs[i].start()
    for copy in outs:
        copy.wait()


def on_device(
    mesh_shape,
    tokens,
    keep_mask,
    cotangent,
    first_gain,
    first_shift,
    attend_in,
    attend_bias,
    attend_out,
    out_bias,
    second_gain,
    second_shift,
    expand_in,
    expand_bias,
    contract_out,
    contract_bias,
):
    n_dp, n_ctx, n_t = mesh_shape
    images, slots, width = tokens.shape
    piece, _, wide = attend_in.shape
    hidden = expand_in.shape[1]
    cut = expand_bias.shape[1]
    rows = images * slots
    group = n_dp * n_ctx // 2
    total = slots * n_ctx
    heads = wide // HD
    turn = piece % LANES == 0
    per = width // LANES
    early_rows = 4 * per + hidden // LANES
    late_rows = 2 * per + 8 * ((2 * wide // LANES + 7) // 8)
    sizes = (n_dp, n_ctx, n_t, images, slots, width, wide, hidden, piece, cut)
    vmem = pl.BlockSpec(memory_space=pltpu.VMEM)
    hbm = pl.BlockSpec(memory_space=pl.ANY)
    scratch = [
        pltpu.VMEM((rows, width), BF16),
        pltpu.VMEM((rows, width), BF16),
        pltpu.VMEM((wide, piece), BF16),
        pltpu.VMEM((hidden, piece), BF16),
        pltpu.VMEM((2 * ROWS, LANES), F32),
        pltpu.VMEM((3, group, 2, piece, wide), BF16),
        pltpu.VMEM((group, 2, piece, n_t * wide), BF16),
        pltpu.VMEM((group, 2, piece, hidden), BF16),
        pltpu.VMEM((group, 2, piece, hidden), BF16),
        pltpu.VMEM((group, 2, 2 * ROWS, LANES), F32),
        pltpu.VMEM((ROWS, width), F32),
        pltpu.VMEM((rows, width), F32),
        pltpu.VMEM((rows, width), BF16),
        pltpu.VMEM((images, total, 3 * wide), BF16),
        pltpu.VMEM((images, heads * slots, total), F32),
        pltpu.VMEM((images, heads * slots, total), F32),
        pltpu.VMEM((n_ctx, images * heads, total), F32),
        pltpu.VMEM((n_ctx, images * heads, total), F32),
        pltpu.VMEM((rows, n_t * wide), BF16),
        pltpu.VMEM((rows, width), F32),
        pltpu.VMEM((rows, width), BF16),
        pltpu.VMEM((rows, hidden), F32),
        pltpu.VMEM((rows, hidden), BF16),
        pltpu.VMEM((rows, hidden), BF16),
        pltpu.VMEM((rows, width), BF16),
        pltpu.VMEM((rows, width), BF16),
        pltpu.VMEM((rows, width), BF16),
        pltpu.VMEM((2, slots, width), BF16),
        pltpu.VMEM((2, slots, width), BF16),
        pltpu.VMEM((2, slots, width), BF16),
        pltpu.VMEM((2, slots, width), BF16),
        pltpu.VMEM((2, slots, width), BF16),
        pltpu.VMEM((2, slots, width), BF16),
        pltpu.VMEM((slots, width), F32),
        pltpu.VMEM((rows, width), BF16),
        pltpu.VMEM((slots, width), BF16),
        pltpu.VMEM((slots, n_t * wide), BF16),
        pltpu.VMEM((images, total, wide), BF16),
        pltpu.VMEM((rows, 3 * wide), BF16),
        pltpu.VMEM((slots, width), BF16),
        pltpu.VMEM((slots, width), BF16),
        pltpu.VMEM((ROWS, width), F32),
        pltpu.VMEM((early_rows, LANES), F32),
        pltpu.VMEM((early_rows, LANES), F32),
        pltpu.VMEM((group - 1, early_rows, LANES), F32),
        pltpu.VMEM((n_t - 1, 4 * per, LANES), F32),
        pltpu.VMEM((late_rows, LANES), F32),
        pltpu.VMEM((late_rows, LANES), F32),
        pltpu.VMEM((group - 1, late_rows, LANES), F32),
        pltpu.VMEM((n_t - 1, 2 * per, LANES), F32),
        pltpu.VMEM((3, group, 2, piece, wide), BF16),
        pltpu.VMEM((group, 2, piece, n_t * wide), BF16),
        pltpu.VMEM((group, 2, piece, hidden), BF16),
        pltpu.VMEM((group, 2, piece, hidden), BF16),
        pltpu.VMEM((3, group, piece, wide), BF16),
        pltpu.VMEM((group, piece, n_t * wide), BF16),
        pltpu.VMEM((group, piece, hidden), BF16),
        pltpu.VMEM((group, piece, hidden), BF16),
        pltpu.VMEM((group, 3, piece, wide), BF16),
        pltpu.VMEM((group, piece, n_t * wide), BF16),
        pltpu.VMEM((group, piece, hidden), BF16),
        pltpu.VMEM((group, piece, hidden), BF16),
        pltpu.VMEM((group - 1, 3, piece, wide), BF16),
        pltpu.VMEM((group - 1, piece, n_t * wide), BF16),
        pltpu.VMEM((group - 1, piece, hidden), BF16),
        pltpu.VMEM((group - 1, piece, hidden), BF16),
        pltpu.VMEM((piece, n_t * wide), BF16),
        pltpu.VMEM((n_t - 1, piece, wide), BF16),
    ]
    shapes = (
        (3, piece, wide),
        (wide, piece) if turn else (piece, wide),
        (piece, hidden),
        (hidden, piece) if turn else (piece, hidden),
    )
    scratch += [pltpu.VMEM(shape, F32) for shape in shapes]
    copies = 260 + 20 * group
    scratch += [
        pltpu.SemaphoreType.DMA((copies,)),
        pltpu.SemaphoreType.DMA((copies,)),
        pltpu.SemaphoreType.DMA((48,)),
    ]
    results = [jax.ShapeDtypeStruct((rows, width), BF16)] * 2
    results += [jax.ShapeDtypeStruct(shape, F32) for shape in shapes]
    outs = pl.pallas_call(
        functools.partial(block_kernel, sizes),
        out_shape=(*results, jax.ShapeDtypeStruct((ROWS, width), F32)),
        in_specs=[hbm, hbm, vmem, hbm, hbm, hbm, hbm] + [vmem] * 8,
        out_specs=(hbm,) * 7,
        scratch_shapes=scratch,
        compiler_params=pltpu.CompilerParams(
            collective_id=0, has_side_effects=True, vmem_limit_bytes=63 << 20
        ),
    )(
        tokens.reshape(rows, width),
        cotangent.reshape(rows, width),
        keep_mask,
        jnp.transpose(attend_in, (1, 0, 2)),
        attend_out,
        expand_in,
        contract_out,
        *[
            v.reshape(1, piece)
            for v in (first_gain, first_shift, out_bias, second_gain, second_shift, contract_bias)
        ],
        expand_bias.T,
        attend_bias,
    )
    vector = jax.ShapeDtypeStruct((1, piece), F32)
    small = [vector] * 6 + [
        jax.ShapeDtypeStruct((cut, hidden // HD), F32),
        jax.ShapeDtypeStruct((2, heads, cut), F32),
    ]
    placed = pl.pallas_call(
        functools.partial(finish_kernel, (n_ctx, piece, cut, wide, hidden, width)),
        out_shape=(*results, *small),
        in_specs=[hbm] * 7,
        out_specs=(hbm,) * 14,
        scratch_shapes=[pltpu.VMEM(r.shape, r.dtype) for r in (*results, *small)]
        + [pltpu.VMEM((ROWS, width), F32), pltpu.SemaphoreType.DMA((3, 9))],
        compiler_params=pltpu.CompilerParams(vmem_limit_bytes=63 << 20),
    )(*outs)
    block_out, tokens_grad, d_win, d_wot, d_wup, d_wdt = placed[:6]
    vectors = [v.reshape(piece) for v in placed[6:12]]
    return (
        block_out.reshape(tokens.shape),
        tokens_grad.reshape(tokens.shape),
        vectors[0],
        vectors[1],
        jnp.transpose(d_win, (1, 0, 2)),
        placed[13],
        d_wot if turn else d_wot.T,
        vectors[2],
        vectors[3],
        vectors[4],
        d_wup,
        placed[12].T,
        d_wdt if turn else d_wdt.T,
        vectors[5],
    )


def solution(mesh):
    shape = (mesh.shape["dp"], mesh.shape["ctx"], mesh.shape["tensor"])
    vector = P(("dp", "ctx"))
    params = (
        vector,
        vector,
        P(("dp", "ctx"), None, "tensor"),
        P(None, "tensor", ("dp", "ctx")),
        P("tensor", ("dp", "ctx")),
        vector,
        vector,
        vector,
        P(("dp", "ctx"), "tensor"),
        P("tensor", ("dp", "ctx")),
        P("tensor", ("dp", "ctx")),
        vector,
    )
    rows = P("dp", "ctx", None)
    return jax.shard_map(
        functools.partial(on_device, shape),
        mesh=mesh,
        in_specs=(rows, P("dp", None), rows, *params),
        out_specs=(rows, rows, *params),
        check_vma=False,
    )
```
